32 devices in a mesh: lat: 8 (over z, core), lon: 4 (over y, x).
Axes of the slice: x: 2, y: 2, z: 4, core: 2. Of those that a mesh axis runs over, the one named last changes fastest.
Arguments:
- tokens: bfloat16 [4, 48, 96, 192], P(None, 'lat', 'lon'), may hold values from -6 to 6
- cotangent: bfloat16 [4, 48, 96, 192], P(None, 'lat', 'lon'), may hold values from -6 to 6
- norm_gain: float32 [192], replicated, may hold values from 0.1 to 1.9
- inproj_weight: bfloat16 [192, 576], replicated, may hold values from -0.4375 to 0.4375
- outproj_weight: bfloat16 [192, 192], replicated, may hold values from -0.4375 to 0.4375
- bias: float32 [2, 8, 6, 144, 144], P(None, 'lat'), may hold values from -4 to 4
Outputs:
- grad_input: bfloat16 [4, 48, 96, 192], P(None, 'lat', 'lon')
- bias_grad: float32 [2, 8, 6, 144, 144], P(None, 'lat', None, 'lon')
The draws below stay inside these ranges and needn't reach their ends.
All inputs are finite; a program needn't handle non-finite values.
Results may differ from the reference program's by a relative error of at most 0.017.
Values may be sent and summed in bfloat16 or wider, within the bound.
No kernel may reach another device: no remote copies, remote signals or barrier semaphores. Data moves between devices by JAX's collectives and lax.ppermute only.
A program may use at most 64 MiB of HBM per device.

```python
import jax
import jax.numpy as jnp
from jax import lax

C = 192
HEADS = 6
WZ = 2
WH = 6
WW = 12
WT = 144
ZWIN = 2
LATW = 8
LONW = 8
LEVELS = 4
ROWS = 48
COLS = 96


def steps_of(stream_key, dims, pieces, low, largest):
    level, own = 1.0, jax.random.fold_in(stream_key, 6)
    for axis_at, shards_of in pieces:
        heights = jnp.exp(jax.random.uniform(jax.random.fold_in(own, axis_at), (shards_of,), jnp.float32, low / len(pieces), largest / len(pieces)))
        level = level * jnp.repeat(heights, dims[axis_at] // shards_of).reshape([-1 if axis == axis_at else 1 for axis in range(len(dims))])
    return level


def bell_draw(key, extent, scale, most, shards=(), kind=jnp.bfloat16):
    array = jax.random.normal(key, extent, jnp.float32) * scale
    if len(shards) > 0:
        array = steps_of(key, extent, shards, -0.22, 0.18) * array
    return jnp.clip(array, min=-most, max=most).astype(kind)


def setup_inputs(seed: int = 0) -> dict:
    keys = jax.random.split(jax.random.key(seed), 7)
    return {
        "tokens": bell_draw(keys[0], (LEVELS, ROWS, COLS, C), 1.0, 6.0, ((1, 8), (2, 4))),
        "cotangent": bell_draw(keys[1], (LEVELS, ROWS, COLS, C), 2.0, 6.0, ((1, 8), (2, 4))),
        "norm_gain": jnp.clip(1.0 + 0.18 * jax.random.normal(keys[2], (C,), jnp.float32), 0.1, 1.9),
        "inproj_weight": bell_draw(keys[3], (C, 3 * C), C ** -0.5, 0.4375),
        "outproj_weight": bell_draw(keys[4], (C, C), C ** -0.5, 0.4375),
        "bias": bell_draw(keys[5], (ZWIN, LATW, HEADS, WT, WT), 1.0, 4.0, ((1, 8),), jnp.float32),
    }


epsilon = 1e-05

def allowed_pairs(level_win, lat_window, level_total, row_total):
    positions = jnp.arange(WZ * WH * WW, dtype=jnp.int32)
    level_pos = level_win * WZ + positions // (WH * WW)
    row_pos = lat_window * WH + positions // WW % WH
    labels = (level_pos >= level_total - WZ // 2).astype(jnp.int32) * 2 + (row_pos >= row_total - WH // 2).astype(jnp.int32)
    return labels[:, None] == labels[None, :]

def to_windows(field):
    level_total, row_total, col_total, channels = field.shape
    blocks = field.reshape(level_total // WZ, WZ, row_total // WH, WH, col_total // WW, WW, channels)
    blocks = blocks.transpose(0, 2, 4, 1, 3, 5, 6)
    return blocks.reshape(level_total // WZ, row_total // WH, col_total // WW, WZ * WH * WW, channels)

def from_windows(blocks):
    level_win, lat_win, lon_win, token_count, channels = blocks.shape
    field = blocks.reshape(level_win, lat_win, lon_win, WZ, WH, WW, channels)
    field = field.transpose(0, 3, 1, 4, 2, 5, 6)
    return field.reshape(level_win * WZ, lat_win * WH, lon_win * WW, channels)

def band_backward(band_in, band_grad, gain, inproj_weight, outproj_weight, band_bias, allowed):
    window_count, token_count, channels = band_in.shape
    head_count = band_bias.shape[0]
    head_dim = channels // head_count
    scaling = head_dim ** (-0.5)
    floats = band_in.astype(jnp.float32)
    centred = floats - lax.optimization_barrier(jnp.mean(floats, axis=-1, keepdims=True))
    inverse_rms = lax.rsqrt(lax.optimization_barrier(jnp.mean(centred * centred, axis=-1, keepdims=True)) + epsilon)
    standard = centred * inverse_rms
    normed = (standard * gain.astype(jnp.float32)).astype(jnp.bfloat16)
    projected = jnp.dot(normed.reshape(-1, channels), inproj_weight, preferred_element_type=jnp.float32).astype(jnp.bfloat16)
    projected = projected.reshape(window_count, token_count, 3, head_count, head_dim).astype(jnp.float32)
    query_rows = projected[:, :, 0]
    key_rows = projected[:, :, 1]
    value_rows = projected[:, :, 2]
    scores = jnp.einsum('nihd,njhd->nhij', query_rows, key_rows) * scaling + band_bias[None].astype(jnp.float32)
    weights = jnp.where(allowed[None, None], jnp.exp(scores), 0.0)
    probabilities = weights / lax.optimization_barrier(jnp.sum(weights, axis=-1, keepdims=True))
    upstream = jnp.dot(band_grad.reshape(-1, channels), outproj_weight.T, preferred_element_type=jnp.float32).astype(jnp.bfloat16)
    upstream = upstream.reshape(window_count, token_count, head_count, head_dim).astype(jnp.float32)
    dprobs = jnp.einsum('nihd,njhd->nhij', upstream, value_rows)
    inner_sum = lax.optimization_barrier(jnp.sum(probabilities * dprobs, axis=-1, keepdims=True))
    dscores = probabilities * (dprobs - inner_sum)
    bias_part = lax.optimization_barrier(jnp.sum(dscores, axis=0))
    probs_low = probabilities.astype(jnp.bfloat16).astype(jnp.float32)
    dscores_low = dscores.astype(jnp.bfloat16).astype(jnp.float32)
    dquery = (jnp.einsum('nhij,njhd->nihd', dscores_low, key_rows) * scaling).astype(jnp.bfloat16)
    dkeys = (jnp.einsum('nhij,nihd->njhd', dscores_low, query_rows) * scaling).astype(jnp.bfloat16)
    dvalues = jnp.einsum('nhij,nihd->njhd', probs_low, upstream).astype(jnp.bfloat16)
    dprojected = jnp.stack([dquery, dkeys, dvalues], axis=2).reshape(-1, 3 * channels)
    dnormed = jnp.dot(dprojected, inproj_weight.T, preferred_element_type=jnp.float32)
    dnormed = dnormed.reshape(window_count, token_count, channels)
    scaled = dnormed * gain.astype(jnp.float32)
    grad_moved = inverse_rms * (scaled - lax.optimization_barrier(jnp.mean(scaled, axis=-1, keepdims=True)) - standard * lax.optimization_barrier(jnp.mean(scaled * standard, axis=-1, keepdims=True)))
    return (grad_moved.astype(jnp.bfloat16), bias_part)

def reference(tokens, cotangent, norm_gain, inproj_weight, outproj_weight, bias):
    forward_shift = (-(WZ // 2), -(WH // 2), -(WW // 2))
    moved = jnp.roll(tokens, forward_shift, axis=(0, 1, 2))
    moved_grad = jnp.roll(cotangent, forward_shift, axis=(0, 1, 2))
    in_windows = to_windows(moved).reshape(ZWIN * LATW, LONW, WT, C)
    grad_windows = to_windows(moved_grad).reshape(ZWIN * LATW, LONW, WT, C)
    bias_flat = bias.reshape(ZWIN * LATW, HEADS, WT, WT)
    band_ids = jnp.arange(ZWIN * LATW, dtype=jnp.int32)

    def one_band(operands):
        band_in, band_grad, band_bias, band_id = operands
        allowed = allowed_pairs(band_id // LATW, band_id % LATW, LEVELS, ROWS)
        return band_backward(band_in, band_grad, norm_gain, inproj_weight, outproj_weight, band_bias, allowed)
    grad_blocks, bias_parts = lax.map(one_band, (in_windows, grad_windows, bias_flat, band_ids))
    grad_field = from_windows(grad_blocks.reshape(ZWIN, LATW, LONW, WT, C))
    grad_input = jnp.roll(grad_field, (WZ // 2, WH // 2, WW // 2), axis=(0, 1, 2))
    return (grad_input, bias_parts.reshape(ZWIN, LATW, HEADS, WT, WT))
```

```python
import functools

import jax
import jax.numpy as jnp
import numpy as np
from jax import lax
from jax.experimental import pallas as pl
from jax.experimental.pallas import tpu as pltpu
from jax.sharding import PartitionSpec as P

WZ = 2
WH = 6
WW = 12
WT = WZ * WH * WW
HALF_ROWS = WH // 2
HALF_COLS = WW // 2
SIDE = 8
LEVEL = WH * WW
MAIN = 128
REM = WT - MAIN
LOG2E = 1.4426950408889634
epsilon = 1e-05
F32 = jnp.float32
BF16 = jnp.bfloat16
NT = (((1,), (1,)), ((), ()))


def dot(a, b):
    return jnp.dot(a, b, preferred_element_type=F32)


def dot_nt(a, b):
    return lax.dot_general(a, b, NT, preferred_element_type=F32)


def round_up(value, to):
    return (value + to - 1) // to * to


def window_order(cols):
    windows = cols // WW
    part = HALF_ROWS * cols
    side = HALF_ROWS * SIDE
    table = np.zeros((windows * LEVEL, 2 * part + 2 * side), np.float32)
    for c in range(windows):
        for r in range(WH):
            for w in range(WW):
                col = c * WW + w + HALF_COLS
                low, row = divmod(r, HALF_ROWS)
                if col < cols:
                    at = low * part + row * cols + col
                else:
                    at = 2 * part + low * side + row * SIDE + col - cols
                table[c * LEVEL + r * WW + w, at] = 1.0
    return table


def query_choice(parts, heads):
    chunk = WT // parts
    table = np.zeros((parts, round_up(chunk, 16), MAIN + heads * REM), np.float32)
    for j in range(parts):
        for i in range(chunk):
            query = j * chunk + i
            if query < MAIN:
                table[j, i, query] = 1.0
            else:
                table[j, i, MAIN + query - MAIN :: REM] = 1.0
    return table


def send_kernel(tok, cot, below, right, corner):
    levels = tok.shape[0]
    for which, src in enumerate((tok, cot)):
        for level in range(levels):
            to = which * levels + level
            for row in range(HALF_ROWS):
                upper = src[level, row]
                below[to, row] = upper
                corner[to, row] = upper[:SIDE]
                right[to, row] = src[level, HALF_ROWS + row][:SIDE]


def prep_kernel(heads, lat_count, bias, inproj, bias_t, weights):
    channels = inproj.shape[0]
    level_windows = bias.shape[0]
    for part in range(3):
        weights[part] = inproj[:, part * channels : (part + 1) * channels]
    last_lat = lax.axis_index("lat") == lat_count - 1

    def labels(index, window):
        level_label = (index >= LEVEL) & (window == level_windows - 1)
        in_level = jnp.where(index >= LEVEL, index - LEVEL, index)
        row_label = (in_level >= LEVEL // 2) & last_lat
        return level_label.astype(jnp.int32) * 2 + row_label.astype(jnp.int32)

    for window in range(level_windows):
        key_index = lax.broadcasted_iota(jnp.int32, (WT, MAIN), 0)
        query_index = lax.broadcasted_iota(jnp.int32, (WT, MAIN), 1)
        allowed = labels(key_index, window) == labels(query_index, window)
        for head in range(heads):
            piece = jnp.transpose(bias[window, head, :MAIN, :]) * LOG2E
            bias_t[window, :, head * MAIN : (head + 1) * MAIN] = jnp.where(allowed, piece, -1e30)
        key_index = lax.broadcasted_iota(jnp.int32, (WT, heads * REM), 0)
        allowed = labels(key_index, window) == labels(jnp.full_like(key_index, WT - 1), window)
        rest = jnp.concatenate([bias[window, head, MAIN:, :] for head in range(heads)], axis=0)
        bias_t[window, :, heads * MAIN :] = jnp.where(allowed, jnp.transpose(rest) * LOG2E, -1e30)


def layer_kernel(
    heads, parts, tok, cot, below, right, corner, gain_ref, weights, outproj, bias_t, perm, perm_t, choice,
    g_inner, g_below, g_right, g_corner, *rest,
):
    chunks, bias_acc = rest[:-1], rest[-1]
    levels, _, cols, channels = tok.shape
    head_dim = channels // heads
    scaling = head_dim ** (-0.5)
    level_windows = levels // WZ
    lon_windows = cols // WW
    chunk = WT // parts
    wide = choice.shape[1]
    gain = gain_ref[...]
    wq, wk, wv = weights[0], weights[1], weights[2]
    out_w = outproj[...]
    lane_head = lax.broadcasted_iota(jnp.int32, (1, channels), 1) // head_dim
    head_masks = [(lane_head == head).astype(F32).astype(BF16) for head in range(heads)]
    rest_lane = lax.broadcasted_iota(jnp.int32, (1, heads * REM), 1) // REM
    rest_masks = [(rest_lane == head).astype(F32).astype(BF16) for head in range(heads)]
    me = lax.axis_index("lon")
    picks = jnp.concatenate(
        [choice[lax.rem(me + d, parts)] for d in range(parts)], axis=0
    )

    def gathered(source, offset, level):
        rows = [source[level, HALF_ROWS + row] for row in range(HALF_ROWS)]
        for piece in (below, right, corner):
            rows += [piece[offset + level, row] for row in range(HALF_ROWS)]
        stacked = jnp.concatenate([row.astype(F32) for row in rows], axis=0).astype(BF16)
        return dot(perm[...], stacked)

    def stack_heads(value):
        main = [value[:MAIN] * mask for mask in head_masks]
        left = [value[MAIN:] * mask for mask in head_masks]
        return jnp.concatenate(main + left, axis=0)

    def level_window(window, _):
        at = [lax.rem(window * WZ + WZ // 2 + li, levels) for li in range(WZ)]
        t_parts = [gathered(tok, 0, level) for level in at]
        g_parts = [gathered(cot, levels, level) for level in at]
        grads = []
        for c in range(lon_windows):
            cut = slice(c * LEVEL, (c + 1) * LEVEL)
            t = jnp.concatenate([part[cut] for part in t_parts], axis=0)
            g = jnp.concatenate([part[cut] for part in g_parts], axis=0).astype(BF16)
            centred = t - jnp.mean(t, axis=-1, keepdims=True)
            inverse_rms = lax.rsqrt(jnp.mean(centred * centred, axis=-1, keepdims=True) + epsilon)
            standard = centred * inverse_rms
            normed = (standard * gain).astype(BF16)
            q = dot(normed, wq).astype(BF16)
            k32 = dot(normed, wk)
            k = k32.astype(BF16)
            k_t = jnp.transpose(k32).astype(BF16)
            v = dot(normed, wv).astype(BF16)
            u = dot_nt(g, out_w).astype(BF16)
            qs = stack_heads(q)
            us = stack_heads(u)
            total = qs.shape[0]
            p_low, ds_low, dq_t = [], [], []
            dq_rest = None
            for start in range(0, total, 2 * MAIN):
                stop = min(start + 2 * MAIN, total)
                s = dot_nt(k, qs[start:stop])
                dp = dot_nt(v, us[start:stop])
                e = jnp.exp2(s * (scaling * LOG2E) + bias_t[window, :, start:stop])
                p = e * (1.0 / jnp.sum(e, axis=0, keepdims=True))
                ds = p * (dp - jnp.sum(p * dp, axis=0, keepdims=True))
                if c == 0:
                    bias_acc[:, start:stop] = ds
                else:
                    bias_acc[:, start:stop] += ds
                p_low.append(p.astype(BF16))
                low = ds.astype(BF16)
                ds_low.append(low)
                if stop - start == 2 * MAIN:
                    head = start // MAIN
                    both = dot(k_t[head * head_dim : (head + 2) * head_dim], low)
                    dq_t += [both[:head_dim, :MAIN], both[head_dim:, MAIN:]]
                else:
                    flat = dot(jnp.transpose(ds).astype(BF16), k)
                    dq_rest = flat[:REM]
                    for head in range(1, heads):
                        dq_rest = jnp.where(
                            lane_head == head, flat[head * REM : (head + 1) * REM], dq_rest
                        )
            dq = jnp.concatenate([jnp.transpose(jnp.concatenate(dq_t, axis=0)), dq_rest], axis=0)
            dq = (dq * scaling).astype(BF16)
            dk = (dot(jnp.concatenate(ds_low, axis=1), qs) * scaling).astype(BF16)
            dv = dot(jnp.concatenate(p_low, axis=1), us).astype(BF16)
            scaled = (dot_nt(dq, wq) + dot_nt(dk, wk) + dot_nt(dv, wv)) * gain
            grads.append(
                inverse_rms
                * (
                    scaled
                    - jnp.mean(scaled, axis=-1, keepdims=True)
                    - standard * jnp.mean(scaled * standard, axis=-1, keepdims=True)
                )
            )
        for li, level in enumerate(at):
            rows = slice(li * LEVEL, (li + 1) * LEVEL)
            joined = jnp.concatenate([grad[rows] for grad in grads], axis=0).astype(BF16)
            spread = dot(perm_t[...], joined)
            base = 0
            for out, width in ((g_inner, cols), (g_below, cols), (g_right, SIDE), (g_corner, SIDE)):
                for row in range(HALF_ROWS):
                    out[level, row] = spread[base : base + width].astype(BF16)
                    base += width
        left = bias_acc[:, heads * MAIN :].astype(BF16)
        for head in range(heads):
            mine = bias_acc[:, head * MAIN : (head + 1) * MAIN].astype(BF16)
            turned = dot_nt(picks[:, :MAIN], mine) + dot_nt(picks[:, MAIN:] * rest_masks[head], left)
            for d in range(parts):
                chunks[d][window * heads + head] = turned[d * wide : d * wide + chunk].astype(BF16)
        return 0

    lax.fori_loop(0, level_windows, level_window, 0)


def join_kernel(g_inner, below, right, corner, *rest):
    chunks, (grad_input, bias_grad) = rest[:-2], rest[-2:]
    levels, _, cols, _ = g_inner.shape
    for level in range(levels):
        for row in range(HALF_ROWS):
            for base, wide, side in ((0, below, corner), (HALF_ROWS, g_inner, right)):
                whole = wide[level, row].astype(F32)
                first = whole[:SIDE] + side[level, row].astype(F32)
                joined = jnp.concatenate([first, whole[SIDE:]], axis=0)
                grad_input[level, base + row] = joined.astype(BF16)
    for i in range(bias_grad.shape[0]):
        total = chunks[0][i].astype(F32)
        for other in chunks[1:]:
            total += other[i].astype(F32)
        bias_grad[i] = total


def vmem(count):
    return [pl.BlockSpec(memory_space=pltpu.VMEM)] * count


def call(kernel, outs, args, flops=0, scratch=()):
    moved = sum(x.size * x.dtype.itemsize for x in list(args) + list(outs))
    return pl.pallas_call(
        kernel,
        out_shape=outs,
        in_specs=vmem(len(args)),
        out_specs=vmem(len(outs)),
        scratch_shapes=list(scratch),
        compiler_params=pltpu.CompilerParams(vmem_limit_bytes=40 * 2**20),
        cost_estimate=pl.CostEstimate(flops=flops, bytes_accessed=moved, transcendentals=0),
    )(*args)


def shift(value, rows, cols):
    lat_count, lon_count = lax.axis_size("lat"), lax.axis_size("lon")
    pairs = []
    for i in range(lat_count):
        for j in range(lon_count):
            to = (i + rows) % lat_count * lon_count + (j + cols) % lon_count
            pairs.append((i * lon_count + j, to))
    return lax.ppermute(value, ("lat", "lon"), pairs)


def local(tokens, cotangent, norm_gain, inproj_weight, outproj_weight, bias):
    levels, rows, cols, channels = tokens.shape
    level_windows, _, heads = bias.shape[:3]
    lat_count, lon_count = lax.axis_size("lat"), lax.axis_size("lon")
    chunk = WT // lon_count
    struct = jax.ShapeDtypeStruct

    wide = (HALF_ROWS, cols, channels)
    side = (HALF_ROWS, SIDE, channels)
    below, right, corner = call(
        send_kernel,
        [struct((2 * levels,) + shape, BF16) for shape in (wide, side, side)],
        (tokens, cotangent),
    )
    below = shift(below, -1, 0)
    right = shift(right, 0, -1)
    corner = shift(corner, -1, -1)
    bias_t, weights = call(
        functools.partial(prep_kernel, heads, lat_count),
        [
            struct((level_windows, WT, heads * WT), F32),
            struct((3, channels, channels), BF16),
        ],
        (bias.reshape(level_windows, heads, WT, WT), inproj_weight),
        flops=10**8,
    )
    order = window_order(cols)
    results = call(
        functools.partial(layer_kernel, heads, lon_count),
        [struct((levels,) + shape, BF16) for shape in (wide, wide, side, side)]
        + [struct((level_windows * heads, chunk, WT), BF16)] * lon_count,
        (
            tokens, cotangent, below, right, corner, norm_gain.reshape(1, channels),
            weights, outproj_weight, bias_t,
            jnp.asarray(order, BF16), jnp.asarray(order.T, BF16),
            jnp.asarray(query_choice(lon_count, heads), BF16),
        ),
        flops=10**9,
        scratch=[pltpu.VMEM((WT, heads * WT), F32)],
    )
    g_inner, g_below, g_right, g_corner = results[:4]
    chunks = results[4:]
    below = shift(g_below, 1, 0)
    right = shift(g_right, 0, 1)
    corner = shift(g_corner, 1, 1)
    arrived = [chunks[0]] + [shift(chunks[d], 0, d) for d in range(1, lon_count)]
    grad_input, bias_grad = call(
        join_kernel,
        [
            struct((levels, rows, cols, channels), BF16),
            struct((level_windows * heads, chunk, WT), F32),
        ],
        [g_inner, below, right, corner] + arrived,
    )
    return grad_input, bias_grad.reshape(level_windows, 1, heads, chunk, WT)


def solution(mesh):
    placed = (
        P(None, "lat", "lon", None),
        P(None, "lat", "lon", None),
        P(),
        P(),
        P(),
        P(None, "lat", None, None, None),
    )
    return jax.shard_map(
        local,
        mesh=mesh,
        in_specs=placed,
        out_specs=(P(None, "lat", "lon", None), P(None, "lat", None, "lon", None)),
        check_vma=False,
    )
```

```python
import functools

import jax
import jax.numpy as jnp
import numpy as np
from jax import lax
from jax.experimental import pallas as pl
from jax.experimental.pallas import tpu as pltpu
from jax.sharding import PartitionSpec as P

WZ = 2
WH = 6
WW = 12
WT = WZ * WH * WW
HALF_ROWS = WH // 2
HALF_COLS = WW // 2
SIDE = 8
LEVEL = WH * WW
LANES = 128
LOG2E = 1.4426950408889634
epsilon = 1e-05
F32 = jnp.float32
BF16 = jnp.bfloat16
NT = (((1,), (1,)), ((), ()))


def dot(a, b):
    return jnp.dot(a, b, preferred_element_type=F32)


def dot_nt(a, b):
    return lax.dot_general(a, b, NT, preferred_element_type=F32)


def round_up(value, to):
    return (value + to - 1) // to * to


class Chunks:
    def __init__(self, parts, heads):
        self.parts, self.heads = parts, heads
        self.size = WT // parts
        self.main = self.size // 16 * 16
        self.rest = self.size - self.main
        self.rest_rows = round_up(heads * self.rest, 16)
        self.rows = self.main + self.rest_rows
        self.used = heads * self.main + self.rest_rows
        self.width = round_up(self.used, LANES)

    def queries(self):
        table = np.zeros((self.parts, self.rows, WT), np.float32)
        for j in range(self.parts):
            for i in range(self.main):
                table[j, i, j * self.size + i] = 1.0
            for h in range(self.heads):
                for i in range(self.rest):
                    table[j, self.main + h * self.rest + i, j * self.size + self.main + i] = 1.0
        return table

    def columns(self):
        table = np.zeros((self.parts, 1, self.width), np.int32)
        for j in range(self.parts):
            for h in range(self.heads):
                at = j * self.size
                table[j, 0, h * self.main : (h + 1) * self.main] = at + np.arange(self.main)
                low = self.heads * self.main + h * self.rest
                table[j, 0, low : low + self.rest] = at + self.main + np.arange(self.rest)
        return table


def window_order(cols):
    windows = cols // WW
    part, side = HALF_ROWS * cols, HALF_ROWS * SIDE
    table = np.zeros((windows * WT, WZ * (2 * part + 2 * side)), np.float32)
    for c in range(windows):
        for z in range(WZ):
            for r in range(WH):
                for w in range(WW):
                    col = c * WW + w + HALF_COLS
                    low, row = divmod(r, HALF_ROWS)
                    if col < cols:
                        at = WZ * low * part + z * part + row * cols + col
                    else:
                        at = WZ * 2 * part + WZ * low * side + z * side + row * SIDE + col - cols
                    table[((c * WZ + z) * WH + r) * WW + w, at] = 1.0
    return table


def send_kernel(tok_hbm, cot_hbm, inner, below, right, corner, tok, cot, sems):
    copies = [
        pltpu.make_async_copy(tok_hbm, tok, sems.at[0]),
        pltpu.make_async_copy(cot_hbm, cot, sems.at[1]),
    ]
    for copy in copies:
        copy.start()
    for copy in copies:
        copy.wait()
    levels, channels = tok.shape[0], tok.shape[3]

    def packed(level, row):
        t, g = tok[level, row].astype(F32), cot[level, row].astype(F32)
        return jnp.concatenate([t[:, :LANES], g[:, :LANES], t[:, LANES:], g[:, LANES:]], axis=1)

    for a in range(levels // WZ):
        at = [(a * WZ + WZ // 2 + z) % levels for z in range(WZ)]
        low = [packed(level, row) for level in at for row in range(HALF_ROWS)]
        high = [packed(level, HALF_ROWS + row) for level in at for row in range(HALF_ROWS)]
        below[a] = jnp.concatenate(low, axis=0).astype(BF16)
        inner[a] = jnp.concatenate(high, axis=0).astype(BF16)
        corner[a] = jnp.concatenate([piece[:SIDE] for piece in low], axis=0).astype(BF16)
        right[a] = jnp.concatenate([piece[:SIDE] for piece in high], axis=0).astype(BF16)


def prep_kernel(chunks, lat_count, bias, inproj, columns, bias_t, weights):
    channels = inproj.shape[0]
    level_windows = bias.shape[0]
    for part in range(3):
        weights[part] = inproj[:, part * channels : (part + 1) * channels]
    last_lat = lax.axis_index("lat") == lat_count - 1
    me = lax.axis_index("lon")
    parts, size, main = chunks.parts, chunks.size, chunks.main

    def labels(index, window):
        level_label = (index >= LEVEL) & (window == level_windows - 1)
        in_level = jnp.where(index >= LEVEL, index - LEVEL, index)
        row_label = (in_level >= LEVEL // 2) & last_lat
        return level_label.astype(jnp.int32) * 2 + row_label.astype(jnp.int32)

    key_index = lax.broadcasted_iota(jnp.int32, (WT, chunks.width), 0)
    for window in range(level_windows):
        key_labels = labels(key_index, window)
        for j in range(parts):
            heads = range(chunks.heads)
            low = j * size
            rows = []
            if main:
                rows += [bias[window, h, low : low + main, :] for h in heads]
            if chunks.rest:
                rows += [bias[window, h, low + main : low + size, :] for h in heads]
            spare = chunks.width - chunks.heads * size
            if spare:
                rows.append(jnp.zeros((spare, WT), F32))
            turned = jnp.transpose(jnp.concatenate(rows, axis=0)) * LOG2E
            allowed = key_labels == labels(columns[j], window)
            bias_t[window, lax.rem(j - me + parts, parts)] = jnp.where(allowed, turned, -1e30)


def head_masks(chunks, channels):
    head_dim = channels // chunks.heads
    lane_head = lax.broadcasted_iota(jnp.int32, (1, channels), 1) // head_dim
    lanes = [lane_head == h for h in range(chunks.heads)]
    rest = None
    if chunks.rest:
        row = lax.broadcasted_iota(jnp.int32, (chunks.rest_rows, channels), 0)
        lane = lax.broadcasted_iota(jnp.int32, (chunks.rest_rows, channels), 1) // head_dim
        rest = jnp.zeros((chunks.rest_rows, channels), F32)
        for h in range(chunks.heads):
            inside = (row >= h * chunks.rest) & (row < (h + 1) * chunks.rest) & (lane == h)
            rest = jnp.where(inside, 1.0, rest)
    return lanes, rest


def stack_heads(chunks, value, d, lane_masks, rest_mask):
    low = d * chunks.rows
    main = value[low : low + chunks.main]
    pieces = [main * mask for mask in lane_masks] if chunks.main else []
    if chunks.rest:
        pieces.append(value[low + chunks.main : low + chunks.rows] * rest_mask)
    if chunks.width > chunks.used:
        pieces.append(jnp.zeros((chunks.width - chunks.used, value.shape[1]), value.dtype))
    return jnp.concatenate(pieces, axis=0)


def rolled(ref, parts):
    me = lax.axis_index("lon")
    return jnp.concatenate([ref[lax.rem(me + d, parts)] for d in range(parts)], axis=0)


def scores_kernel(
    chunks, inner, below, right, corner, gain_ref, weights, outproj, bias_t, perm, queries,
    standard_out, scale_out, keys_out, query_out, up_out, p_out, ds_out, *rest,
):
    sent, bias_acc = rest[:-1], rest[-1]
    parts, width = chunks.parts, chunks.width
    channels = outproj.shape[0]
    scaling = (channels // chunks.heads) ** (-0.5)
    windows = perm.shape[0] // WT
    gain = gain_ref[...]
    lanes, rest_mask = head_masks(chunks, channels)
    lanes = [mask.astype(F32).astype(BF16) for mask in lanes]
    rest_mask = rest_mask.astype(BF16) if chunks.rest else None
    choose = rolled(queries, parts)

    def level_window(a, _):
        pieces = jnp.concatenate([inner[a], below[a], right[a], corner[a]], axis=0)
        moved = dot(perm[...], pieces)
        spare = channels - LANES
        t = jnp.concatenate([moved[:, :LANES], moved[:, 2 * LANES : 2 * LANES + spare]], axis=1)
        g = jnp.concatenate([moved[:, LANES : 2 * LANES], moved[:, 2 * LANES + spare :]], axis=1)
        centred = t - jnp.mean(t, axis=-1, keepdims=True)
        inverse_rms = lax.rsqrt(jnp.mean(centred * centred, axis=-1, keepdims=True) + epsilon)
        standard = centred * inverse_rms
        standard_out[a] = standard
        scale_out[a] = jnp.broadcast_to(inverse_rms, (windows * WT, LANES))
        normed = (standard * gain).astype(BF16)
        q = dot(normed, weights[0]).astype(BF16)
        k = dot(normed, weights[1]).astype(BF16)
        v = dot(normed, weights[2]).astype(BF16)
        u = dot_nt(g.astype(BF16), outproj[...]).astype(BF16)
        keys_out[a] = k
        for c in range(windows):
            cut = slice(c * WT, (c + 1) * WT)
            query = dot(choose, q[cut]).astype(BF16)
            up = dot(choose, u[cut]).astype(BF16)
            query_out[a, c] = query
            up_out[a, c] = up
            for d in range(parts):
                at = slice(d * width, (d + 1) * width)
                s = dot_nt(k[cut], stack_heads(chunks, query, d, lanes, rest_mask))
                dp = dot_nt(v[cut], stack_heads(chunks, up, d, lanes, rest_mask))
                e = jnp.exp2(s * (scaling * LOG2E) + bias_t[a, d])
                p = e * (1.0 / jnp.sum(e, axis=0, keepdims=True))
                ds = p * (dp - jnp.sum(p * dp, axis=0, keepdims=True))
                p_out[a, c, :, at] = p.astype(BF16)
                ds_out[a, c, :, at] = ds.astype(BF16)
                if c > 0:
                    ds += bias_acc[d]
                if c == windows - 1:
                    sent[d][a] = ds.astype(BF16)
                else:
                    bias_acc[d] = ds
        return 0

    lax.fori_loop(0, inner.shape[0], level_window, 0)


def tokens_kernel(
    chunks, standard_in, scale_in, keys, queries_in, ups, p_in, ds_in, gain_ref, weights, perm_t, queries,
    g_inner, g_below, g_right, g_corner,
):
    parts, width = chunks.parts, chunks.width
    channels = keys.shape[-1]
    scaling = (channels // chunks.heads) ** (-0.5)
    windows = p_in.shape[1]
    gain = gain_ref[...]
    lanes, rest_mask = head_masks(chunks, channels)
    low_lanes = [mask.astype(F32).astype(BF16) for mask in lanes]
    low_rest = rest_mask.astype(BF16) if chunks.rest else None
    choose_t = jnp.transpose(rolled(queries, parts).astype(F32)).astype(BF16)

    def level_window(a, _):
        dqs, dks, dvs = [], [], []
        for c in range(windows):
            query, up = queries_in[a, c], ups[a, c]
            qs = jnp.concatenate(
                [stack_heads(chunks, query, d, low_lanes, low_rest) for d in range(parts)], axis=0
            )
            us = jnp.concatenate(
                [stack_heads(chunks, up, d, low_lanes, low_rest) for d in range(parts)], axis=0
            )
            ds = ds_in[a, c]
            dks.append((dot(ds, qs) * scaling).astype(BF16))
            dvs.append(dot(p_in[a, c], us).astype(BF16))
            flat = dot(jnp.transpose(ds), keys[a, c * WT : (c + 1) * WT])
            rows = []
            for d in range(parts):
                base = d * width
                if chunks.main:
                    picked = flat[base : base + chunks.main]
                    for h in range(1, chunks.heads):
                        low = base + h * chunks.main
                        picked = jnp.where(lanes[h], flat[low : low + chunks.main], picked)
                    rows.append(picked)
                if chunks.rest:
                    low = base + chunks.heads * chunks.main
                    rows.append(flat[low : low + chunks.rest_rows] * rest_mask)
            picked = (jnp.concatenate(rows, axis=0) * scaling).astype(BF16)
            dqs.append(dot(choose_t, picked).astype(BF16))
        dq, dk, dv = (jnp.concatenate(parts_of, axis=0) for parts_of in (dqs, dks, dvs))
        scaled = (dot_nt(dq, weights[0]) + dot_nt(dk, weights[1]) + dot_nt(dv, weights[2])) * gain
        standard = standard_in[a]
        inverse_rms = scale_in[a][:, :1]
        grad = inverse_rms * (
            scaled
            - jnp.mean(scaled, axis=-1, keepdims=True)
            - standard * jnp.mean(scaled * standard, axis=-1, keepdims=True)
        )
        spread = dot(perm_t[...], grad.astype(BF16)).astype(BF16)
        base = 0
        for out in (g_inner, g_below, g_right, g_corner):
            rows = out.shape[1]
            out[a] = spread[base : base + rows]
            base += rows
        return 0

    lax.fori_loop(0, p_in.shape[0], level_window, 0)


def join_kernel(inner, below, right, corner, grad_input):
    levels, _, cols, _ = grad_input.shape
    for a in range(levels // WZ):
        pieces = [ref[a].astype(F32) for ref in (below, corner, inner, right)]
        for z in range(WZ):
            level = (a * WZ + WZ // 2 + z) % levels
            for row in range(HALF_ROWS):
                at = z * HALF_ROWS + row
                for base, wide, side in ((0, *pieces[:2]), (HALF_ROWS, *pieces[2:])):
                    whole = wide[at * cols : (at + 1) * cols]
                    first = whole[:SIDE] + side[at * SIDE : (at + 1) * SIDE]
                    joined = jnp.concatenate([first, whole[SIDE:]], axis=0)
                    grad_input[level, base + row] = joined.astype(BF16)


def bias_kernel(chunks, *refs):
    arrived, bias_grad = refs[:-1], refs[-1]
    main, rest, heads = chunks.main, chunks.rest, chunks.heads
    for a in range(arrived[0].shape[0]):
        total = arrived[0][a].astype(F32)
        for other in arrived[1:]:
            total += other[a].astype(F32)
        turned = jnp.transpose(total)
        for h in range(heads):
            if main:
                bias_grad[a * heads + h, :main] = turned[h * main : (h + 1) * main]
            if rest:
                low = heads * main + h * rest
                bias_grad[a * heads + h, main:] = turned[low : low + rest]


def vmem(count):
    return [pl.BlockSpec(memory_space=pltpu.VMEM)] * count


def call(kernel, outs, args, flops=0, scratch=(), specs=None):
    moved = sum(x.size * x.dtype.itemsize for x in list(args) + list(outs))
    return pl.pallas_call(
        kernel,
        out_shape=outs,
        in_specs=specs or vmem(len(args)),
        out_specs=vmem(len(outs)),
        scratch_shapes=list(scratch),
        compiler_params=pltpu.CompilerParams(vmem_limit_bytes=40 * 2**20),
        cost_estimate=pl.CostEstimate(flops=flops, bytes_accessed=moved, transcendentals=0),
    )(*args)


def shift(value, rows, cols):
    lat_count, lon_count = lax.axis_size("lat"), lax.axis_size("lon")
    pairs = []
    for i in range(lat_count):
        for j in range(lon_count):
            to = (i + rows) % lat_count * lon_count + (j + cols) % lon_count
            pairs.append((i * lon_count + j, to))
    return lax.ppermute(value, ("lat", "lon"), pairs)


def local(tokens, cotangent, norm_gain, inproj_weight, outproj_weight, bias):
    levels, rows, cols, channels = tokens.shape
    level_windows, _, heads = bias.shape[:3]
    lat_count, lon_count = lax.axis_size("lat"), lax.axis_size("lon")
    chunks = Chunks(lon_count, heads)
    windows = cols // WW
    struct = jax.ShapeDtypeStruct
    wide, side = WZ * HALF_ROWS * cols, WZ * HALF_ROWS * SIDE
    gain = norm_gain.reshape(1, channels)
    order = window_order(cols)
    queries = jnp.asarray(chunks.queries(), BF16)

    inner, below, right, corner = call(
        send_kernel,
        [struct((level_windows, size, 2 * channels), BF16) for size in (wide, wide, side, side)],
        (tokens, cotangent),
        specs=[pl.BlockSpec(memory_space=pl.ANY)] * 2,
        scratch=[pltpu.VMEM(tokens.shape, BF16)] * 2 + [pltpu.SemaphoreType.DMA((2,))],
    )
    below = shift(below, -1, 0)
    right = shift(right, 0, -1)
    corner = shift(corner, -1, -1)
    bias_t, weights = call(
        functools.partial(prep_kernel, chunks, lat_count),
        [
            struct((level_windows, lon_count, WT, chunks.width), F32),
            struct((3, channels, channels), BF16),
        ],
        (bias.reshape(level_windows, heads, WT, WT), inproj_weight, jnp.asarray(chunks.columns())),
        flops=10**8,
    )
    per_window = (level_windows, windows)
    results = call(
        functools.partial(scores_kernel, chunks),
        [
            struct((level_windows, windows * WT, channels), F32),
            struct((level_windows, windows * WT, LANES), F32),
            struct((level_windows, windows * WT, channels), BF16),
            struct(per_window + (lon_count * chunks.rows, channels), BF16),
            struct(per_window + (lon_count * chunks.rows, channels), BF16),
            struct(per_window + (WT, lon_count * chunks.width), BF16),
            struct(per_window + (WT, lon_count * chunks.width), BF16),
        ]
        + [struct((level_windows, WT, chunks.width), BF16)] * lon_count,
        (
            inner, below, right, corner, gain, weights, outproj_weight, bias_t,
            jnp.asarray(order, BF16), queries,
        ),
        flops=10**9,
        scratch=[pltpu.VMEM((lon_count, WT, chunks.width), F32)],
    )
    kept, sent = results[:7], results[7:]
    arrived = [sent[0]] + [shift(sent[d], 0, d) for d in range(1, lon_count)]
    g_inner, below, right, corner = call(
        functools.partial(tokens_kernel, chunks),
        [struct((level_windows, size, channels), BF16) for size in (wide, wide, side, side)],
        (*kept, gain, weights, jnp.asarray(order.T, BF16), queries),
        flops=10**9,
    )
    below = shift(below, 1, 0)
    right = shift(right, 0, 1)
    corner = shift(corner, 1, 1)
    (bias_grad,) = call(
        functools.partial(bias_kernel, chunks),
        [struct((level_windows * heads, chunks.size, WT), F32)],
        arrived,
    )
    (grad_input,) = call(
        join_kernel, [struct(tokens.shape, BF16)], [g_inner, below, right, corner]
    )
    return grad_input, bias_grad.reshape(level_windows, 1, heads, chunks.size, WT)


def solution(mesh):
    placed = (
        P(None, "lat", "lon", None),
        P(None, "lat", "lon", None),
        P(),
        P(),
        P(),
        P(None, "lat", None, None, None),
    )
    return jax.shard_map(
        local,
        mesh=mesh,
        in_specs=placed,
        out_specs=(P(None, "lat", "lon", None), P(None, "lat", None, "lon", None)),
        check_vma=False,
    )
```

```python
import functools

import jax
import jax.numpy as jnp
import numpy as np
from jax import lax
from jax.experimental import pallas as pl
from jax.experimental.pallas import tpu as pltpu
from jax.sharding import PartitionSpec as P

WZ = 2
WH = 6
WW = 12
WT = WZ * WH * WW
HALF_ROWS = WH // 2
HALF_COLS = WW // 2
SIDE = 8
LEVEL = WH * WW
LANES = 128
LOG2E = 1.4426950408889634
epsilon = 1e-05
F32 = jnp.float32
BF16 = jnp.bfloat16
NT = (((1,), (1,)), ((), ()))


def dot(a, b):
    return jnp.dot(a, b, preferred_element_type=F32)


def dot_nt(a, b):
    return lax.dot_general(a, b, NT, preferred_element_type=F32)


def round_up(value, to):
    return (value + to - 1) // to * to


class Chunks:
    def __init__(self, parts, heads):
        self.parts, self.heads = parts, heads
        self.size = WT // parts
        self.main = self.size // 16 * 16
        self.rest = self.size - self.main
        self.rest_rows = round_up(heads * self.rest, 16)
        self.rows = self.main + self.rest_rows
        self.used = heads * self.main + self.rest_rows
        self.width = round_up(self.used, LANES)

    def queries(self):
        table = np.zeros((self.parts, self.rows, WT), np.float32)
        for j in range(self.parts):
            for i in range(self.main):
                table[j, i, j * self.size + i] = 1.0
            for h in range(self.heads):
                for i in range(self.rest):
                    table[j, self.main + h * self.rest + i, j * self.size + self.main + i] = 1.0
        return table

    def columns(self, j):
        lane = lax.broadcasted_iota(jnp.int32, (1, self.width), 1)
        low = self.heads * self.main
        main, left = lane, self.main + lane - low
        for h in range(1, self.heads):
            main -= jnp.where(lane >= h * self.main, self.main, 0)
            left -= jnp.where(lane >= low + h * self.rest, self.rest, 0)
        return j * self.size + jnp.where(lane < low, main, left)


def side_order(cols):
    part = HALF_ROWS * cols
    table = np.zeros((round_up(WZ * WH * HALF_COLS, 16), 2 * WZ * part), np.float32)
    for z in range(WZ):
        for r in range(WH):
            low, row = divmod(r, HALF_ROWS)
            for w in range(HALF_COLS):
                table[(z * WH + r) * HALF_COLS + w, (low * WZ + z) * part + row * cols + w] = 1.0
    return table


def window_order(cols, c):
    last = c == cols // WW - 1
    part = HALF_ROWS * cols
    near = 2 * WZ * part
    table = np.zeros((WT, near + last * round_up(WZ * WH * HALF_COLS, 16)), np.float32)
    for z in range(WZ):
        for r in range(WH):
            for w in range(WW):
                col = c * WW + w + HALF_COLS
                low, row = divmod(r, HALF_ROWS)
                if col < cols:
                    at = (low * WZ + z) * part + row * cols + col
                else:
                    at = near + (z * WH + r) * HALF_COLS + col - cols
                table[(z * WH + r) * WW + w, at] = 1.0
    return table


def send_kernel(tok_hbm, cot_hbm, inner, below, tok, cot, sems):
    copies = [
        pltpu.make_async_copy(tok_hbm, tok, sems.at[0]),
        pltpu.make_async_copy(cot_hbm, cot, sems.at[1]),
    ]
    for copy in copies:
        copy.start()
    for copy in copies:
        copy.wait()
    levels = tok.shape[0]

    def packed(level, row):
        t, g = tok[level, row].astype(F32), cot[level, row].astype(F32)
        return jnp.concatenate([t[:, :LANES], g[:, :LANES], t[:, LANES:], g[:, LANES:]], axis=1)

    for a in range(levels // WZ):
        at = [(a * WZ + WZ // 2 + z) % levels for z in range(WZ)]
        for out, base in ((below, 0), (inner, HALF_ROWS)):
            rows = [packed(level, base + row) for level in at for row in range(HALF_ROWS)]
            out[a] = jnp.concatenate(rows, axis=0).astype(BF16)


def side_kernel(inner, below, order, weights, side):
    for a in range(inner.shape[0]):
        side[a] = dot(order[...], jnp.concatenate([inner[a], below[a]], axis=0)).astype(BF16)


def prep_kernel(chunks, lat_count, bias_hbm, inproj_hbm, bias_t, weights, bias, inproj, sems):
    level_windows = bias.shape[0]
    copies = [
        pltpu.make_async_copy(bias_hbm.at[a], bias.at[a], sems.at[a]) for a in range(level_windows)
    ]
    copies.append(pltpu.make_async_copy(inproj_hbm, inproj, sems.at[level_windows]))
    for copy in copies:
        copy.start()
    last_lat = lax.axis_index("lat") == lat_count - 1
    me = lax.axis_index("lon")
    parts, size, main = chunks.parts, chunks.size, chunks.main

    def labels(index, window):
        level_label = (index >= LEVEL) & (window == level_windows - 1)
        in_level = jnp.where(index >= LEVEL, index - LEVEL, index)
        row_label = (in_level >= LEVEL // 2) & last_lat
        return level_label.astype(jnp.int32) * 2 + row_label.astype(jnp.int32)

    key_index = lax.broadcasted_iota(jnp.int32, (WT, chunks.width), 0)
    for window in range(level_windows):
        copies[window].wait()
        key_labels = labels(key_index, window)
        for j in range(parts):
            heads = range(chunks.heads)
            low = j * size
            rows = []
            if main:
                rows += [bias[window, h, low : low + main, :] for h in heads]
            if chunks.rest:
                rows += [bias[window, h, low + main : low + size, :] for h in heads]
            spare = chunks.width - chunks.heads * size
            if spare:
                rows.append(jnp.zeros((spare, WT), F32))
            turned = jnp.transpose(jnp.concatenate(rows, axis=0)) * LOG2E
            allowed = key_labels == labels(chunks.columns(j), window)
            bias_t[window, lax.rem(j - me + parts, parts)] = jnp.where(allowed, turned, -1e30)
    copies[-1].wait()
    channels = inproj.shape[0]
    for part in range(3):
        weights[part] = inproj[:, part * channels : (part + 1) * channels]


def head_masks(chunks, channels):
    head_dim = channels // chunks.heads
    lane_head = lax.broadcasted_iota(jnp.int32, (1, channels), 1) // head_dim
    lanes = [lane_head == h for h in range(chunks.heads)]
    rest = None
    if chunks.rest:
        row = lax.broadcasted_iota(jnp.int32, (chunks.rest_rows, channels), 0)
        lane = lax.broadcasted_iota(jnp.int32, (chunks.rest_rows, channels), 1) // head_dim
        rest = jnp.zeros((chunks.rest_rows, channels), F32)
        for h in range(chunks.heads):
            inside = (row >= h * chunks.rest) & (row < (h + 1) * chunks.rest) & (lane == h)
            rest = jnp.where(inside, 1.0, rest)
    return lanes, rest


def stack_heads(chunks, value, d, lane_masks, rest_mask):
    low = d * chunks.rows
    main = value[low : low + chunks.main]
    pieces = [main * mask for mask in lane_masks] if chunks.main else []
    if chunks.rest:
        pieces.append(value[low + chunks.main : low + chunks.rows] * rest_mask)
    if chunks.width > chunks.used:
        pieces.append(jnp.zeros((chunks.width - chunks.used, value.shape[1]), value.dtype))
    return jnp.concatenate(pieces, axis=0)


def rolled(ref, parts):
    me = lax.axis_index("lon")
    return jnp.concatenate([ref[lax.rem(me + d, parts)] for d in range(parts)], axis=0)


def scores_kernel(chunks, near, first, last, *refs):
    pieces, refs = refs[:near], refs[near:]
    gain_ref, weights, outproj, bias_t, perm, queries, *refs = refs
    before = None
    if not first:
        before, *refs = refs
    standard_out, scale_out, keys_out, query_out, up_out, p_out, ds_out, *totals = refs
    parts, width = chunks.parts, chunks.width
    channels = outproj.shape[0]
    spare = channels - LANES
    scaling = (channels // chunks.heads) ** (-0.5)
    lanes, rest_mask = head_masks(chunks, channels)
    lanes = [mask.astype(F32).astype(BF16) for mask in lanes]
    rest_mask = rest_mask.astype(BF16) if chunks.rest else None
    choose = rolled(queries, parts)
    level_windows = pieces[0].shape[0]
    ts, gs = [], []
    for a in range(level_windows):
        moved = dot(perm[...], jnp.concatenate([piece[a] for piece in pieces], axis=0))
        ts.append(jnp.concatenate([moved[:, :LANES], moved[:, 2 * LANES : 2 * LANES + spare]], axis=1))
        gs.append(jnp.concatenate([moved[:, LANES : 2 * LANES], moved[:, 2 * LANES + spare :]], axis=1))
    t = jnp.concatenate(ts, axis=0)
    g = jnp.concatenate(gs, axis=0).astype(BF16)
    centred = t - jnp.mean(t, axis=-1, keepdims=True)
    inverse_rms = lax.rsqrt(jnp.mean(centred * centred, axis=-1, keepdims=True) + epsilon)
    standard = centred * inverse_rms
    standard_out[...] = standard
    scale_out[...] = jnp.broadcast_to(inverse_rms, scale_out.shape)
    normed = (standard * gain_ref[...]).astype(BF16)
    q = dot(normed, weights[0]).astype(BF16)
    k = dot(normed, weights[1]).astype(BF16)
    v = dot(normed, weights[2]).astype(BF16)
    u = dot_nt(g, outproj[...]).astype(BF16)
    keys_out[...] = k
    for a in range(level_windows):
        cut = slice(a * WT, (a + 1) * WT)
        query = dot(choose, q[cut]).astype(BF16)
        up = dot(choose, u[cut]).astype(BF16)
        query_out[a] = query
        up_out[a] = up
        for d in range(parts):
            at = slice(d * width, (d + 1) * width)
            s = dot_nt(k[cut], stack_heads(chunks, query, d, lanes, rest_mask))
            dp = dot_nt(v[cut], stack_heads(chunks, up, d, lanes, rest_mask))
            e = jnp.exp2(s * (scaling * LOG2E) + bias_t[a, d])
            p = e * (1.0 / jnp.sum(e, axis=0, keepdims=True))
            ds = p * (dp - jnp.sum(p * dp, axis=0, keepdims=True))
            p_out[a, :, at] = p.astype(BF16)
            ds_out[a, :, at] = ds.astype(BF16)
            if not first:
                ds += before[a, d]
            if last:
                totals[d][a] = ds.astype(BF16)
            else:
                totals[0][a, d] = ds


def tokens_kernel(chunks, near, first, *refs):
    standard_in, scale_in, keys, queries_in, ups, p_in, ds_in, gain_ref, weights, perm_t, queries, *refs = refs
    before = None
    if not first:
        before, refs = refs[:2], refs[2:]
    outs = refs
    parts, width = chunks.parts, chunks.width
    channels = keys.shape[-1]
    scaling = (channels // chunks.heads) ** (-0.5)
    lanes, rest_mask = head_masks(chunks, channels)
    low_lanes = [mask.astype(F32).astype(BF16) for mask in lanes]
    low_rest = rest_mask.astype(BF16) if chunks.rest else None
    choose_t = jnp.transpose(rolled(queries, parts).astype(F32)).astype(BF16)
    level_windows = p_in.shape[0]
    dqs, dks, dvs = [], [], []
    for a in range(level_windows):
        query, up = queries_in[a], ups[a]
        qs = jnp.concatenate(
            [stack_heads(chunks, query, d, low_lanes, low_rest) for d in range(parts)], axis=0
        )
        us = jnp.concatenate(
            [stack_heads(chunks, up, d, low_lanes, low_rest) for d in range(parts)], axis=0
        )
        ds = ds_in[a]
        dks.append((dot(ds, qs) * scaling).astype(BF16))
        dvs.append(dot(p_in[a], us).astype(BF16))
        flat = dot(jnp.transpose(ds), keys[a * WT : (a + 1) * WT])
        rows = []
        for d in range(parts):
            base = d * width
            if chunks.main:
                picked = flat[base : base + chunks.main]
                for h in range(1, chunks.heads):
                    low = base + h * chunks.main
                    picked = jnp.where(lanes[h], flat[low : low + chunks.main], picked)
                rows.append(picked)
            if chunks.rest:
                low = base + chunks.heads * chunks.main
                rows.append(flat[low : low + chunks.rest_rows] * rest_mask)
        picked = (jnp.concatenate(rows, axis=0) * scaling).astype(BF16)
        dqs.append(dot(choose_t, picked).astype(BF16))
    dq, dk, dv = (jnp.concatenate(parts_of, axis=0) for parts_of in (dqs, dks, dvs))
    scaled = (dot_nt(dq, weights[0]) + dot_nt(dk, weights[1]) + dot_nt(dv, weights[2])) * gain_ref[...]
    standard = standard_in[...]
    inverse_rms = scale_in[:, :1]
    grad = inverse_rms * (
        scaled
        - jnp.mean(scaled, axis=-1, keepdims=True)
        - standard * jnp.mean(scaled * standard, axis=-1, keepdims=True)
    )
    grad = grad.astype(BF16)
    for a in range(level_windows):
        spread = dot(perm_t[...], grad[a * WT : (a + 1) * WT])
        base = 0
        for i, out in enumerate(outs):
            rows = out.shape[1]
            part = spread[base : base + rows]
            if not first and i < 2:
                part += before[i][a].astype(F32)
            out[a] = part.astype(BF16)
            base += rows


def merge_kernel(inner_in, below_in, side, order_t, inner, below):
    half = inner.shape[1]
    lows = []
    for a in range(inner.shape[0]):
        spread = dot(order_t[...], side[a])
        inner[a] = (inner_in[a].astype(F32) + spread[:half]).astype(BF16)
        lows.append(below_in[a].astype(F32) + spread[half:])
    packed = [low[:, :LANES] for low in lows] + [low[:, LANES:] for low in lows]
    below[...] = jnp.concatenate(packed, axis=1).astype(BF16)


def join_kernel(inner, below, bias_grad, grad_input):
    levels, _, cols, channels = grad_input.shape
    level_windows = levels // WZ
    whole = below[...].astype(F32)
    for a in range(level_windows):
        rest_at = level_windows * LANES + a * (channels - LANES)
        low = jnp.concatenate(
            [whole[:, a * LANES : (a + 1) * LANES], whole[:, rest_at : rest_at + channels - LANES]], axis=1
        )
        high = inner[a].astype(F32)
        for z in range(WZ):
            level = (a * WZ + WZ // 2 + z) % levels
            for row in range(HALF_ROWS):
                at = slice((z * HALF_ROWS + row) * cols, (z * HALF_ROWS + row + 1) * cols)
                grad_input[level, row] = low[at].astype(BF16)
                grad_input[level, HALF_ROWS + row] = high[at].astype(BF16)


def bias_kernel(chunks, *refs):
    arrived, bias_grad = refs[:-1], refs[-1]
    main, rest, heads = chunks.main, chunks.rest, chunks.heads
    for a in range(arrived[0].shape[0]):
        total = arrived[0][a].astype(F32)
        for other in arrived[1:]:
            total += other[a].astype(F32)
        turned = jnp.transpose(total)
        for h in range(heads):
            if main:
                bias_grad[a * heads + h, :main] = turned[h * main : (h + 1) * main]
            if rest:
                low = heads * main + h * rest
                bias_grad[a * heads + h, main:] = turned[low : low + rest]


def vmem(count):
    return [pl.BlockSpec(memory_space=pltpu.VMEM)] * count


def call(kernel, outs, args, flops=0, scratch=(), specs=None):
    moved = sum(x.size * x.dtype.itemsize for x in list(args) + list(outs))
    return pl.pallas_call(
        kernel,
        out_shape=outs,
        in_specs=specs or vmem(len(args)),
        out_specs=vmem(len(outs)),
        scratch_shapes=list(scratch),
        compiler_params=pltpu.CompilerParams(vmem_limit_bytes=40 * 2**20),
        cost_estimate=pl.CostEstimate(flops=flops, bytes_accessed=moved, transcendentals=0),
    )(*args)


def shift(value, axis, by):
    devices = lax.axis_size(axis)
    return lax.ppermute(value, axis, [(i, (i + by) % devices) for i in range(devices)])


def local(tokens, cotangent, norm_gain, inproj_weight, outproj_weight, bias):
    levels, rows, cols, channels = tokens.shape
    level_windows, _, heads = bias.shape[:3]
    lat_count, lon_count = lax.axis_size("lat"), lax.axis_size("lon")
    chunks = Chunks(lon_count, heads)
    windows = cols // WW
    struct = jax.ShapeDtypeStruct
    half = WZ * HALF_ROWS * cols
    gain = norm_gain.reshape(1, channels)
    side_table = side_order(cols)
    tables = [window_order(cols, c) for c in range(windows)]
    queries = jnp.asarray(chunks.queries(), BF16)
    hbm = [pl.BlockSpec(memory_space=pltpu.HBM)] * 2

    inner, below = call(
        send_kernel,
        [struct((level_windows, half, 2 * channels), BF16)] * 2,
        (tokens, cotangent),
        specs=hbm,
        scratch=[pltpu.VMEM(tokens.shape, BF16)] * 2 + [pltpu.SemaphoreType.DMA((2,))],
    )
    below = shift(below, "lat", -1)
    bias = bias.reshape(level_windows, heads, WT, WT)
    bias_t, weights = call(
        functools.partial(prep_kernel, chunks, lat_count),
        [
            struct((level_windows, lon_count, WT, chunks.width), F32),
            struct((3, channels, channels), BF16),
        ],
        (bias, inproj_weight),
        flops=10**9,
        specs=hbm,
        scratch=[
            pltpu.VMEM(bias.shape, F32),
            pltpu.VMEM(inproj_weight.shape, BF16),
            pltpu.SemaphoreType.DMA((level_windows + 1,)),
        ],
    )
    (side,) = call(
        side_kernel,
        [struct((level_windows, side_table.shape[0], 2 * channels), BF16)],
        (inner, below, jnp.asarray(side_table, BF16), weights),
    )
    right = shift(side, "lon", -1)
    per_window = []
    total = []
    for c in range(windows):
        last = c == windows - 1
        pieces = (inner, below) + ((right,) if last else ())
        if last:
            sums = [struct((level_windows, WT, chunks.width), BF16)] * lon_count
        else:
            sums = [struct((level_windows, lon_count, WT, chunks.width), F32)]
        results = call(
            functools.partial(scores_kernel, chunks, len(pieces), c == 0, last),
            [
                struct((level_windows * WT, channels), F32),
                struct((level_windows * WT, LANES), F32),
                struct((level_windows * WT, channels), BF16),
                struct((level_windows, lon_count * chunks.rows, channels), BF16),
                struct((level_windows, lon_count * chunks.rows, channels), BF16),
                struct((level_windows, WT, lon_count * chunks.width), BF16),
                struct((level_windows, WT, lon_count * chunks.width), BF16),
            ]
            + sums,
            (*pieces, gain, weights, outproj_weight, bias_t, jnp.asarray(tables[c], BF16), queries, *total),
            flops=10**9,
        )
        per_window.append(results[:7])
        total = results[7:]
    arrived = [total[0]] + [shift(total[d], "lon", d) for d in range(1, lon_count)]
    grads = []
    for c in reversed(range(windows)):
        last = c == windows - 1
        outs = [struct((level_windows, half, channels), BF16)] * 2
        if last:
            outs.append(struct(side.shape[:2] + (channels,), BF16))
        results = call(
            functools.partial(tokens_kernel, chunks, 2, last),
            outs,
            (*per_window[c], gain, weights, jnp.asarray(tables[c].T, BF16), queries, *grads),
            flops=10**9,
        )
        grads = results[:2]
        if last:
            left = shift(results[2], "lon", 1)
    g_inner, g_below = call(
        merge_kernel,
        [struct((level_windows, half, channels), BF16), struct((half, level_windows * channels), BF16)],
        (*grads, left, jnp.asarray(side_table.T, BF16)),
    )
    above = shift(g_below, "lat", 1)
    (bias_grad,) = call(
        functools.partial(bias_kernel, chunks),
        [struct((level_windows * heads, chunks.size, WT), F32)],
        arrived,
        flops=10**8,
    )
    (grad_input,) = call(
        join_kernel,
        [struct(tokens.shape, BF16)],
        (g_inner, above, bias_grad),
    )
    return grad_input, bias_grad.reshape(level_windows, 1, heads, chunks.size, WT)


def solution(mesh):
    placed = (
        P(None, "lat", "lon", None),
        P(None, "lat", "lon", None),
        P(),
        P(),
        P(),
        P(None, "lat", None, None, None),
    )
    return jax.shard_map(
        local,
        mesh=mesh,
        in_specs=placed,
        out_specs=(P(None, "lat", "lon", None), P(None, "lat", None, "lon", None)),
        check_vma=False,
    )
```

```python
import functools

import jax
import jax.numpy as jnp
import numpy as np
from jax import lax
from jax.experimental import pallas as pl
from jax.experimental.pallas import tpu as pltpu
from jax.sharding import PartitionSpec as P

WZ = 2
WH = 6
WW = 12
WT = WZ * WH * WW
HALF_ROWS = WH // 2
HALF_COLS = WW // 2
SIDE = 8
LEVEL = WH * WW
LANES = 128
LOG2E = 1.4426950408889634
epsilon = 1e-05
F32 = jnp.float32
BF16 = jnp.bfloat16
NT = (((1,), (1,)), ((), ()))


def dot(a, b):
    return jnp.dot(a, b, preferred_element_type=F32)


def dot_nt(a, b):
    return lax.dot_general(a, b, NT, preferred_element_type=F32)


def round_up(value, to):
    return (value + to - 1) // to * to


class Chunks:
    def __init__(self, parts, heads):
        self.parts, self.heads = parts, heads
        self.size = WT // parts
        self.main = self.size // 16 * 16
        self.rest = self.size - self.main
        self.rest_rows = round_up(heads * self.rest, 16)
        self.rows = self.main + self.rest_rows
        self.used = heads * self.main + self.rest_rows
        self.width = round_up(self.used, LANES)

    def queries(self):
        table = np.zeros((self.parts, self.rows, WT), np.float32)
        for j in range(self.parts):
            for i in range(self.main):
                table[j, i, j * self.size + i] = 1.0
            for h in range(self.heads):
                for i in range(self.rest):
                    table[j, self.main + h * self.rest + i, j * self.size + self.main + i] = 1.0
        return table

    def columns(self, j):
        lane = lax.broadcasted_iota(jnp.int32, (1, self.width), 1)
        low = self.heads * self.main
        main, left = lane, self.main + lane - low
        for h in range(1, self.heads):
            main -= jnp.where(lane >= h * self.main, self.main, 0)
            left -= jnp.where(lane >= low + h * self.rest, self.rest, 0)
        return j * self.size + jnp.where(lane < low, main, left)


def side_order(cols):
    part = HALF_ROWS * cols
    table = np.zeros((round_up(WZ * WH * HALF_COLS, 16), 2 * WZ * part), np.float32)
    for z in range(WZ):
        for r in range(WH):
            low, row = divmod(r, HALF_ROWS)
            for w in range(HALF_COLS):
                table[(z * WH + r) * HALF_COLS + w, (low * WZ + z) * part + row * cols + w] = 1.0
    return table


def window_order(cols, c, out):
    last = c == cols // WW - 1
    part, side = HALF_ROWS * cols, HALF_ROWS * SIDE
    near = 2 * WZ * part
    extra = round_up(WZ * WH * HALF_COLS, 16) if out else 2 * WZ * side
    table = np.zeros((WT, near + last * extra), np.float32)
    for z in range(WZ):
        for r in range(WH):
            for w in range(WW):
                col = c * WW + w + HALF_COLS
                low, row = divmod(r, HALF_ROWS)
                if col < cols:
                    at = (low * WZ + z) * part + row * cols + col
                elif out:
                    at = near + (z * WH + r) * HALF_COLS + col - cols
                else:
                    at = near + (low * WZ + z) * side + row * SIDE + col - cols
                table[(z * WH + r) * WW + w, at] = 1.0
    return table


def send_kernel(tok, cot, inner, below, right, corner):
    levels = tok.shape[0]

    def packed(level, row):
        t, g = tok[level, row].astype(F32), cot[level, row].astype(F32)
        return jnp.concatenate([t[:, :LANES], g[:, :LANES], t[:, LANES:], g[:, LANES:]], axis=1)

    for a in range(levels // WZ):
        at = [(a * WZ + WZ // 2 + z) % levels for z in range(WZ)]
        for whole, side, base in ((below, corner, 0), (inner, right, HALF_ROWS)):
            rows = [packed(level, base + row) for level in at for row in range(HALF_ROWS)]
            whole[a] = jnp.concatenate(rows, axis=0).astype(BF16)
            side[a] = jnp.concatenate([row[:SIDE] for row in rows], axis=0).astype(BF16)


def prep_kernel(chunks, lat_count, bias, bias_t):
    level_windows = bias.shape[0]
    last_lat = lax.axis_index("lat") == lat_count - 1
    me = lax.axis_index("lon")
    parts, size, main = chunks.parts, chunks.size, chunks.main

    def labels(index, window):
        level_label = (index >= LEVEL) & (window == level_windows - 1)
        in_level = jnp.where(index >= LEVEL, index - LEVEL, index)
        row_label = (in_level >= LEVEL // 2) & last_lat
        return level_label.astype(jnp.int32) * 2 + row_label.astype(jnp.int32)

    key_index = lax.broadcasted_iota(jnp.int32, (WT, chunks.width), 0)
    for window in range(level_windows):
        key_labels = labels(key_index, window)
        for j in range(parts):
            heads = range(chunks.heads)
            low = j * size
            rows = []
            if main:
                rows += [bias[window, h, low : low + main, :] for h in heads]
            if chunks.rest:
                rows += [bias[window, h, low + main : low + size, :] for h in heads]
            spare = chunks.width - chunks.heads * size
            if spare:
                rows.append(jnp.zeros((spare, WT), F32))
            turned = jnp.transpose(jnp.concatenate(rows, axis=0)) * LOG2E
            allowed = key_labels == labels(chunks.columns(j), window)
            bias_t[window, lax.rem(j - me + parts, parts)] = jnp.where(allowed, turned, -1e30)


def head_masks(chunks, channels):
    head_dim = channels // chunks.heads
    lane_head = lax.broadcasted_iota(jnp.int32, (1, channels), 1) // head_dim
    lanes = [lane_head == h for h in range(chunks.heads)]
    rest = None
    if chunks.rest:
        row = lax.broadcasted_iota(jnp.int32, (chunks.rest_rows, channels), 0)
        lane = lax.broadcasted_iota(jnp.int32, (chunks.rest_rows, channels), 1) // head_dim
        rest = jnp.zeros((chunks.rest_rows, channels), F32)
        for h in range(chunks.heads):
            inside = (row >= h * chunks.rest) & (row < (h + 1) * chunks.rest) & (lane == h)
            rest = jnp.where(inside, 1.0, rest)
    return lanes, rest


def stack_heads(chunks, value, d, lane_masks, rest_mask):
    low = d * chunks.rows
    main = value[low : low + chunks.main]
    pieces = [main * mask for mask in lane_masks] if chunks.main else []
    if chunks.rest:
        pieces.append(value[low + chunks.main : low + chunks.rows] * rest_mask)
    if chunks.width > chunks.used:
        pieces.append(jnp.zeros((chunks.width - chunks.used, value.shape[1]), value.dtype))
    return jnp.concatenate(pieces, axis=0)


def split(inproj):
    channels = inproj.shape[0]
    return [inproj[:, part * channels : (part + 1) * channels] for part in range(3)]


def rolled(ref, parts):
    me = lax.axis_index("lon")
    return jnp.concatenate([ref[lax.rem(me + d, parts)] for d in range(parts)], axis=0)


def scores_kernel(chunks, near, first, last, *refs):
    pieces, refs = refs[:near], refs[near:]
    gain_ref, inproj, outproj, bias_t, perm, queries, *refs = refs
    weights = split(inproj)
    before = None
    if not first:
        before, *refs = refs
    standard_out, scale_out, keys_out, query_out, up_out, p_out, ds_out, *totals = refs
    parts, width = chunks.parts, chunks.width
    channels = outproj.shape[0]
    spare = channels - LANES
    scaling = (channels // chunks.heads) ** (-0.5)
    lanes, rest_mask = head_masks(chunks, channels)
    lanes = [mask.astype(F32).astype(BF16) for mask in lanes]
    rest_mask = rest_mask.astype(BF16) if chunks.rest else None
    choose = rolled(queries, parts)
    level_windows = pieces[0].shape[0]
    ts, gs = [], []
    for a in range(level_windows):
        moved = dot(perm[...], jnp.concatenate([piece[a] for piece in pieces], axis=0))
        ts.append(jnp.concatenate([moved[:, :LANES], moved[:, 2 * LANES : 2 * LANES + spare]], axis=1))
        gs.append(jnp.concatenate([moved[:, LANES : 2 * LANES], moved[:, 2 * LANES + spare :]], axis=1))
    t = jnp.concatenate(ts, axis=0)
    g = jnp.concatenate(gs, axis=0).astype(BF16)
    centred = t - jnp.mean(t, axis=-1, keepdims=True)
    inverse_rms = lax.rsqrt(jnp.mean(centred * centred, axis=-1, keepdims=True) + epsilon)
    standard = centred * inverse_rms
    standard_out[...] = standard
    scale_out[...] = jnp.broadcast_to(inverse_rms, scale_out.shape)
    normed = (standard * gain_ref[...]).astype(BF16)
    q = dot(normed, weights[0]).astype(BF16)
    k = dot(normed, weights[1]).astype(BF16)
    v = dot(normed, weights[2]).astype(BF16)
    u = dot_nt(g, outproj[...]).astype(BF16)
    keys_out[...] = k
    for a in range(level_windows):
        cut = slice(a * WT, (a + 1) * WT)
        query = dot(choose, q[cut]).astype(BF16)
        up = dot(choose, u[cut]).astype(BF16)
        query_out[a] = query
        up_out[a] = up
        for d in range(parts):
            at = slice(d * width, (d + 1) * width)
            s = dot_nt(k[cut], stack_heads(chunks, query, d, lanes, rest_mask))
            dp = dot_nt(v[cut], stack_heads(chunks, up, d, lanes, rest_mask))
            e = jnp.exp2(s * (scaling * LOG2E) + bias_t[a, d])
            p = e * (1.0 / jnp.sum(e, axis=0, keepdims=True))
            ds = p * (dp - jnp.sum(p * dp, axis=0, keepdims=True))
            p_out[a, :, at] = p.astype(BF16)
            ds_out[a, :, at] = ds.astype(BF16)
            if not first:
                ds += before[a, d]
            if last:
                totals[d][a] = ds.astype(BF16)
            else:
                totals[0][a, d] = ds


def tokens_kernel(chunks, near, first, *refs):
    standard_in, scale_in, keys, queries_in, ups, p_in, ds_in, gain_ref, inproj, perm_t, queries, *refs = refs
    weights = split(inproj)
    before = None
    if not first:
        before, refs = refs[:2], refs[2:]
    outs = refs
    parts, width = chunks.parts, chunks.width
    channels = keys.shape[-1]
    scaling = (channels // chunks.heads) ** (-0.5)
    lanes, rest_mask = head_masks(chunks, channels)
    low_lanes = [mask.astype(F32).astype(BF16) for mask in lanes]
    low_rest = rest_mask.astype(BF16) if chunks.rest else None
    choose_t = jnp.transpose(rolled(queries, parts).astype(F32)).astype(BF16)
    level_windows = p_in.shape[0]
    dqs, dks, dvs = [], [], []
    for a in range(level_windows):
        query, up = queries_in[a], ups[a]
        qs = jnp.concatenate(
            [stack_heads(chunks, query, d, low_lanes, low_rest) for d in range(parts)], axis=0
        )
        us = jnp.concatenate(
            [stack_heads(chunks, up, d, low_lanes, low_rest) for d in range(parts)], axis=0
        )
        ds = ds_in[a]
        dks.append((dot(ds, qs) * scaling).astype(BF16))
        dvs.append(dot(p_in[a], us).astype(BF16))
        flat = dot(jnp.transpose(ds), keys[a * WT : (a + 1) * WT])
        rows = []
        for d in range(parts):
            base = d * width
            if chunks.main:
                picked = flat[base : base + chunks.main]
                for h in range(1, chunks.heads):
                    low = base + h * chunks.main
                    picked = jnp.where(lanes[h], flat[low : low + chunks.main], picked)
                rows.append(picked)
            if chunks.rest:
                low = base + chunks.heads * chunks.main
                rows.append(flat[low : low + chunks.rest_rows] * rest_mask)
        picked = (jnp.concatenate(rows, axis=0) * scaling).astype(BF16)
        dqs.append(dot(choose_t, picked).astype(BF16))
    dq, dk, dv = (jnp.concatenate(parts_of, axis=0) for parts_of in (dqs, dks, dvs))
    scaled = (dot_nt(dq, weights[0]) + dot_nt(dk, weights[1]) + dot_nt(dv, weights[2])) * gain_ref[...]
    standard = standard_in[...]
    inverse_rms = scale_in[:, :1]
    grad = inverse_rms * (
        scaled
        - jnp.mean(scaled, axis=-1, keepdims=True)
        - standard * jnp.mean(scaled * standard, axis=-1, keepdims=True)
    )
    grad = grad.astype(BF16)
    for a in range(level_windows):
        spread = dot(perm_t[...], grad[a * WT : (a + 1) * WT])
        base = 0
        for i, out in enumerate(outs):
            rows = out.shape[1]
            part = spread[base : base + rows]
            if not first and i < 2:
                part += before[i][a].astype(F32)
            out[a] = part.astype(BF16)
            base += rows


def merge_kernel(inner_in, below_in, side, order_t, inner, below):
    half = inner.shape[1]
    lows = []
    for a in range(inner.shape[0]):
        spread = dot(order_t[...], side[a])
        inner[a] = (inner_in[a].astype(F32) + spread[:half]).astype(BF16)
        lows.append(below_in[a].astype(F32) + spread[half:])
    packed = [low[:, :LANES] for low in lows] + [low[:, LANES:] for low in lows]
    below[...] = jnp.concatenate(packed, axis=1).astype(BF16)


def join_kernel(inner, below, grad_input, joined):
    joined[...] = jnp.zeros(joined.shape, F32)
    levels, _, cols, channels = grad_input.shape
    level_windows = levels // WZ
    whole = below[...].astype(F32)
    for a in range(level_windows):
        rest_at = level_windows * LANES + a * (channels - LANES)
        low = jnp.concatenate(
            [whole[:, a * LANES : (a + 1) * LANES], whole[:, rest_at : rest_at + channels - LANES]], axis=1
        )
        high = inner[a].astype(F32)
        for z in range(WZ):
            level = (a * WZ + WZ // 2 + z) % levels
            for row in range(HALF_ROWS):
                at = slice((z * HALF_ROWS + row) * cols, (z * HALF_ROWS + row + 1) * cols)
                grad_input[level, row] = low[at].astype(BF16)
                grad_input[level, HALF_ROWS + row] = high[at].astype(BF16)


def bias_kernel(chunks, joined, *refs):
    arrived, bias_grad = refs[:-1], refs[-1]
    main, rest, heads = chunks.main, chunks.rest, chunks.heads
    for a in range(arrived[0].shape[0]):
        total = arrived[0][a].astype(F32)
        for other in arrived[1:]:
            total += other[a].astype(F32)
        turned = jnp.transpose(total)
        for h in range(heads):
            at = (a * heads + h) * chunks.size
            if main:
                bias_grad[at : at + main, 0, :] = turned[h * main : (h + 1) * main]
            if rest:
                low = heads * main + h * rest
                bias_grad[at + main : at + chunks.size, 0, :] = turned[low : low + rest]


def vmem(count):
    return [pl.BlockSpec(memory_space=pltpu.VMEM)] * count


def call(kernel, outs, args, flops=0):
    return pl.pallas_call(
        kernel,
        out_shape=outs,
        in_specs=vmem(len(args)),
        out_specs=vmem(len(outs)),
        compiler_params=pltpu.CompilerParams(vmem_limit_bytes=40 * 2**20),
        cost_estimate=pl.CostEstimate(flops=flops, bytes_accessed=0, transcendentals=0),
    )(*args)


def shift(value, rows, cols):
    lat_count, lon_count = lax.axis_size("lat"), lax.axis_size("lon")
    pairs = []
    for i in range(lat_count):
        for j in range(lon_count):
            to = (i + rows) % lat_count * lon_count + (j + cols) % lon_count
            pairs.append((i * lon_count + j, to))
    return lax.ppermute(value, ("lat", "lon"), pairs)


def local(tokens, cotangent, norm_gain, inproj_weight, outproj_weight, bias):
    levels, rows, cols, channels = tokens.shape
    level_windows, _, heads = bias.shape[:3]
    lat_count, lon_count = lax.axis_size("lat"), lax.axis_size("lon")
    chunks = Chunks(lon_count, heads)
    windows = cols // WW
    struct = jax.ShapeDtypeStruct
    half, side = WZ * HALF_ROWS * cols, WZ * HALF_ROWS * SIDE
    gain = norm_gain.reshape(1, channels)
    side_table = side_order(cols)
    queries = jnp.asarray(chunks.queries(), BF16)

    inner, below, right, corner = call(
        send_kernel,
        [struct((level_windows, size, 2 * channels), BF16) for size in (half, half, side, side)],
        (tokens, cotangent),
    )
    below = shift(below, -1, 0)
    right = shift(right, 0, -1)
    corner = shift(corner, -1, -1)
    (bias_t,) = call(
        functools.partial(prep_kernel, chunks, lat_count),
        [struct((level_windows, lon_count, WT, chunks.width), F32)],
        (bias.reshape(level_windows, heads, WT, WT),),
        flops=10**9,
    )
    per_window = []
    total = []
    for c in range(windows):
        last = c == windows - 1
        pieces = (inner, below) + ((right, corner) if last else ())
        if last:
            sums = [struct((level_windows, WT, chunks.width), BF16)] * lon_count
        else:
            sums = [struct((level_windows, lon_count, WT, chunks.width), F32)]
        order = jnp.asarray(window_order(cols, c, False), BF16)
        results = call(
            functools.partial(scores_kernel, chunks, len(pieces), c == 0, last),
            [
                struct((level_windows * WT, channels), F32),
                struct((level_windows * WT, LANES), F32),
                struct((level_windows * WT, channels), BF16),
                struct((level_windows, lon_count * chunks.rows, channels), BF16),
                struct((level_windows, lon_count * chunks.rows, channels), BF16),
                struct((level_windows, WT, lon_count * chunks.width), BF16),
                struct((level_windows, WT, lon_count * chunks.width), BF16),
            ]
            + sums,
            (*pieces, gain, inproj_weight, outproj_weight, bias_t, order, queries, *total),
            flops=10**9,
        )
        per_window.append(results[:7])
        total = results[7:]
    arrived = [total[0]] + [shift(total[d], 0, d) for d in range(1, lon_count)]
    grads = []
    for c in reversed(range(windows)):
        last = c == windows - 1
        outs = [struct((level_windows, half, channels), BF16)] * 2
        if last:
            outs.append(struct((level_windows, side_table.shape[0], channels), BF16))
        order = jnp.asarray(window_order(cols, c, True).T, BF16)
        results = call(
            functools.partial(tokens_kernel, chunks, 2, last),
            outs,
            (*per_window[c], gain, inproj_weight, order, queries, *grads),
        )
        grads = results[:2]
        if last:
            left = shift(results[2], 0, 1)
    g_inner, g_below = call(
        merge_kernel,
        [struct((level_windows, half, channels), BF16), struct((half, level_windows * channels), BF16)],
        (*grads, left, jnp.asarray(side_table.T, BF16)),
    )
    above = shift(g_below, 1, 0)
    grad_input, joined = call(
        join_kernel, [struct(tokens.shape, BF16), struct((8, LANES), F32)], (g_inner, above)
    )
    (bias_grad,) = call(
        functools.partial(bias_kernel, chunks),
        [struct((level_windows * heads * chunks.size, 1, WT), F32)],
        (joined, *arrived),
    )
    bias_grad = bias_grad.reshape(level_windows, heads, chunks.size, 1, WT)
    return grad_input, jnp.transpose(bias_grad, (0, 3, 1, 2, 4))


def solution(mesh):
    placed = (
        P(None, "lat", "lon", None),
        P(None, "lat", "lon", None),
        P(),
        P(),
        P(),
        P(None, "lat", None, None, None),
    )
    return jax.shard_map(
        local,
        mesh=mesh,
        in_specs=placed,
        out_specs=(P(None, "lat", "lon", None), P(None, "lat", None, "lon", None)),
        check_vma=False,
    )
```

```python
import functools

import jax
import jax.numpy as jnp
import numpy as np
from jax import lax
from jax.experimental import pallas as pl
from jax.experimental.pallas import tpu as pltpu
from jax.sharding import PartitionSpec as P

WZ = 2
WH = 6
WW = 12
WT = WZ * WH * WW
HALF_ROWS = WH // 2
HALF_COLS = WW // 2
SIDE = 8
LEVEL = WH * WW
LANES = 128
LOG2E = 1.4426950408889634
epsilon = 1e-05
F32 = jnp.float32
BF16 = jnp.bfloat16
NT = (((1,), (1,)), ((), ()))


def dot(a, b):
    return jnp.dot(a, b, preferred_element_type=F32)


def dot_nt(a, b):
    return lax.dot_general(a, b, NT, preferred_element_type=F32)


def round_up(value, to):
    return (value + to - 1) // to * to


class Chunks:
    def __init__(self, parts, heads):
        self.parts, self.heads = parts, heads
        self.size = WT // parts
        self.main = self.size // 16 * 16
        self.rest = self.size - self.main
        self.rest_rows = round_up(heads * self.rest, 16)
        self.rows = self.main + self.rest_rows
        self.used = heads * self.main + self.rest_rows
        self.width = round_up(self.used, LANES)

    def queries(self):
        table = np.zeros((self.parts, self.rows, WT), np.float32)
        for j in range(self.parts):
            for i in range(self.main):
                table[j, i, j * self.size + i] = 1.0
            for h in range(self.heads):
                for i in range(self.rest):
                    table[j, self.main + h * self.rest + i, j * self.size + self.main + i] = 1.0
        return table

    def columns(self, j):
        lane = lax.broadcasted_iota(jnp.int32, (1, self.width), 1)
        low = self.heads * self.main
        main, left = lane, self.main + lane - low
        for h in range(1, self.heads):
            main -= jnp.where(lane >= h * self.main, self.main, 0)
            left -= jnp.where(lane >= low + h * self.rest, self.rest, 0)
        return j * self.size + jnp.where(lane < low, main, left)


def window_order(cols, c):
    last = c == cols // WW - 1
    part, side = HALF_ROWS * cols, HALF_ROWS * SIDE
    near = 2 * WZ * part
    table = np.zeros((WT, near + last * 2 * WZ * side), np.float32)
    for z in range(WZ):
        for r in range(WH):
            for w in range(WW):
                col = c * WW + w + HALF_COLS
                low, row = divmod(r, HALF_ROWS)
                if col < cols:
                    at = (low * WZ + z) * part + row * cols + col
                else:
                    at = near + (low * WZ + z) * side + row * SIDE + col - cols
                table[(z * WH + r) * WW + w, at] = 1.0
    return table


def send_kernel(tok_hbm, cot_hbm, inner, below, right, corner, tok, cot, sems):
    copies = [
        pltpu.make_async_copy(tok_hbm, tok, sems.at[0]),
        pltpu.make_async_copy(cot_hbm, cot, sems.at[1]),
    ]
    for copy in copies:
        copy.start()
    for copy in copies:
        copy.wait()
    levels = tok.shape[0]

    def packed(level, row):
        t, g = tok[level, row].astype(F32), cot[level, row].astype(F32)
        return jnp.concatenate([t[:, :LANES], g[:, :LANES], t[:, LANES:], g[:, LANES:]], axis=1)

    for a in range(levels // WZ):
        at = [(a * WZ + WZ // 2 + z) % levels for z in range(WZ)]
        for whole, side, base in ((below, corner, 0), (inner, right, HALF_ROWS)):
            rows = [packed(level, base + row) for level in at for row in range(HALF_ROWS)]
            whole[a] = jnp.concatenate(rows, axis=0).astype(BF16)
            side[a] = jnp.concatenate([row[:SIDE] for row in rows], axis=0).astype(BF16)


def prep_kernel(chunks, lat_count, bias, bias_t):
    level_windows = bias.shape[0]
    last_lat = lax.axis_index("lat") == lat_count - 1
    me = lax.axis_index("lon")
    parts, size, main = chunks.parts, chunks.size, chunks.main

    def labels(index, window):
        level_label = (index >= LEVEL) & (window == level_windows - 1)
        in_level = jnp.where(index >= LEVEL, index - LEVEL, index)
        row_label = (in_level >= LEVEL // 2) & last_lat
        return level_label.astype(jnp.int32) * 2 + row_label.astype(jnp.int32)

    key_index = lax.broadcasted_iota(jnp.int32, (WT, chunks.width), 0)
    for window in range(level_windows):
        key_labels = labels(key_index, window)
        for j in range(parts):
            heads = range(chunks.heads)
            low = j * size
            rows = []
            if main:
                rows += [bias[window, h, low : low + main, :] for h in heads]
            if chunks.rest:
                rows += [bias[window, h, low + main : low + size, :] for h in heads]
            spare = chunks.width - chunks.heads * size
            if spare:
                rows.append(jnp.zeros((spare, WT), F32))
            turned = jnp.transpose(jnp.concatenate(rows, axis=0)) * LOG2E
            allowed = key_labels == labels(chunks.columns(j), window)
            bias_t[window, lax.rem(j - me + parts, parts)] = jnp.where(allowed, turned, -1e30)


def head_masks(chunks, channels):
    head_dim = channels // chunks.heads
    lane_head = lax.broadcasted_iota(jnp.int32, (1, channels), 1) // head_dim
    lanes = [lane_head == h for h in range(chunks.heads)]
    rest = None
    if chunks.rest:
        row = lax.broadcasted_iota(jnp.int32, (chunks.rest_rows, channels), 0)
        lane = lax.broadcasted_iota(jnp.int32, (chunks.rest_rows, channels), 1) // head_dim
        rest = jnp.zeros((chunks.rest_rows, channels), F32)
        for h in range(chunks.heads):
            inside = (row >= h * chunks.rest) & (row < (h + 1) * chunks.rest) & (lane == h)
            rest = jnp.where(inside, 1.0, rest)
    return lanes, rest


def stack_heads(chunks, value, d, lane_masks, rest_mask):
    low = d * chunks.rows
    main = value[low : low + chunks.main]
    pieces = [main * mask for mask in lane_masks] if chunks.main else []
    if chunks.rest:
        pieces.append(value[low + chunks.main : low + chunks.rows] * rest_mask)
    if chunks.width > chunks.used:
        pieces.append(jnp.zeros((chunks.width - chunks.used, value.shape[1]), value.dtype))
    return jnp.concatenate(pieces, axis=0)


def split(inproj):
    channels = inproj.shape[0]
    return [inproj[:, part * channels : (part + 1) * channels] for part in range(3)]


def rolled(ref, parts):
    me = lax.axis_index("lon")
    return jnp.concatenate([ref[lax.rem(me + d, parts)] for d in range(parts)], axis=0)


def scores_kernel(chunks, near, first, last, *refs):
    pieces, refs = refs[:near], refs[near:]
    gain_ref, inproj, outproj, bias_t, perm, queries, *refs = refs
    weights = split(inproj)
    before = None
    if not first:
        before, *refs = refs
    standard_out, scale_out, keys_out, query_out, up_out, p_out, ds_out, *totals = refs
    parts, width = chunks.parts, chunks.width
    channels = outproj.shape[0]
    spare = channels - LANES
    scaling = (channels // chunks.heads) ** (-0.5)
    lanes, rest_mask = head_masks(chunks, channels)
    lanes = [mask.astype(F32).astype(BF16) for mask in lanes]
    rest_mask = rest_mask.astype(BF16) if chunks.rest else None
    choose = rolled(queries, parts)
    me = lax.axis_index("lon")
    level_windows = pieces[0].shape[0]
    ts, gs = [], []
    for a in range(level_windows):
        moved = dot(perm[...], jnp.concatenate([piece[a] for piece in pieces], axis=0))
        ts.append(jnp.concatenate([moved[:, :LANES], moved[:, 2 * LANES : 2 * LANES + spare]], axis=1))
        gs.append(jnp.concatenate([moved[:, LANES : 2 * LANES], moved[:, 2 * LANES + spare :]], axis=1))
    t = jnp.concatenate(ts, axis=0)
    g = jnp.concatenate(gs, axis=0).astype(BF16)
    centred = t - jnp.mean(t, axis=-1, keepdims=True)
    inverse_rms = lax.rsqrt(jnp.mean(centred * centred, axis=-1, keepdims=True) + epsilon)
    standard = centred * inverse_rms
    standard_out[...] = standard
    scale_out[...] = jnp.broadcast_to(inverse_rms, scale_out.shape)
    normed = (standard * gain_ref[...]).astype(BF16)
    q = dot(normed, weights[0]).astype(BF16)
    k = dot(normed, weights[1]).astype(BF16)
    v = dot(normed, weights[2]).astype(BF16)
    u = dot_nt(g, outproj[...]).astype(BF16)
    keys_out[...] = k
    for a in range(level_windows):
        cut = slice(a * WT, (a + 1) * WT)
        query = dot(choose, q[cut]).astype(BF16)
        up = dot(choose, u[cut]).astype(BF16)
        query_out[a] = query
        up_out[a] = up
        for d in range(parts):
            at = slice(d * width, (d + 1) * width)
            s = dot_nt(k[cut], stack_heads(chunks, query, d, lanes, rest_mask))
            dp = dot_nt(v[cut], stack_heads(chunks, up, d, lanes, rest_mask))
            e = jnp.exp2(s * (scaling * LOG2E) + bias_t[a, d])
            p = e * (1.0 / jnp.sum(e, axis=0, keepdims=True))
            ds = p * (dp - jnp.sum(p * dp, axis=0, keepdims=True))
            p_out[a, :, at] = p.astype(BF16)
            ds_out[a, :, at] = ds.astype(BF16)
            if not first:
                ds += before[a, d]
            if last:
                totals[0][lax.rem(me + d, parts), a] = ds.astype(BF16)
            else:
                totals[0][a, d] = ds


def tokens_kernel(chunks, near, first, *refs):
    standard_in, scale_in, keys, queries_in, ups, p_in, ds_in, gain_ref, inproj, perm_t, queries, *refs = refs
    weights = split(inproj)
    before = None
    if not first:
        before, refs = refs[:2], refs[2:]
    outs = refs
    parts, width = chunks.parts, chunks.width
    channels = keys.shape[-1]
    scaling = (channels // chunks.heads) ** (-0.5)
    lanes, rest_mask = head_masks(chunks, channels)
    low_lanes = [mask.astype(F32).astype(BF16) for mask in lanes]
    low_rest = rest_mask.astype(BF16) if chunks.rest else None
    choose_t = jnp.transpose(rolled(queries, parts).astype(F32)).astype(BF16)
    level_windows = p_in.shape[0]
    dqs, dks, dvs = [], [], []
    for a in range(level_windows):
        query, up = queries_in[a], ups[a]
        qs = jnp.concatenate(
            [stack_heads(chunks, query, d, low_lanes, low_rest) for d in range(parts)], axis=0
        )
        us = jnp.concatenate(
            [stack_heads(chunks, up, d, low_lanes, low_rest) for d in range(parts)], axis=0
        )
        ds = ds_in[a]
        dks.append((dot(ds, qs) * scaling).astype(BF16))
        dvs.append(dot(p_in[a], us).astype(BF16))
        flat = dot(jnp.transpose(ds), keys[a * WT : (a + 1) * WT])
        rows = []
        for d in range(parts):
            base = d * width
            if chunks.main:
                picked = flat[base : base + chunks.main]
                for h in range(1, chunks.heads):
                    low = base + h * chunks.main
                    picked = jnp.where(lanes[h], flat[low : low + chunks.main], picked)
                rows.append(picked)
            if chunks.rest:
                low = base + chunks.heads * chunks.main
                rows.append(flat[low : low + chunks.rest_rows] * rest_mask)
        picked = (jnp.concatenate(rows, axis=0) * scaling).astype(BF16)
        dqs.append(dot(choose_t, picked).astype(BF16))
    dq, dk, dv = (jnp.concatenate(parts_of, axis=0) for parts_of in (dqs, dks, dvs))
    scaled = (dot_nt(dq, weights[0]) + dot_nt(dk, weights[1]) + dot_nt(dv, weights[2])) * gain_ref[...]
    standard = standard_in[...]
    inverse_rms = scale_in[:, :1]
    grad = inverse_rms * (
        scaled
        - jnp.mean(scaled, axis=-1, keepdims=True)
        - standard * jnp.mean(scaled * standard, axis=-1, keepdims=True)
    )
    grad = grad.astype(BF16)
    lows = []
    for a in range(level_windows):
        spread = dot(perm_t[...], grad[a * WT : (a + 1) * WT])
        base = 0
        for i, out in enumerate(outs):
            rows = out.shape[-2]
            part = spread[base : base + rows]
            if not first and i < 2:
                part += before[i][a].astype(F32)
            if not first and i == 1:
                lows.append(part)
            else:
                out[a] = part.astype(BF16)
            base += rows
    if not first:
        packed = [low[:, :LANES] for low in lows] + [low[:, LANES:] for low in lows]
        outs[1][...] = jnp.concatenate(packed, axis=1).astype(BF16)


def join_kernel(inner, below, right, corner, after, grad_input):
    levels, _, cols, channels = grad_input.shape
    level_windows = levels // WZ
    whole = below[...].astype(F32)
    for a in range(level_windows):
        rest_at = level_windows * LANES + a * (channels - LANES)
        low = jnp.concatenate(
            [whole[:, a * LANES : (a + 1) * LANES], whole[:, rest_at : rest_at + channels - LANES]], axis=1
        )
        parts = ((low, corner[a].astype(F32), 0), (inner[a].astype(F32), right[a].astype(F32), HALF_ROWS))
        for z in range(WZ):
            level = (a * WZ + WZ // 2 + z) % levels
            for row in range(HALF_ROWS):
                at = z * HALF_ROWS + row
                for wide, side, base in parts:
                    first = wide[at * cols : at * cols + SIDE] + side[at * SIDE : (at + 1) * SIDE]
                    rest = wide[at * cols + SIDE : (at + 1) * cols]
                    grad_input[level, base + row] = jnp.concatenate([first, rest], axis=0).astype(BF16)


def bias_kernel(chunks, arrived, bias_grad, after):
    after[...] = jnp.zeros(after.shape, F32)
    main, rest, heads = chunks.main, chunks.rest, chunks.heads
    for a in range(arrived.shape[1]):
        total = arrived[0, a].astype(F32)
        for d in range(1, chunks.parts):
            total += arrived[d, a].astype(F32)
        turned = jnp.transpose(total)
        for h in range(heads):
            at = (a * heads + h) * chunks.size
            if main:
                bias_grad[at : at + main, 0, :] = turned[h * main : (h + 1) * main]
            if rest:
                low = heads * main + h * rest
                bias_grad[at + main : at + chunks.size, 0, :] = turned[low : low + rest]


def vmem(count):
    return [pl.BlockSpec(memory_space=pltpu.VMEM)] * count


def call(kernel, outs, args, flops=0, specs=None, scratch=(), limit=40):
    return pl.pallas_call(
        kernel,
        out_shape=outs,
        in_specs=specs or vmem(len(args)),
        out_specs=vmem(len(outs)),
        scratch_shapes=list(scratch),
        compiler_params=pltpu.CompilerParams(vmem_limit_bytes=limit * 2**20),
        cost_estimate=pl.CostEstimate(flops=flops, bytes_accessed=0, transcendentals=0),
    )(*args)


def shift(value, rows, cols):
    lat_count, lon_count = lax.axis_size("lat"), lax.axis_size("lon")
    pairs = []
    for i in range(lat_count):
        for j in range(lon_count):
            to = (i + rows) % lat_count * lon_count + (j + cols) % lon_count
            pairs.append((i * lon_count + j, to))
    return lax.ppermute(value, ("lat", "lon"), pairs)


def local(tokens, cotangent, norm_gain, inproj_weight, outproj_weight, bias):
    levels, rows, cols, channels = tokens.shape
    level_windows, _, heads = bias.shape[:3]
    lat_count, lon_count = lax.axis_size("lat"), lax.axis_size("lon")
    chunks = Chunks(lon_count, heads)
    windows = cols // WW
    struct = jax.ShapeDtypeStruct
    half, side = WZ * HALF_ROWS * cols, WZ * HALF_ROWS * SIDE
    gain = norm_gain.reshape(1, channels)
    queries = jnp.asarray(chunks.queries(), BF16)

    inner, below, right, corner = call(
        send_kernel,
        [struct((level_windows, size, 2 * channels), BF16) for size in (half, half, side, side)],
        (tokens, cotangent),
        specs=[pl.BlockSpec(memory_space=pltpu.HBM)] * 2,
        scratch=[pltpu.VMEM(tokens.shape, BF16)] * 2 + [pltpu.SemaphoreType.DMA((2,))],
        limit=56,
    )
    below = shift(below, -1, 0)
    right = shift(right, 0, -1)
    corner = shift(corner, -1, -1)
    (bias_t,) = call(
        functools.partial(prep_kernel, chunks, lat_count),
        [struct((level_windows, lon_count, WT, chunks.width), F32)],
        (bias.reshape(level_windows, heads, WT, WT),),
        flops=10**9,
    )
    per_window = []
    total = []
    for c in range(windows):
        last = c == windows - 1
        pieces = (inner, below) + ((right, corner) if last else ())
        if last:
            sums = [struct((lon_count, level_windows, WT, chunks.width), BF16)]
        else:
            sums = [struct((level_windows, lon_count, WT, chunks.width), F32)]
        order = jnp.asarray(window_order(cols, c), BF16)
        results = call(
            functools.partial(scores_kernel, chunks, len(pieces), c == 0, last),
            [
                struct((level_windows * WT, channels), F32),
                struct((level_windows * WT, LANES), F32),
                struct((level_windows * WT, channels), BF16),
                struct((level_windows, lon_count * chunks.rows, channels), BF16),
                struct((level_windows, lon_count * chunks.rows, channels), BF16),
                struct((level_windows, WT, lon_count * chunks.width), BF16),
                struct((level_windows, WT, lon_count * chunks.width), BF16),
            ]
            + sums,
            (*pieces, gain, inproj_weight, outproj_weight, bias_t, order, queries, *total),
            flops=10**9,
        )
        per_window.append(results[:7])
        total = results[7:]
    arrived = lax.all_to_all(total[0], "lon", 0, 0, tiled=True)
    wide = struct((level_windows, half, channels), BF16)
    thin = struct((level_windows, side, channels), BF16)
    grads = []
    for c in reversed(range(windows)):
        last = c == windows - 1
        order = jnp.asarray(window_order(cols, c).T, BF16)
        results = call(
            functools.partial(tokens_kernel, chunks, 2, last),
            [wide, wide, thin, thin] if last else [wide, struct((half, level_windows * channels), BF16)],
            (*per_window[c], gain, inproj_weight, order, queries, *grads),
            flops=10**9 * (not last),
        )
        grads = results[:2]
        if last:
            left, corner = shift(results[2], 0, 1), shift(results[3], 1, 1)
    above = shift(grads[1], 1, 0)
    bias_grad, after = call(
        functools.partial(bias_kernel, chunks),
        [struct((level_windows * heads * chunks.size, 1, WT), F32), struct((8, LANES), F32)],
        (arrived,),
        flops=10**9,
    )
    (grad_input,) = call(
        join_kernel, [struct(tokens.shape, BF16)], (grads[0], above, left, corner, after)
    )
    bias_grad = bias_grad.reshape(level_windows, heads, chunks.size, 1, WT)
    return grad_input, jnp.transpose(bias_grad, (0, 3, 1, 2, 4))


def solution(mesh):
    placed = (
        P(None, "lat", "lon", None),
        P(None, "lat", "lon", None),
        P(),
        P(),
        P(),
        P(None, "lat", None, None, None),
    )
    return jax.shard_map(
        local,
        mesh=mesh,
        in_specs=placed,
        out_specs=(P(None, "lat", "lon", None), P(None, "lat", None, "lon", None)),
        check_vma=False,
    )
```

```python
import functools

import jax
import jax.numpy as jnp
import numpy as np
from jax import lax
from jax.experimental import pallas as pl
from jax.experimental.pallas import tpu as pltpu
from jax.sharding import PartitionSpec as P

WZ = 2
WH = 6
WW = 12
WT = WZ * WH * WW
HALF_ROWS = WH // 2
HALF_COLS = WW // 2
SIDE = 8
LEVEL = WH * WW
LANES = 128
LOG2E = 1.4426950408889634
epsilon = 1e-05
F32 = jnp.float32
BF16 = jnp.bfloat16
NT = (((1,), (1,)), ((), ()))


def dot(a, b):
    return jnp.dot(a, b, preferred_element_type=F32)


def dot_nt(a, b):
    return lax.dot_general(a, b, NT, preferred_element_type=F32)


def round_up(value, to):
    return (value + to - 1) // to * to


class Chunks:
    def __init__(self, parts, heads):
        self.parts, self.heads = parts, heads
        self.size = WT // parts
        self.main = self.size // 16 * 16
        self.rest = self.size - self.main
        self.rest_rows = round_up(heads * self.rest, 16)
        self.rows = self.main + self.rest_rows
        self.used = heads * self.main + self.rest_rows
        self.width = round_up(self.used, LANES)

    def queries(self):
        table = np.zeros((self.parts, self.rows, WT), np.float32)
        for j in range(self.parts):
            for i in range(self.main):
                table[j, i, j * self.size + i] = 1.0
            for h in range(self.heads):
                for i in range(self.rest):
                    table[j, self.main + h * self.rest + i, j * self.size + self.main + i] = 1.0
        return table

    def columns(self, j):
        lane = lax.broadcasted_iota(jnp.int32, (1, self.width), 1)
        low = self.heads * self.main
        main, left = lane, self.main + lane - low
        for h in range(1, self.heads):
            main -= jnp.where(lane >= h * self.main, self.main, 0)
            left -= jnp.where(lane >= low + h * self.rest, self.rest, 0)
        return j * self.size + jnp.where(lane < low, main, left)


def side_order(cols):
    part = HALF_ROWS * cols
    table = np.zeros((round_up(WZ * WH * HALF_COLS, 16), 2 * WZ * part), np.float32)
    for z in range(WZ):
        for r in range(WH):
            low, row = divmod(r, HALF_ROWS)
            for w in range(HALF_COLS):
                table[(z * WH + r) * HALF_COLS + w, (low * WZ + z) * part + row * cols + w] = 1.0
    return table


def window_order(cols, c, out):
    last = c == cols // WW - 1
    part, side = HALF_ROWS * cols, HALF_ROWS * SIDE
    near = 2 * WZ * part
    extra = round_up(WZ * WH * HALF_COLS, 16) if out else 2 * WZ * side
    table = np.zeros((WT, near + last * extra), np.float32)
    for z in range(WZ):
        for r in range(WH):
            for w in range(WW):
                col = c * WW + w + HALF_COLS
                low, row = divmod(r, HALF_ROWS)
                if col < cols:
                    at = (low * WZ + z) * part + row * cols + col
                elif out:
                    at = near + (z * WH + r) * HALF_COLS + col - cols
                else:
                    at = near + (low * WZ + z) * side + row * SIDE + col - cols
                table[(z * WH + r) * WW + w, at] = 1.0
    return table


def send_kernel(both, inner, below, right, corner):
    levels = both.shape[0]
    for a in range(levels // WZ):
        at = [(a * WZ + WZ // 2 + z) % levels for z in range(WZ)]
        for whole, side, base in ((below, corner, 0), (inner, right, HALF_ROWS)):
            rows = [both[level, base + row].astype(F32) for level in at for row in range(HALF_ROWS)]
            whole[a] = jnp.concatenate(rows, axis=0).astype(BF16)
            side[a] = jnp.concatenate([row[:SIDE] for row in rows], axis=0).astype(BF16)


def prep_kernel(chunks, lat_count, bias, bias_t):
    level_windows = bias.shape[0]
    last_lat = lax.axis_index("lat") == lat_count - 1
    me = lax.axis_index("lon")
    parts, size, main = chunks.parts, chunks.size, chunks.main

    def labels(index, window):
        level_label = (index >= LEVEL) & (window == level_windows - 1)
        in_level = jnp.where(index >= LEVEL, index - LEVEL, index)
        row_label = (in_level >= LEVEL // 2) & last_lat
        return level_label.astype(jnp.int32) * 2 + row_label.astype(jnp.int32)

    key_index = lax.broadcasted_iota(jnp.int32, (WT, chunks.width), 0)
    for window in range(level_windows):
        key_labels = labels(key_index, window)
        for j in range(parts):
            heads = range(chunks.heads)
            low = j * size
            rows = []
            if main:
                rows += [bias[window, h, low : low + main, :] for h in heads]
            if chunks.rest:
                rows += [bias[window, h, low + main : low + size, :] for h in heads]
            spare = chunks.width - chunks.heads * size
            if spare:
                rows.append(jnp.zeros((spare, WT), F32))
            turned = jnp.transpose(jnp.concatenate(rows, axis=0)) * LOG2E
            allowed = key_labels == labels(chunks.columns(j), window)
            slot = me ^ j if parts & (parts - 1) == 0 else lax.rem(j - me + parts, parts)
            bias_t[window, slot] = jnp.where(allowed, turned, -1e30)


def head_masks(chunks, channels):
    head_dim = channels // chunks.heads
    lane_head = lax.broadcasted_iota(jnp.int32, (1, channels), 1) // head_dim
    lanes = [lane_head == h for h in range(chunks.heads)]
    rest = None
    if chunks.rest:
        row = lax.broadcasted_iota(jnp.int32, (chunks.rest_rows, channels), 0)
        lane = lax.broadcasted_iota(jnp.int32, (chunks.rest_rows, channels), 1) // head_dim
        rest = jnp.zeros((chunks.rest_rows, channels), F32)
        for h in range(chunks.heads):
            inside = (row >= h * chunks.rest) & (row < (h + 1) * chunks.rest) & (lane == h)
            rest = jnp.where(inside, 1.0, rest)
    return lanes, rest


def stack_heads(chunks, value, d, lane_masks, rest_mask):
    low = d * chunks.rows
    main = value[low : low + chunks.main]
    pieces = [main * mask for mask in lane_masks] if chunks.main else []
    if chunks.rest:
        pieces.append(value[low + chunks.main : low + chunks.rows] * rest_mask)
    if chunks.width > chunks.used:
        pieces.append(jnp.zeros((chunks.width - chunks.used, value.shape[1]), value.dtype))
    return jnp.concatenate(pieces, axis=0)


def split(inproj):
    channels = inproj.shape[0]
    return [inproj[:, part * channels : (part + 1) * channels] for part in range(3)]


def partner(me, d, parts):
    return me ^ d if parts & (parts - 1) == 0 else (me + d) % parts


def rolled(ref, parts):
    me = lax.axis_index("lon")
    return jnp.concatenate([ref[partner(me, d, parts)] for d in range(parts)], axis=0)


def scores_kernel(chunks, near, first, last, *refs):
    pieces, refs = refs[:near], refs[near:]
    gain_ref, inproj, outproj, bias_t, perm, queries, *refs = refs
    weights = split(inproj)
    before = None
    if not first:
        before, *refs = refs
    standard_out, scale_out, keys_out, query_out, up_out, p_out, ds_out, *totals = refs
    parts, width = chunks.parts, chunks.width
    channels = outproj.shape[0]
    scaling = (channels // chunks.heads) ** (-0.5)
    lanes, rest_mask = head_masks(chunks, channels)
    lanes = [mask.astype(F32).astype(BF16) for mask in lanes]
    rest_mask = rest_mask.astype(BF16) if chunks.rest else None
    choose = rolled(queries, parts)
    level_windows = pieces[0].shape[0]
    tile = channels // LANES * LANES
    from_tile = jnp.concatenate([jnp.zeros((channels, channels - tile), BF16), outproj[...]], axis=1)
    ts, us = [], []
    for a in range(level_windows):
        moved = dot(perm[...], jnp.concatenate([piece[a] for piece in pieces], axis=0))
        ts.append(moved[:, :channels])
        us.append(dot_nt(moved[:, tile:].astype(BF16), from_tile).astype(BF16))
    t = jnp.concatenate(ts, axis=0)
    centred = t - jnp.mean(t, axis=-1, keepdims=True)
    inverse_rms = lax.rsqrt(jnp.mean(centred * centred, axis=-1, keepdims=True) + epsilon)
    standard = centred * inverse_rms
    standard_out[...] = standard
    scale_out[...] = jnp.broadcast_to(inverse_rms, scale_out.shape)
    normed = (standard * gain_ref[...]).astype(BF16)
    q = dot(normed, weights[0]).astype(BF16)
    k = dot(normed, weights[1]).astype(BF16)
    v = dot(normed, weights[2]).astype(BF16)
    keys_out[...] = k
    for a in range(level_windows):
        cut = slice(a * WT, (a + 1) * WT)
        query = dot(choose, q[cut]).astype(BF16)
        up = dot(choose, us[a]).astype(BF16)
        query_out[a] = query
        up_out[a] = up
        for d in range(parts):
            at = slice(d * width, (d + 1) * width)
            s = dot_nt(k[cut], stack_heads(chunks, query, d, lanes, rest_mask))
            dp = dot_nt(v[cut], stack_heads(chunks, up, d, lanes, rest_mask))
            e = jnp.exp2(s * (scaling * LOG2E) + bias_t[a, d])
            p = e * (1.0 / jnp.sum(e, axis=0, keepdims=True))
            ds = p * (dp - jnp.sum(p * dp, axis=0, keepdims=True))
            p_out[a, :, at] = p.astype(BF16)
            ds_out[a, :, at] = ds.astype(BF16)
            if not first:
                ds += before[a, d]
            if last:
                totals[d][a] = ds.astype(BF16)
            else:
                totals[0][a, d] = ds


def tokens_kernel(chunks, near, first, *refs):
    standard_in, scale_in, keys, queries_in, ups, p_in, ds_in, gain_ref, inproj, perm_t, queries, *refs = refs
    weights = split(inproj)
    before = None
    if not first:
        before, refs = refs[:2], refs[2:]
    outs = refs
    parts, width = chunks.parts, chunks.width
    channels = keys.shape[-1]
    scaling = (channels // chunks.heads) ** (-0.5)
    lanes, rest_mask = head_masks(chunks, channels)
    low_lanes = [mask.astype(F32).astype(BF16) for mask in lanes]
    low_rest = rest_mask.astype(BF16) if chunks.rest else None
    choose_t = jnp.transpose(rolled(queries, parts).astype(F32)).astype(BF16)
    level_windows = p_in.shape[0]
    dqs, dks, dvs = [], [], []
    for a in range(level_windows):
        query, up = queries_in[a], ups[a]
        qs = jnp.concatenate(
            [stack_heads(chunks, query, d, low_lanes, low_rest) for d in range(parts)], axis=0
        )
        us = jnp.concatenate(
            [stack_heads(chunks, up, d, low_lanes, low_rest) for d in range(parts)], axis=0
        )
        ds = ds_in[a]
        dks.append((dot(ds, qs) * scaling).astype(BF16))
        dvs.append(dot(p_in[a], us).astype(BF16))
        flat = dot(jnp.transpose(ds), keys[a * WT : (a + 1) * WT])
        rows = []
        for d in range(parts):
            base = d * width
            if chunks.main:
                picked = flat[base : base + chunks.main]
                for h in range(1, chunks.heads):
                    low = base + h * chunks.main
                    picked = jnp.where(lanes[h], flat[low : low + chunks.main], picked)
                rows.append(picked)
            if chunks.rest:
                low = base + chunks.heads * chunks.main
                rows.append(flat[low : low + chunks.rest_rows] * rest_mask)
        picked = (jnp.concatenate(rows, axis=0) * scaling).astype(BF16)
        dqs.append(dot(choose_t, picked).astype(BF16))
    dq, dk, dv = (jnp.concatenate(parts_of, axis=0) for parts_of in (dqs, dks, dvs))
    scaled = (dot_nt(dq, weights[0]) + dot_nt(dk, weights[1]) + dot_nt(dv, weights[2])) * gain_ref[...]
    standard = standard_in[...]
    inverse_rms = scale_in[:, :1]
    grad = inverse_rms * (
        scaled
        - jnp.mean(scaled, axis=-1, keepdims=True)
        - standard * jnp.mean(scaled * standard, axis=-1, keepdims=True)
    )
    grad = grad.astype(BF16)
    for a in range(level_windows):
        spread = dot(perm_t[...], grad[a * WT : (a + 1) * WT])
        base = 0
        for i, out in enumerate(outs):
            rows = out.shape[1]
            part = spread[base : base + rows]
            if not first and i < 2:
                part += before[i][a].astype(F32)
            out[a] = part.astype(BF16)
            base += rows


def merge_kernel(inner_in, below_in, side, order_t, inner, below):
    half = inner.shape[1]
    lows = []
    for a in range(inner.shape[0]):
        spread = dot(order_t[...], side[a])
        inner[a] = (inner_in[a].astype(F32) + spread[:half]).astype(BF16)
        lows.append(below_in[a].astype(F32) + spread[half:])
    packed = [low[:, :LANES] for low in lows] + [low[:, LANES:] for low in lows]
    below[...] = jnp.concatenate(packed, axis=1).astype(BF16)


def join_kernel(inner, below, after, grad_input):
    levels, _, cols, channels = grad_input.shape
    level_windows = levels // WZ
    whole = below[...].astype(F32)
    for a in range(level_windows):
        rest_at = level_windows * LANES + a * (channels - LANES)
        low = jnp.concatenate(
            [whole[:, a * LANES : (a + 1) * LANES], whole[:, rest_at : rest_at + channels - LANES]], axis=1
        )
        high = inner[a].astype(F32)
        for z in range(WZ):
            level = (a * WZ + WZ // 2 + z) % levels
            for row in range(HALF_ROWS):
                at = slice((z * HALF_ROWS + row) * cols, (z * HALF_ROWS + row + 1) * cols)
                grad_input[level, row] = low[at].astype(BF16)
                grad_input[level, HALF_ROWS + row] = high[at].astype(BF16)


def bias_kernel(chunks, *refs):
    *arrived, bias_grad, after = refs
    after[...] = jnp.zeros(after.shape, F32)
    main, rest, heads = chunks.main, chunks.rest, chunks.heads
    for a in range(arrived[0].shape[0]):
        total = arrived[0][a].astype(F32)
        for other in arrived[1:]:
            total += other[a].astype(F32)
        turned = jnp.transpose(total)
        for h in range(heads):
            at = (a * heads + h) * chunks.size
            if main:
                bias_grad[at : at + main, 0, :] = turned[h * main : (h + 1) * main]
            if rest:
                low = heads * main + h * rest
                bias_grad[at + main : at + chunks.size, 0, :] = turned[low : low + rest]


def vmem(count):
    return [pl.BlockSpec(memory_space=pltpu.VMEM)] * count


def call(kernel, outs, args, flops=0):
    return pl.pallas_call(
        kernel,
        out_shape=outs,
        in_specs=vmem(len(args)),
        out_specs=vmem(len(outs)),
        compiler_params=pltpu.CompilerParams(vmem_limit_bytes=40 * 2**20),
        cost_estimate=pl.CostEstimate(flops=flops, bytes_accessed=0, transcendentals=0),
    )(*args)


def shift(value, rows, cols):
    lat_count, lon_count = lax.axis_size("lat"), lax.axis_size("lon")
    pairs = []
    for i in range(lat_count):
        for j in range(lon_count):
            to = (i + rows) % lat_count * lon_count + (j + cols) % lon_count
            pairs.append((i * lon_count + j, to))
    return lax.ppermute(value, ("lat", "lon"), pairs)


def local(tokens, cotangent, norm_gain, inproj_weight, outproj_weight, bias):
    levels, rows, cols, channels = tokens.shape
    level_windows, _, heads = bias.shape[:3]
    lat_count, lon_count = lax.axis_size("lat"), lax.axis_size("lon")
    chunks = Chunks(lon_count, heads)
    windows = cols // WW
    struct = jax.ShapeDtypeStruct
    half, side = WZ * HALF_ROWS * cols, WZ * HALF_ROWS * SIDE
    gain = norm_gain.reshape(1, channels)
    side_table = side_order(cols)
    queries = jnp.asarray(chunks.queries(), BF16)

    inner, below, right, corner = call(
        send_kernel,
        [struct((level_windows, size, 2 * channels), BF16) for size in (half, half, side, side)],
        (jnp.concatenate([tokens, cotangent], axis=-1),),
    )
    below = shift(below, -1, 0)
    right = shift(right, 0, -1)
    corner = shift(corner, -1, -1)
    (bias_t,) = call(
        functools.partial(prep_kernel, chunks, lat_count),
        [struct((level_windows, lon_count, WT, chunks.width), F32)],
        (bias.reshape(level_windows, heads, WT, WT),),
        flops=10**9,
    )
    per_window = []
    total = []
    for c in range(windows):
        last = c == windows - 1
        pieces = (inner, below) + ((right, corner) if last else ())
        if last:
            sums = [struct((level_windows, WT, chunks.width), BF16)] * lon_count
        else:
            sums = [struct((level_windows, lon_count, WT, chunks.width), F32)]
        order = jnp.asarray(window_order(cols, c, False), BF16)
        results = call(
            functools.partial(scores_kernel, chunks, len(pieces), c == 0, last),
            [
                struct((level_windows * WT, channels), F32),
                struct((level_windows * WT, LANES), F32),
                struct((level_windows * WT, channels), BF16),
                struct((level_windows, lon_count * chunks.rows, channels), BF16),
                struct((level_windows, lon_count * chunks.rows, channels), BF16),
                struct((level_windows, WT, lon_count * chunks.width), BF16),
                struct((level_windows, WT, lon_count * chunks.width), BF16),
            ]
            + sums,
            (*pieces, gain, inproj_weight, outproj_weight, bias_t, order, queries, *total),
            flops=10**9,
        )
        per_window.append(results[:7])
        total = results[7:]
    arrived = [total[0]]
    for d in range(1, lon_count):
        pairs = [(i, partner(i, d, lon_count)) for i in range(lon_count)]
        arrived.append(lax.ppermute(total[d], "lon", pairs))
    grads = []
    for c in reversed(range(windows)):
        last = c == windows - 1
        outs = [struct((level_windows, half, channels), BF16)] * 2
        if last:
            outs.append(struct((level_windows, side_table.shape[0], channels), BF16))
        order = jnp.asarray(window_order(cols, c, True).T, BF16)
        results = call(
            functools.partial(tokens_kernel, chunks, 2, last),
            outs,
            (*per_window[c], gain, inproj_weight, order, queries, *grads),
        )
        grads = results[:2]
        if last:
            left = shift(results[2], 0, 1)
    g_inner, g_below = call(
        merge_kernel,
        [struct((level_windows, half, channels), BF16), struct((half, level_windows * channels), BF16)],
        (*grads, left, jnp.asarray(side_table.T, BF16)),
    )
    above = shift(g_below, 1, 0)
    bias_grad, after = call(
        functools.partial(bias_kernel, chunks),
        [struct((level_windows * heads * chunks.size, 1, WT), F32), struct((8, LANES), F32)],
        arrived,
        flops=10**9,
    )
    (grad_input,) = call(join_kernel, [struct(tokens.shape, BF16)], (g_inner, above, after))
    bias_grad = bias_grad.reshape(level_windows, heads, chunks.size, 1, WT)
    return grad_input, jnp.transpose(bias_grad, (0, 3, 1, 2, 4))


def solution(mesh):
    placed = (
        P(None, "lat", "lon", None),
        P(None, "lat", "lon", None),
        P(),
        P(),
        P(),
        P(None, "lat", None, None, None),
    )
    return jax.shard_map(
        local,
        mesh=mesh,
        in_specs=placed,
        out_specs=(P(None, "lat", "lon", None), P(None, "lat", None, "lon", None)),
        check_vma=False,
    )
```

```python
import functools

import jax
import jax.numpy as jnp
import numpy as np
from jax import lax
from jax.experimental import pallas as pl
from jax.experimental.pallas import tpu as pltpu
from jax.sharding import PartitionSpec as P

WZ = 2
WH = 6
WW = 12
WT = WZ * WH * WW
HALF_ROWS = WH // 2
HALF_COLS = WW // 2
SIDE = 8
LEVEL = WH * WW
LANES = 128
LOG2E = 1.4426950408889634
epsilon = 1e-05
F32 = jnp.float32
BF16 = jnp.bfloat16
NT = (((1,), (1,)), ((), ()))


def dot(a, b):
    return jnp.dot(a, b, preferred_element_type=F32)


def dot_nt(a, b):
    return lax.dot_general(a, b, NT, preferred_element_type=F32)


def round_up(value, to):
    return (value + to - 1) // to * to


class Chunks:
    def __init__(self, parts, heads):
        self.parts, self.heads = parts, heads
        self.size = WT // parts
        self.main = self.size // 16 * 16
        self.rest = self.size - self.main
        self.rest_rows = round_up(heads * self.rest, 16)
        self.rows = self.main + self.rest_rows
        self.used = heads * self.main + self.rest_rows
        self.width = round_up(self.used, LANES)

    def queries(self):
        table = np.zeros((self.parts, self.rows, WT), np.float32)
        for j in range(self.parts):
            for i in range(self.main):
                table[j, i, j * self.size + i] = 1.0
            for h in range(self.heads):
                for i in range(self.rest):
                    table[j, self.main + h * self.rest + i, j * self.size + self.main + i] = 1.0
        return table

    def columns(self, j):
        lane = lax.broadcasted_iota(jnp.int32, (1, self.width), 1)
        low = self.heads * self.main
        main, left = lane, self.main + lane - low
        for h in range(1, self.heads):
            main -= jnp.where(lane >= h * self.main, self.main, 0)
            left -= jnp.where(lane >= low + h * self.rest, self.rest, 0)
        return j * self.size + jnp.where(lane < low, main, left)


def window_order(cols, c):
    last = c == cols // WW - 1
    part, side = HALF_ROWS * cols, HALF_ROWS * SIDE
    near = 2 * WZ * part
    table = np.zeros((WT, near + last * 2 * WZ * side), np.float32)
    for z in range(WZ):
        for r in range(WH):
            for w in range(WW):
                col = c * WW + w + HALF_COLS
                low, row = divmod(r, HALF_ROWS)
                if col < cols:
                    at = (low * WZ + z) * part + row * cols + col
                else:
                    at = near + (low * WZ + z) * side + row * SIDE + col - cols
                table[(z * WH + r) * WW + w, at] = 1.0
    return table


def send_kernel(both, inner, below, right, corner):
    levels = both.shape[0]
    for a in range(levels // WZ):
        at = [(a * WZ + WZ // 2 + z) % levels for z in range(WZ)]
        for whole, side, base in ((below, corner, 0), (inner, right, HALF_ROWS)):
            rows = [both[level, base + row].astype(F32) for level in at for row in range(HALF_ROWS)]
            whole[a] = jnp.concatenate(rows, axis=0).astype(BF16)
            side[a] = jnp.concatenate([row[:SIDE] for row in rows], axis=0).astype(BF16)


def prep_kernel(chunks, lat_count, bias, bias_t):
    level_windows = bias.shape[0]
    last_lat = lax.axis_index("lat") == lat_count - 1
    me = lax.axis_index("lon")
    parts, size, main = chunks.parts, chunks.size, chunks.main

    def labels(index, window):
        level_label = (index >= LEVEL) & (window == level_windows - 1)
        in_level = jnp.where(index >= LEVEL, index - LEVEL, index)
        row_label = (in_level >= LEVEL // 2) & last_lat
        return level_label.astype(jnp.int32) * 2 + row_label.astype(jnp.int32)

    key_index = lax.broadcasted_iota(jnp.int32, (WT, chunks.width), 0)
    for window in range(level_windows):
        key_labels = labels(key_index, window)
        for j in range(parts):
            heads = range(chunks.heads)
            low = j * size
            rows = []
            if main:
                rows += [bias[window, h, low : low + main, :] for h in heads]
            if chunks.rest:
                rows += [bias[window, h, low + main : low + size, :] for h in heads]
            spare = chunks.width - chunks.heads * size
            if spare:
                rows.append(jnp.zeros((spare, WT), F32))
            turned = jnp.transpose(jnp.concatenate(rows, axis=0)) * LOG2E
            allowed = key_labels == labels(chunks.columns(j), window)
            slot = me ^ j if parts & (parts - 1) == 0 else lax.rem(j - me + parts, parts)
            bias_t[window, slot] = jnp.where(allowed, turned, -1e30)


def head_masks(chunks, channels):
    head_dim = channels // chunks.heads
    lane_head = lax.broadcasted_iota(jnp.int32, (1, channels), 1) // head_dim
    lanes = [lane_head == h for h in range(chunks.heads)]
    rest = None
    if chunks.rest:
        row = lax.broadcasted_iota(jnp.int32, (chunks.rest_rows, channels), 0)
        lane = lax.broadcasted_iota(jnp.int32, (chunks.rest_rows, channels), 1) // head_dim
        rest = jnp.zeros((chunks.rest_rows, channels), F32)
        for h in range(chunks.heads):
            inside = (row >= h * chunks.rest) & (row < (h + 1) * chunks.rest) & (lane == h)
            rest = jnp.where(inside, 1.0, rest)
    return lanes, rest


def stack_heads(chunks, value, d, lane_masks, rest_mask):
    low = d * chunks.rows
    main = value[low : low + chunks.main]
    pieces = [main * mask for mask in lane_masks] if chunks.main else []
    if chunks.rest:
        pieces.append(value[low + chunks.main : low + chunks.rows] * rest_mask)
    if chunks.width > chunks.used:
        pieces.append(jnp.zeros((chunks.width - chunks.used, value.shape[1]), value.dtype))
    return jnp.concatenate(pieces, axis=0)


def split(inproj):
    channels = inproj.shape[0]
    return [inproj[:, part * channels : (part + 1) * channels] for part in range(3)]


def partner(me, d, parts):
    return me ^ d if parts & (parts - 1) == 0 else (me + d) % parts


def rolled(ref, parts):
    me = lax.axis_index("lon")
    return jnp.concatenate([ref[partner(me, d, parts)] for d in range(parts)], axis=0)


def scores_kernel(chunks, near, first, last, *refs):
    pieces, refs = refs[:near], refs[near:]
    gain_ref, inproj, outproj, bias_t, perm, queries, *refs = refs
    weights = split(inproj)
    before = None
    if not first:
        before, *refs = refs
    standard_out, scale_out, keys_out, query_out, up_out, p_out, ds_out, *totals = refs
    parts, width = chunks.parts, chunks.width
    channels = outproj.shape[0]
    scaling = (channels // chunks.heads) ** (-0.5)
    lanes, rest_mask = head_masks(chunks, channels)
    lanes = [mask.astype(F32).astype(BF16) for mask in lanes]
    rest_mask = rest_mask.astype(BF16) if chunks.rest else None
    choose = rolled(queries, parts)
    level_windows = pieces[0].shape[0]
    tile = channels // LANES * LANES
    from_tile = jnp.concatenate([jnp.zeros((channels, channels - tile), BF16), outproj[...]], axis=1)
    ts, us = [], []
    for a in range(level_windows):
        moved = dot(perm[...], jnp.concatenate([piece[a] for piece in pieces], axis=0))
        ts.append(moved[:, :channels])
        us.append(dot_nt(moved[:, tile:].astype(BF16), from_tile).astype(BF16))
    t = jnp.concatenate(ts, axis=0)
    centred = t - jnp.mean(t, axis=-1, keepdims=True)
    inverse_rms = lax.rsqrt(jnp.mean(centred * centred, axis=-1, keepdims=True) + epsilon)
    standard = centred * inverse_rms
    standard_out[...] = standard
    scale_out[...] = jnp.broadcast_to(inverse_rms, scale_out.shape)
    normed = (standard * gain_ref[...]).astype(BF16)
    q = dot(normed, weights[0]).astype(BF16)
    k = dot(normed, weights[1]).astype(BF16)
    v = dot(normed, weights[2]).astype(BF16)
    keys_out[...] = k
    for a in range(level_windows):
        cut = slice(a * WT, (a + 1) * WT)
        query = dot(choose, q[cut]).astype(BF16)
        up = dot(choose, us[a]).astype(BF16)
        query_out[a] = query
        up_out[a] = up
        for d in range(parts):
            at = slice(d * width, (d + 1) * width)
            s = dot_nt(k[cut], stack_heads(chunks, query, d, lanes, rest_mask))
            dp = dot_nt(v[cut], stack_heads(chunks, up, d, lanes, rest_mask))
            e = jnp.exp2(s * (scaling * LOG2E) + bias_t[a, d])
            p = e * (1.0 / jnp.sum(e, axis=0, keepdims=True))
            ds = p * (dp - jnp.sum(p * dp, axis=0, keepdims=True))
            p_out[a, :, at] = p.astype(BF16)
            ds_out[a, :, at] = ds.astype(BF16)
            if not first:
                ds += before[a, d]
            if last:
                totals[d][a] = ds.astype(BF16)
            else:
                totals[0][a, d] = ds


def tokens_kernel(chunks, near, first, *refs):
    standard_in, scale_in, keys, queries_in, ups, p_in, ds_in, gain_ref, inproj, perm_t, queries, *refs = refs
    weights = split(inproj)
    before = None
    if not first:
        before, refs = refs[:2], refs[2:]
    outs = refs
    parts, width = chunks.parts, chunks.width
    channels = keys.shape[-1]
    scaling = (channels // chunks.heads) ** (-0.5)
    lanes, rest_mask = head_masks(chunks, channels)
    low_lanes = [mask.astype(F32).astype(BF16) for mask in lanes]
    low_rest = rest_mask.astype(BF16) if chunks.rest else None
    choose_t = jnp.transpose(rolled(queries, parts).astype(F32)).astype(BF16)
    level_windows = p_in.shape[0]
    dqs, dks, dvs = [], [], []
    for a in range(level_windows):
        query, up = queries_in[a], ups[a]
        qs = jnp.concatenate(
            [stack_heads(chunks, query, d, low_lanes, low_rest) for d in range(parts)], axis=0
        )
        us = jnp.concatenate(
            [stack_heads(chunks, up, d, low_lanes, low_rest) for d in range(parts)], axis=0
        )
        ds = ds_in[a]
        dks.append((dot(ds, qs) * scaling).astype(BF16))
        dvs.append(dot(p_in[a], us).astype(BF16))
        flat = dot(jnp.transpose(ds), keys[a * WT : (a + 1) * WT])
        rows = []
        for d in range(parts):
            base = d * width
            if chunks.main:
                picked = flat[base : base + chunks.main]
                for h in range(1, chunks.heads):
                    low = base + h * chunks.main
                    picked = jnp.where(lanes[h], flat[low : low + chunks.main], picked)
                rows.append(picked)
            if chunks.rest:
                low = base + chunks.heads * chunks.main
                rows.append(flat[low : low + chunks.rest_rows] * rest_mask)
        picked = (jnp.concatenate(rows, axis=0) * scaling).astype(BF16)
        dqs.append(dot(choose_t, picked).astype(BF16))
    dq, dk, dv = (jnp.concatenate(parts_of, axis=0) for parts_of in (dqs, dks, dvs))
    scaled = (dot_nt(dq, weights[0]) + dot_nt(dk, weights[1]) + dot_nt(dv, weights[2])) * gain_ref[...]
    standard = standard_in[...]
    inverse_rms = scale_in[:, :1]
    grad = inverse_rms * (
        scaled
        - jnp.mean(scaled, axis=-1, keepdims=True)
        - standard * jnp.mean(scaled * standard, axis=-1, keepdims=True)
    )
    grad = grad.astype(BF16)
    lows = []
    for a in range(level_windows):
        spread = dot(perm_t[...], grad[a * WT : (a + 1) * WT])
        base = 0
        for i, out in enumerate(outs):
            rows = out.shape[-2]
            part = spread[base : base + rows]
            if not first and i < 2:
                part += before[i][a].astype(F32)
            if not first and i == 1:
                lows.append(part)
            else:
                out[a] = part.astype(BF16)
            base += rows
    if not first:
        packed = [low[:, :LANES] for low in lows] + [low[:, LANES:] for low in lows]
        outs[1][...] = jnp.concatenate(packed, axis=1).astype(BF16)


def join_kernel(inner, below, right, corner, after, grad_input):
    levels, _, cols, channels = grad_input.shape
    level_windows = levels // WZ
    whole = below[...].astype(F32)
    for a in range(level_windows):
        rest_at = level_windows * LANES + a * (channels - LANES)
        low = jnp.concatenate(
            [whole[:, a * LANES : (a + 1) * LANES], whole[:, rest_at : rest_at + channels - LANES]], axis=1
        )
        parts = ((low, corner[a].astype(F32), 0), (inner[a].astype(F32), right[a].astype(F32), HALF_ROWS))
        for z in range(WZ):
            level = (a * WZ + WZ // 2 + z) % levels
            for row in range(HALF_ROWS):
                at = z * HALF_ROWS + row
                for wide, side, base in parts:
                    first = wide[at * cols : at * cols + SIDE] + side[at * SIDE : (at + 1) * SIDE]
                    rest = wide[at * cols + SIDE : (at + 1) * cols]
                    grad_input[level, base + row] = jnp.concatenate([first, rest], axis=0).astype(BF16)


def bias_kernel(chunks, *refs):
    *arrived, bias_grad, after = refs
    after[...] = jnp.zeros(after.shape, F32)
    main, rest, heads = chunks.main, chunks.rest, chunks.heads
    for a in range(arrived[0].shape[0]):
        total = arrived[0][a].astype(F32)
        for other in arrived[1:]:
            total += other[a].astype(F32)
        turned = jnp.transpose(total)
        for h in range(heads):
            at = (a * heads + h) * chunks.size
            if main:
                bias_grad[at : at + main, 0, :] = turned[h * main : (h + 1) * main]
            if rest:
                low = heads * main + h * rest
                bias_grad[at + main : at + chunks.size, 0, :] = turned[low : low + rest]


def vmem(count):
    return [pl.BlockSpec(memory_space=pltpu.VMEM)] * count


def call(kernel, outs, args, flops=0):
    return pl.pallas_call(
        kernel,
        out_shape=outs,
        in_specs=vmem(len(args)),
        out_specs=vmem(len(outs)),
        compiler_params=pltpu.CompilerParams(vmem_limit_bytes=40 * 2**20),
        cost_estimate=pl.CostEstimate(flops=flops, bytes_accessed=0, transcendentals=0),
    )(*args)


def shift(value, rows, cols):
    lat_count, lon_count = lax.axis_size("lat"), lax.axis_size("lon")
    pairs = []
    for i in range(lat_count):
        for j in range(lon_count):
            to = (i + rows) % lat_count * lon_count + (j + cols) % lon_count
            pairs.append((i * lon_count + j, to))
    return lax.ppermute(value, ("lat", "lon"), pairs)


def local(tokens, cotangent, norm_gain, inproj_weight, outproj_weight, bias):
    levels, rows, cols, channels = tokens.shape
    level_windows, _, heads = bias.shape[:3]
    lat_count, lon_count = lax.axis_size("lat"), lax.axis_size("lon")
    chunks = Chunks(lon_count, heads)
    windows = cols // WW
    struct = jax.ShapeDtypeStruct
    half, side = WZ * HALF_ROWS * cols, WZ * HALF_ROWS * SIDE
    gain = norm_gain.reshape(1, channels)
    queries = jnp.asarray(chunks.queries(), BF16)

    inner, below, right, corner = call(
        send_kernel,
        [struct((level_windows, size, 2 * channels), BF16) for size in (half, half, side, side)],
        (jnp.concatenate([tokens, cotangent], axis=-1),),
    )
    below = shift(below, -1, 0)
    right = shift(right, 0, -1)
    corner = shift(corner, -1, -1)
    (bias_t,) = call(
        functools.partial(prep_kernel, chunks, lat_count),
        [struct((level_windows, lon_count, WT, chunks.width), F32)],
        (bias.reshape(level_windows, heads, WT, WT),),
        flops=10**9,
    )
    per_window = []
    total = []
    for c in range(windows):
        last = c == windows - 1
        pieces = (inner, below) + ((right, corner) if last else ())
        if last:
            sums = [struct((level_windows, WT, chunks.width), BF16)] * lon_count
        else:
            sums = [struct((level_windows, lon_count, WT, chunks.width), F32)]
        order = jnp.asarray(window_order(cols, c), BF16)
        results = call(
            functools.partial(scores_kernel, chunks, len(pieces), c == 0, last),
            [
                struct((level_windows * WT, channels), F32),
                struct((level_windows * WT, LANES), F32),
                struct((level_windows * WT, channels), BF16),
                struct((level_windows, lon_count * chunks.rows, channels), BF16),
                struct((level_windows, lon_count * chunks.rows, channels), BF16),
                struct((level_windows, WT, lon_count * chunks.width), BF16),
                struct((level_windows, WT, lon_count * chunks.width), BF16),
            ]
            + sums,
            (*pieces, gain, inproj_weight, outproj_weight, bias_t, order, queries, *total),
            flops=10**9,
        )
        per_window.append(results[:7])
        total = results[7:]
    arrived = [total[0]]
    for d in range(1, lon_count):
        pairs = [(i, partner(i, d, lon_count)) for i in range(lon_count)]
        arrived.append(lax.ppermute(total[d], "lon", pairs))
    wide = struct((level_windows, half, channels), BF16)
    thin = struct((level_windows, side, channels), BF16)
    grads = []
    for c in reversed(range(windows)):
        last = c == windows - 1
        order = jnp.asarray(window_order(cols, c).T, BF16)
        results = call(
            functools.partial(tokens_kernel, chunks, 2, last),
            [wide, wide, thin, thin] if last else [wide, struct((half, level_windows * channels), BF16)],
            (*per_window[c], gain, inproj_weight, order, queries, *grads),
        )
        grads = results[:2]
        if last:
            left, corner = shift(results[2], 0, 1), shift(results[3], 1, 1)
    above = shift(grads[1], 1, 0)
    bias_grad, after = call(
        functools.partial(bias_kernel, chunks),
        [struct((level_windows * heads * chunks.size, 1, WT), F32), struct((8, LANES), F32)],
        arrived,
    )
    (grad_input,) = call(join_kernel, [struct(tokens.shape, BF16)], (grads[0], above, left, corner, after))
    bias_grad = bias_grad.reshape(level_windows, heads, chunks.size, 1, WT)
    return grad_input, jnp.transpose(bias_grad, (0, 3, 1, 2, 4))


def solution(mesh):
    placed = (
        P(None, "lat", "lon", None),
        P(None, "lat", "lon", None),
        P(),
        P(),
        P(),
        P(None, "lat", None, None, None),
    )
    return jax.shard_map(
        local,
        mesh=mesh,
        in_specs=placed,
        out_specs=(P(None, "lat", "lon", None), P(None, "lat", None, "lon", None)),
        check_vma=False,
    )
```

```python
import functools

import jax
import jax.numpy as jnp
import numpy as np
from jax import lax
from jax.experimental import pallas as pl
from jax.experimental.pallas import tpu as pltpu
from jax.sharding import PartitionSpec as P

WZ = 2
WH = 6
WW = 12
WT = WZ * WH * WW
HALF_ROWS = WH // 2
HALF_COLS = WW // 2
SIDE = 8
LEVEL = WH * WW
LANES = 128
LOG2E = 1.4426950408889634
epsilon = 1e-05
F32 = jnp.float32
BF16 = jnp.bfloat16
NT = (((1,), (1,)), ((), ()))


def dot(a, b):
    return jnp.dot(a, b, preferred_element_type=F32)


def dot_nt(a, b):
    return lax.dot_general(a, b, NT, preferred_element_type=F32)


def round_up(value, to):
    return (value + to - 1) // to * to


class Chunks:
    def __init__(self, parts, heads):
        self.parts, self.heads = parts, heads
        self.size = WT // parts
        self.main = self.size // 16 * 16
        self.rest = self.size - self.main
        self.rest_rows = round_up(heads * self.rest, 16)
        self.rows = self.main + self.rest_rows
        self.used = heads * self.main + self.rest_rows
        self.width = round_up(self.used, LANES)

    def queries(self):
        table = np.zeros((self.parts, self.rows, WT), np.float32)
        for j in range(self.parts):
            for i in range(self.main):
                table[j, i, j * self.size + i] = 1.0
            for h in range(self.heads):
                for i in range(self.rest):
                    table[j, self.main + h * self.rest + i, j * self.size + self.main + i] = 1.0
        return table

    def columns(self, j):
        lane = lax.broadcasted_iota(jnp.int32, (1, self.width), 1)
        low = self.heads * self.main
        main, left = lane, self.main + lane - low
        for h in range(1, self.heads):
            main -= jnp.where(lane >= h * self.main, self.main, 0)
            left -= jnp.where(lane >= low + h * self.rest, self.rest, 0)
        return j * self.size + jnp.where(lane < low, main, left)


def window_order(cols, c):
    last = c == cols // WW - 1
    part, side = HALF_ROWS * cols, HALF_ROWS * SIDE
    near = 2 * WZ * part
    table = np.zeros((WT, near + last * 2 * WZ * side), np.float32)
    for z in range(WZ):
        for r in range(WH):
            for w in range(WW):
                col = c * WW + w + HALF_COLS
                low, row = divmod(r, HALF_ROWS)
                if col < cols:
                    at = (low * WZ + z) * part + row * cols + col
                else:
                    at = near + (low * WZ + z) * side + row * SIDE + col - cols
                table[(z * WH + r) * WW + w, at] = 1.0
    return table


def send_kernel(both, inner, below):
    levels = both.shape[0]
    for a in range(levels // WZ):
        at = [(a * WZ + WZ // 2 + z) % levels for z in range(WZ)]
        for whole, base in ((below, 0), (inner, HALF_ROWS)):
            rows = [both[level, base + row].astype(F32) for level in at for row in range(HALF_ROWS)]
            whole[a] = jnp.concatenate(rows, axis=0).astype(BF16)


def side_kernel(both, after, right, corner):
    levels = both.shape[0]
    for a in range(levels // WZ):
        at = [(a * WZ + WZ // 2 + z) % levels for z in range(WZ)]
        for side, base in ((corner, 0), (right, HALF_ROWS)):
            rows = [both[level, base + row].astype(F32)[:SIDE] for level in at for row in range(HALF_ROWS)]
            side[a] = jnp.concatenate(rows, axis=0).astype(BF16)


def prep_kernel(chunks, lat_count, bias, bias_t, after):
    after[...] = jnp.zeros(after.shape, F32)
    level_windows = bias.shape[0]
    last_lat = lax.axis_index("lat") == lat_count - 1
    me = lax.axis_index("lon")
    parts, size, main = chunks.parts, chunks.size, chunks.main

    def labels(index, window):
        level_label = (index >= LEVEL) & (window == level_windows - 1)
        in_level = jnp.where(index >= LEVEL, index - LEVEL, index)
        row_label = (in_level >= LEVEL // 2) & last_lat
        return level_label.astype(jnp.int32) * 2 + row_label.astype(jnp.int32)

    key_index = lax.broadcasted_iota(jnp.int32, (WT, chunks.width), 0)
    for window in range(level_windows):
        key_labels = labels(key_index, window)
        for j in range(parts):
            heads = range(chunks.heads)
            low = j * size
            rows = []
            if main:
                rows += [bias[window, h, low : low + main, :] for h in heads]
            if chunks.rest:
                rows += [bias[window, h, low + main : low + size, :] for h in heads]
            spare = chunks.width - chunks.heads * size
            if spare:
                rows.append(jnp.zeros((spare, WT), F32))
            turned = jnp.transpose(jnp.concatenate(rows, axis=0)) * LOG2E
            allowed = key_labels == labels(chunks.columns(j), window)
            slot = me ^ j if parts & (parts - 1) == 0 else lax.rem(j - me + parts, parts)
            bias_t[window, slot] = jnp.where(allowed, turned, -1e30)


def head_masks(chunks, channels):
    head_dim = channels // chunks.heads
    lane_head = lax.broadcasted_iota(jnp.int32, (1, channels), 1) // head_dim
    lanes = [lane_head == h for h in range(chunks.heads)]
    rest = None
    if chunks.rest:
        row = lax.broadcasted_iota(jnp.int32, (chunks.rest_rows, channels), 0)
        lane = lax.broadcasted_iota(jnp.int32, (chunks.rest_rows, channels), 1) // head_dim
        rest = jnp.zeros((chunks.rest_rows, channels), F32)
        for h in range(chunks.heads):
            inside = (row >= h * chunks.rest) & (row < (h + 1) * chunks.rest) & (lane == h)
            rest = jnp.where(inside, 1.0, rest)
    return lanes, rest


def stack_heads(chunks, value, d, lane_masks, rest_mask):
    low = d * chunks.rows
    main = value[low : low + chunks.main]
    pieces = [main * mask for mask in lane_masks] if chunks.main else []
    if chunks.rest:
        pieces.append(value[low + chunks.main : low + chunks.rows] * rest_mask)
    if chunks.width > chunks.used:
        pieces.append(jnp.zeros((chunks.width - chunks.used, value.shape[1]), value.dtype))
    return jnp.concatenate(pieces, axis=0)


def split(inproj):
    channels = inproj.shape[0]
    return [inproj[:, part * channels : (part + 1) * channels] for part in range(3)]


def partner(me, d, parts):
    return me ^ d if parts & (parts - 1) == 0 else (me + d) % parts


def rolled(ref, parts):
    me = lax.axis_index("lon")
    return jnp.concatenate([ref[partner(me, d, parts)] for d in range(parts)], axis=0)


def scores_kernel(chunks, near, first, last, *refs):
    pieces, refs = refs[:near], refs[near:]
    gain_ref, inproj, outproj, bias_t, perm, queries, *refs = refs
    weights = split(inproj)
    before = None
    if not first:
        before, *refs = refs
    standard_out, scale_out, keys_out, query_out, up_out, p_out, ds_out, *totals = refs
    parts, width = chunks.parts, chunks.width
    channels = outproj.shape[0]
    scaling = (channels // chunks.heads) ** (-0.5)
    lanes, rest_mask = head_masks(chunks, channels)
    lanes = [mask.astype(F32).astype(BF16) for mask in lanes]
    rest_mask = rest_mask.astype(BF16) if chunks.rest else None
    choose = rolled(queries, parts)
    level_windows = pieces[0].shape[0]
    tile = channels // LANES * LANES
    from_tile = jnp.concatenate([jnp.zeros((channels, channels - tile), BF16), outproj[...]], axis=1)
    ts, us = [], []
    for a in range(level_windows):
        moved = dot(perm[...], jnp.concatenate([piece[a] for piece in pieces], axis=0))
        ts.append(moved[:, :channels])
        us.append(dot_nt(moved[:, tile:].astype(BF16), from_tile).astype(BF16))
    t = jnp.concatenate(ts, axis=0)
    centred = t - jnp.mean(t, axis=-1, keepdims=True)
    inverse_rms = lax.rsqrt(jnp.mean(centred * centred, axis=-1, keepdims=True) + epsilon)
    standard = centred * inverse_rms
    standard_out[...] = standard
    scale_out[...] = jnp.broadcast_to(inverse_rms, scale_out.shape)
    normed = (standard * gain_ref[...]).astype(BF16)
    q = dot(normed, weights[0]).astype(BF16)
    k = dot(normed, weights[1]).astype(BF16)
    v = dot(normed, weights[2]).astype(BF16)
    keys_out[...] = k
    for a in range(level_windows):
        cut = slice(a * WT, (a + 1) * WT)
        query = dot(choose, q[cut]).astype(BF16)
        up = dot(choose, us[a]).astype(BF16)
        query_out[a] = query
        up_out[a] = up
        for d in range(parts):
            at = slice(d * width, (d + 1) * width)
            s = dot_nt(k[cut], stack_heads(chunks, query, d, lanes, rest_mask))
            dp = dot_nt(v[cut], stack_heads(chunks, up, d, lanes, rest_mask))
            e = jnp.exp2(s * (scaling * LOG2E) + bias_t[a, d])
            p = e * (1.0 / jnp.sum(e, axis=0, keepdims=True))
            ds = p * (dp - jnp.sum(p * dp, axis=0, keepdims=True))
            p_out[a, :, at] = p.astype(BF16)
            ds_out[a, :, at] = ds.astype(BF16)
            if not first:
                ds += before[a, d]
            if last:
                totals[d][a] = ds.astype(BF16)
            else:
                totals[0][a, d] = ds


def tokens_kernel(chunks, near, first, *refs):
    standard_in, scale_in, keys, queries_in, ups, p_in, ds_in, gain_ref, inproj, perm_t, queries, *refs = refs
    weights = split(inproj)
    before = None
    if not first:
        before, refs = refs[:2], refs[2:]
    outs = refs
    parts, width = chunks.parts, chunks.width
    channels = keys.shape[-1]
    scaling = (channels // chunks.heads) ** (-0.5)
    lanes, rest_mask = head_masks(chunks, channels)
    low_lanes = [mask.astype(F32).astype(BF16) for mask in lanes]
    low_rest = rest_mask.astype(BF16) if chunks.rest else None
    choose_t = jnp.transpose(rolled(queries, parts).astype(F32)).astype(BF16)
    level_windows = p_in.shape[0]
    dqs, dks, dvs = [], [], []
    for a in range(level_windows):
        query, up = queries_in[a], ups[a]
        qs = jnp.concatenate(
            [stack_heads(chunks, query, d, low_lanes, low_rest) for d in range(parts)], axis=0
        )
        us = jnp.concatenate(
            [stack_heads(chunks, up, d, low_lanes, low_rest) for d in range(parts)], axis=0
        )
        ds = ds_in[a]
        dks.append((dot(ds, qs) * scaling).astype(BF16))
        dvs.append(dot(p_in[a], us).astype(BF16))
        flat = dot(jnp.transpose(ds), keys[a * WT : (a + 1) * WT])
        rows = []
        for d in range(parts):
            base = d * width
            if chunks.main:
                picked = flat[base : base + chunks.main]
                for h in range(1, chunks.heads):
                    low = base + h * chunks.main
                    picked = jnp.where(lanes[h], flat[low : low + chunks.main], picked)
                rows.append(picked)
            if chunks.rest:
                low = base + chunks.heads * chunks.main
                rows.append(flat[low : low + chunks.rest_rows] * rest_mask)
        picked = (jnp.concatenate(rows, axis=0) * scaling).astype(BF16)
        dqs.append(dot(choose_t, picked).astype(BF16))
    dq, dk, dv = (jnp.concatenate(parts_of, axis=0) for parts_of in (dqs, dks, dvs))
    scaled = (dot_nt(dq, weights[0]) + dot_nt(dk, weights[1]) + dot_nt(dv, weights[2])) * gain_ref[...]
    standard = standard_in[...]
    inverse_rms = scale_in[:, :1]
    grad = inverse_rms * (
        scaled
        - jnp.mean(scaled, axis=-1, keepdims=True)
        - standard * jnp.mean(scaled * standard, axis=-1, keepdims=True)
    )
    grad = grad.astype(BF16)
    lows = []
    for a in range(level_windows):
        spread = dot(perm_t[...], grad[a * WT : (a + 1) * WT])
        base = 0
        for i, out in enumerate(outs):
            rows = out.shape[-2]
            part = spread[base : base + rows]
            if not first and i < 2:
                part += before[i][a].astype(F32)
            if not first and i == 1:
                lows.append(part)
            else:
                out[a] = part.astype(BF16)
            base += rows
    if not first:
        packed = [low[:, :LANES] for low in lows] + [low[:, LANES:] for low in lows]
        outs[1][...] = jnp.concatenate(packed, axis=1).astype(BF16)


def join_kernel(inner, below, right, corner, after, grad_input):
    levels, _, cols, channels = grad_input.shape
    level_windows = levels // WZ
    whole = below[...].astype(F32)
    for a in range(level_windows):
        rest_at = level_windows * LANES + a * (channels - LANES)
        low = jnp.concatenate(
            [whole[:, a * LANES : (a + 1) * LANES], whole[:, rest_at : rest_at + channels - LANES]], axis=1
        )
        parts = ((low, corner[a].astype(F32), 0), (inner[a].astype(F32), right[a].astype(F32), HALF_ROWS))
        for z in range(WZ):
            level = (a * WZ + WZ // 2 + z) % levels
            for row in range(HALF_ROWS):
                at = z * HALF_ROWS + row
                for wide, side, base in parts:
                    first = wide[at * cols : at * cols + SIDE] + side[at * SIDE : (at + 1) * SIDE]
                    rest = wide[at * cols + SIDE : (at + 1) * cols]
                    grad_input[level, base + row] = jnp.concatenate([first, rest], axis=0).astype(BF16)


def bias_kernel(chunks, *refs):
    *arrived, bias_grad, after = refs
    after[...] = jnp.zeros(after.shape, F32)
    main, rest, heads = chunks.main, chunks.rest, chunks.heads
    for a in range(arrived[0].shape[0]):
        total = arrived[0][a].astype(F32)
        for other in arrived[1:]:
            total += other[a].astype(F32)
        turned = jnp.transpose(total)
        for h in range(heads):
            at = (a * heads + h) * chunks.size
            if main:
                bias_grad[at : at + main, 0, :] = turned[h * main : (h + 1) * main]
            if rest:
                low = heads * main + h * rest
                bias_grad[at + main : at + chunks.size, 0, :] = turned[low : low + rest]


def vmem(count):
    return [pl.BlockSpec(memory_space=pltpu.VMEM)] * count


def call(kernel, outs, args, flops=0):
    return pl.pallas_call(
        kernel,
        out_shape=outs,
        in_specs=vmem(len(args)),
        out_specs=vmem(len(outs)),
        compiler_params=pltpu.CompilerParams(vmem_limit_bytes=40 * 2**20),
        cost_estimate=pl.CostEstimate(flops=flops, bytes_accessed=0, transcendentals=0),
    )(*args)


def shift(value, rows, cols):
    lat_count, lon_count = lax.axis_size("lat"), lax.axis_size("lon")
    pairs = []
    for i in range(lat_count):
        for j in range(lon_count):
            to = (i + rows) % lat_count * lon_count + (j + cols) % lon_count
            pairs.append((i * lon_count + j, to))
    return lax.ppermute(value, ("lat", "lon"), pairs)


def local(tokens, cotangent, norm_gain, inproj_weight, outproj_weight, bias):
    levels, rows, cols, channels = tokens.shape
    level_windows, _, heads = bias.shape[:3]
    lat_count, lon_count = lax.axis_size("lat"), lax.axis_size("lon")
    chunks = Chunks(lon_count, heads)
    windows = cols // WW
    struct = jax.ShapeDtypeStruct
    half, side = WZ * HALF_ROWS * cols, WZ * HALF_ROWS * SIDE
    gain = norm_gain.reshape(1, channels)
    queries = jnp.asarray(chunks.queries(), BF16)

    both = jnp.concatenate([tokens, cotangent], axis=-1)
    inner, below = call(
        send_kernel, [struct((level_windows, half, 2 * channels), BF16)] * 2, (both,)
    )
    below = shift(below, -1, 0)
    bias_t, after = call(
        functools.partial(prep_kernel, chunks, lat_count),
        [
            struct((level_windows, lon_count, WT, chunks.width), F32),
            struct((8, LANES), F32),
        ],
        (bias.reshape(level_windows, heads, WT, WT),),
    )
    right, corner = call(
        side_kernel, [struct((level_windows, side, 2 * channels), BF16)] * 2, (both, after)
    )
    right = shift(right, 0, -1)
    corner = shift(corner, -1, -1)
    per_window = []
    total = []
    for c in range(windows):
        last = c == windows - 1
        pieces = (inner, below) + ((right, corner) if last else ())
        if last:
            sums = [struct((level_windows, WT, chunks.width), BF16)] * lon_count
        else:
            sums = [struct((level_windows, lon_count, WT, chunks.width), F32)]
        order = jnp.asarray(window_order(cols, c), BF16)
        results = call(
            functools.partial(scores_kernel, chunks, len(pieces), c == 0, last),
            [
                struct((level_windows * WT, channels), F32),
                struct((level_windows * WT, LANES), F32),
                struct((level_windows * WT, channels), BF16),
                struct((level_windows, lon_count * chunks.rows, channels), BF16),
                struct((level_windows, lon_count * chunks.rows, channels), BF16),
                struct((level_windows, WT, lon_count * chunks.width), BF16),
                struct((level_windows, WT, lon_count * chunks.width), BF16),
            ]
            + sums,
            (*pieces, gain, inproj_weight, outproj_weight, bias_t, order, queries, *total),
            flops=10**9,
        )
        per_window.append(results[:7])
        total = results[7:]
    arrived = [total[0]]
    for d in range(1, lon_count):
        pairs = [(i, partner(i, d, lon_count)) for i in range(lon_count)]
        arrived.append(lax.ppermute(total[d], "lon", pairs))
    wide = struct((level_windows, half, channels), BF16)
    thin = struct((level_windows, side, channels), BF16)
    grads = []
    for c in reversed(range(windows)):
        last = c == windows - 1
        order = jnp.asarray(window_order(cols, c).T, BF16)
        results = call(
            functools.partial(tokens_kernel, chunks, 2, last),
            [wide, wide, thin, thin] if last else [wide, struct((half, level_windows * channels), BF16)],
            (*per_window[c], gain, inproj_weight, order, queries, *grads),
        )
        grads = results[:2]
        if last:
            corner = shift(results[3], 1, 1)
            left = shift(results[2], 0, 1)
    above = shift(grads[1], 1, 0)
    bias_grad, after = call(
        functools.partial(bias_kernel, chunks),
        [struct((level_windows * heads * chunks.size, 1, WT), F32), struct((8, LANES), F32)],
        arrived,
    )
    (grad_input,) = call(join_kernel, [struct(tokens.shape, BF16)], (grads[0], above, left, corner, after))
    bias_grad = bias_grad.reshape(level_windows, heads, chunks.size, 1, WT)
    return grad_input, jnp.transpose(bias_grad, (0, 3, 1, 2, 4))


def solution(mesh):
    placed = (
        P(None, "lat", "lon", None),
        P(None, "lat", "lon", None),
        P(),
        P(),
        P(),
        P(None, "lat", None, None, None),
    )
    return jax.shard_map(
        local,
        mesh=mesh,
        in_specs=placed,
        out_specs=(P(None, "lat", "lon", None), P(None, "lat", None, "lon", None)),
        check_vma=False,
    )
```

```python
import functools

import jax
import jax.numpy as jnp
import numpy as np
from jax import lax
from jax.experimental import pallas as pl
from jax.experimental.pallas import tpu as pltpu
from jax.sharding import PartitionSpec as P

WZ = 2
WH = 6
WW = 12
WT = WZ * WH * WW
HALF_ROWS = WH // 2
HALF_COLS = WW // 2
SIDE = 8
LEVEL = WH * WW
LANES = 128
LOG2E = 1.4426950408889634
epsilon = 1e-05
F32 = jnp.float32
BF16 = jnp.bfloat16
NT = (((1,), (1,)), ((), ()))


def dot(a, b):
    return jnp.dot(a, b, preferred_element_type=F32)


def dot_nt(a, b):
    return lax.dot_general(a, b, NT, preferred_element_type=F32)


def round_up(value, to):
    return (value + to - 1) // to * to


class Chunks:
    def __init__(self, parts, heads):
        self.parts, self.heads = parts, heads
        self.size = WT // parts
        self.main = self.size // 16 * 16
        self.rest = self.size - self.main
        self.rest_rows = round_up(heads * self.rest, 16)
        self.rows = self.main + self.rest_rows
        self.used = heads * self.main + self.rest_rows
        self.width = round_up(self.used, LANES)

    def queries(self):
        table = np.zeros((self.parts, self.rows, WT), np.float32)
        for j in range(self.parts):
            for i in range(self.main):
                table[j, i, j * self.size + i] = 1.0
            for h in range(self.heads):
                for i in range(self.rest):
                    table[j, self.main + h * self.rest + i, j * self.size + self.main + i] = 1.0
        return table

    def columns(self, j):
        lane = lax.broadcasted_iota(jnp.int32, (1, self.width), 1)
        low = self.heads * self.main
        main, left = lane, self.main + lane - low
        for h in range(1, self.heads):
            main -= jnp.where(lane >= h * self.main, self.main, 0)
            left -= jnp.where(lane >= low + h * self.rest, self.rest, 0)
        return j * self.size + jnp.where(lane < low, main, left)


def narrow_order(cols):
    kept = cols - HALF_COLS
    table = np.zeros((round_up(WZ * HALF_ROWS * kept, 16), WZ * HALF_ROWS * cols), np.float32)
    for i in range(WZ * HALF_ROWS):
        for w in range(kept):
            table[i * kept + w, i * cols + HALF_COLS + w] = 1.0
    return table


def window_order(cols, c, narrow):
    last = c == cols // WW - 1
    part, side = HALF_ROWS * cols, HALF_ROWS * SIDE
    kept = cols - HALF_COLS if narrow else cols
    near = WZ * part + round_up(WZ * HALF_ROWS * kept, 16)
    table = np.zeros((WT, near + last * 2 * WZ * side), np.float32)
    for z in range(WZ):
        for r in range(WH):
            for w in range(WW):
                col = c * WW + w + HALF_COLS
                low, row = divmod(r, HALF_ROWS)
                if col >= cols:
                    at = near + (low * WZ + z) * side + row * SIDE + col - cols
                elif low:
                    at = WZ * part + (z * HALF_ROWS + row) * kept + col - (cols - kept)
                else:
                    at = z * part + row * cols + col
                table[(z * WH + r) * WW + w, at] = 1.0
    return table


def level_rows(field, a, base):
    levels = field.shape[0]
    at = [(a * WZ + WZ // 2 + z) % levels for z in range(WZ)]
    return [field[level, base + row].astype(F32) for level in at for row in range(HALF_ROWS)]


def send_kernel(both, narrow, below):
    for a in range(below.shape[0]):
        rows = jnp.concatenate(level_rows(both, a, 0), axis=0).astype(BF16)
        below[a] = dot(narrow[...], rows).astype(BF16)


def side_kernel(both, bias, inner, right, corner):
    for a in range(inner.shape[0]):
        low, high = level_rows(both, a, 0), level_rows(both, a, HALF_ROWS)
        inner[a] = jnp.concatenate(high, axis=0).astype(BF16)
        right[a] = jnp.concatenate([row[:SIDE] for row in high], axis=0).astype(BF16)
        corner[a] = jnp.concatenate([row[:SIDE] for row in low], axis=0).astype(BF16)


def prep_kernel(chunks, lat_count, bias, bias_t):
    level_windows = bias.shape[0]
    last_lat = lax.axis_index("lat") == lat_count - 1
    me = lax.axis_index("lon")
    parts, size, main = chunks.parts, chunks.size, chunks.main

    def labels(index, window):
        level_label = (index >= LEVEL) & (window == level_windows - 1)
        in_level = jnp.where(index >= LEVEL, index - LEVEL, index)
        row_label = (in_level >= LEVEL // 2) & last_lat
        return level_label.astype(jnp.int32) * 2 + row_label.astype(jnp.int32)

    key_index = lax.broadcasted_iota(jnp.int32, (WT, chunks.width), 0)
    for window in range(level_windows):
        key_labels = labels(key_index, window)
        for j in range(parts):
            heads = range(chunks.heads)
            low = j * size
            rows = []
            if main:
                rows += [bias[window, h, low : low + main, :] for h in heads]
            if chunks.rest:
                rows += [bias[window, h, low + main : low + size, :] for h in heads]
            spare = chunks.width - chunks.heads * size
            if spare:
                rows.append(jnp.zeros((spare, WT), F32))
            turned = jnp.transpose(jnp.concatenate(rows, axis=0)) * LOG2E
            allowed = key_labels == labels(chunks.columns(j), window)
            slot = me ^ j if parts & (parts - 1) == 0 else lax.rem(j - me + parts, parts)
            bias_t[window, slot] = jnp.where(allowed, turned, -1e30)


def head_masks(chunks, channels):
    head_dim = channels // chunks.heads
    lane_head = lax.broadcasted_iota(jnp.int32, (1, channels), 1) // head_dim
    lanes = [lane_head == h for h in range(chunks.heads)]
    rest = None
    if chunks.rest:
        row = lax.broadcasted_iota(jnp.int32, (chunks.rest_rows, channels), 0)
        lane = lax.broadcasted_iota(jnp.int32, (chunks.rest_rows, channels), 1) // head_dim
        rest = jnp.zeros((chunks.rest_rows, channels), F32)
        for h in range(chunks.heads):
            inside = (row >= h * chunks.rest) & (row < (h + 1) * chunks.rest) & (lane == h)
            rest = jnp.where(inside, 1.0, rest)
    return lanes, rest


def stack_heads(chunks, value, d, lane_masks, rest_mask):
    low = d * chunks.rows
    main = value[low : low + chunks.main]
    pieces = [main * mask for mask in lane_masks] if chunks.main else []
    if chunks.rest:
        pieces.append(value[low + chunks.main : low + chunks.rows] * rest_mask)
    if chunks.width > chunks.used:
        pieces.append(jnp.zeros((chunks.width - chunks.used, value.shape[1]), value.dtype))
    return jnp.concatenate(pieces, axis=0)


def split(inproj):
    channels = inproj.shape[0]
    return [inproj[:, part * channels : (part + 1) * channels] for part in range(3)]


def partner(me, d, parts):
    return me ^ d if parts & (parts - 1) == 0 else (me + d) % parts


def rolled(ref, parts):
    me = lax.axis_index("lon")
    return jnp.concatenate([ref[partner(me, d, parts)] for d in range(parts)], axis=0)


def scores_kernel(chunks, near, first, last, *refs):
    pieces, refs = refs[:near], refs[near:]
    gain_ref, inproj, outproj, bias_t, perm, queries, *refs = refs
    weights = split(inproj)
    before = None
    if not first:
        before, *refs = refs
    standard_out, scale_out, keys_out, query_out, up_out, p_out, ds_out, *totals = refs
    parts, width = chunks.parts, chunks.width
    channels = outproj.shape[0]
    scaling = (channels // chunks.heads) ** (-0.5)
    lanes, rest_mask = head_masks(chunks, channels)
    lanes = [mask.astype(F32).astype(BF16) for mask in lanes]
    rest_mask = rest_mask.astype(BF16) if chunks.rest else None
    choose = rolled(queries, parts)
    level_windows = pieces[0].shape[0]
    tile = channels // LANES * LANES
    from_tile = jnp.concatenate([jnp.zeros((channels, channels - tile), BF16), outproj[...]], axis=1)
    ts, us = [], []
    for a in range(level_windows):
        moved = dot(perm[...], jnp.concatenate([piece[a] for piece in pieces], axis=0))
        ts.append(moved[:, :channels])
        us.append(dot_nt(moved[:, tile:].astype(BF16), from_tile).astype(BF16))
    t = jnp.concatenate(ts, axis=0)
    centred = t - jnp.mean(t, axis=-1, keepdims=True)
    inverse_rms = lax.rsqrt(jnp.mean(centred * centred, axis=-1, keepdims=True) + epsilon)
    standard = centred * inverse_rms
    standard_out[...] = standard
    scale_out[...] = jnp.broadcast_to(inverse_rms, scale_out.shape)
    normed = (standard * gain_ref[...]).astype(BF16)
    q = dot(normed, weights[0]).astype(BF16)
    k = dot(normed, weights[1]).astype(BF16)
    v = dot(normed, weights[2]).astype(BF16)
    keys_out[...] = k
    for a in range(level_windows):
        cut = slice(a * WT, (a + 1) * WT)
        query = dot(choose, q[cut]).astype(BF16)
        up = dot(choose, us[a]).astype(BF16)
        query_out[a] = query
        up_out[a] = up
        for d in range(parts):
            at = slice(d * width, (d + 1) * width)
            s = dot_nt(k[cut], stack_heads(chunks, query, d, lanes, rest_mask))
            dp = dot_nt(v[cut], stack_heads(chunks, up, d, lanes, rest_mask))
            e = jnp.exp2(s * (scaling * LOG2E) + bias_t[a, d])
            p = e * (1.0 / jnp.sum(e, axis=0, keepdims=True))
            ds = p * (dp - jnp.sum(p * dp, axis=0, keepdims=True))
            p_out[a, :, at] = p.astype(BF16)
            ds_out[a, :, at] = ds.astype(BF16)
            if not first:
                ds += before[a, d]
            if last:
                totals[d][a] = ds.astype(BF16)
            else:
                totals[0][a, d] = ds


def tokens_kernel(chunks, near, first, *refs):
    standard_in, scale_in, keys, queries_in, ups, p_in, ds_in, gain_ref, inproj, perm_t, queries, *refs = refs
    weights = split(inproj)
    before = None
    if not first:
        before, refs = refs[:2], refs[2:]
    outs = refs
    parts, width = chunks.parts, chunks.width
    channels = keys.shape[-1]
    head_dim = channels // chunks.heads
    scaling = head_dim ** (-0.5)
    lanes, rest_mask = head_masks(chunks, channels)
    low_lanes = [mask.astype(F32).astype(BF16) for mask in lanes]
    low_rest = rest_mask.astype(BF16) if chunks.rest else None
    choose_t = jnp.transpose(rolled(queries, parts).astype(F32)).astype(BF16)
    level_windows = p_in.shape[0]
    dqs, dks, dvs = [], [], []
    for a in range(level_windows):
        query, up = queries_in[a], ups[a]
        qs = jnp.concatenate(
            [stack_heads(chunks, query, d, low_lanes, low_rest) for d in range(parts)], axis=0
        )
        us = jnp.concatenate(
            [stack_heads(chunks, up, d, low_lanes, low_rest) for d in range(parts)], axis=0
        )
        ds = ds_in[a]
        dks.append((dot(ds, qs) * scaling).astype(BF16))
        dvs.append(dot(p_in[a], us).astype(BF16))
        turned = jnp.transpose(ds)
        key = keys[a * WT : (a + 1) * WT]
        main = []
        for lane in range(0, channels, LANES):
            low = lane // head_dim
            many = min(LANES // head_dim, chunks.heads - low)
            if not chunks.main:
                break
            some = [turned[d * width + low * chunks.main :][: many * chunks.main] for d in range(parts)]
            flat = dot(jnp.concatenate(some, axis=0), key[:, lane : lane + LANES])
            tiles = []
            for d in range(parts):
                picked = flat[d * many * chunks.main :][: chunks.main]
                for h in range(1, many):
                    mask = lanes[low + h][:, lane : lane + LANES]
                    picked = jnp.where(mask, flat[(d * many + h) * chunks.main :][: chunks.main], picked)
                tiles.append(picked)
            main.append(tiles)
        if chunks.rest:
            low = chunks.heads * chunks.main
            some = [turned[d * width + low :][: chunks.rest_rows] for d in range(parts)]
            left = dot(jnp.concatenate(some, axis=0), key)
        rows = []
        for d in range(parts):
            if chunks.main:
                rows.append(jnp.concatenate([tiles[d] for tiles in main], axis=1))
            if chunks.rest:
                rows.append(left[d * chunks.rest_rows : (d + 1) * chunks.rest_rows] * rest_mask)
        picked = (jnp.concatenate(rows, axis=0) * scaling).astype(BF16)
        dqs.append(dot(choose_t, picked).astype(BF16))
    dq, dk, dv = (jnp.concatenate(parts_of, axis=0) for parts_of in (dqs, dks, dvs))
    scaled = (dot_nt(dq, weights[0]) + dot_nt(dk, weights[1]) + dot_nt(dv, weights[2])) * gain_ref[...]
    standard = standard_in[...]
    inverse_rms = scale_in[:, :1]
    grad = inverse_rms * (
        scaled
        - jnp.mean(scaled, axis=-1, keepdims=True)
        - standard * jnp.mean(scaled * standard, axis=-1, keepdims=True)
    )
    grad = grad.astype(BF16)
    lows = []
    for a in range(level_windows):
        spread = dot(perm_t[...], grad[a * WT : (a + 1) * WT])
        base = 0
        for i, out in enumerate(outs):
            rows = out.shape[-2]
            part = spread[base : base + rows]
            if not first and i < 2:
                part += before[i][a].astype(F32)
            if not first and i == 1:
                lows.append(part)
            else:
                out[a] = part.astype(BF16)
            base += rows
    if not first:
        packed = [low[:, :LANES] for low in lows] + [low[:, LANES:] for low in lows]
        outs[1][...] = jnp.concatenate(packed, axis=1).astype(BF16)


def join_kernel(inner, below, right, corner, after, grad_input):
    levels, _, cols, channels = grad_input.shape
    level_windows = levels // WZ
    whole = below[...].astype(F32)
    for a in range(level_windows):
        rest_at = level_windows * LANES + a * (channels - LANES)
        low = jnp.concatenate(
            [whole[:, a * LANES : (a + 1) * LANES], whole[:, rest_at : rest_at + channels - LANES]], axis=1
        )
        parts = ((low, corner[a].astype(F32), 0), (inner[a].astype(F32), right[a].astype(F32), HALF_ROWS))
        for z in range(WZ):
            level = (a * WZ + WZ // 2 + z) % levels
            for row in range(HALF_ROWS):
                at = z * HALF_ROWS + row
                for wide, side, base in parts:
                    first = wide[at * cols : at * cols + SIDE] + side[at * SIDE : (at + 1) * SIDE]
                    rest = wide[at * cols + SIDE : (at + 1) * cols]
                    grad_input[level, base + row] = jnp.concatenate([first, rest], axis=0).astype(BF16)


def bias_kernel(chunks, *refs):
    *arrived, bias_grad, after = refs
    after[...] = jnp.zeros(after.shape, F32)
    main, rest, heads = chunks.main, chunks.rest, chunks.heads
    for a in range(arrived[0].shape[0]):
        total = arrived[0][a].astype(F32)
        for other in arrived[1:]:
            total += other[a].astype(F32)
        turned = jnp.transpose(total)
        for h in range(heads):
            at = (a * heads + h) * chunks.size
            if main:
                bias_grad[at : at + main, 0, :] = turned[h * main : (h + 1) * main]
            if rest:
                low = heads * main + h * rest
                bias_grad[at + main : at + chunks.size, 0, :] = turned[low : low + rest]


def vmem(count):
    return [pl.BlockSpec(memory_space=pltpu.VMEM)] * count


def call(kernel, outs, args, flops=0):
    return pl.pallas_call(
        kernel,
        out_shape=outs,
        in_specs=vmem(len(args)),
        out_specs=vmem(len(outs)),
        compiler_params=pltpu.CompilerParams(vmem_limit_bytes=40 * 2**20),
        cost_estimate=pl.CostEstimate(flops=flops, bytes_accessed=0, transcendentals=0),
    )(*args)


def shift(value, rows, cols):
    lat_count, lon_count = lax.axis_size("lat"), lax.axis_size("lon")
    pairs = []
    for i in range(lat_count):
        for j in range(lon_count):
            to = (i + rows) % lat_count * lon_count + (j + cols) % lon_count
            pairs.append((i * lon_count + j, to))
    return lax.ppermute(value, ("lat", "lon"), pairs)


def local(tokens, cotangent, norm_gain, inproj_weight, outproj_weight, bias):
    levels, rows, cols, channels = tokens.shape
    level_windows, _, heads = bias.shape[:3]
    lat_count, lon_count = lax.axis_size("lat"), lax.axis_size("lon")
    chunks = Chunks(lon_count, heads)
    windows = cols // WW
    struct = jax.ShapeDtypeStruct
    half, side = WZ * HALF_ROWS * cols, WZ * HALF_ROWS * SIDE
    gain = norm_gain.reshape(1, channels)
    queries = jnp.asarray(chunks.queries(), BF16)

    bias = bias.reshape(level_windows, heads, WT, WT)
    both = jnp.concatenate([tokens, cotangent], axis=-1)
    narrow = narrow_order(cols)
    (below,) = call(
        send_kernel,
        [struct((level_windows, narrow.shape[0], 2 * channels), BF16)],
        (both, jnp.asarray(narrow, BF16)),
    )
    below = shift(below, -1, 0)
    inner, right, corner = call(
        side_kernel,
        [struct((level_windows, size, 2 * channels), BF16) for size in (half, side, side)],
        (both, bias),
    )
    right = shift(right, 0, -1)
    corner = shift(corner, -1, -1)
    (bias_t,) = call(
        functools.partial(prep_kernel, chunks, lat_count),
        [struct((level_windows, lon_count, WT, chunks.width), F32)],
        (bias,),
    )
    per_window = []
    total = []
    for c in range(windows):
        last = c == windows - 1
        pieces = (inner, below) + ((right, corner) if last else ())
        if last:
            sums = [struct((level_windows, WT, chunks.width), BF16)] * lon_count
        else:
            sums = [struct((level_windows, lon_count, WT, chunks.width), F32)]
        order = jnp.asarray(window_order(cols, c, True), BF16)
        results = call(
            functools.partial(scores_kernel, chunks, len(pieces), c == 0, last),
            [
                struct((level_windows * WT, channels), F32),
                struct((level_windows * WT, LANES), F32),
                struct((level_windows * WT, channels), BF16),
                struct((level_windows, lon_count * chunks.rows, channels), BF16),
                struct((level_windows, lon_count * chunks.rows, channels), BF16),
                struct((level_windows, WT, lon_count * chunks.width), BF16),
                struct((level_windows, WT, lon_count * chunks.width), BF16),
            ]
            + sums,
            (*pieces, gain, inproj_weight, outproj_weight, bias_t, order, queries, *total),
            flops=10**9,
        )
        per_window.append(results[:7])
        total = results[7:]
    arrived = [total[0]]
    for d in range(1, lon_count):
        pairs = [(i, partner(i, d, lon_count)) for i in range(lon_count)]
        arrived.append(lax.ppermute(total[d], "lon", pairs))
    wide = struct((level_windows, half, channels), BF16)
    thin = struct((level_windows, side, channels), BF16)
    grads = []
    for c in reversed(range(windows)):
        last = c == windows - 1
        order = jnp.asarray(window_order(cols, c, False).T, BF16)
        results = call(
            functools.partial(tokens_kernel, chunks, 2, last),
            [wide, wide, thin, thin] if last else [wide, struct((half, level_windows * channels), BF16)],
            (*per_window[c], gain, inproj_weight, order, queries, *grads),
        )
        grads = results[:2]
        if last:
            left, corner = shift(results[2], 0, 1), shift(results[3], 1, 1)
    above = shift(grads[1], 1, 0)
    bias_grad, after = call(
        functools.partial(bias_kernel, chunks),
        [struct((level_windows * heads * chunks.size, 1, WT), F32), struct((8, LANES), F32)],
        arrived,
    )
    (grad_input,) = call(join_kernel, [struct(tokens.shape, BF16)], (grads[0], above, left, corner, after))
    bias_grad = bias_grad.reshape(level_windows, heads, chunks.size, 1, WT)
    return grad_input, jnp.transpose(bias_grad, (0, 3, 1, 2, 4))


def solution(mesh):
    placed = (
        P(None, "lat", "lon", None),
        P(None, "lat", "lon", None),
        P(),
        P(),
        P(),
        P(None, "lat", None, None, None),
    )
    return jax.shard_map(
        local,
        mesh=mesh,
        in_specs=placed,
        out_specs=(P(None, "lat", "lon", None), P(None, "lat", None, "lon", None)),
        check_vma=False,
    )
```

```python
import functools

import jax
import jax.numpy as jnp
import numpy as np
from jax import lax
from jax.experimental import pallas as pl
from jax.experimental.pallas import tpu as pltpu
from jax.sharding import PartitionSpec as P

WZ = 2
WH = 6
WW = 12
WT = WZ * WH * WW
HALF_ROWS = WH // 2
HALF_COLS = WW // 2
SIDE = 8
LEVEL = WH * WW
LANES = 128
LOG2E = 1.4426950408889634
epsilon = 1e-05
F32 = jnp.float32
BF16 = jnp.bfloat16
NT = (((1,), (1,)), ((), ()))


def dot(a, b):
    return jnp.dot(a, b, preferred_element_type=F32)


def dot_nt(a, b):
    return lax.dot_general(a, b, NT, preferred_element_type=F32)


def round_up(value, to):
    return (value + to - 1) // to * to


class Chunks:
    def __init__(self, parts, heads):
        self.parts, self.heads = parts, heads
        self.size = WT // parts
        self.main = self.size // 16 * 16
        self.rest = self.size - self.main
        self.rest_rows = round_up(heads * self.rest, 16)
        self.rows = self.main + self.rest_rows
        self.used = heads * self.main + self.rest_rows
        self.width = round_up(self.used, LANES)

    def queries(self):
        table = np.zeros((self.parts, self.rows, WT), np.float32)
        for j in range(self.parts):
            for i in range(self.main):
                table[j, i, j * self.size + i] = 1.0
            for h in range(self.heads):
                for i in range(self.rest):
                    table[j, self.main + h * self.rest + i, j * self.size + self.main + i] = 1.0
        return table

    def columns(self, j):
        lane = lax.broadcasted_iota(jnp.int32, (1, self.width), 1)
        low = self.heads * self.main
        main, left = lane, self.main + lane - low
        for h in range(1, self.heads):
            main -= jnp.where(lane >= h * self.main, self.main, 0)
            left -= jnp.where(lane >= low + h * self.rest, self.rest, 0)
        return j * self.size + jnp.where(lane < low, main, left)


def window_order(cols, c, narrow):
    last = c == cols // WW - 1
    part, side = HALF_ROWS * cols, HALF_ROWS * SIDE
    kept = cols - HALF_COLS if narrow else cols
    near = WZ * part + round_up(WZ * HALF_ROWS * kept, 16)
    table = np.zeros((WT, near + last * 2 * WZ * side), np.float32)
    for z in range(WZ):
        for r in range(WH):
            for w in range(WW):
                col = c * WW + w + HALF_COLS
                low, row = divmod(r, HALF_ROWS)
                if col >= cols:
                    at = near + (low * WZ + z) * side + row * SIDE + col - cols
                elif low:
                    at = WZ * part + (z * HALF_ROWS + row) * kept + col - (cols - kept)
                else:
                    at = z * part + row * cols + col
                table[(z * WH + r) * WW + w, at] = 1.0
    return table


def level_rows(field, a, base):
    levels = field.shape[0]
    at = [(a * WZ + WZ // 2 + z) % levels for z in range(WZ)]
    return [field[level, base + row].astype(F32) for level in at for row in range(HALF_ROWS)]


def send_kernel(both, inner, below, right, corner):
    cols = both.shape[2]
    kept = cols - HALF_COLS
    shape = (below.shape[1], WZ * HALF_ROWS * cols)
    row = lax.broadcasted_iota(jnp.int32, shape, 0)
    target = row + HALF_COLS
    for i in range(1, WZ * HALF_ROWS):
        target += jnp.where(row >= i * kept, HALF_COLS, 0)
    kept_rows = (lax.broadcasted_iota(jnp.int32, shape, 1) == target) & (row < WZ * HALF_ROWS * kept)
    narrow = kept_rows.astype(F32).astype(BF16)
    for a in range(inner.shape[0]):
        low, high = level_rows(both, a, 0), level_rows(both, a, HALF_ROWS)
        below[a] = dot(narrow, jnp.concatenate(low, axis=0).astype(BF16)).astype(BF16)
        inner[a] = jnp.concatenate(high, axis=0).astype(BF16)
        right[a] = jnp.concatenate([row[:SIDE] for row in high], axis=0).astype(BF16)
        corner[a] = jnp.concatenate([row[:SIDE] for row in low], axis=0).astype(BF16)


def prep_kernel(chunks, lat_count, bias, bias_t):
    level_windows = bias.shape[0]
    last_lat = lax.axis_index("lat") == lat_count - 1
    me = lax.axis_index("lon")
    parts, size, main = chunks.parts, chunks.size, chunks.main

    def labels(index, window):
        level_label = (index >= LEVEL) & (window == level_windows - 1)
        in_level = jnp.where(index >= LEVEL, index - LEVEL, index)
        row_label = (in_level >= LEVEL // 2) & last_lat
        return level_label.astype(jnp.int32) * 2 + row_label.astype(jnp.int32)

    key_index = lax.broadcasted_iota(jnp.int32, (WT, chunks.width), 0)
    for window in range(level_windows):
        key_labels = labels(key_index, window)
        for j in range(parts):
            heads = range(chunks.heads)
            low = j * size
            rows = []
            if main:
                rows += [bias[window, h, low : low + main, :] for h in heads]
            if chunks.rest:
                rows += [bias[window, h, low + main : low + size, :] for h in heads]
            spare = chunks.width - chunks.heads * size
            if spare:
                rows.append(jnp.zeros((spare, WT), F32))
            turned = jnp.transpose(jnp.concatenate(rows, axis=0)) * LOG2E
            allowed = key_labels == labels(chunks.columns(j), window)
            slot = me ^ j if parts & (parts - 1) == 0 else lax.rem(j - me + parts, parts)
            bias_t[window, slot] = jnp.where(allowed, turned, -1e30)


def head_masks(chunks, channels):
    head_dim = channels // chunks.heads
    lane_head = lax.broadcasted_iota(jnp.int32, (1, channels), 1) // head_dim
    lanes = [lane_head == h for h in range(chunks.heads)]
    rest = None
    if chunks.rest:
        row = lax.broadcasted_iota(jnp.int32, (chunks.rest_rows, channels), 0)
        lane = lax.broadcasted_iota(jnp.int32, (chunks.rest_rows, channels), 1) // head_dim
        rest = jnp.zeros((chunks.rest_rows, channels), F32)
        for h in range(chunks.heads):
            inside = (row >= h * chunks.rest) & (row < (h + 1) * chunks.rest) & (lane == h)
            rest = jnp.where(inside, 1.0, rest)
    return lanes, rest


def stack_heads(chunks, value, d, lane_masks, rest_mask):
    low = d * chunks.rows
    main = value[low : low + chunks.main]
    pieces = [main * mask for mask in lane_masks] if chunks.main else []
    if chunks.rest:
        pieces.append(value[low + chunks.main : low + chunks.rows] * rest_mask)
    if chunks.width > chunks.used:
        pieces.append(jnp.zeros((chunks.width - chunks.used, value.shape[1]), value.dtype))
    return jnp.concatenate(pieces, axis=0)


def split(inproj):
    channels = inproj.shape[0]
    return [inproj[:, part * channels : (part + 1) * channels] for part in range(3)]


def partner(me, d, parts):
    return me ^ d if parts & (parts - 1) == 0 else (me + d) % parts


def rolled(ref, parts):
    me = lax.axis_index("lon")
    return jnp.concatenate([ref[partner(me, d, parts)] for d in range(parts)], axis=0)


def scores_kernel(chunks, near, first, last, *refs):
    pieces, refs = refs[:near], refs[near:]
    gain_ref, inproj, outproj, bias_t, perm, queries, *refs = refs
    weights = split(inproj)
    before = None
    if not first:
        before, *refs = refs
    standard_out, scale_out, keys_out, query_out, up_out, p_out, ds_out, *totals = refs
    parts, width = chunks.parts, chunks.width
    channels = outproj.shape[0]
    scaling = (channels // chunks.heads) ** (-0.5)
    lanes, rest_mask = head_masks(chunks, channels)
    lanes = [mask.astype(F32).astype(BF16) for mask in lanes]
    rest_mask = rest_mask.astype(BF16) if chunks.rest else None
    choose = rolled(queries, parts)
    level_windows = pieces[0].shape[0]
    tile = channels // LANES * LANES
    from_tile = jnp.concatenate([jnp.zeros((channels, channels - tile), BF16), outproj[...]], axis=1)
    ts, us = [], []
    for a in range(level_windows):
        moved = dot(perm[...], jnp.concatenate([piece[a] for piece in pieces], axis=0))
        ts.append(moved[:, :channels])
        us.append(dot_nt(moved[:, tile:].astype(BF16), from_tile).astype(BF16))
    t = jnp.concatenate(ts, axis=0)
    centred = t - jnp.mean(t, axis=-1, keepdims=True)
    inverse_rms = lax.rsqrt(jnp.mean(centred * centred, axis=-1, keepdims=True) + epsilon)
    standard = centred * inverse_rms
    standard_out[...] = standard
    scale_out[...] = jnp.broadcast_to(inverse_rms, scale_out.shape)
    normed = (standard * gain_ref[...]).astype(BF16)
    q = dot(normed, weights[0]).astype(BF16)
    k = dot(normed, weights[1]).astype(BF16)
    v = dot(normed, weights[2]).astype(BF16)
    keys_out[...] = k
    for a in range(level_windows):
        cut = slice(a * WT, (a + 1) * WT)
        query = dot(choose, q[cut]).astype(BF16)
        up = dot(choose, us[a]).astype(BF16)
        query_out[a] = query
        up_out[a] = up
        for d in range(parts):
            at = slice(d * width, (d + 1) * width)
            s = dot_nt(k[cut], stack_heads(chunks, query, d, lanes, rest_mask))
            dp = dot_nt(v[cut], stack_heads(chunks, up, d, lanes, rest_mask))
            e = jnp.exp2(s * (scaling * LOG2E) + bias_t[a, d])
            p = e * (1.0 / jnp.sum(e, axis=0, keepdims=True))
            ds = p * (dp - jnp.sum(p * dp, axis=0, keepdims=True))
            p_out[a, :, at] = p.astype(BF16)
            ds_out[a, :, at] = ds.astype(BF16)
            if not first:
                ds += before[a, d]
            if last:
                totals[d][a] = ds.astype(BF16)
            else:
                totals[0][a, d] = ds


def tokens_kernel(chunks, near, first, *refs):
    standard_in, scale_in, keys, queries_in, ups, p_in, ds_in, gain_ref, inproj, perm_t, queries, *refs = refs
    weights = split(inproj)
    before = None
    if not first:
        before, refs = refs[:2], refs[2:]
    outs = refs
    parts, width = chunks.parts, chunks.width
    channels = keys.shape[-1]
    head_dim = channels // chunks.heads
    scaling = head_dim ** (-0.5)
    lanes, rest_mask = head_masks(chunks, channels)
    low_lanes = [mask.astype(F32).astype(BF16) for mask in lanes]
    low_rest = rest_mask.astype(BF16) if chunks.rest else None
    choose_t = jnp.transpose(rolled(queries, parts).astype(F32)).astype(BF16)
    level_windows = p_in.shape[0]
    dqs, dks, dvs = [], [], []
    for a in range(level_windows):
        query, up = queries_in[a], ups[a]
        qs = jnp.concatenate(
            [stack_heads(chunks, query, d, low_lanes, low_rest) for d in range(parts)], axis=0
        )
        us = jnp.concatenate(
            [stack_heads(chunks, up, d, low_lanes, low_rest) for d in range(parts)], axis=0
        )
        ds = ds_in[a]
        dks.append((dot(ds, qs) * scaling).astype(BF16))
        dvs.append(dot(p_in[a], us).astype(BF16))
        turned = jnp.transpose(ds)
        key = keys[a * WT : (a + 1) * WT]
        main = []
        for lane in range(0, channels, LANES):
            low = lane // head_dim
            many = min(LANES // head_dim, chunks.heads - low)
            if not chunks.main:
                break
            some = [turned[d * width + low * chunks.main :][: many * chunks.main] for d in range(parts)]
            flat = dot(jnp.concatenate(some, axis=0), key[:, lane : lane + LANES])
            tiles = []
            for d in range(parts):
                picked = flat[d * many * chunks.main :][: chunks.main]
                for h in range(1, many):
                    mask = lanes[low + h][:, lane : lane + LANES]
                    picked = jnp.where(mask, flat[(d * many + h) * chunks.main :][: chunks.main], picked)
                tiles.append(picked)
            main.append(tiles)
        if chunks.rest:
            low = chunks.heads * chunks.main
            some = [turned[d * width + low :][: chunks.rest_rows] for d in range(parts)]
            left = dot(jnp.concatenate(some, axis=0), key)
        rows = []
        for d in range(parts):
            if chunks.main:
                rows.append(jnp.concatenate([tiles[d] for tiles in main], axis=1))
            if chunks.rest:
                rows.append(left[d * chunks.rest_rows : (d + 1) * chunks.rest_rows] * rest_mask)
        picked = (jnp.concatenate(rows, axis=0) * scaling).astype(BF16)
        dqs.append(dot(choose_t, picked).astype(BF16))
    dq, dk, dv = (jnp.concatenate(parts_of, axis=0) for parts_of in (dqs, dks, dvs))
    scaled = (dot_nt(dq, weights[0]) + dot_nt(dk, weights[1]) + dot_nt(dv, weights[2])) * gain_ref[...]
    standard = standard_in[...]
    inverse_rms = scale_in[:, :1]
    grad = inverse_rms * (
        scaled
        - jnp.mean(scaled, axis=-1, keepdims=True)
        - standard * jnp.mean(scaled * standard, axis=-1, keepdims=True)
    )
    grad = grad.astype(BF16)
    lows = []
    for a in range(level_windows):
        spread = dot(perm_t[...], grad[a * WT : (a + 1) * WT])
        base = 0
        for i, out in enumerate(outs):
            rows = out.shape[-2]
            part = spread[base : base + rows]
            if not first and i < 2:
                part += before[i][a].astype(F32)
            if not first and i == 1:
                lows.append(part)
            else:
                out[a] = part.astype(BF16)
            base += rows
    if not first:
        packed = [low[:, :LANES] for low in lows] + [low[:, LANES:] for low in lows]
        outs[1][...] = jnp.concatenate(packed, axis=1).astype(BF16)


def join_kernel(corner, below, right, inner, after, grad_input):
    levels, _, cols, channels = grad_input.shape
    level_windows = levels // WZ
    whole = below[...].astype(F32)
    for a in range(level_windows):
        rest_at = level_windows * LANES + a * (channels - LANES)
        low = jnp.concatenate(
            [whole[:, a * LANES : (a + 1) * LANES], whole[:, rest_at : rest_at + channels - LANES]], axis=1
        )
        parts = ((low, corner[a].astype(F32), 0), (inner[a].astype(F32), right[a].astype(F32), HALF_ROWS))
        for z in range(WZ):
            level = (a * WZ + WZ // 2 + z) % levels
            for row in range(HALF_ROWS):
                at = z * HALF_ROWS + row
                for wide, side, base in parts:
                    first = wide[at * cols : at * cols + SIDE] + side[at * SIDE : (at + 1) * SIDE]
                    rest = wide[at * cols + SIDE : (at + 1) * cols]
                    grad_input[level, base + row] = jnp.concatenate([first, rest], axis=0).astype(BF16)


def bias_kernel(chunks, *refs):
    *arrived, bias_grad, after = refs
    after[...] = jnp.zeros(after.shape, F32)
    main, rest, heads = chunks.main, chunks.rest, chunks.heads
    for a in range(arrived[0].shape[0]):
        total = arrived[0][a].astype(F32)
        for other in arrived[1:]:
            total += other[a].astype(F32)
        turned = jnp.transpose(total)
        for h in range(heads):
            at = (a * heads + h) * chunks.size
            if main:
                bias_grad[at : at + main, 0, :] = turned[h * main : (h + 1) * main]
            if rest:
                low = heads * main + h * rest
                bias_grad[at + main : at + chunks.size, 0, :] = turned[low : low + rest]


def vmem(count):
    return [pl.BlockSpec(memory_space=pltpu.VMEM)] * count


def call(kernel, outs, args, flops=0):
    return pl.pallas_call(
        kernel,
        out_shape=outs,
        in_specs=vmem(len(args)),
        out_specs=vmem(len(outs)),
        compiler_params=pltpu.CompilerParams(vmem_limit_bytes=40 * 2**20),
        cost_estimate=pl.CostEstimate(flops=flops, bytes_accessed=0, transcendentals=0),
    )(*args)


def shift(value, rows, cols):
    lat_count, lon_count = lax.axis_size("lat"), lax.axis_size("lon")
    pairs = []
    for i in range(lat_count):
        for j in range(lon_count):
            to = (i + rows) % lat_count * lon_count + (j + cols) % lon_count
            pairs.append((i * lon_count + j, to))
    return lax.ppermute(value, ("lat", "lon"), pairs)


def local(tokens, cotangent, norm_gain, inproj_weight, outproj_weight, bias):
    levels, rows, cols, channels = tokens.shape
    level_windows, _, heads = bias.shape[:3]
    lat_count, lon_count = lax.axis_size("lat"), lax.axis_size("lon")
    chunks = Chunks(lon_count, heads)
    windows = cols // WW
    struct = jax.ShapeDtypeStruct
    half, side = WZ * HALF_ROWS * cols, WZ * HALF_ROWS * SIDE
    gain = norm_gain.reshape(1, channels)
    queries = jnp.asarray(chunks.queries(), BF16)

    bias = bias.reshape(level_windows, heads, WT, WT)
    both = jnp.concatenate([tokens, cotangent], axis=-1)
    narrow = round_up(WZ * HALF_ROWS * (cols - HALF_COLS), 16)
    inner, below, right, corner = call(
        send_kernel,
        [struct((level_windows, size, 2 * channels), BF16) for size in (half, narrow, side, side)],
        (both,),
    )
    below = shift(below, -1, 0)
    right = shift(right, 0, -1)
    corner = shift(corner, -1, -1)
    (bias_t,) = call(
        functools.partial(prep_kernel, chunks, lat_count),
        [struct((level_windows, lon_count, WT, chunks.width), F32)],
        (bias,),
    )
    per_window = []
    total = []
    for c in range(windows):
        last = c == windows - 1
        pieces = (inner, below) + ((right, corner) if last else ())
        if last:
            sums = [struct((level_windows, WT, chunks.width), BF16)] * lon_count
        else:
            sums = [struct((level_windows, lon_count, WT, chunks.width), F32)]
        order = jnp.asarray(window_order(cols, c, True), BF16)
        results = call(
            functools.partial(scores_kernel, chunks, len(pieces), c == 0, last),
            [
                struct((level_windows * WT, channels), F32),
                struct((level_windows * WT, LANES), F32),
                struct((level_windows * WT, channels), BF16),
                struct((level_windows, lon_count * chunks.rows, channels), BF16),
                struct((level_windows, lon_count * chunks.rows, channels), BF16),
                struct((level_windows, WT, lon_count * chunks.width), BF16),
                struct((level_windows, WT, lon_count * chunks.width), BF16),
            ]
            + sums,
            (*pieces, gain, inproj_weight, outproj_weight, bias_t, order, queries, *total),
            flops=10**9,
        )
        per_window.append(results[:7])
        total = results[7:]
    arrived = [total[0]]
    for d in range(1, lon_count):
        pairs = [(i, partner(i, d, lon_count)) for i in range(lon_count)]
        arrived.append(lax.ppermute(total[d], "lon", pairs))
    wide = struct((level_windows, half, channels), BF16)
    thin = struct((level_windows, side, channels), BF16)
    grads = []
    for c in reversed(range(windows)):
        last = c == windows - 1
        order = jnp.asarray(window_order(cols, c, False).T, BF16)
        results = call(
            functools.partial(tokens_kernel, chunks, 2, last),
            [wide, wide, thin, thin] if last else [wide, struct((half, level_windows * channels), BF16)],
            (*per_window[c], gain, inproj_weight, order, queries, *grads),
        )
        grads = results[:2]
        if last:
            left, corner = shift(results[2], 0, 1), shift(results[3], 1, 1)
    above = shift(grads[1], 1, 0)
    bias_grad, after = call(
        functools.partial(bias_kernel, chunks),
        [struct((level_windows * heads * chunks.size, 1, WT), F32), struct((8, LANES), F32)],
        arrived,
    )
    (grad_input,) = call(join_kernel, [struct(tokens.shape, BF16)], (corner, above, left, grads[0], after))
    bias_grad = bias_grad.reshape(level_windows, heads, chunks.size, 1, WT)
    return grad_input, jnp.transpose(bias_grad, (0, 3, 1, 2, 4))


def solution(mesh):
    placed = (
        P(None, "lat", "lon", None),
        P(None, "lat", "lon", None),
        P(),
        P(),
        P(),
        P(None, "lat", None, None, None),
    )
    return jax.shard_map(
        local,
        mesh=mesh,
        in_specs=placed,
        out_specs=(P(None, "lat", "lon", None), P(None, "lat", None, "lon", None)),
        check_vma=False,
    )
```

```python
import functools

import jax
import jax.numpy as jnp
import numpy as np
from jax import lax
from jax.experimental import pallas as pl
from jax.experimental.pallas import tpu as pltpu
from jax.sharding import PartitionSpec as P

WZ = 2
WH = 6
WW = 12
WT = WZ * WH * WW
HALF_ROWS = WH // 2
HALF_COLS = WW // 2
SIDE = 8
LEVEL = WH * WW
LANES = 128
LOG2E = 1.4426950408889634
epsilon = 1e-05
F32 = jnp.float32
BF16 = jnp.bfloat16
NT = (((1,), (1,)), ((), ()))


def dot(a, b):
    return jnp.dot(a, b, preferred_element_type=F32)


def dot_nt(a, b):
    return lax.dot_general(a, b, NT, preferred_element_type=F32)


def round_up(value, to):
    return (value + to - 1) // to * to


class Chunks:
    def __init__(self, parts, heads):
        self.parts, self.heads = parts, heads
        self.size = WT // parts
        self.main = self.size // 16 * 16
        self.rest = self.size - self.main
        self.rest_rows = round_up(heads * self.rest, 16)
        self.rows = self.main + self.rest_rows
        self.used = heads * self.main + self.rest_rows
        self.width = round_up(self.used, LANES)

    def queries(self):
        table = np.zeros((self.parts, self.rows, WT), np.float32)
        for j in range(self.parts):
            for i in range(self.main):
                table[j, i, j * self.size + i] = 1.0
            for h in range(self.heads):
                for i in range(self.rest):
                    table[j, self.main + h * self.rest + i, j * self.size + self.main + i] = 1.0
        return table

    def columns(self, j):
        lane = lax.broadcasted_iota(jnp.int32, (1, self.width), 1)
        low = self.heads * self.main
        main, left = lane, self.main + lane - low
        for h in range(1, self.heads):
            main -= jnp.where(lane >= h * self.main, self.main, 0)
            left -= jnp.where(lane >= low + h * self.rest, self.rest, 0)
        return j * self.size + jnp.where(lane < low, main, left)


def side_order(cols):
    part = HALF_ROWS * cols
    table = np.zeros((round_up(WZ * WH * HALF_COLS, 16), 2 * WZ * part), np.float32)
    for z in range(WZ):
        for r in range(WH):
            low, row = divmod(r, HALF_ROWS)
            for w in range(HALF_COLS):
                table[(z * WH + r) * HALF_COLS + w, (low * WZ + z) * part + row * cols + w] = 1.0
    return table


def window_order(cols, c, out):
    last = c == cols // WW - 1
    part, side = HALF_ROWS * cols, HALF_ROWS * SIDE
    kept = cols if out else cols - HALF_COLS
    near = WZ * part + round_up(WZ * HALF_ROWS * kept, 16)
    extra = round_up(WZ * WH * HALF_COLS, 16) if out else 2 * WZ * side
    table = np.zeros((WT, near + last * extra), np.float32)
    for z in range(WZ):
        for r in range(WH):
            for w in range(WW):
                col = c * WW + w + HALF_COLS
                low, row = divmod(r, HALF_ROWS)
                if col >= cols and out:
                    at = near + (z * WH + r) * HALF_COLS + col - cols
                elif col >= cols:
                    at = near + (low * WZ + z) * side + row * SIDE + col - cols
                elif low:
                    at = WZ * part + (z * HALF_ROWS + row) * kept + col - (cols - kept)
                else:
                    at = z * part + row * cols + col
                table[(z * WH + r) * WW + w, at] = 1.0
    return table


def level_rows(field, a, base):
    levels = field.shape[0]
    at = [(a * WZ + WZ // 2 + z) % levels for z in range(WZ)]
    return [field[level, base + row].astype(F32) for level in at for row in range(HALF_ROWS)]


def send_kernel(both, inner, below, right, corner):
    cols = both.shape[2]
    kept = cols - HALF_COLS
    shape = (below.shape[1], WZ * HALF_ROWS * cols)
    row = lax.broadcasted_iota(jnp.int32, shape, 0)
    target = row + HALF_COLS
    for i in range(1, WZ * HALF_ROWS):
        target += jnp.where(row >= i * kept, HALF_COLS, 0)
    kept_rows = (lax.broadcasted_iota(jnp.int32, shape, 1) == target) & (row < WZ * HALF_ROWS * kept)
    narrow = kept_rows.astype(F32).astype(BF16)
    for a in range(inner.shape[0]):
        low, high = level_rows(both, a, 0), level_rows(both, a, HALF_ROWS)
        below[a] = dot(narrow, jnp.concatenate(low, axis=0).astype(BF16)).astype(BF16)
        inner[a] = jnp.concatenate(high, axis=0).astype(BF16)
        right[a] = jnp.concatenate([row[:SIDE] for row in high], axis=0).astype(BF16)
        corner[a] = jnp.concatenate([row[:SIDE] for row in low], axis=0).astype(BF16)


def prep_kernel(chunks, lat_count, bias, bias_t):
    level_windows = bias.shape[0]
    last_lat = lax.axis_index("lat") == lat_count - 1
    me = lax.axis_index("lon")
    parts, size, main = chunks.parts, chunks.size, chunks.main

    def labels(index, window):
        level_label = (index >= LEVEL) & (window == level_windows - 1)
        in_level = jnp.where(index >= LEVEL, index - LEVEL, index)
        row_label = (in_level >= LEVEL // 2) & last_lat
        return level_label.astype(jnp.int32) * 2 + row_label.astype(jnp.int32)

    key_index = lax.broadcasted_iota(jnp.int32, (WT, chunks.width), 0)
    for window in range(level_windows):
        key_labels = labels(key_index, window)
        for j in range(parts):
            heads = range(chunks.heads)
            low = j * size
            rows = []
            if main:
                rows += [bias[window, h, low : low + main, :] for h in heads]
            if chunks.rest:
                rows += [bias[window, h, low + main : low + size, :] for h in heads]
            spare = chunks.width - chunks.heads * size
            if spare:
                rows.append(jnp.zeros((spare, WT), F32))
            turned = jnp.transpose(jnp.concatenate(rows, axis=0)) * LOG2E
            allowed = key_labels == labels(chunks.columns(j), window)
            bias_t[window, me ^ j] = jnp.where(allowed, turned, -1e30)


def head_masks(chunks, channels):
    head_dim = channels // chunks.heads
    lane_head = lax.broadcasted_iota(jnp.int32, (1, channels), 1) // head_dim
    lanes = [lane_head == h for h in range(chunks.heads)]
    rest = None
    if chunks.rest:
        row = lax.broadcasted_iota(jnp.int32, (chunks.rest_rows, channels), 0)
        lane = lax.broadcasted_iota(jnp.int32, (chunks.rest_rows, channels), 1) // head_dim
        rest = jnp.zeros((chunks.rest_rows, channels), F32)
        for h in range(chunks.heads):
            inside = (row >= h * chunks.rest) & (row < (h + 1) * chunks.rest) & (lane == h)
            rest = jnp.where(inside, 1.0, rest)
    return lanes, rest


def stack_heads(chunks, value, d, lane_masks, rest_mask):
    low = d * chunks.rows
    main = value[low : low + chunks.main]
    pieces = [main * mask for mask in lane_masks] if chunks.main else []
    if chunks.rest:
        pieces.append(value[low + chunks.main : low + chunks.rows] * rest_mask)
    if chunks.width > chunks.used:
        pieces.append(jnp.zeros((chunks.width - chunks.used, value.shape[1]), value.dtype))
    return jnp.concatenate(pieces, axis=0)


def split(inproj):
    channels = inproj.shape[0]
    return [inproj[:, part * channels : (part + 1) * channels] for part in range(3)]


def halving(parts, a):
    bits = [1 << i for i in range(parts.bit_length() - 1)]
    return bits if a % 2 else bits[::-1]


def held(parts, bits, stages):
    given = sum(bits[:stages])
    return [d for d in range(parts) if not d & given]


def place(d, total, keep, bit, kept, sent):
    if d in keep:
        kept[keep.index(d)] = total
    else:
        sent[keep.index(d ^ bit)] = total.astype(BF16)


def rolled(ref, parts):
    me = lax.axis_index("lon")
    return jnp.concatenate([ref[me ^ d] for d in range(parts)], axis=0)


def scores_kernel(chunks, near, first, last, *refs):
    pieces, refs = refs[:near], refs[near:]
    gain_ref, inproj, outproj, bias_t, perm, queries, *refs = refs
    weights = split(inproj)
    before = None
    if not first:
        before, *refs = refs
    standard_out, scale_out, keys_out, query_out, up_out, p_out, ds_out, *totals = refs
    parts, width = chunks.parts, chunks.width
    channels = outproj.shape[0]
    scaling = (channels // chunks.heads) ** (-0.5)
    lanes, rest_mask = head_masks(chunks, channels)
    lanes = [mask.astype(F32).astype(BF16) for mask in lanes]
    rest_mask = rest_mask.astype(BF16) if chunks.rest else None
    choose = rolled(queries, parts)
    level_windows = pieces[0].shape[0]
    tile = channels // LANES * LANES
    from_tile = jnp.concatenate([jnp.zeros((channels, channels - tile), BF16), outproj[...]], axis=1)
    ts, us = [], []
    for a in range(level_windows):
        moved = dot(perm[...], jnp.concatenate([piece[a] for piece in pieces], axis=0))
        ts.append(moved[:, :channels])
        us.append(dot_nt(moved[:, tile:].astype(BF16), from_tile).astype(BF16))
    t = jnp.concatenate(ts, axis=0)
    centred = t - jnp.mean(t, axis=-1, keepdims=True)
    inverse_rms = lax.rsqrt(jnp.mean(centred * centred, axis=-1, keepdims=True) + epsilon)
    standard = centred * inverse_rms
    standard_out[...] = standard
    scale_out[...] = jnp.broadcast_to(inverse_rms, scale_out.shape)
    normed = (standard * gain_ref[...]).astype(BF16)
    q = dot(normed, weights[0]).astype(BF16)
    k = dot(normed, weights[1]).astype(BF16)
    v = dot(normed, weights[2]).astype(BF16)
    keys_out[...] = k
    for a in range(level_windows):
        cut = slice(a * WT, (a + 1) * WT)
        query = dot(choose, q[cut]).astype(BF16)
        up = dot(choose, us[a]).astype(BF16)
        query_out[a] = query
        up_out[a] = up
        for d in range(parts):
            at = slice(d * width, (d + 1) * width)
            s = dot_nt(k[cut], stack_heads(chunks, query, d, lanes, rest_mask))
            dp = dot_nt(v[cut], stack_heads(chunks, up, d, lanes, rest_mask))
            e = jnp.exp2(s * (scaling * LOG2E) + bias_t[a, d])
            p = e * (1.0 / jnp.sum(e, axis=0, keepdims=True))
            ds = p * (dp - jnp.sum(p * dp, axis=0, keepdims=True))
            p_out[a, :, at] = p.astype(BF16)
            ds_out[a, :, at] = ds.astype(BF16)
            if not first:
                ds += before[a, d]
            if last:
                bits = halving(parts, a)
                place(d, ds, held(parts, bits, 1), bits[0], totals[2 * a], totals[2 * a + 1])
            else:
                totals[0][a, d] = ds


def tokens_kernel(chunks, near, first, *refs):
    standard_in, scale_in, keys, queries_in, ups, p_in, ds_in, gain_ref, inproj, perm_t, queries, *refs = refs
    weights = split(inproj)
    before = None
    if not first:
        before, refs = refs[:2], refs[2:]
    outs = refs
    parts, width = chunks.parts, chunks.width
    channels = keys.shape[-1]
    head_dim = channels // chunks.heads
    scaling = head_dim ** (-0.5)
    lanes, rest_mask = head_masks(chunks, channels)
    low_lanes = [mask.astype(F32).astype(BF16) for mask in lanes]
    low_rest = rest_mask.astype(BF16) if chunks.rest else None
    choose_t = jnp.transpose(rolled(queries, parts).astype(F32)).astype(BF16)
    level_windows = p_in.shape[0]
    dqs, dks, dvs = [], [], []
    for a in range(level_windows):
        query, up = queries_in[a], ups[a]
        qs = jnp.concatenate(
            [stack_heads(chunks, query, d, low_lanes, low_rest) for d in range(parts)], axis=0
        )
        us = jnp.concatenate(
            [stack_heads(chunks, up, d, low_lanes, low_rest) for d in range(parts)], axis=0
        )
        ds = ds_in[a]
        dks.append((dot(ds, qs) * scaling).astype(BF16))
        dvs.append(dot(p_in[a], us).astype(BF16))
        turned = jnp.transpose(ds)
        key = keys[a * WT : (a + 1) * WT]
        main = []
        for lane in range(0, channels, LANES):
            low = lane // head_dim
            many = min(LANES // head_dim, chunks.heads - low)
            if not chunks.main:
                break
            some = [turned[d * width + low * chunks.main :][: many * chunks.main] for d in range(parts)]
            flat = dot(jnp.concatenate(some, axis=0), key[:, lane : lane + LANES])
            tiles = []
            for d in range(parts):
                picked = flat[d * many * chunks.main :][: chunks.main]
                for h in range(1, many):
                    mask = lanes[low + h][:, lane : lane + LANES]
                    picked = jnp.where(mask, flat[(d * many + h) * chunks.main :][: chunks.main], picked)
                tiles.append(picked)
            main.append(tiles)
        if chunks.rest:
            low = chunks.heads * chunks.main
            some = [turned[d * width + low :][: chunks.rest_rows] for d in range(parts)]
            left = dot(jnp.concatenate(some, axis=0), key)
        rows = []
        for d in range(parts):
            if chunks.main:
                rows.append(jnp.concatenate([tiles[d] for tiles in main], axis=1))
            if chunks.rest:
                rows.append(left[d * chunks.rest_rows : (d + 1) * chunks.rest_rows] * rest_mask)
        picked = (jnp.concatenate(rows, axis=0) * scaling).astype(BF16)
        dqs.append(dot(choose_t, picked).astype(BF16))
    dq, dk, dv = (jnp.concatenate(parts_of, axis=0) for parts_of in (dqs, dks, dvs))
    scaled = (dot_nt(dq, weights[0]) + dot_nt(dk, weights[1]) + dot_nt(dv, weights[2])) * gain_ref[...]
    standard = standard_in[...]
    inverse_rms = scale_in[:, :1]
    grad = inverse_rms * (
        scaled
        - jnp.mean(scaled, axis=-1, keepdims=True)
        - standard * jnp.mean(scaled * standard, axis=-1, keepdims=True)
    )
    grad = grad.astype(BF16)
    for a in range(level_windows):
        spread = dot(perm_t[...], grad[a * WT : (a + 1) * WT])
        base = 0
        for i, out in enumerate(outs):
            rows = out.shape[1]
            part = spread[base : base + rows]
            if not first and i < 2:
                part += before[i][a].astype(F32)
            out[a] = part.astype(BF16)
            base += rows


def merge_kernel(inner_in, below_in, side, order_t, inner, below):
    half = inner.shape[1]
    lows = []
    for a in range(inner.shape[0]):
        spread = dot(order_t[...], side[a])
        inner[a] = (inner_in[a].astype(F32) + spread[:half]).astype(BF16)
        lows.append(below_in[a].astype(F32) + spread[half:])
    packed = [low[:, :LANES] for low in lows] + [low[:, LANES:] for low in lows]
    below[...] = jnp.concatenate(packed, axis=1).astype(BF16)


def join_kernel(inner, below, after, grad_input):
    levels, _, cols, channels = grad_input.shape
    level_windows = levels // WZ
    whole = below[...].astype(F32)
    for a in range(level_windows):
        rest_at = level_windows * LANES + a * (channels - LANES)
        low = jnp.concatenate(
            [whole[:, a * LANES : (a + 1) * LANES], whole[:, rest_at : rest_at + channels - LANES]], axis=1
        )
        high = inner[a].astype(F32)
        for z in range(WZ):
            level = (a * WZ + WZ // 2 + z) % levels
            for row in range(HALF_ROWS):
                at = slice((z * HALF_ROWS + row) * cols, (z * HALF_ROWS + row + 1) * cols)
                grad_input[level, row] = low[at].astype(BF16)
                grad_input[level, HALF_ROWS + row] = high[at].astype(BF16)


def fold_kernel(parts, stage, *refs):
    many = len(refs) // 4
    ins, outs = refs[: 2 * many], refs[2 * many :]
    for a in range(many):
        bits = halving(parts, a)
        keep = held(parts, bits, stage + 2)
        for i, d in enumerate(held(parts, bits, stage + 1)):
            total = ins[2 * a][i] + ins[2 * a + 1][i].astype(F32)
            place(d, total, keep, bits[stage + 1], outs[2 * a], outs[2 * a + 1])


def bias_kernel(chunks, *refs):
    *parts, bias_grad, after = refs
    after[...] = jnp.zeros(after.shape, F32)
    main, rest, heads = chunks.main, chunks.rest, chunks.heads
    for a in range(len(parts) // 2):
        total = parts[2 * a][0] + parts[2 * a + 1][0].astype(F32)
        turned = jnp.transpose(total)
        for h in range(heads):
            at = (a * heads + h) * chunks.size
            if main:
                bias_grad[at : at + main, 0, :] = turned[h * main : (h + 1) * main]
            if rest:
                low = heads * main + h * rest
                bias_grad[at + main : at + chunks.size, 0, :] = turned[low : low + rest]


def vmem(count):
    return [pl.BlockSpec(memory_space=pltpu.VMEM)] * count


def call(kernel, outs, args, flops=0):
    return pl.pallas_call(
        kernel,
        out_shape=outs,
        in_specs=vmem(len(args)),
        out_specs=vmem(len(outs)),
        compiler_params=pltpu.CompilerParams(vmem_limit_bytes=40 * 2**20),
        cost_estimate=pl.CostEstimate(flops=flops, bytes_accessed=0, transcendentals=0),
    )(*args)


def shift(value, rows, cols):
    lat_count, lon_count = lax.axis_size("lat"), lax.axis_size("lon")
    pairs = []
    for i in range(lat_count):
        for j in range(lon_count):
            to = (i + rows) % lat_count * lon_count + (j + cols) % lon_count
            pairs.append((i * lon_count + j, to))
    return lax.ppermute(value, ("lat", "lon"), pairs)


def local(tokens, cotangent, norm_gain, inproj_weight, outproj_weight, bias):
    levels, rows, cols, channels = tokens.shape
    level_windows, _, heads = bias.shape[:3]
    lat_count, lon_count = lax.axis_size("lat"), lax.axis_size("lon")
    chunks = Chunks(lon_count, heads)
    windows = cols // WW
    struct = jax.ShapeDtypeStruct
    half, side = WZ * HALF_ROWS * cols, WZ * HALF_ROWS * SIDE
    gain = norm_gain.reshape(1, channels)
    side_table = side_order(cols)
    queries = jnp.asarray(chunks.queries(), BF16)

    bias = bias.reshape(level_windows, heads, WT, WT)
    both = jnp.concatenate([tokens, cotangent], axis=-1)
    narrow = round_up(WZ * HALF_ROWS * (cols - HALF_COLS), 16)
    inner, below, right, corner = call(
        send_kernel,
        [struct((level_windows, size, 2 * channels), BF16) for size in (half, narrow, side, side)],
        (both,),
    )
    below = shift(below, -1, 0)
    right = shift(right, 0, -1)
    corner = shift(corner, -1, -1)
    (bias_t,) = call(
        functools.partial(prep_kernel, chunks, lat_count),
        [struct((level_windows, lon_count, WT, chunks.width), F32)],
        (bias,),
    )

    def half_slots(many):
        return [struct((many, WT, chunks.width), kind) for kind in (F32, BF16)] * level_windows

    per_window = []
    total = []
    for c in range(windows):
        last = c == windows - 1
        pieces = (inner, below) + ((right, corner) if last else ())
        if last:
            sums = half_slots(lon_count // 2)
        else:
            sums = [struct((level_windows, lon_count, WT, chunks.width), F32)]
        order = jnp.asarray(window_order(cols, c, False), BF16)
        results = call(
            functools.partial(scores_kernel, chunks, len(pieces), c == 0, last),
            [
                struct((level_windows * WT, channels), F32),
                struct((level_windows * WT, LANES), F32),
                struct((level_windows * WT, channels), BF16),
                struct((level_windows, lon_count * chunks.rows, channels), BF16),
                struct((level_windows, lon_count * chunks.rows, channels), BF16),
                struct((level_windows, WT, lon_count * chunks.width), BF16),
                struct((level_windows, WT, lon_count * chunks.width), BF16),
            ]
            + sums,
            (*pieces, gain, inproj_weight, outproj_weight, bias_t, order, queries, *total),
            flops=10**9,
        )
        per_window.append(results[:7])
        total = results[7:]
    stages = len(halving(lon_count, 0))
    for stage in range(stages):
        arrived = []
        for a in range(level_windows):
            bit = halving(lon_count, a)[stage]
            pairs = [(i, i ^ bit) for i in range(lon_count)]
            arrived += [total[2 * a], lax.ppermute(total[2 * a + 1], "lon", pairs)]
        if stage < stages - 1:
            total = call(
                functools.partial(fold_kernel, lon_count, stage),
                half_slots(lon_count >> (stage + 2)),
                arrived,
            )
    grads = []
    for c in reversed(range(windows)):
        last = c == windows - 1
        outs = [struct((level_windows, half, channels), BF16)] * 2
        if last:
            outs.append(struct((level_windows, side_table.shape[0], channels), BF16))
        order = jnp.asarray(window_order(cols, c, True).T, BF16)
        results = call(
            functools.partial(tokens_kernel, chunks, 2, last),
            outs,
            (*per_window[c], gain, inproj_weight, order, queries, *grads),
        )
        grads = results[:2]
        if last:
            left = shift(results[2], 0, 1)
    g_inner, g_below = call(
        merge_kernel,
        [struct((level_windows, half, channels), BF16), struct((half, level_windows * channels), BF16)],
        (*grads, left, jnp.asarray(side_table.T, BF16)),
    )
    above = shift(g_below, 1, 0)
    bias_grad, after = call(
        functools.partial(bias_kernel, chunks),
        [struct((level_windows * heads * chunks.size, 1, WT), F32), struct((8, LANES), F32)],
        arrived,
    )
    (grad_input,) = call(join_kernel, [struct(tokens.shape, BF16)], (g_inner, above, after))
    bias_grad = bias_grad.reshape(level_windows, heads, chunks.size, 1, WT)
    return grad_input, jnp.transpose(bias_grad, (0, 3, 1, 2, 4))


def solution(mesh):
    placed = (
        P(None, "lat", "lon", None),
        P(None, "lat", "lon", None),
        P(),
        P(),
        P(),
        P(None, "lat", None, None, None),
    )
    return jax.shard_map(
        local,
        mesh=mesh,
        in_specs=placed,
        out_specs=(P(None, "lat", "lon", None), P(None, "lat", None, "lon", None)),
        check_vma=False,
    )
```

```python
import functools

import jax
import jax.numpy as jnp
import numpy as np
from jax import lax
from jax.experimental import pallas as pl
from jax.experimental.pallas import tpu as pltpu
from jax.sharding import PartitionSpec as P

WZ = 2
WH = 6
WW = 12
WT = WZ * WH * WW
HALF_ROWS = WH // 2
HALF_COLS = WW // 2
SIDE = 8
LEVEL = WH * WW
LANES = 128
LOG2E = 1.4426950408889634
epsilon = 1e-05
F32 = jnp.float32
BF16 = jnp.bfloat16
NT = (((1,), (1,)), ((), ()))


def dot(a, b):
    return jnp.dot(a, b, preferred_element_type=F32)


def dot_nt(a, b):
    return lax.dot_general(a, b, NT, preferred_element_type=F32)


def round_up(value, to):
    return (value + to - 1) // to * to


class Chunks:
    def __init__(self, parts, heads):
        self.parts, self.heads = parts, heads
        self.size = WT // parts
        self.main = self.size // 16 * 16
        self.rest = self.size - self.main
        self.rest_rows = round_up(heads * self.rest, 16)
        self.rows = self.main + self.rest_rows
        self.used = heads * self.main + self.rest_rows
        self.width = round_up(self.used, LANES)

    def queries(self):
        table = np.zeros((self.parts, self.rows, WT), np.float32)
        for j in range(self.parts):
            for i in range(self.main):
                table[j, i, j * self.size + i] = 1.0
            for h in range(self.heads):
                for i in range(self.rest):
                    table[j, self.main + h * self.rest + i, j * self.size + self.main + i] = 1.0
        return table

    def columns(self, j):
        lane = lax.broadcasted_iota(jnp.int32, (1, self.width), 1)
        low = self.heads * self.main
        main, left = lane, self.main + lane - low
        for h in range(1, self.heads):
            main -= jnp.where(lane >= h * self.main, self.main, 0)
            left -= jnp.where(lane >= low + h * self.rest, self.rest, 0)
        return j * self.size + jnp.where(lane < low, main, left)


def window_order(cols, c, narrow):
    last = c == cols // WW - 1
    part, side = HALF_ROWS * cols, HALF_ROWS * SIDE
    kept = cols - HALF_COLS if narrow else cols
    near = WZ * part + round_up(WZ * HALF_ROWS * kept, 16)
    table = np.zeros((WT, near + last * 2 * WZ * side), np.float32)
    for z in range(WZ):
        for r in range(WH):
            for w in range(WW):
                col = c * WW + w + HALF_COLS
                low, row = divmod(r, HALF_ROWS)
                if col >= cols:
                    at = near + (low * WZ + z) * side + row * SIDE + col - cols
                elif low:
                    at = WZ * part + (z * HALF_ROWS + row) * kept + col - (cols - kept)
                else:
                    at = z * part + row * cols + col
                table[(z * WH + r) * WW + w, at] = 1.0
    return table


def level_rows(field, a, base):
    levels = field.shape[0]
    at = [(a * WZ + WZ // 2 + z) % levels for z in range(WZ)]
    return [field[level, base + row].astype(F32) for level in at for row in range(HALF_ROWS)]


def send_kernel(both, inner, below, right, corner):
    cols = both.shape[2]
    kept = cols - HALF_COLS
    shape = (below.shape[1], WZ * HALF_ROWS * cols)
    row = lax.broadcasted_iota(jnp.int32, shape, 0)
    target = row + HALF_COLS
    for i in range(1, WZ * HALF_ROWS):
        target += jnp.where(row >= i * kept, HALF_COLS, 0)
    kept_rows = (lax.broadcasted_iota(jnp.int32, shape, 1) == target) & (row < WZ * HALF_ROWS * kept)
    narrow = kept_rows.astype(F32).astype(BF16)
    for a in range(inner.shape[0]):
        low, high = level_rows(both, a, 0), level_rows(both, a, HALF_ROWS)
        below[a] = dot(narrow, jnp.concatenate(low, axis=0).astype(BF16)).astype(BF16)
        inner[a] = jnp.concatenate(high, axis=0).astype(BF16)
        right[a] = jnp.concatenate([row[:SIDE] for row in high], axis=0).astype(BF16)
        corner[a] = jnp.concatenate([row[:SIDE] for row in low], axis=0).astype(BF16)


def prep_kernel(chunks, lat_count, bias, bias_t):
    level_windows = bias.shape[0]
    last_lat = lax.axis_index("lat") == lat_count - 1
    me = lax.axis_index("lon")
    parts, size, main = chunks.parts, chunks.size, chunks.main

    def labels(index, window):
        level_label = (index >= LEVEL) & (window == level_windows - 1)
        in_level = jnp.where(index >= LEVEL, index - LEVEL, index)
        row_label = (in_level >= LEVEL // 2) & last_lat
        return level_label.astype(jnp.int32) * 2 + row_label.astype(jnp.int32)

    key_index = lax.broadcasted_iota(jnp.int32, (WT, chunks.width), 0)
    for window in range(level_windows):
        key_labels = labels(key_index, window)
        for j in range(parts):
            heads = range(chunks.heads)
            low = j * size
            rows = []
            if main:
                rows += [bias[window, h, low : low + main, :] for h in heads]
            if chunks.rest:
                rows += [bias[window, h, low + main : low + size, :] for h in heads]
            spare = chunks.width - chunks.heads * size
            if spare:
                rows.append(jnp.zeros((spare, WT), F32))
            turned = jnp.transpose(jnp.concatenate(rows, axis=0))
            allowed = key_labels == labels(chunks.columns(j), window)
            slot = me ^ j if parts & (parts - 1) == 0 else lax.rem(j - me + parts, parts)
            bias_t[window, slot] = jnp.where(allowed, turned, -1e30)


def head_masks(chunks, channels):
    head_dim = channels // chunks.heads
    lane_head = lax.broadcasted_iota(jnp.int32, (1, channels), 1) // head_dim
    lanes = [lane_head == h for h in range(chunks.heads)]
    rest = None
    if chunks.rest:
        row = lax.broadcasted_iota(jnp.int32, (chunks.rest_rows, channels), 0)
        lane = lax.broadcasted_iota(jnp.int32, (chunks.rest_rows, channels), 1) // head_dim
        rest = jnp.zeros((chunks.rest_rows, channels), F32)
        for h in range(chunks.heads):
            inside = (row >= h * chunks.rest) & (row < (h + 1) * chunks.rest) & (lane == h)
            rest = jnp.where(inside, 1.0, rest)
    return lanes, rest


def stack_heads(chunks, value, d, lane_masks, rest_mask):
    low = d * chunks.rows
    main = value[low : low + chunks.main]
    pieces = [main * mask for mask in lane_masks] if chunks.main else []
    if chunks.rest:
        pieces.append(value[low + chunks.main : low + chunks.rows] * rest_mask)
    if chunks.width > chunks.used:
        pieces.append(jnp.zeros((chunks.width - chunks.used, value.shape[1]), value.dtype))
    return jnp.concatenate(pieces, axis=0)


def split(inproj):
    channels = inproj.shape[0]
    return [inproj[:, part * channels : (part + 1) * channels] for part in range(3)]


def partner(me, d, parts):
    return me ^ d if parts & (parts - 1) == 0 else (me + d) % parts


def rolled(ref, parts):
    me = lax.axis_index("lon")
    return jnp.concatenate([ref[partner(me, d, parts)] for d in range(parts)], axis=0)


def scores_kernel(chunks, near, first, last, *refs):
    pieces, refs = refs[:near], refs[near:]
    gain_ref, inproj, outproj, bias_t, perm, queries, *refs = refs
    weights = split(inproj)
    before = None
    if not first:
        before, *refs = refs
    standard_out, scale_out, keys_out, query_out, up_out, p_out, ds_out, *totals = refs
    parts, width = chunks.parts, chunks.width
    channels = outproj.shape[0]
    scaling = (channels // chunks.heads) ** (-0.5)
    lanes, rest_mask = head_masks(chunks, channels)
    lanes = [mask.astype(F32).astype(BF16) for mask in lanes]
    rest_mask = rest_mask.astype(BF16) if chunks.rest else None
    choose = rolled(queries, parts)
    level_windows = pieces[0].shape[0]
    tile = channels // LANES * LANES
    from_tile = jnp.concatenate([jnp.zeros((channels, channels - tile), BF16), outproj[...]], axis=1)
    ts, us = [], []
    for a in range(level_windows):
        moved = dot(perm[...], jnp.concatenate([piece[a] for piece in pieces], axis=0))
        ts.append(moved[:, :channels])
        us.append(dot_nt(moved[:, tile:].astype(BF16), from_tile).astype(BF16))
    t = jnp.concatenate(ts, axis=0)
    centred = t - jnp.mean(t, axis=-1, keepdims=True)
    inverse_rms = lax.rsqrt(jnp.mean(centred * centred, axis=-1, keepdims=True) + epsilon)
    standard = centred * inverse_rms
    standard_out[...] = standard
    scale_out[...] = jnp.broadcast_to(inverse_rms, scale_out.shape)
    normed = (standard * gain_ref[...]).astype(BF16)
    q = dot(normed, weights[0]).astype(BF16)
    k = dot(normed, weights[1]).astype(BF16)
    v = dot(normed, weights[2]).astype(BF16)
    keys_out[...] = k
    for a in range(level_windows):
        cut = slice(a * WT, (a + 1) * WT)
        query = dot(choose, q[cut]).astype(BF16)
        up = dot(choose, us[a]).astype(BF16)
        query_out[a] = query
        up_out[a] = up
        for d in range(parts):
            at = slice(d * width, (d + 1) * width)
            s = dot_nt(k[cut], stack_heads(chunks, query, d, lanes, rest_mask))
            dp = dot_nt(v[cut], stack_heads(chunks, up, d, lanes, rest_mask))
            e = jnp.exp2(s * (scaling * LOG2E) + bias_t[a, d])
            p = e * (1.0 / jnp.sum(e, axis=0, keepdims=True))
            ds = p * (dp - jnp.sum(p * dp, axis=0, keepdims=True))
            p_out[a, :, at] = p.astype(BF16)
            ds_out[a, :, at] = ds.astype(BF16)
            if not first:
                ds += before[a, d]
            if last:
                totals[d][a] = ds.astype(BF16)
            else:
                totals[0][a, d] = ds


def tokens_kernel(chunks, near, first, *refs):
    standard_in, scale_in, keys, queries_in, ups, p_in, ds_in, gain_ref, inproj, perm_t, queries, *refs = refs
    weights = split(inproj)
    before = None
    if not first:
        before, refs = refs[:2], refs[2:]
    outs = refs
    parts, width = chunks.parts, chunks.width
    channels = keys.shape[-1]
    head_dim = channels // chunks.heads
    scaling = head_dim ** (-0.5)
    lanes, rest_mask = head_masks(chunks, channels)
    low_lanes = [mask.astype(F32).astype(BF16) for mask in lanes]
    low_rest = rest_mask.astype(BF16) if chunks.rest else None
    choose_t = jnp.transpose(rolled(queries, parts).astype(F32)).astype(BF16)
    level_windows = p_in.shape[0]
    dqs, dks, dvs = [], [], []
    for a in range(level_windows):
        query, up = queries_in[a], ups[a]
        qs = jnp.concatenate(
            [stack_heads(chunks, query, d, low_lanes, low_rest) for d in range(parts)], axis=0
        )
        us = jnp.concatenate(
            [stack_heads(chunks, up, d, low_lanes, low_rest) for d in range(parts)], axis=0
        )
        ds = ds_in[a]
        dks.append((dot(ds, qs) * scaling).astype(BF16))
        dvs.append(dot(p_in[a], us).astype(BF16))
        turned = jnp.transpose(ds)
        key = keys[a * WT : (a + 1) * WT]
        main = []
        for lane in range(0, channels, LANES):
            low = lane // head_dim
            many = min(LANES // head_dim, chunks.heads - low)
            if not chunks.main:
                break
            some = [turned[d * width + low * chunks.main :][: many * chunks.main] for d in range(parts)]
            flat = dot(jnp.concatenate(some, axis=0), key[:, lane : lane + LANES])
            tiles = []
            for d in range(parts):
                picked = flat[d * many * chunks.main :][: chunks.main]
                for h in range(1, many):
                    mask = lanes[low + h][:, lane : lane + LANES]
                    picked = jnp.where(mask, flat[(d * many + h) * chunks.main :][: chunks.main], picked)
                tiles.append(picked)
            main.append(tiles)
        if chunks.rest:
            low = chunks.heads * chunks.main
            some = [turned[d * width + low :][: chunks.rest_rows] for d in range(parts)]
            left = dot(jnp.concatenate(some, axis=0), key)
        rows = []
        for d in range(parts):
            if chunks.main:
                rows.append(jnp.concatenate([tiles[d] for tiles in main], axis=1))
            if chunks.rest:
                rows.append(left[d * chunks.rest_rows : (d + 1) * chunks.rest_rows] * rest_mask)
        picked = (jnp.concatenate(rows, axis=0) * scaling).astype(BF16)
        dqs.append(dot(choose_t, picked).astype(BF16))
    dq, dk, dv = (jnp.concatenate(parts_of, axis=0) for parts_of in (dqs, dks, dvs))
    scaled = (dot_nt(dq, weights[0]) + dot_nt(dk, weights[1]) + dot_nt(dv, weights[2])) * gain_ref[...]
    standard = standard_in[...]
    inverse_rms = scale_in[:, :1]
    grad = inverse_rms * (
        scaled
        - jnp.mean(scaled, axis=-1, keepdims=True)
        - standard * jnp.mean(scaled * standard, axis=-1, keepdims=True)
    )
    grad = grad.astype(BF16)
    lows = []
    for a in range(level_windows):
        spread = dot(perm_t[...], grad[a * WT : (a + 1) * WT])
        base = 0
        for i, out in enumerate(outs):
            rows = out.shape[-2]
            part = spread[base : base + rows]
            if not first and i < 2:
                part += before[i][a].astype(F32)
            if not first and i == 1:
                lows.append(part)
            else:
                out[a] = part.astype(BF16)
            base += rows
    if not first:
        packed = [low[:, :LANES] for low in lows] + [low[:, LANES:] for low in lows]
        outs[1][...] = jnp.concatenate(packed, axis=1).astype(BF16)


def join_kernel(corner, below, right, inner, after, grad_input):
    levels, _, cols, channels = grad_input.shape
    level_windows = levels // WZ
    whole = below[...].astype(F32)
    for a in range(level_windows):
        rest_at = level_windows * LANES + a * (channels - LANES)
        low = jnp.concatenate(
            [whole[:, a * LANES : (a + 1) * LANES], whole[:, rest_at : rest_at + channels - LANES]], axis=1
        )
        parts = ((low, corner[a].astype(F32), 0), (inner[a].astype(F32), right[a].astype(F32), HALF_ROWS))
        for z in range(WZ):
            level = (a * WZ + WZ // 2 + z) % levels
            for row in range(HALF_ROWS):
                at = z * HALF_ROWS + row
                for wide, side, base in parts:
                    first = wide[at * cols : at * cols + SIDE] + side[at * SIDE : (at + 1) * SIDE]
                    rest = wide[at * cols + SIDE : (at + 1) * cols]
                    grad_input[level, base + row] = jnp.concatenate([first, rest], axis=0).astype(BF16)


def bias_kernel(chunks, *refs):
    *arrived, bias_grad, after = refs
    after[...] = jnp.zeros(after.shape, F32)
    main, rest, heads = chunks.main, chunks.rest, chunks.heads
    for a in range(arrived[0].shape[0]):
        total = arrived[0][a].astype(F32)
        for other in arrived[1:]:
            total += other[a].astype(F32)
        turned = jnp.transpose(total)
        for h in range(heads):
            at = (a * heads + h) * chunks.size
            if main:
                bias_grad[at : at + main, 0, :] = turned[h * main : (h + 1) * main]
            if rest:
                low = heads * main + h * rest
                bias_grad[at + main : at + chunks.size, 0, :] = turned[low : low + rest]


def vmem(count):
    return [pl.BlockSpec(memory_space=pltpu.VMEM)] * count


def call(kernel, outs, args, flops=0):
    return pl.pallas_call(
        kernel,
        out_shape=outs,
        in_specs=vmem(len(args)),
        out_specs=vmem(len(outs)),
        compiler_params=pltpu.CompilerParams(vmem_limit_bytes=40 * 2**20),
        cost_estimate=pl.CostEstimate(flops=flops, bytes_accessed=0, transcendentals=0),
    )(*args)


def shift(value, rows, cols):
    lat_count, lon_count = lax.axis_size("lat"), lax.axis_size("lon")
    pairs = []
    for i in range(lat_count):
        for j in range(lon_count):
            to = (i + rows) % lat_count * lon_count + (j + cols) % lon_count
            pairs.append((i * lon_count + j, to))
    return lax.ppermute(value, ("lat", "lon"), pairs)


def local(tokens, cotangent, norm_gain, inproj_weight, outproj_weight, bias):
    levels, rows, cols, channels = tokens.shape
    level_windows, _, heads = bias.shape[:3]
    lat_count, lon_count = lax.axis_size("lat"), lax.axis_size("lon")
    chunks = Chunks(lon_count, heads)
    windows = cols // WW
    struct = jax.ShapeDtypeStruct
    half, side = WZ * HALF_ROWS * cols, WZ * HALF_ROWS * SIDE
    gain = norm_gain.reshape(1, channels)
    queries = jnp.asarray(chunks.queries(), BF16)

    bias = bias.reshape(level_windows, heads, WT, WT)
    both = jnp.concatenate([tokens, cotangent], axis=-1)
    narrow = round_up(WZ * HALF_ROWS * (cols - HALF_COLS), 16)
    inner, below, right, corner = call(
        send_kernel,
        [struct((level_windows, size, 2 * channels), BF16) for size in (half, narrow, side, side)],
        (both,),
    )
    below = shift(below, -1, 0)
    right = shift(right, 0, -1)
    corner = shift(corner, -1, -1)
    (bias_t,) = call(
        functools.partial(prep_kernel, chunks, lat_count),
        [struct((level_windows, lon_count, WT, chunks.width), F32)],
        (bias * LOG2E,),
    )
    per_window = []
    total = []
    for c in range(windows):
        last = c == windows - 1
        pieces = (inner, below) + ((right, corner) if last else ())
        if last:
            sums = [struct((level_windows, WT, chunks.width), BF16)] * lon_count
        else:
            sums = [struct((level_windows, lon_count, WT, chunks.width), F32)]
        order = jnp.asarray(window_order(cols, c, True), BF16)
        results = call(
            functools.partial(scores_kernel, chunks, len(pieces), c == 0, last),
            [
                struct((level_windows * WT, channels), F32),
                struct((level_windows * WT, LANES), F32),
                struct((level_windows * WT, channels), BF16),
                struct((level_windows, lon_count * chunks.rows, channels), BF16),
                struct((level_windows, lon_count * chunks.rows, channels), BF16),
                struct((level_windows, WT, lon_count * chunks.width), BF16),
                struct((level_windows, WT, lon_count * chunks.width), BF16),
            ]
            + sums,
            (*pieces, gain, inproj_weight, outproj_weight, bias_t, order, queries, *total),
            flops=10**9,
        )
        per_window.append(results[:7])
        total = results[7:]
    arrived = [total[0]]
    for d in range(1, lon_count):
        pairs = [(i, partner(i, d, lon_count)) for i in range(lon_count)]
        arrived.append(lax.ppermute(total[d], "lon", pairs))
    wide = struct((level_windows, half, channels), BF16)
    thin = struct((level_windows, side, channels), BF16)
    grads = []
    for c in reversed(range(windows)):
        last = c == windows - 1
        order = jnp.asarray(window_order(cols, c, False).T, BF16)
        results = call(
            functools.partial(tokens_kernel, chunks, 2, last),
            [wide, wide, thin, thin] if last else [wide, struct((half, level_windows * channels), BF16)],
            (*per_window[c], gain, inproj_weight, order, queries, *grads),
        )
        grads = results[:2]
        if last:
            left, corner = shift(results[2], 0, 1), shift(results[3], 1, 1)
    above = shift(grads[1], 1, 0)
    bias_grad, after = call(
        functools.partial(bias_kernel, chunks),
        [struct((level_windows * heads * chunks.size, 1, WT), F32), struct((8, LANES), F32)],
        arrived,
    )
    (grad_input,) = call(join_kernel, [struct(tokens.shape, BF16)], (corner, above, left, grads[0], after))
    bias_grad = bias_grad.reshape(level_windows, heads, chunks.size, 1, WT)
    return grad_input, jnp.transpose(bias_grad, (0, 3, 1, 2, 4))


def solution(mesh):
    placed = (
        P(None, "lat", "lon", None),
        P(None, "lat", "lon", None),
        P(),
        P(),
        P(),
        P(None, "lat", None, None, None),
    )
    return jax.shard_map(
        local,
        mesh=mesh,
        in_specs=placed,
        out_specs=(P(None, "lat", "lon", None), P(None, "lat", None, "lon", None)),
        check_vma=False,
    )
```

```python
import functools

import jax
import jax.numpy as jnp
import numpy as np
from jax import lax
from jax.experimental import pallas as pl
from jax.experimental.pallas import tpu as pltpu
from jax.sharding import PartitionSpec as P

WZ = 2
WH = 6
WW = 12
WT = WZ * WH * WW
HALF_ROWS = WH // 2
HALF_COLS = WW // 2
SIDE = 8
LEVEL = WH * WW
LANES = 128
LOG2E = 1.4426950408889634
epsilon = 1e-05
F32 = jnp.float32
BF16 = jnp.bfloat16
NT = (((1,), (1,)), ((), ()))


def dot(a, b):
    return jnp.dot(a, b, preferred_element_type=F32)


def dot_nt(a, b):
    return lax.dot_general(a, b, NT, preferred_element_type=F32)


def round_up(value, to):
    return (value + to - 1) // to * to


class Chunks:
    def __init__(self, parts, heads):
        self.parts, self.heads = parts, heads
        self.size = WT // parts
        self.main = self.size // 16 * 16
        self.rest = self.size - self.main
        self.rest_rows = round_up(heads * self.rest, 16)
        self.rows = self.main + self.rest_rows
        self.used = heads * self.main + self.rest_rows
        self.width = round_up(self.used, LANES)

    def columns(self, j):
        lane = lax.broadcasted_iota(jnp.int32, (1, self.width), 1)
        low = self.heads * self.main
        main, left = lane, self.main + lane - low
        for h in range(1, self.heads):
            main -= jnp.where(lane >= h * self.main, self.main, 0)
            left -= jnp.where(lane >= low + h * self.rest, self.rest, 0)
        return j * self.size + jnp.where(lane < low, main, left)


def window_order(cols, c, narrow):
    last = c == cols // WW - 1
    part, side = HALF_ROWS * cols, HALF_ROWS * SIDE
    kept = cols - HALF_COLS if narrow else cols
    tail = narrow and last
    inner = WZ * (side if tail else part)
    near = inner + round_up(WZ * HALF_ROWS * kept, 16)
    table = np.zeros((WT, near + last * 2 * WZ * side), np.float32)
    for z in range(WZ):
        for r in range(WH):
            for w in range(WW):
                col = c * WW + w + HALF_COLS
                low, row = divmod(r, HALF_ROWS)
                if col >= cols:
                    at = near + (low * WZ + z) * side + row * SIDE + col - cols
                elif low:
                    at = inner + (z * HALF_ROWS + row) * kept + col - (cols - kept)
                elif tail:
                    at = z * side + row * SIDE + col - (cols - SIDE)
                else:
                    at = z * part + row * cols + col
                table[(z * WH + r) * WW + w, at] = 1.0
    return table


def level_rows(field, a, base):
    levels = field.shape[0]
    at = [(a * WZ + WZ // 2 + z) % levels for z in range(WZ)]
    return [field[level, base + row].astype(F32) for level in at for row in range(HALF_ROWS)]


def send_kernel(both, inner, below, right, corner, tail):
    cols = both.shape[2]
    kept = cols - HALF_COLS
    shape = (below.shape[1], WZ * HALF_ROWS * cols)
    row = lax.broadcasted_iota(jnp.int32, shape, 0)
    target = row + HALF_COLS
    for i in range(1, WZ * HALF_ROWS):
        target += jnp.where(row >= i * kept, HALF_COLS, 0)
    kept_rows = (lax.broadcasted_iota(jnp.int32, shape, 1) == target) & (row < WZ * HALF_ROWS * kept)
    narrow = kept_rows.astype(F32).astype(BF16)
    for a in range(inner.shape[0]):
        low, high = level_rows(both, a, 0), level_rows(both, a, HALF_ROWS)
        below[a] = dot(narrow, jnp.concatenate(low, axis=0).astype(BF16)).astype(BF16)
        inner[a] = jnp.concatenate(high, axis=0).astype(BF16)
        right[a] = jnp.concatenate([row[:SIDE] for row in high], axis=0).astype(BF16)
        tail[a] = jnp.concatenate([row[cols - SIDE :] for row in high], axis=0).astype(BF16)
        corner[a] = jnp.concatenate([row[:SIDE] for row in low], axis=0).astype(BF16)


def prep_kernel(chunks, lat_count, bias, bias_t):
    level_windows = bias.shape[0]
    last_lat = lax.axis_index("lat") == lat_count - 1
    parts, size, main = chunks.parts, chunks.size, chunks.main

    def labels(index, window):
        level_label = (index >= LEVEL) & (window == level_windows - 1)
        in_level = jnp.where(index >= LEVEL, index - LEVEL, index)
        row_label = (in_level >= LEVEL // 2) & last_lat
        return level_label.astype(jnp.int32) * 2 + row_label.astype(jnp.int32)

    key_index = lax.broadcasted_iota(jnp.int32, (WT, chunks.width), 0)
    for window in range(level_windows):
        key_labels = labels(key_index, window)
        for j in range(parts):
            heads = range(chunks.heads)
            low = j * size
            rows = []
            if main:
                rows += [bias[window, h, low : low + main, :] for h in heads]
            if chunks.rest:
                rows += [bias[window, h, low + main : low + size, :] for h in heads]
            spare = chunks.width - chunks.heads * size
            if spare:
                rows.append(jnp.zeros((spare, WT), F32))
            turned = jnp.transpose(jnp.concatenate(rows, axis=0)) * LOG2E
            allowed = key_labels == labels(chunks.columns(j), window)
            bias_t[window, j] = jnp.where(allowed, turned, -1e30)


def head_masks(chunks, channels):
    head_dim = channels // chunks.heads
    lane_head = lax.broadcasted_iota(jnp.int32, (1, channels), 1) // head_dim
    lanes = [lane_head == h for h in range(chunks.heads)]
    rest = None
    if chunks.rest:
        row = lax.broadcasted_iota(jnp.int32, (chunks.rest_rows, channels), 0)
        lane = lax.broadcasted_iota(jnp.int32, (chunks.rest_rows, channels), 1) // head_dim
        rest = jnp.zeros((chunks.rest_rows, channels), F32)
        for h in range(chunks.heads):
            inside = (row >= h * chunks.rest) & (row < (h + 1) * chunks.rest) & (lane == h)
            rest = jnp.where(inside, 1.0, rest)
    return lanes, rest


def stack_heads(chunks, value, j, lane_masks, rest_mask):
    low = j * chunks.size
    pieces = []
    if chunks.main:
        main = value[low : low + chunks.main].astype(BF16)
        pieces += [main * mask for mask in lane_masks]
    if chunks.rest:
        rows = [value[low + chunks.main : low + chunks.size]] * chunks.heads
        spare = chunks.rest_rows - chunks.heads * chunks.rest
        if spare:
            rows.append(jnp.zeros((spare, value.shape[1]), F32))
        pieces.append(jnp.concatenate(rows, axis=0).astype(BF16) * rest_mask)
    if chunks.width > chunks.used:
        pieces.append(jnp.zeros((chunks.width - chunks.used, value.shape[1]), BF16))
    return jnp.concatenate(pieces, axis=0)


def split(inproj):
    channels = inproj.shape[0]
    return [inproj[:, part * channels : (part + 1) * channels] for part in range(3)]


def partner(me, d, parts):
    return me ^ d if parts & (parts - 1) == 0 else (me + d) % parts


def scores_kernel(chunks, near, first, last, *refs):
    pieces, refs = refs[:near], refs[near:]
    gain_ref, inproj, outproj, bias_t, perm, *refs = refs
    weights = split(inproj)
    before = None
    if not first:
        before, *refs = refs
    standard_out, scale_out, keys_out, query_out, up_out, p_out, ds_out, *totals, turn = refs
    parts, width = chunks.parts, chunks.width
    channels = outproj.shape[0]
    scaling = (channels // chunks.heads) ** (-0.5)
    lanes, rest_mask = head_masks(chunks, channels)
    lanes = [mask.astype(F32).astype(BF16) for mask in lanes]
    rest_mask = rest_mask.astype(BF16) if chunks.rest else None
    me = lax.axis_index("lon")
    level_windows = pieces[0].shape[0]
    tile = channels // LANES * LANES
    from_tile = jnp.concatenate([jnp.zeros((channels, channels - tile), BF16), outproj[...]], axis=1)
    ts, us = [], []
    for a in range(level_windows):
        moved = dot(perm[...], jnp.concatenate([piece[a] for piece in pieces], axis=0))
        ts.append(moved[:, :channels])
        us.append(dot_nt(moved[:, tile:].astype(BF16), from_tile))
    t = jnp.concatenate(ts, axis=0)
    centred = t - jnp.mean(t, axis=-1, keepdims=True)
    inverse_rms = lax.rsqrt(jnp.mean(centred * centred, axis=-1, keepdims=True) + epsilon)
    standard = centred * inverse_rms
    standard_out[...] = standard
    scale_out[...] = jnp.broadcast_to(inverse_rms, scale_out.shape)
    normed = (standard * gain_ref[...]).astype(BF16)
    q = dot(normed, weights[0])
    query_out[...] = q
    k = dot(normed, weights[1]).astype(BF16)
    v = dot(normed, weights[2]).astype(BF16)
    keys_out[...] = k
    for a in range(level_windows):
        cut = slice(a * WT, (a + 1) * WT)
        query, up = q[cut], us[a]
        up_out[cut] = up
        for d in range(parts):
            at = slice(d * width, (d + 1) * width)
            s = dot_nt(k[cut], stack_heads(chunks, query, d, lanes, rest_mask))
            dp = dot_nt(v[cut], stack_heads(chunks, up, d, lanes, rest_mask))
            e = jnp.exp2(s * (scaling * LOG2E) + bias_t[a, d])
            p = e * (1.0 / jnp.sum(e, axis=0, keepdims=True))
            ds = p * (dp - jnp.sum(p * dp, axis=0, keepdims=True))
            p_out[a, :, at] = p.astype(BF16)
            ds_out[a, :, at] = ds.astype(BF16)
            if not first:
                ds += before[a, d]
            if last:
                turn[d] = ds.astype(BF16)
            else:
                totals[0][a, d] = ds
        if last:
            for d in range(parts):
                totals[d][a] = turn[partner(me, d, parts)]


def tokens_kernel(chunks, near, first, *refs):
    standard_in, scale_in, keys, queries_in, ups, p_in, ds_in, gain_ref, inproj, perm_t, *refs = refs
    weights = split(inproj)
    before = None
    if not first:
        before, refs = refs[:2], refs[2:]
    outs = refs
    parts, width = chunks.parts, chunks.width
    channels = keys.shape[-1]
    head_dim = channels // chunks.heads
    scaling = head_dim ** (-0.5)
    lanes, rest_mask = head_masks(chunks, channels)
    low_lanes = [mask.astype(F32).astype(BF16) for mask in lanes]
    low_rest = rest_mask.astype(BF16) if chunks.rest else None
    level_windows = p_in.shape[0]
    dqs, dks, dvs = [], [], []
    for a in range(level_windows):
        cut = slice(a * WT, (a + 1) * WT)
        query, up = queries_in[cut], ups[cut]
        qs = jnp.concatenate(
            [stack_heads(chunks, query, d, low_lanes, low_rest) for d in range(parts)], axis=0
        )
        us = jnp.concatenate(
            [stack_heads(chunks, up, d, low_lanes, low_rest) for d in range(parts)], axis=0
        )
        ds = ds_in[a]
        dks.append((dot(ds, qs) * scaling).astype(BF16))
        dvs.append(dot(p_in[a], us).astype(BF16))
        turned = jnp.transpose(ds)
        key = keys[a * WT : (a + 1) * WT]
        main = []
        for lane in range(0, channels, LANES):
            low = lane // head_dim
            many = min(LANES // head_dim, chunks.heads - low)
            if not chunks.main:
                break
            some = [turned[d * width + low * chunks.main :][: many * chunks.main] for d in range(parts)]
            flat = dot(jnp.concatenate(some, axis=0), key[:, lane : lane + LANES])
            tiles = []
            for d in range(parts):
                picked = flat[d * many * chunks.main :][: chunks.main]
                for h in range(1, many):
                    mask = lanes[low + h][:, lane : lane + LANES]
                    picked = jnp.where(mask, flat[(d * many + h) * chunks.main :][: chunks.main], picked)
                tiles.append(picked)
            main.append(tiles)
        if chunks.rest:
            low = chunks.heads * chunks.main
            some = [turned[d * width + low :][: chunks.rest_rows] for d in range(parts)]
            left = dot(jnp.concatenate(some, axis=0), key)
        rows = []
        for d in range(parts):
            if chunks.main:
                rows.append(jnp.concatenate([tiles[d] for tiles in main], axis=1))
            if chunks.rest:
                some = left[d * chunks.rest_rows : (d + 1) * chunks.rest_rows] * rest_mask
                total = some[: chunks.rest]
                for h in range(1, chunks.heads):
                    total += some[h * chunks.rest : (h + 1) * chunks.rest]
                rows.append(total)
        dqs.append((jnp.concatenate(rows, axis=0) * scaling).astype(BF16))
    dq, dk, dv = (jnp.concatenate(parts_of, axis=0) for parts_of in (dqs, dks, dvs))
    scaled = (dot_nt(dq, weights[0]) + dot_nt(dk, weights[1]) + dot_nt(dv, weights[2])) * gain_ref[...]
    standard = standard_in[...]
    inverse_rms = scale_in[:, :1]
    grad = inverse_rms * (
        scaled
        - jnp.mean(scaled, axis=-1, keepdims=True)
        - standard * jnp.mean(scaled * standard, axis=-1, keepdims=True)
    )
    grad = grad.astype(BF16)
    lows = []
    for a in range(level_windows):
        spread = dot(perm_t[...], grad[a * WT : (a + 1) * WT])
        base = 0
        for i, out in enumerate(outs):
            rows = out.shape[-2]
            part = spread[base : base + rows]
            if not first and i < 2:
                part += before[i][a].astype(F32)
            if not first and i == 1:
                lows.append(part)
            else:
                out[a] = part.astype(BF16)
            base += rows
    if not first:
        packed = [low[:, :LANES] for low in lows] + [low[:, LANES:] for low in lows]
        outs[1][...] = jnp.concatenate(packed, axis=1).astype(BF16)


def join_kernel(corner, below, right, inner, after, grad_input):
    levels, _, cols, channels = grad_input.shape
    level_windows = levels // WZ
    whole = below[...].astype(F32)
    for a in range(level_windows):
        rest_at = level_windows * LANES + a * (channels - LANES)
        low = jnp.concatenate(
            [whole[:, a * LANES : (a + 1) * LANES], whole[:, rest_at : rest_at + channels - LANES]], axis=1
        )
        parts = ((low, corner[a].astype(F32), 0), (inner[a].astype(F32), right[a].astype(F32), HALF_ROWS))
        for z in range(WZ):
            level = (a * WZ + WZ // 2 + z) % levels
            for row in range(HALF_ROWS):
                at = z * HALF_ROWS + row
                for wide, side, base in parts:
                    first = wide[at * cols : at * cols + SIDE] + side[at * SIDE : (at + 1) * SIDE]
                    rest = wide[at * cols + SIDE : (at + 1) * cols]
                    grad_input[level, base + row] = jnp.concatenate([first, rest], axis=0).astype(BF16)


def bias_kernel(chunks, *refs):
    *arrived, bias_grad, after = refs
    after[...] = jnp.zeros(after.shape, F32)
    main, rest, heads = chunks.main, chunks.rest, chunks.heads
    for a in range(arrived[0].shape[0]):
        total = arrived[0][a].astype(F32)
        for other in arrived[1:]:
            total += other[a].astype(F32)
        turned = jnp.transpose(total)
        for h in range(heads):
            at = (a * heads + h) * chunks.size
            if main:
                bias_grad[at : at + main, 0, :] = turned[h * main : (h + 1) * main]
            if rest:
                low = heads * main + h * rest
                bias_grad[at + main : at + chunks.size, 0, :] = turned[low : low + rest]


def vmem(count):
    return [pl.BlockSpec(memory_space=pltpu.VMEM)] * count


def call(kernel, outs, args, flops=0, scratch=()):
    return pl.pallas_call(
        kernel,
        out_shape=outs,
        in_specs=vmem(len(args)),
        out_specs=vmem(len(outs)),
        scratch_shapes=list(scratch),
        compiler_params=pltpu.CompilerParams(vmem_limit_bytes=40 * 2**20),
        cost_estimate=pl.CostEstimate(flops=flops, bytes_accessed=0, transcendentals=0),
    )(*args)


def shift(value, rows, cols):
    lat_count, lon_count = lax.axis_size("lat"), lax.axis_size("lon")
    pairs = []
    for i in range(lat_count):
        for j in range(lon_count):
            to = (i + rows) % lat_count * lon_count + (j + cols) % lon_count
            pairs.append((i * lon_count + j, to))
    return lax.ppermute(value, ("lat", "lon"), pairs)


def local(tokens, cotangent, norm_gain, inproj_weight, outproj_weight, bias):
    levels, rows, cols, channels = tokens.shape
    level_windows, _, heads = bias.shape[:3]
    lat_count, lon_count = lax.axis_size("lat"), lax.axis_size("lon")
    chunks = Chunks(lon_count, heads)
    windows = cols // WW
    struct = jax.ShapeDtypeStruct
    half, side = WZ * HALF_ROWS * cols, WZ * HALF_ROWS * SIDE
    gain = norm_gain.reshape(1, channels)

    bias = bias.reshape(level_windows, heads, WT, WT)
    both = jnp.concatenate([tokens, cotangent], axis=-1)
    narrow = round_up(WZ * HALF_ROWS * (cols - HALF_COLS), 16)
    inner, below, right, corner, tail = call(
        send_kernel,
        [struct((level_windows, size, 2 * channels), BF16) for size in (half, narrow, side, side, side)],
        (both,),
    )
    below = shift(below, -1, 0)
    right = shift(right, 0, -1)
    corner = shift(corner, -1, -1)
    (bias_t,) = call(
        functools.partial(prep_kernel, chunks, lat_count),
        [struct((level_windows, lon_count, WT, chunks.width), F32)],
        (bias,),
    )
    per_window = []
    total = []
    for c in range(windows):
        last = c == windows - 1
        pieces = (tail, below, right, corner) if last else (inner, below)
        if last:
            sums = [struct((level_windows, WT, chunks.width), BF16)] * lon_count
        else:
            sums = [struct((level_windows, lon_count, WT, chunks.width), F32)]
        order = jnp.asarray(window_order(cols, c, True), BF16)
        results = call(
            functools.partial(scores_kernel, chunks, len(pieces), c == 0, last),
            [
                struct((level_windows * WT, channels), F32),
                struct((level_windows * WT, LANES), F32),
                struct((level_windows * WT, channels), BF16),
                struct((level_windows * WT, channels), F32),
                struct((level_windows * WT, channels), F32),
                struct((level_windows, WT, lon_count * chunks.width), BF16),
                struct((level_windows, WT, lon_count * chunks.width), BF16),
            ]
            + sums,
            (*pieces, gain, inproj_weight, outproj_weight, bias_t, order, *total),
            flops=10**9,
            scratch=[pltpu.VMEM((lon_count, WT, chunks.width), BF16)],
        )
        per_window.append(results[:7])
        total = results[7:]
    arrived = [total[0]]
    for d in range(1, lon_count):
        pairs = [(i, partner(i, d, lon_count)) for i in range(lon_count)]
        arrived.append(lax.ppermute(total[d], "lon", pairs))
    wide = struct((level_windows, half, channels), BF16)
    thin = struct((level_windows, side, channels), BF16)
    grads = []
    for c in reversed(range(windows)):
        last = c == windows - 1
        order = jnp.asarray(window_order(cols, c, False).T, BF16)
        results = call(
            functools.partial(tokens_kernel, chunks, 2, last),
            [wide, wide, thin, thin] if last else [wide, struct((half, level_windows * channels), BF16)],
            (*per_window[c], gain, inproj_weight, order, *grads),
        )
        grads = results[:2]
        if last:
            left, corner = shift(results[2], 0, 1), shift(results[3], 1, 1)
    above = shift(grads[1], 1, 0)
    bias_grad, after = call(
        functools.partial(bias_kernel, chunks),
        [struct((level_windows * heads * chunks.size, 1, WT), F32), struct((8, LANES), F32)],
        arrived,
    )
    (grad_input,) = call(join_kernel, [struct(tokens.shape, BF16)], (corner, above, left, grads[0], after))
    bias_grad = bias_grad.reshape(level_windows, heads, chunks.size, 1, WT)
    return grad_input, jnp.transpose(bias_grad, (0, 3, 1, 2, 4))


def solution(mesh):
    placed = (
        P(None, "lat", "lon", None),
        P(None, "lat", "lon", None),
        P(),
        P(),
        P(),
        P(None, "lat", None, None, None),
    )
    return jax.shard_map(
        local,
        mesh=mesh,
        in_specs=placed,
        out_specs=(P(None, "lat", "lon", None), P(None, "lat", None, "lon", None)),
        check_vma=False,
    )
```

```python
import functools

import jax
import jax.numpy as jnp
import numpy as np
from jax import lax
from jax.experimental import pallas as pl
from jax.experimental.pallas import tpu as pltpu
from jax.sharding import PartitionSpec as P

WZ = 2
WH = 6
WW = 12
WT = WZ * WH * WW
HALF_ROWS = WH // 2
HALF_COLS = WW // 2
SIDE = 8
LEVEL = WH * WW
LANES = 128
LOG2E = 1.4426950408889634
epsilon = 1e-05
F32 = jnp.float32
BF16 = jnp.bfloat16
NT = (((1,), (1,)), ((), ()))


def dot(a, b):
    return jnp.dot(a, b, preferred_element_type=F32)


def dot_nt(a, b):
    return lax.dot_general(a, b, NT, preferred_element_type=F32)


def round_up(value, to):
    return (value + to - 1) // to * to


class Chunks:
    def __init__(self, parts, heads):
        self.parts, self.heads = parts, heads
        self.size = WT // parts
        self.main = self.size // 16 * 16
        self.rest = self.size - self.main
        self.rest_rows = round_up(heads * self.rest, 16)
        self.rows = self.main + self.rest_rows
        self.used = heads * self.main + self.rest_rows
        self.width = round_up(self.used, LANES)

    def columns(self, j):
        lane = lax.broadcasted_iota(jnp.int32, (1, self.width), 1)
        low = self.heads * self.main
        main, left = lane, self.main + lane - low
        for h in range(1, self.heads):
            main -= jnp.where(lane >= h * self.main, self.main, 0)
            left -= jnp.where(lane >= low + h * self.rest, self.rest, 0)
        return j * self.size + jnp.where(lane < low, main, left)


def window_order(cols, c, narrow):
    last = c == cols // WW - 1
    part, side = HALF_ROWS * cols, HALF_ROWS * SIDE
    kept = cols - HALF_COLS if narrow else cols
    tail = narrow and last
    inner = WZ * (side if tail else part)
    near = inner + round_up(WZ * HALF_ROWS * kept, 16)
    table = np.zeros((WT, near + last * 2 * WZ * side), np.float32)
    for z in range(WZ):
        for r in range(WH):
            for w in range(WW):
                col = c * WW + w + HALF_COLS
                low, row = divmod(r, HALF_ROWS)
                if col >= cols:
                    at = near + (low * WZ + z) * side + row * SIDE + col - cols
                elif low:
                    at = inner + (z * HALF_ROWS + row) * kept + col - (cols - kept)
                elif tail:
                    at = z * side + row * SIDE + col - (cols - SIDE)
                else:
                    at = z * part + row * cols + col
                table[(z * WH + r) * WW + w, at] = 1.0
    return table


def level_rows(field, a, base):
    levels = field.shape[0]
    at = [(a * WZ + WZ // 2 + z) % levels for z in range(WZ)]
    return [field[level, base + row].astype(F32) for level in at for row in range(HALF_ROWS)]


def send_kernel(both, inner, below, right, corner, tail):
    cols = both.shape[2]
    kept = cols - HALF_COLS
    shape = (below.shape[1], WZ * HALF_ROWS * cols)
    row = lax.broadcasted_iota(jnp.int32, shape, 0)
    target = row + HALF_COLS
    for i in range(1, WZ * HALF_ROWS):
        target += jnp.where(row >= i * kept, HALF_COLS, 0)
    kept_rows = (lax.broadcasted_iota(jnp.int32, shape, 1) == target) & (row < WZ * HALF_ROWS * kept)
    narrow = kept_rows.astype(F32).astype(BF16)
    for a in range(inner.shape[0]):
        low, high = level_rows(both, a, 0), level_rows(both, a, HALF_ROWS)
        below[a] = dot(narrow, jnp.concatenate(low, axis=0).astype(BF16)).astype(BF16)
        inner[a] = jnp.concatenate(high, axis=0).astype(BF16)
        right[a] = jnp.concatenate([row[:SIDE] for row in high], axis=0).astype(BF16)
        tail[a] = jnp.concatenate([row[cols - SIDE :] for row in high], axis=0).astype(BF16)
        corner[a] = jnp.concatenate([row[:SIDE] for row in low], axis=0).astype(BF16)


def prep_kernel(chunks, lat_count, bias, bias_t):
    level_windows = bias.shape[0]
    last_lat = lax.axis_index("lat") == lat_count - 1
    parts, size, main = chunks.parts, chunks.size, chunks.main

    def labels(index, window):
        level_label = (index >= LEVEL) & (window == level_windows - 1)
        in_level = jnp.where(index >= LEVEL, index - LEVEL, index)
        row_label = (in_level >= LEVEL // 2) & last_lat
        return level_label.astype(jnp.int32) * 2 + row_label.astype(jnp.int32)

    key_index = lax.broadcasted_iota(jnp.int32, (WT, chunks.width), 0)
    for window in range(level_windows):
        key_labels = labels(key_index, window)
        for j in range(parts):
            heads = range(chunks.heads)
            low = j * size
            rows = []
            if main:
                rows += [bias[window, h, low : low + main, :] for h in heads]
            if chunks.rest:
                rows += [bias[window, h, low + main : low + size, :] for h in heads]
            spare = chunks.width - chunks.heads * size
            if spare:
                rows.append(jnp.zeros((spare, WT), F32))
            turned = jnp.transpose(jnp.concatenate(rows, axis=0)) * LOG2E
            allowed = key_labels == labels(chunks.columns(j), window)
            bias_t[window, j] = jnp.where(allowed, turned, -1e30)


def head_masks(chunks, channels):
    head_dim = channels // chunks.heads
    lane_head = lax.broadcasted_iota(jnp.int32, (1, channels), 1) // head_dim
    lanes = [lane_head == h for h in range(chunks.heads)]
    rest = None
    if chunks.rest:
        row = lax.broadcasted_iota(jnp.int32, (chunks.rest_rows, channels), 0)
        lane = lax.broadcasted_iota(jnp.int32, (chunks.rest_rows, channels), 1) // head_dim
        rest = jnp.zeros((chunks.rest_rows, channels), F32)
        for h in range(chunks.heads):
            inside = (row >= h * chunks.rest) & (row < (h + 1) * chunks.rest) & (lane == h)
            rest = jnp.where(inside, 1.0, rest)
    return lanes, rest


def stack_heads(chunks, value, j, lane_masks, rest_mask):
    low = j * chunks.size
    pieces = []
    if chunks.main:
        main = value[low : low + chunks.main].astype(BF16)
        pieces += [main * mask for mask in lane_masks]
    if chunks.rest:
        rows = [value[low + chunks.main : low + chunks.size]] * chunks.heads
        spare = chunks.rest_rows - chunks.heads * chunks.rest
        if spare:
            rows.append(jnp.zeros((spare, value.shape[1]), F32))
        pieces.append(jnp.concatenate(rows, axis=0).astype(BF16) * rest_mask)
    if chunks.width > chunks.used:
        pieces.append(jnp.zeros((chunks.width - chunks.used, value.shape[1]), BF16))
    return jnp.concatenate(pieces, axis=0)


def split(inproj):
    channels = inproj.shape[0]
    return [inproj[:, part * channels : (part + 1) * channels] for part in range(3)]


def pack(columns):
    used = columns[0].shape[1]
    whole = used // LANES * LANES
    tiles = [part[:, i : i + LANES] for part in columns for i in range(0, whole, LANES)]
    left = jnp.concatenate([part[:, whole:] for part in columns], axis=1)
    while left.shape[1] >= LANES:
        tiles.append(left[:, :LANES])
        left = left[:, LANES:]
    if left.shape[1]:
        tiles.append(jnp.concatenate([left[: WT // 2, : LANES // 2], left[WT // 2 :, : LANES // 2]], axis=1))
    return jnp.concatenate(tiles, axis=0)


def unpack(rows, many, used):
    whole = used // LANES
    tiles = [rows[i * WT : (i + 1) * WT] for i in range(rows.shape[0] // WT)]
    left = tiles[many * whole :]
    if rows.shape[0] % WT:
        last = rows[len(tiles) * WT :]
        left.append(jnp.concatenate([last[:, : LANES // 2], last[:, LANES // 2 :]], axis=0))
    left = jnp.concatenate(left, axis=1) if left else None
    rest = used - whole * LANES
    columns = []
    for a in range(many):
        part = tiles[a * whole : (a + 1) * whole]
        if rest:
            part.append(left[:, a * rest : (a + 1) * rest])
        columns.append(jnp.concatenate(part, axis=1))
    return columns


def partner(me, d, parts):
    return me ^ d if parts & (parts - 1) == 0 else (me + d) % parts


def scores_kernel(chunks, near, first, last, *refs):
    pieces, refs = refs[:near], refs[near:]
    gain_ref, inproj, outproj, bias_t, perm, *refs = refs
    weights = split(inproj)
    before = None
    if not first:
        before, *refs = refs
    standard_out, scale_out, keys_out, query_out, up_out, p_out, ds_out, *totals, turn = refs
    parts, width = chunks.parts, chunks.width
    channels = outproj.shape[0]
    scaling = (channels // chunks.heads) ** (-0.5)
    lanes, rest_mask = head_masks(chunks, channels)
    lanes = [mask.astype(F32).astype(BF16) for mask in lanes]
    rest_mask = rest_mask.astype(BF16) if chunks.rest else None
    me = lax.axis_index("lon")
    level_windows = pieces[0].shape[0]
    tile = channels // LANES * LANES
    from_tile = jnp.concatenate([jnp.zeros((channels, channels - tile), BF16), outproj[...]], axis=1)
    ts, us = [], []
    for a in range(level_windows):
        moved = dot(perm[...], jnp.concatenate([piece[a] for piece in pieces], axis=0))
        ts.append(moved[:, :channels])
        us.append(dot_nt(moved[:, tile:].astype(BF16), from_tile))
    t = jnp.concatenate(ts, axis=0)
    centred = t - jnp.mean(t, axis=-1, keepdims=True)
    inverse_rms = lax.rsqrt(jnp.mean(centred * centred, axis=-1, keepdims=True) + epsilon)
    standard = centred * inverse_rms
    standard_out[...] = standard
    scale_out[...] = jnp.broadcast_to(inverse_rms, scale_out.shape)
    normed = (standard * gain_ref[...]).astype(BF16)
    q = dot(normed, weights[0])
    query_out[...] = q
    k = dot(normed, weights[1]).astype(BF16)
    v = dot(normed, weights[2]).astype(BF16)
    keys_out[...] = k
    for a in range(level_windows):
        cut = slice(a * WT, (a + 1) * WT)
        query, up = q[cut], us[a]
        up_out[cut] = up
        for d in range(parts):
            at = slice(d * width, (d + 1) * width)
            s = dot_nt(k[cut], stack_heads(chunks, query, d, lanes, rest_mask))
            dp = dot_nt(v[cut], stack_heads(chunks, up, d, lanes, rest_mask))
            e = jnp.exp2(s * (scaling * LOG2E) + bias_t[a, d])
            p = e * (1.0 / jnp.sum(e, axis=0, keepdims=True))
            ds = p * (dp - jnp.sum(p * dp, axis=0, keepdims=True))
            p_out[a, :, at] = p.astype(BF16)
            ds_out[a, :, at] = ds.astype(BF16)
            if not first:
                ds += before[a, d]
            if last:
                turn[a, d] = ds
            else:
                totals[0][a, d] = ds
    if last:
        for d in range(parts):
            j = partner(me, d, parts)
            columns = [turn[a, j][:, : chunks.used] for a in range(level_windows)]
            totals[d][...] = pack(columns).astype(BF16)


def tokens_kernel(chunks, first, *refs):
    standard_in, scale_in, keys, queries_in, ups, p_in, ds_in, gain_ref, inproj, perm_t, *refs = refs
    weights = split(inproj)
    before = None
    if not first:
        before, refs = refs[:2], refs[2:]
    outs = refs
    parts, width = chunks.parts, chunks.width
    channels = keys.shape[-1]
    head_dim = channels // chunks.heads
    scaling = head_dim ** (-0.5)
    lanes, rest_mask = head_masks(chunks, channels)
    low_lanes = [mask.astype(F32).astype(BF16) for mask in lanes]
    low_rest = rest_mask.astype(BF16) if chunks.rest else None
    level_windows = p_in.shape[0]
    dqs, dks, dvs = [], [], []
    for a in range(level_windows):
        cut = slice(a * WT, (a + 1) * WT)
        query, up = queries_in[cut], ups[cut]
        qs = jnp.concatenate(
            [stack_heads(chunks, query, d, low_lanes, low_rest) for d in range(parts)], axis=0
        )
        us = jnp.concatenate(
            [stack_heads(chunks, up, d, low_lanes, low_rest) for d in range(parts)], axis=0
        )
        ds = ds_in[a]
        dks.append((dot(ds, qs) * scaling).astype(BF16))
        dvs.append(dot(p_in[a], us).astype(BF16))
        turned = jnp.transpose(ds)
        key = keys[a * WT : (a + 1) * WT]
        main = []
        for lane in range(0, channels, LANES):
            low = lane // head_dim
            many = min(LANES // head_dim, chunks.heads - low)
            if not chunks.main:
                break
            some = [turned[d * width + low * chunks.main :][: many * chunks.main] for d in range(parts)]
            flat = dot(jnp.concatenate(some, axis=0), key[:, lane : lane + LANES])
            tiles = []
            for d in range(parts):
                picked = flat[d * many * chunks.main :][: chunks.main]
                for h in range(1, many):
                    mask = lanes[low + h][:, lane : lane + LANES]
                    picked = jnp.where(mask, flat[(d * many + h) * chunks.main :][: chunks.main], picked)
                tiles.append(picked)
            main.append(tiles)
        if chunks.rest:
            low = chunks.heads * chunks.main
            some = [turned[d * width + low :][: chunks.rest_rows] for d in range(parts)]
            left = dot(jnp.concatenate(some, axis=0), key)
        rows = []
        for d in range(parts):
            if chunks.main:
                rows.append(jnp.concatenate([tiles[d] for tiles in main], axis=1))
            if chunks.rest:
                some = left[d * chunks.rest_rows : (d + 1) * chunks.rest_rows] * rest_mask
                total = some[: chunks.rest]
                for h in range(1, chunks.heads):
                    total += some[h * chunks.rest : (h + 1) * chunks.rest]
                rows.append(total)
        dqs.append((jnp.concatenate(rows, axis=0) * scaling).astype(BF16))
    dq, dk, dv = (jnp.concatenate(parts_of, axis=0) for parts_of in (dqs, dks, dvs))
    scaled = (dot_nt(dq, weights[0]) + dot_nt(dk, weights[1]) + dot_nt(dv, weights[2])) * gain_ref[...]
    standard = standard_in[...]
    inverse_rms = scale_in[:, :1]
    grad = inverse_rms * (
        scaled
        - jnp.mean(scaled, axis=-1, keepdims=True)
        - standard * jnp.mean(scaled * standard, axis=-1, keepdims=True)
    )
    grad = grad.astype(BF16)
    lows = []
    for a in range(level_windows):
        spread = dot(perm_t[...], grad[a * WT : (a + 1) * WT])
        base = 0
        for i, out in enumerate(outs):
            rows = out.shape[-2]
            part = spread[base : base + rows]
            if not first and i < 2:
                part += before[i][a].astype(F32)
            if not first and i == 1:
                lows.append(part)
            else:
                out[a] = part.astype(BF16)
            base += rows
    if not first:
        packed = [low[:, :LANES] for low in lows] + [low[:, LANES:] for low in lows]
        outs[1][...] = jnp.concatenate(packed, axis=1).astype(BF16)


def stage_kernel(chunks, windows, *refs):
    per_window, refs = refs[: 7 * windows], refs[7 * windows :]
    gain_ref, inproj, *refs = refs
    orders, refs = refs[:windows], refs[windows:]
    g_inner, g_below, right, corner, *partial = refs
    for i in range(windows):
        ins = (*per_window[7 * i : 7 * (i + 1)], gain_ref, inproj, orders[i])
        if i == 0:
            tokens_kernel(chunks, True, *ins, *partial, right, corner)
        else:
            tokens_kernel(chunks, False, *ins, *partial, g_inner, g_below)


def join_kernel(corner, below, right, inner, after, grad_input):
    levels, _, cols, channels = grad_input.shape
    level_windows = levels // WZ
    whole = below[...].astype(F32)
    for a in range(level_windows):
        rest_at = level_windows * LANES + a * (channels - LANES)
        low = jnp.concatenate(
            [whole[:, a * LANES : (a + 1) * LANES], whole[:, rest_at : rest_at + channels - LANES]], axis=1
        )
        parts = ((low, corner[a].astype(F32), 0), (inner[a].astype(F32), right[a].astype(F32), HALF_ROWS))
        for z in range(WZ):
            level = (a * WZ + WZ // 2 + z) % levels
            for row in range(HALF_ROWS):
                at = z * HALF_ROWS + row
                for wide, side, base in parts:
                    first = wide[at * cols : at * cols + SIDE] + side[at * SIDE : (at + 1) * SIDE]
                    rest = wide[at * cols + SIDE : (at + 1) * cols]
                    grad_input[level, base + row] = jnp.concatenate([first, rest], axis=0).astype(BF16)


def bias_kernel(chunks, *refs):
    *arrived, bias_grad, after = refs
    after[...] = jnp.zeros(after.shape, F32)
    main, rest, heads = chunks.main, chunks.rest, chunks.heads
    total = arrived[0][...].astype(F32)
    for other in arrived[1:]:
        total += other[...].astype(F32)
    many = bias_grad.shape[0] // (heads * chunks.size)
    for a, columns in enumerate(unpack(total, many, chunks.used)):
        turned = jnp.transpose(columns)
        for h in range(heads):
            at = (a * heads + h) * chunks.size
            if main:
                bias_grad[at : at + main, 0, :] = turned[h * main : (h + 1) * main]
            if rest:
                low = heads * main + h * rest
                bias_grad[at + main : at + chunks.size, 0, :] = turned[low : low + rest]


def vmem(count):
    return [pl.BlockSpec(memory_space=pltpu.VMEM)] * count


def call(kernel, outs, args, flops=0, scratch=()):
    return pl.pallas_call(
        kernel,
        out_shape=outs,
        in_specs=vmem(len(args)),
        out_specs=vmem(len(outs)),
        scratch_shapes=list(scratch),
        compiler_params=pltpu.CompilerParams(vmem_limit_bytes=40 * 2**20),
        cost_estimate=pl.CostEstimate(flops=flops, bytes_accessed=0, transcendentals=0),
    )(*args)


def shift(value, rows, cols):
    lat_count, lon_count = lax.axis_size("lat"), lax.axis_size("lon")
    pairs = []
    for i in range(lat_count):
        for j in range(lon_count):
            to = (i + rows) % lat_count * lon_count + (j + cols) % lon_count
            pairs.append((i * lon_count + j, to))
    return lax.ppermute(value, ("lat", "lon"), pairs)


def local(tokens, cotangent, norm_gain, inproj_weight, outproj_weight, bias):
    levels, rows, cols, channels = tokens.shape
    level_windows, _, heads = bias.shape[:3]
    lat_count, lon_count = lax.axis_size("lat"), lax.axis_size("lon")
    chunks = Chunks(lon_count, heads)
    windows = cols // WW
    struct = jax.ShapeDtypeStruct
    half, side = WZ * HALF_ROWS * cols, WZ * HALF_ROWS * SIDE
    gain = norm_gain.reshape(1, channels)

    bias = bias.reshape(level_windows, heads, WT, WT)
    both = jnp.concatenate([tokens, cotangent], axis=-1)
    narrow = round_up(WZ * HALF_ROWS * (cols - HALF_COLS), 16)
    inner, below, right, corner, tail = call(
        send_kernel,
        [struct((level_windows, size, 2 * channels), BF16) for size in (half, narrow, side, side, side)],
        (both,),
    )
    below = shift(below, -1, 0)
    right = shift(right, 0, -1)
    corner = shift(corner, -1, -1)
    (bias_t,) = call(
        functools.partial(prep_kernel, chunks, lat_count),
        [struct((level_windows, lon_count, WT, chunks.width), F32)],
        (bias,),
    )
    packed = level_windows * chunks.used * WT // LANES
    per_window = []
    total = []
    for c in range(windows):
        last = c == windows - 1
        pieces = (tail, below, right, corner) if last else (inner, below)
        if last:
            sums = [struct((packed, LANES), BF16)] * lon_count
        else:
            sums = [struct((level_windows, lon_count, WT, chunks.width), F32)]
        order = jnp.asarray(window_order(cols, c, True), BF16)
        results = call(
            functools.partial(scores_kernel, chunks, len(pieces), c == 0, last),
            [
                struct((level_windows * WT, channels), F32),
                struct((level_windows * WT, LANES), F32),
                struct((level_windows * WT, channels), BF16),
                struct((level_windows * WT, channels), F32),
                struct((level_windows * WT, channels), F32),
                struct((level_windows, WT, lon_count * chunks.width), BF16),
                struct((level_windows, WT, lon_count * chunks.width), BF16),
            ]
            + sums,
            (*pieces, gain, inproj_weight, outproj_weight, bias_t, order, *total),
            flops=10**9,
            scratch=[pltpu.VMEM((level_windows, lon_count, WT, chunks.width), F32)],
        )
        per_window.append(results[:7])
        total = results[7:]
    arrived = [total[0]]
    for d in range(1, lon_count):
        pairs = [(i, partner(i, d, lon_count)) for i in range(lon_count)]
        arrived.append(lax.ppermute(total[d], "lon", pairs))
    wide = struct((level_windows, half, channels), BF16)
    thin = struct((level_windows, side, channels), BF16)
    back = list(reversed(range(windows)))
    g_inner, above, left, corner = call(
        functools.partial(stage_kernel, chunks, windows),
        [wide, struct((half, level_windows * channels), BF16), thin, thin],
        [ref for c in back for ref in per_window[c]]
        + [gain, inproj_weight]
        + [jnp.asarray(window_order(cols, c, False).T, BF16) for c in back],
        scratch=[pltpu.VMEM(wide.shape, BF16)] * 2,
    )
    left, corner, above = shift(left, 0, 1), shift(corner, 1, 1), shift(above, 1, 0)
    bias_grad, after = call(
        functools.partial(bias_kernel, chunks),
        [struct((level_windows * heads * chunks.size, 1, WT), F32), struct((8, LANES), F32)],
        arrived,
    )
    (grad_input,) = call(join_kernel, [struct(tokens.shape, BF16)], (corner, above, left, g_inner, after))
    bias_grad = bias_grad.reshape(level_windows, heads, chunks.size, 1, WT)
    return grad_input, jnp.transpose(bias_grad, (0, 3, 1, 2, 4))


def solution(mesh):
    placed = (
        P(None, "lat", "lon", None),
        P(None, "lat", "lon", None),
        P(),
        P(),
        P(),
        P(None, "lat", None, None, None),
    )
    return jax.shard_map(
        local,
        mesh=mesh,
        in_specs=placed,
        out_specs=(P(None, "lat", "lon", None), P(None, "lat", None, "lon", None)),
        check_vma=False,
    )
```

```python
import functools

import jax
import jax.numpy as jnp
import numpy as np
from jax import lax
from jax.experimental import pallas as pl
from jax.experimental.pallas import tpu as pltpu
from jax.sharding import PartitionSpec as P

WZ = 2
WH = 6
WW = 12
WT = WZ * WH * WW
HALF_ROWS = WH // 2
HALF_COLS = WW // 2
SIDE = 8
LEVEL = WH * WW
LANES = 128
LOG2E = 1.4426950408889634
epsilon = 1e-05
F32 = jnp.float32
BF16 = jnp.bfloat16
NT = (((1,), (1,)), ((), ()))


def dot(a, b):
    return jnp.dot(a, b, preferred_element_type=F32)


def dot_nt(a, b):
    return lax.dot_general(a, b, NT, preferred_element_type=F32)


def round_up(value, to):
    return (value + to - 1) // to * to


class Chunks:
    def __init__(self, parts, heads):
        self.parts, self.heads = parts, heads
        self.size = WT // parts
        self.main = self.size // 16 * 16
        self.rest = self.size - self.main
        self.rest_rows = round_up(heads * self.rest, 16)
        self.rows = self.main + self.rest_rows
        self.used = heads * self.main + self.rest_rows
        self.width = round_up(self.used, LANES)

    def columns(self, j):
        lane = lax.broadcasted_iota(jnp.int32, (1, self.width), 1)
        low = self.heads * self.main
        main, left = lane, self.main + lane - low
        for h in range(1, self.heads):
            main -= jnp.where(lane >= h * self.main, self.main, 0)
            left -= jnp.where(lane >= low + h * self.rest, self.rest, 0)
        return j * self.size + jnp.where(lane < low, main, left)


def side_order(cols):
    part = HALF_ROWS * cols
    table = np.zeros((round_up(WZ * WH * HALF_COLS, 16), 2 * WZ * part), np.float32)
    for z in range(WZ):
        for r in range(WH):
            low, row = divmod(r, HALF_ROWS)
            for w in range(HALF_COLS):
                table[(z * WH + r) * HALF_COLS + w, (low * WZ + z) * part + row * cols + w] = 1.0
    return table


def window_order(cols, c, out):
    last = c == cols // WW - 1
    part, side = HALF_ROWS * cols, HALF_ROWS * SIDE
    kept = cols if out else cols - HALF_COLS
    tail = last and not out
    inner = WZ * (side if tail else part)
    near = inner + round_up(WZ * HALF_ROWS * kept, 16)
    extra = round_up(WZ * WH * HALF_COLS, 16) if out else 2 * WZ * side
    table = np.zeros((WT, near + last * extra), np.float32)
    for z in range(WZ):
        for r in range(WH):
            for w in range(WW):
                col = c * WW + w + HALF_COLS
                low, row = divmod(r, HALF_ROWS)
                if col >= cols and out:
                    at = near + (z * WH + r) * HALF_COLS + col - cols
                elif col >= cols:
                    at = near + (low * WZ + z) * side + row * SIDE + col - cols
                elif low:
                    at = inner + (z * HALF_ROWS + row) * kept + col - (cols - kept)
                elif tail:
                    at = z * side + row * SIDE + col - (cols - SIDE)
                else:
                    at = z * part + row * cols + col
                table[(z * WH + r) * WW + w, at] = 1.0
    return table


def level_rows(field, a, base):
    levels = field.shape[0]
    at = [(a * WZ + WZ // 2 + z) % levels for z in range(WZ)]
    return [field[level, base + row].astype(F32) for level in at for row in range(HALF_ROWS)]


def send_kernel(both, inner, below, right, corner, tail):
    cols = both.shape[2]
    kept = cols - HALF_COLS
    shape = (below.shape[1], WZ * HALF_ROWS * cols)
    row = lax.broadcasted_iota(jnp.int32, shape, 0)
    target = row + HALF_COLS
    for i in range(1, WZ * HALF_ROWS):
        target += jnp.where(row >= i * kept, HALF_COLS, 0)
    kept_rows = (lax.broadcasted_iota(jnp.int32, shape, 1) == target) & (row < WZ * HALF_ROWS * kept)
    narrow = kept_rows.astype(F32).astype(BF16)
    for a in range(inner.shape[0]):
        low, high = level_rows(both, a, 0), level_rows(both, a, HALF_ROWS)
        below[a] = dot(narrow, jnp.concatenate(low, axis=0).astype(BF16)).astype(BF16)
        inner[a] = jnp.concatenate(high, axis=0).astype(BF16)
        right[a] = jnp.concatenate([row[:SIDE] for row in high], axis=0).astype(BF16)
        tail[a] = jnp.concatenate([row[cols - SIDE :] for row in high], axis=0).astype(BF16)
        corner[a] = jnp.concatenate([row[:SIDE] for row in low], axis=0).astype(BF16)


def prep_kernel(chunks, lat_count, bias, bias_t):
    level_windows = bias.shape[0]
    last_lat = lax.axis_index("lat") == lat_count - 1
    parts, size, main = chunks.parts, chunks.size, chunks.main

    def labels(index, window):
        level_label = (index >= LEVEL) & (window == level_windows - 1)
        in_level = jnp.where(index >= LEVEL, index - LEVEL, index)
        row_label = (in_level >= LEVEL // 2) & last_lat
        return level_label.astype(jnp.int32) * 2 + row_label.astype(jnp.int32)

    key_index = lax.broadcasted_iota(jnp.int32, (WT, chunks.width), 0)
    for window in range(level_windows):
        key_labels = labels(key_index, window)
        for j in range(parts):
            heads = range(chunks.heads)
            low = j * size
            rows = []
            if main:
                rows += [bias[window, h, low : low + main, :] for h in heads]
            if chunks.rest:
                rows += [bias[window, h, low + main : low + size, :] for h in heads]
            spare = chunks.width - chunks.heads * size
            if spare:
                rows.append(jnp.zeros((spare, WT), F32))
            turned = jnp.transpose(jnp.concatenate(rows, axis=0)) * LOG2E
            allowed = key_labels == labels(chunks.columns(j), window)
            bias_t[window, j] = jnp.where(allowed, turned, -1e30)


def head_masks(chunks, channels):
    head_dim = channels // chunks.heads
    lane_head = lax.broadcasted_iota(jnp.int32, (1, channels), 1) // head_dim
    lanes = [lane_head == h for h in range(chunks.heads)]
    rest = None
    if chunks.rest:
        row = lax.broadcasted_iota(jnp.int32, (chunks.rest_rows, channels), 0)
        lane = lax.broadcasted_iota(jnp.int32, (chunks.rest_rows, channels), 1) // head_dim
        rest = jnp.zeros((chunks.rest_rows, channels), F32)
        for h in range(chunks.heads):
            inside = (row >= h * chunks.rest) & (row < (h + 1) * chunks.rest) & (lane == h)
            rest = jnp.where(inside, 1.0, rest)
    return lanes, rest


def stack_heads(chunks, value, j, lane_masks, rest_mask):
    low = j * chunks.size
    pieces = []
    if chunks.main:
        main = value[low : low + chunks.main].astype(BF16)
        pieces += [main * mask for mask in lane_masks]
    if chunks.rest:
        rows = [value[low + chunks.main : low + chunks.size]] * chunks.heads
        spare = chunks.rest_rows - chunks.heads * chunks.rest
        if spare:
            rows.append(jnp.zeros((spare, value.shape[1]), F32))
        pieces.append(jnp.concatenate(rows, axis=0).astype(BF16) * rest_mask)
    if chunks.width > chunks.used:
        pieces.append(jnp.zeros((chunks.width - chunks.used, value.shape[1]), BF16))
    return jnp.concatenate(pieces, axis=0)


def split(inproj):
    channels = inproj.shape[0]
    return [inproj[:, part * channels : (part + 1) * channels] for part in range(3)]


def pack(columns):
    used = columns[0].shape[1]
    whole = used // LANES * LANES
    tiles = [part[:, i : i + LANES] for part in columns for i in range(0, whole, LANES)]
    left = jnp.concatenate([part[:, whole:] for part in columns], axis=1)
    while left.shape[1] >= LANES:
        tiles.append(left[:, :LANES])
        left = left[:, LANES:]
    if left.shape[1]:
        tiles.append(jnp.concatenate([left[: WT // 2, : LANES // 2], left[WT // 2 :, : LANES // 2]], axis=1))
    return jnp.concatenate(tiles, axis=0)


def unpack(rows, many, used):
    whole = used // LANES
    tiles = [rows[i * WT : (i + 1) * WT] for i in range(rows.shape[0] // WT)]
    left = tiles[many * whole :]
    if rows.shape[0] % WT:
        last = rows[len(tiles) * WT :]
        left.append(jnp.concatenate([last[:, : LANES // 2], last[:, LANES // 2 :]], axis=0))
    left = jnp.concatenate(left, axis=1) if left else None
    rest = used - whole * LANES
    columns = []
    for a in range(many):
        part = tiles[a * whole : (a + 1) * whole]
        if rest:
            part.append(left[:, a * rest : (a + 1) * rest])
        columns.append(jnp.concatenate(part, axis=1))
    return columns


def partner(me, d, parts):
    return me ^ d if parts & (parts - 1) == 0 else (me + d) % parts


def scores_kernel(chunks, near, first, last, *refs):
    pieces, refs = refs[:near], refs[near:]
    gain_ref, inproj, outproj, bias_t, perm, *refs = refs
    weights = split(inproj)
    before = None
    if not first:
        before, *refs = refs
    standard_out, scale_out, keys_out, query_out, up_out, p_out, ds_out, total_out = refs
    parts, width = chunks.parts, chunks.width
    channels = outproj.shape[0]
    scaling = (channels // chunks.heads) ** (-0.5)
    lanes, rest_mask = head_masks(chunks, channels)
    lanes = [mask.astype(F32).astype(BF16) for mask in lanes]
    rest_mask = rest_mask.astype(BF16) if chunks.rest else None
    me = lax.axis_index("lon")
    level_windows = pieces[0].shape[0]
    tile = channels // LANES * LANES
    from_tile = jnp.concatenate([jnp.zeros((channels, channels - tile), BF16), outproj[...]], axis=1)
    ts, us = [], []
    for a in range(level_windows):
        moved = dot(perm[...], jnp.concatenate([piece[a] for piece in pieces], axis=0))
        ts.append(moved[:, :channels])
        us.append(dot_nt(moved[:, tile:].astype(BF16), from_tile))
    t = jnp.concatenate(ts, axis=0)
    centred = t - jnp.mean(t, axis=-1, keepdims=True)
    inverse_rms = lax.rsqrt(jnp.mean(centred * centred, axis=-1, keepdims=True) + epsilon)
    standard = centred * inverse_rms
    standard_out[...] = standard
    scale_out[...] = jnp.broadcast_to(inverse_rms, scale_out.shape)
    normed = (standard * gain_ref[...]).astype(BF16)
    q = dot(normed, weights[0])
    query_out[...] = q
    k = dot(normed, weights[1]).astype(BF16)
    v = dot(normed, weights[2]).astype(BF16)
    keys_out[...] = k
    for a in range(level_windows):
        cut = slice(a * WT, (a + 1) * WT)
        query, up = q[cut], us[a]
        up_out[cut] = up
        for d in range(parts):
            at = slice(d * width, (d + 1) * width)
            s = dot_nt(k[cut], stack_heads(chunks, query, d, lanes, rest_mask))
            dp = dot_nt(v[cut], stack_heads(chunks, up, d, lanes, rest_mask))
            e = jnp.exp2(s * (scaling * LOG2E) + bias_t[a, d])
            p = e * (1.0 / jnp.sum(e, axis=0, keepdims=True))
            ds = p * (dp - jnp.sum(p * dp, axis=0, keepdims=True))
            p_out[a, :, at] = p.astype(BF16)
            ds_out[a, :, at] = ds.astype(BF16)
            if not first:
                ds += before[a, d]
            if last:
                total_out[a, d] = ds
            else:
                total_out[a, d] = ds


def tokens_kernel(chunks, first, *refs):
    standard_in, scale_in, keys, queries_in, ups, p_in, ds_in, gain_ref, inproj, perm_t, *refs = refs
    weights = split(inproj)
    before = None
    if not first:
        before, refs = refs[:2], refs[2:]
    outs = refs
    parts, width = chunks.parts, chunks.width
    channels = keys.shape[-1]
    head_dim = channels // chunks.heads
    scaling = head_dim ** (-0.5)
    lanes, rest_mask = head_masks(chunks, channels)
    low_lanes = [mask.astype(F32).astype(BF16) for mask in lanes]
    low_rest = rest_mask.astype(BF16) if chunks.rest else None
    level_windows = p_in.shape[0]
    dqs, dks, dvs = [], [], []
    for a in range(level_windows):
        cut = slice(a * WT, (a + 1) * WT)
        query, up = queries_in[cut], ups[cut]
        qs = jnp.concatenate(
            [stack_heads(chunks, query, d, low_lanes, low_rest) for d in range(parts)], axis=0
        )
        us = jnp.concatenate(
            [stack_heads(chunks, up, d, low_lanes, low_rest) for d in range(parts)], axis=0
        )
        ds = ds_in[a]
        dks.append((dot(ds, qs) * scaling).astype(BF16))
        dvs.append(dot(p_in[a], us).astype(BF16))
        turned = jnp.transpose(ds)
        key = keys[a * WT : (a + 1) * WT]
        main = []
        for lane in range(0, channels, LANES):
            low = lane // head_dim
            many = min(LANES // head_dim, chunks.heads - low)
            if not chunks.main:
                break
            some = [turned[d * width + low * chunks.main :][: many * chunks.main] for d in range(parts)]
            flat = dot(jnp.concatenate(some, axis=0), key[:, lane : lane + LANES])
            tiles = []
            for d in range(parts):
                picked = flat[d * many * chunks.main :][: chunks.main]
                for h in range(1, many):
                    mask = lanes[low + h][:, lane : lane + LANES]
                    picked = jnp.where(mask, flat[(d * many + h) * chunks.main :][: chunks.main], picked)
                tiles.append(picked)
            main.append(tiles)
        if chunks.rest:
            low = chunks.heads * chunks.main
            some = [turned[d * width + low :][: chunks.rest_rows] for d in range(parts)]
            left = dot(jnp.concatenate(some, axis=0), key)
        rows = []
        for d in range(parts):
            if chunks.main:
                rows.append(jnp.concatenate([tiles[d] for tiles in main], axis=1))
            if chunks.rest:
                some = left[d * chunks.rest_rows : (d + 1) * chunks.rest_rows] * rest_mask
                total = some[: chunks.rest]
                for h in range(1, chunks.heads):
                    total += some[h * chunks.rest : (h + 1) * chunks.rest]
                rows.append(total)
        dqs.append((jnp.concatenate(rows, axis=0) * scaling).astype(BF16))
    dq, dk, dv = (jnp.concatenate(parts_of, axis=0) for parts_of in (dqs, dks, dvs))
    scaled = (dot_nt(dq, weights[0]) + dot_nt(dk, weights[1]) + dot_nt(dv, weights[2])) * gain_ref[...]
    standard = standard_in[...]
    inverse_rms = scale_in[:, :1]
    grad = inverse_rms * (
        scaled
        - jnp.mean(scaled, axis=-1, keepdims=True)
        - standard * jnp.mean(scaled * standard, axis=-1, keepdims=True)
    )
    grad = grad.astype(BF16)
    for a in range(level_windows):
        spread = dot(perm_t[...], grad[a * WT : (a + 1) * WT])
        base = 0
        for i, out in enumerate(outs):
            rows = out.shape[1]
            part = spread[base : base + rows]
            if not first and i < 2:
                part += before[i][a].astype(F32)
            out[a] = part.astype(BF16)
            base += rows


def first_kernel(chunks, *refs):
    *ins, total, inner, below, side = refs[:14]
    messages = refs[14:]
    me = lax.axis_index("lon")
    for d, message in enumerate(messages):
        j = partner(me, d, chunks.parts)
        columns = [total[a, j][:, : chunks.used] for a in range(total.shape[0])]
        message[...] = pack(columns).astype(BF16)
    tokens_kernel(chunks, True, *ins, inner, below, side)


def merge_kernel(inner_in, below_in, side, order_t, inner, below):
    half = inner.shape[1]
    lows = []
    for a in range(inner.shape[0]):
        spread = dot(order_t[...], side[a])
        inner[a] = (inner_in[a].astype(F32) + spread[:half]).astype(BF16)
        lows.append(below_in[a].astype(F32) + spread[half:])
    packed = [low[:, :LANES] for low in lows] + [low[:, LANES:] for low in lows]
    below[...] = jnp.concatenate(packed, axis=1).astype(BF16)


def join_kernel(inner, below, after, grad_input):
    levels, _, cols, channels = grad_input.shape
    level_windows = levels // WZ
    whole = below[...].astype(F32)
    for a in range(level_windows):
        rest_at = level_windows * LANES + a * (channels - LANES)
        low = jnp.concatenate(
            [whole[:, a * LANES : (a + 1) * LANES], whole[:, rest_at : rest_at + channels - LANES]], axis=1
        )
        high = inner[a].astype(F32)
        for z in range(WZ):
            level = (a * WZ + WZ // 2 + z) % levels
            for row in range(HALF_ROWS):
                at = slice((z * HALF_ROWS + row) * cols, (z * HALF_ROWS + row + 1) * cols)
                grad_input[level, row] = low[at].astype(BF16)
                grad_input[level, HALF_ROWS + row] = high[at].astype(BF16)


def bias_kernel(chunks, *refs):
    *arrived, bias_grad, after = refs
    after[...] = jnp.zeros(after.shape, F32)
    main, rest, heads = chunks.main, chunks.rest, chunks.heads
    total = arrived[0][...].astype(F32)
    for other in arrived[1:]:
        total += other[...].astype(F32)
    many = bias_grad.shape[0] // (heads * chunks.size)
    for a, columns in enumerate(unpack(total, many, chunks.used)):
        turned = jnp.transpose(columns)
        for h in range(heads):
            at = (a * heads + h) * chunks.size
            if main:
                bias_grad[at : at + main, 0, :] = turned[h * main : (h + 1) * main]
            if rest:
                low = heads * main + h * rest
                bias_grad[at + main : at + chunks.size, 0, :] = turned[low : low + rest]


def vmem(count):
    return [pl.BlockSpec(memory_space=pltpu.VMEM)] * count


def call(kernel, outs, args, flops=0, scratch=()):
    return pl.pallas_call(
        kernel,
        out_shape=outs,
        in_specs=vmem(len(args)),
        out_specs=vmem(len(outs)),
        scratch_shapes=list(scratch),
        compiler_params=pltpu.CompilerParams(vmem_limit_bytes=40 * 2**20),
        cost_estimate=pl.CostEstimate(flops=flops, bytes_accessed=0, transcendentals=0),
    )(*args)


def shift(value, rows, cols):
    lat_count, lon_count = lax.axis_size("lat"), lax.axis_size("lon")
    pairs = []
    for i in range(lat_count):
        for j in range(lon_count):
            to = (i + rows) % lat_count * lon_count + (j + cols) % lon_count
            pairs.append((i * lon_count + j, to))
    return lax.ppermute(value, ("lat", "lon"), pairs)


def local(tokens, cotangent, norm_gain, inproj_weight, outproj_weight, bias):
    levels, rows, cols, channels = tokens.shape
    level_windows, _, heads = bias.shape[:3]
    lat_count, lon_count = lax.axis_size("lat"), lax.axis_size("lon")
    chunks = Chunks(lon_count, heads)
    windows = cols // WW
    struct = jax.ShapeDtypeStruct
    half, side = WZ * HALF_ROWS * cols, WZ * HALF_ROWS * SIDE
    gain = norm_gain.reshape(1, channels)
    side_table = side_order(cols)

    bias = bias.reshape(level_windows, heads, WT, WT)
    both = jnp.concatenate([tokens, cotangent], axis=-1)
    narrow = round_up(WZ * HALF_ROWS * (cols - HALF_COLS), 16)
    inner, below, right, corner, tail = call(
        send_kernel,
        [struct((level_windows, size, 2 * channels), BF16) for size in (half, narrow, side, side, side)],
        (both,),
    )
    below = shift(below, -1, 0)
    right = shift(right, 0, -1)
    corner = shift(corner, -1, -1)
    (bias_t,) = call(
        functools.partial(prep_kernel, chunks, lat_count),
        [struct((level_windows, lon_count, WT, chunks.width), F32)],
        (bias,),
    )
    packed = level_windows * chunks.used * WT // LANES
    per_window = []
    total = []
    for c in range(windows):
        last = c == windows - 1
        pieces = (tail, below, right, corner) if last else (inner, below)
        sums = [struct((level_windows, lon_count, WT, chunks.width), F32)]
        order = jnp.asarray(window_order(cols, c, False), BF16)
        results = call(
            functools.partial(scores_kernel, chunks, len(pieces), c == 0, last),
            [
                struct((level_windows * WT, channels), F32),
                struct((level_windows * WT, LANES), F32),
                struct((level_windows * WT, channels), BF16),
                struct((level_windows * WT, channels), F32),
                struct((level_windows * WT, channels), F32),
                struct((level_windows, WT, lon_count * chunks.width), BF16),
                struct((level_windows, WT, lon_count * chunks.width), BF16),
            ]
            + sums,
            (*pieces, gain, inproj_weight, outproj_weight, bias_t, order, *total),
            flops=10**9,
        )
        per_window.append(results[:7])
        total = results[7:]
    wide = struct((level_windows, half, channels), BF16)
    grads = []
    for c in reversed(range(windows)):
        order = jnp.asarray(window_order(cols, c, True).T, BF16)
        ins = (*per_window[c], gain, inproj_weight, order)
        if c == windows - 1:
            results = call(
                functools.partial(first_kernel, chunks),
                [wide, wide, struct((level_windows, side_table.shape[0], channels), BF16)]
                + [struct((packed, LANES), BF16)] * lon_count,
                (*ins, *total),
            )
            left = shift(results[2], 0, 1)
            arrived = [results[3]]
            for d in range(1, lon_count):
                pairs = [(i, partner(i, d, lon_count)) for i in range(lon_count)]
                arrived.append(lax.ppermute(results[3 + d], "lon", pairs))
        else:
            results = call(functools.partial(tokens_kernel, chunks, False), [wide] * 2, (*ins, *grads))
        grads = results[:2]
    g_inner, g_below = call(
        merge_kernel,
        [wide, struct((half, level_windows * channels), BF16)],
        (*grads, left, jnp.asarray(side_table.T, BF16)),
    )
    above = shift(g_below, 1, 0)
    bias_grad, after = call(
        functools.partial(bias_kernel, chunks),
        [struct((level_windows * heads * chunks.size, 1, WT), F32), struct((8, LANES), F32)],
        arrived,
    )
    (grad_input,) = call(join_kernel, [struct(tokens.shape, BF16)], (g_inner, above, after))
    bias_grad = bias_grad.reshape(level_windows, heads, chunks.size, 1, WT)
    return grad_input, jnp.transpose(bias_grad, (0, 3, 1, 2, 4))


def solution(mesh):
    placed = (
        P(None, "lat", "lon", None),
        P(None, "lat", "lon", None),
        P(),
        P(),
        P(),
        P(None, "lat", None, None, None),
    )
    return jax.shard_map(
        local,
        mesh=mesh,
        in_specs=placed,
        out_specs=(P(None, "lat", "lon", None), P(None, "lat", None, "lon", None)),
        check_vma=False,
    )
```

```python
import functools

import jax
import jax.numpy as jnp
import numpy as np
from jax import lax
from jax.experimental import pallas as pl
from jax.experimental.pallas import tpu as pltpu
from jax.sharding import PartitionSpec as P

WZ = 2
WH = 6
WW = 12
WT = WZ * WH * WW
HALF_ROWS = WH // 2
HALF_COLS = WW // 2
SIDE = 8
LEVEL = WH * WW
LANES = 128
LOG2E = 1.4426950408889634
epsilon = 1e-05
F32 = jnp.float32
BF16 = jnp.bfloat16
NT = (((1,), (1,)), ((), ()))


def dot(a, b):
    return jnp.dot(a, b, preferred_element_type=F32)


def dot_nt(a, b):
    return lax.dot_general(a, b, NT, preferred_element_type=F32)


def round_up(value, to):
    return (value + to - 1) // to * to


class Chunks:
    def __init__(self, parts, heads):
        self.parts, self.heads = parts, heads
        self.size = WT // parts
        self.main = self.size // 16 * 16
        self.rest = self.size - self.main
        self.rest_rows = round_up(heads * self.rest, 16)
        self.rows = self.main + self.rest_rows
        self.used = heads * self.main + self.rest_rows
        self.width = round_up(self.used, LANES)

    def columns(self, j):
        lane = lax.broadcasted_iota(jnp.int32, (1, self.width), 1)
        low = self.heads * self.main
        main, left = lane, self.main + lane - low
        for h in range(1, self.heads):
            main -= jnp.where(lane >= h * self.main, self.main, 0)
            left -= jnp.where(lane >= low + h * self.rest, self.rest, 0)
        return j * self.size + jnp.where(lane < low, main, left)


def side_order(cols):
    part = HALF_ROWS * cols
    table = np.zeros((round_up(WZ * WH * HALF_COLS, 16), 2 * WZ * part), np.float32)
    for z in range(WZ):
        for r in range(WH):
            low, row = divmod(r, HALF_ROWS)
            for w in range(HALF_COLS):
                table[(z * WH + r) * HALF_COLS + w, (low * WZ + z) * part + row * cols + w] = 1.0
    return table


def window_order(cols, c, out):
    last = c == cols // WW - 1
    part, side = HALF_ROWS * cols, HALF_ROWS * SIDE
    kept = cols if out else cols - HALF_COLS
    tail = last and not out
    inner = WZ * (side if tail else part)
    near = inner + round_up(WZ * HALF_ROWS * kept, 16)
    extra = round_up(WZ * WH * HALF_COLS, 16) if out else 2 * WZ * side
    table = np.zeros((WT, near + last * extra), np.float32)
    for z in range(WZ):
        for r in range(WH):
            for w in range(WW):
                col = c * WW + w + HALF_COLS
                low, row = divmod(r, HALF_ROWS)
                if col >= cols and out:
                    at = near + (z * WH + r) * HALF_COLS + col - cols
                elif col >= cols:
                    at = near + (low * WZ + z) * side + row * SIDE + col - cols
                elif low:
                    at = inner + (z * HALF_ROWS + row) * kept + col - (cols - kept)
                elif tail:
                    at = z * side + row * SIDE + col - (cols - SIDE)
                else:
                    at = z * part + row * cols + col
                table[(z * WH + r) * WW + w, at] = 1.0
    return table


def level_rows(field, a, base):
    levels = field.shape[0]
    at = [(a * WZ + WZ // 2 + z) % levels for z in range(WZ)]
    return [field[level, base + row].astype(F32) for level in at for row in range(HALF_ROWS)]


def send_kernel(both, inner, below, right, corner, tail):
    cols = both.shape[2]
    kept = cols - HALF_COLS
    shape = (below.shape[1], WZ * HALF_ROWS * cols)
    row = lax.broadcasted_iota(jnp.int32, shape, 0)
    target = row + HALF_COLS
    for i in range(1, WZ * HALF_ROWS):
        target += jnp.where(row >= i * kept, HALF_COLS, 0)
    kept_rows = (lax.broadcasted_iota(jnp.int32, shape, 1) == target) & (row < WZ * HALF_ROWS * kept)
    narrow = kept_rows.astype(F32).astype(BF16)
    for a in range(inner.shape[0]):
        low, high = level_rows(both, a, 0), level_rows(both, a, HALF_ROWS)
        below[a] = dot(narrow, jnp.concatenate(low, axis=0).astype(BF16)).astype(BF16)
        inner[a] = jnp.concatenate(high, axis=0).astype(BF16)
        right[a] = jnp.concatenate([row[:SIDE] for row in high], axis=0).astype(BF16)
        tail[a] = jnp.concatenate([row[cols - SIDE :] for row in high], axis=0).astype(BF16)
        corner[a] = jnp.concatenate([row[:SIDE] for row in low], axis=0).astype(BF16)


def prep_kernel(chunks, lat_count, bias, bias_t):
    level_windows = bias.shape[0]
    last_lat = lax.axis_index("lat") == lat_count - 1
    parts, size, main = chunks.parts, chunks.size, chunks.main

    def labels(index, window):
        level_label = (index >= LEVEL) & (window == level_windows - 1)
        in_level = jnp.where(index >= LEVEL, index - LEVEL, index)
        row_label = (in_level >= LEVEL // 2) & last_lat
        return level_label.astype(jnp.int32) * 2 + row_label.astype(jnp.int32)

    key_index = lax.broadcasted_iota(jnp.int32, (WT, chunks.width), 0)
    for window in range(level_windows):
        key_labels = labels(key_index, window)
        for j in range(parts):
            heads = range(chunks.heads)
            low = j * size
            rows = []
            if main:
                rows += [bias[window, h, low : low + main, :] for h in heads]
            if chunks.rest:
                rows += [bias[window, h, low + main : low + size, :] for h in heads]
            spare = chunks.width - chunks.heads * size
            if spare:
                rows.append(jnp.zeros((spare, WT), F32))
            turned = jnp.transpose(jnp.concatenate(rows, axis=0)) * LOG2E
            allowed = key_labels == labels(chunks.columns(j), window)
            bias_t[window, j] = jnp.where(allowed, turned, -1e30)


def head_masks(chunks, channels):
    head_dim = channels // chunks.heads
    lane_head = lax.broadcasted_iota(jnp.int32, (1, channels), 1) // head_dim
    lanes = [lane_head == h for h in range(chunks.heads)]
    rest = None
    if chunks.rest:
        row = lax.broadcasted_iota(jnp.int32, (chunks.rest_rows, channels), 0)
        lane = lax.broadcasted_iota(jnp.int32, (chunks.rest_rows, channels), 1) // head_dim
        rest = jnp.zeros((chunks.rest_rows, channels), F32)
        for h in range(chunks.heads):
            inside = (row >= h * chunks.rest) & (row < (h + 1) * chunks.rest) & (lane == h)
            rest = jnp.where(inside, 1.0, rest)
    return lanes, rest


def stack_heads(chunks, value, j, lane_masks, rest_mask):
    low = j * chunks.size
    pieces = []
    if chunks.main:
        main = value[low : low + chunks.main].astype(BF16)
        pieces += [main * mask for mask in lane_masks]
    if chunks.rest:
        rows = [value[low + chunks.main : low + chunks.size]] * chunks.heads
        spare = chunks.rest_rows - chunks.heads * chunks.rest
        if spare:
            rows.append(jnp.zeros((spare, value.shape[1]), F32))
        pieces.append(jnp.concatenate(rows, axis=0).astype(BF16) * rest_mask)
    if chunks.width > chunks.used:
        pieces.append(jnp.zeros((chunks.width - chunks.used, value.shape[1]), BF16))
    return jnp.concatenate(pieces, axis=0)


def split(inproj):
    channels = inproj.shape[0]
    return [inproj[:, part * channels : (part + 1) * channels] for part in range(3)]


def pack(columns):
    used = columns[0].shape[1]
    whole = used // LANES * LANES
    tiles = [part[:, i : i + LANES] for part in columns for i in range(0, whole, LANES)]
    left = jnp.concatenate([part[:, whole:] for part in columns], axis=1)
    while left.shape[1] >= LANES:
        tiles.append(left[:, :LANES])
        left = left[:, LANES:]
    if left.shape[1]:
        tiles.append(jnp.concatenate([left[: WT // 2, : LANES // 2], left[WT // 2 :, : LANES // 2]], axis=1))
    return jnp.concatenate(tiles, axis=0)


def unpack(rows, many, used):
    whole = used // LANES
    tiles = [rows[i * WT : (i + 1) * WT] for i in range(rows.shape[0] // WT)]
    left = tiles[many * whole :]
    if rows.shape[0] % WT:
        last = rows[len(tiles) * WT :]
        left.append(jnp.concatenate([last[:, : LANES // 2], last[:, LANES // 2 :]], axis=0))
    left = jnp.concatenate(left, axis=1) if left else None
    rest = used - whole * LANES
    columns = []
    for a in range(many):
        part = tiles[a * whole : (a + 1) * whole]
        if rest:
            part.append(left[:, a * rest : (a + 1) * rest])
        columns.append(jnp.concatenate(part, axis=1))
    return columns


def partner(me, d, parts):
    return me ^ d if parts & (parts - 1) == 0 else (me + d) % parts


def scores_kernel(chunks, near, first, last, *refs):
    pieces, refs = refs[:near], refs[near:]
    gain_ref, inproj, outproj, bias_t, perm, *refs = refs
    weights = split(inproj)
    before = None
    if not first:
        before, *refs = refs
    standard_out, scale_out, keys_out, query_out, up_out, p_out, ds_out, total_out = refs
    parts, width = chunks.parts, chunks.width
    channels = outproj.shape[0]
    scaling = (channels // chunks.heads) ** (-0.5)
    lanes, rest_mask = head_masks(chunks, channels)
    lanes = [mask.astype(F32).astype(BF16) for mask in lanes]
    rest_mask = rest_mask.astype(BF16) if chunks.rest else None
    me = lax.axis_index("lon")
    level_windows = pieces[0].shape[0]
    tile = channels // LANES * LANES
    from_tile = jnp.concatenate([jnp.zeros((channels, channels - tile), BF16), outproj[...]], axis=1)
    ts, us = [], []
    for a in range(level_windows):
        moved = dot(perm[...], jnp.concatenate([piece[a] for piece in pieces], axis=0))
        ts.append(moved[:, :channels])
        us.append(dot_nt(moved[:, tile:].astype(BF16), from_tile))
    t = jnp.concatenate(ts, axis=0)
    centred = t - jnp.mean(t, axis=-1, keepdims=True)
    inverse_rms = lax.rsqrt(jnp.mean(centred * centred, axis=-1, keepdims=True) + epsilon)
    standard = centred * inverse_rms
    standard_out[...] = standard
    scale_out[...] = jnp.broadcast_to(inverse_rms, scale_out.shape)
    normed = (standard * gain_ref[...]).astype(BF16)
    q = dot(normed, weights[0])
    query_out[...] = q
    k = dot(normed, weights[1]).astype(BF16)
    v = dot(normed, weights[2]).astype(BF16)
    keys_out[...] = k
    for a in range(level_windows):
        cut = slice(a * WT, (a + 1) * WT)
        query, up = q[cut], us[a]
        up_out[cut] = up
        for d in range(parts):
            at = slice(d * width, (d + 1) * width)
            s = dot_nt(k[cut], stack_heads(chunks, query, d, lanes, rest_mask))
            dp = dot_nt(v[cut], stack_heads(chunks, up, d, lanes, rest_mask))
            e = jnp.exp2(s * (scaling * LOG2E) + bias_t[a, d])
            p = e * (1.0 / jnp.sum(e, axis=0, keepdims=True))
            ds = p * (dp - jnp.sum(p * dp, axis=0, keepdims=True))
            p_out[a, :, at] = p.astype(BF16)
            ds_out[a, :, at] = ds.astype(BF16)
            if not first:
                ds += before[a, d]
            if last:
                total_out[a, d] = ds
            else:
                total_out[a, d] = ds


def tokens_kernel(chunks, first, *refs):
    standard_in, scale_in, keys, queries_in, ups, p_in, ds_in, gain_ref, inproj, perm_t, *refs = refs
    weights = split(inproj)
    before = None
    if not first:
        before, refs = refs[:2], refs[2:]
    outs = refs
    parts, width = chunks.parts, chunks.width
    channels = keys.shape[-1]
    head_dim = channels // chunks.heads
    scaling = head_dim ** (-0.5)
    lanes, rest_mask = head_masks(chunks, channels)
    low_lanes = [mask.astype(F32).astype(BF16) for mask in lanes]
    low_rest = rest_mask.astype(BF16) if chunks.rest else None
    level_windows = p_in.shape[0]
    dqs, dks, dvs = [], [], []
    for a in range(level_windows):
        cut = slice(a * WT, (a + 1) * WT)
        query, up = queries_in[cut], ups[cut]
        qs = jnp.concatenate(
            [stack_heads(chunks, query, d, low_lanes, low_rest) for d in range(parts)], axis=0
        )
        us = jnp.concatenate(
            [stack_heads(chunks, up, d, low_lanes, low_rest) for d in range(parts)], axis=0
        )
        ds = ds_in[a]
        dks.append((dot(ds, qs) * scaling).astype(BF16))
        dvs.append(dot(p_in[a], us).astype(BF16))
        turned = jnp.transpose(ds)
        key = keys[a * WT : (a + 1) * WT]
        main = []
        for lane in range(0, channels, LANES):
            low = lane // head_dim
            many = min(LANES // head_dim, chunks.heads - low)
            if not chunks.main:
                break
            some = [turned[d * width + low * chunks.main :][: many * chunks.main] for d in range(parts)]
            flat = dot(jnp.concatenate(some, axis=0), key[:, lane : lane + LANES])
            tiles = []
            for d in range(parts):
                picked = flat[d * many * chunks.main :][: chunks.main]
                for h in range(1, many):
                    mask = lanes[low + h][:, lane : lane + LANES]
                    picked = jnp.where(mask, flat[(d * many + h) * chunks.main :][: chunks.main], picked)
                tiles.append(picked)
            main.append(tiles)
        if chunks.rest:
            low = chunks.heads * chunks.main
            some = [turned[d * width + low :][: chunks.rest_rows] for d in range(parts)]
            left = dot(jnp.concatenate(some, axis=0), key)
        rows = []
        for d in range(parts):
            if chunks.main:
                rows.append(jnp.concatenate([tiles[d] for tiles in main], axis=1))
            if chunks.rest:
                some = left[d * chunks.rest_rows : (d + 1) * chunks.rest_rows] * rest_mask
                total = some[: chunks.rest]
                for h in range(1, chunks.heads):
                    total += some[h * chunks.rest : (h + 1) * chunks.rest]
                rows.append(total)
        dqs.append((jnp.concatenate(rows, axis=0) * scaling).astype(BF16))
    dq, dk, dv = (jnp.concatenate(parts_of, axis=0) for parts_of in (dqs, dks, dvs))
    scaled = (dot_nt(dq, weights[0]) + dot_nt(dk, weights[1]) + dot_nt(dv, weights[2])) * gain_ref[...]
    standard = standard_in[...]
    inverse_rms = scale_in[:, :1]
    grad = inverse_rms * (
        scaled
        - jnp.mean(scaled, axis=-1, keepdims=True)
        - standard * jnp.mean(scaled * standard, axis=-1, keepdims=True)
    )
    grad = grad.astype(BF16)
    for a in range(level_windows):
        spread = dot(perm_t[...], grad[a * WT : (a + 1) * WT])
        base = 0
        for i, out in enumerate(outs):
            rows = out.shape[1]
            part = spread[base : base + rows]
            if not first and i < 2:
                part += before[i][a].astype(F32)
            out[a] = part.astype(BF16)
            base += rows


def first_kernel(chunks, *refs):
    *ins, total, inner, below, side = refs[:14]
    messages = refs[14:]
    me = lax.axis_index("lon")
    for d, message in enumerate(messages):
        j = partner(me, d, chunks.parts)
        columns = [total[a, j][:, : chunks.used] for a in range(total.shape[0])]
        message[...] = pack(columns).astype(BF16)
    tokens_kernel(chunks, True, *ins, inner, below, side)


def merge_kernel(inner_in, below_in, side, order_t, inner, below):
    half = inner.shape[1]
    lows = []
    for a in range(inner.shape[0]):
        spread = dot(order_t[...], side[a])
        inner[a] = (inner_in[a].astype(F32) + spread[:half]).astype(BF16)
        lows.append(below_in[a].astype(F32) + spread[half:])
    packed = [low[:, :LANES] for low in lows] + [low[:, LANES:] for low in lows]
    below[...] = jnp.concatenate(packed, axis=1).astype(BF16)


def put_rows(level_window, a, rows):
    levels, many, cols, _ = rows.shape
    for z in range(WZ):
        level = (a * WZ + WZ // 2 + z) % levels
        for row in range(many):
            at = (z * many + row) * cols
            rows[level, row] = level_window[at : at + cols].astype(BF16)


def upper_kernel(inner, grad_input, done, rows, sem):
    for a in range(inner.shape[0]):
        put_rows(inner[a].astype(F32), a, rows)
    copy = pltpu.make_async_copy(rows, grad_input.at[:, HALF_ROWS:], sem)
    copy.start()
    done[...] = jnp.zeros(done.shape, F32)
    copy.wait()


def lower_kernel(below, after, upper, grad_input, rows, sem):
    level_windows = rows.shape[0] // WZ
    channels = rows.shape[3]
    whole = below[...].astype(F32)
    for a in range(level_windows):
        rest_at = level_windows * LANES + a * (channels - LANES)
        low = jnp.concatenate(
            [whole[:, a * LANES : (a + 1) * LANES], whole[:, rest_at : rest_at + channels - LANES]], axis=1
        )
        put_rows(low, a, rows)
    copy = pltpu.make_async_copy(rows, grad_input.at[:, :HALF_ROWS], sem)
    copy.start()
    copy.wait()


def bias_kernel(chunks, *refs):
    *arrived, _, bias_grad, after = refs
    after[...] = jnp.zeros(after.shape, F32)
    main, rest, heads = chunks.main, chunks.rest, chunks.heads
    total = arrived[0][...].astype(F32)
    for other in arrived[1:]:
        total += other[...].astype(F32)
    many = bias_grad.shape[0] // (heads * chunks.size)
    for a, columns in enumerate(unpack(total, many, chunks.used)):
        turned = jnp.transpose(columns)
        for h in range(heads):
            at = (a * heads + h) * chunks.size
            if main:
                bias_grad[at : at + main, 0, :] = turned[h * main : (h + 1) * main]
            if rest:
                low = heads * main + h * rest
                bias_grad[at + main : at + chunks.size, 0, :] = turned[low : low + rest]


def vmem(count):
    return [pl.BlockSpec(memory_space=pltpu.VMEM)] * count


def call(kernel, outs, args, flops=0, scratch=(), ins=None, specs=None, aliases=None):
    return pl.pallas_call(
        kernel,
        out_shape=outs,
        in_specs=ins or vmem(len(args)),
        out_specs=specs or vmem(len(outs)),
        input_output_aliases=aliases or {},
        scratch_shapes=list(scratch),
        compiler_params=pltpu.CompilerParams(vmem_limit_bytes=40 * 2**20),
        cost_estimate=pl.CostEstimate(flops=flops, bytes_accessed=0, transcendentals=0),
    )(*args)


def shift(value, rows, cols):
    lat_count, lon_count = lax.axis_size("lat"), lax.axis_size("lon")
    pairs = []
    for i in range(lat_count):
        for j in range(lon_count):
            to = (i + rows) % lat_count * lon_count + (j + cols) % lon_count
            pairs.append((i * lon_count + j, to))
    return lax.ppermute(value, ("lat", "lon"), pairs)


def local(tokens, cotangent, norm_gain, inproj_weight, outproj_weight, bias):
    levels, rows, cols, channels = tokens.shape
    level_windows, _, heads = bias.shape[:3]
    lat_count, lon_count = lax.axis_size("lat"), lax.axis_size("lon")
    chunks = Chunks(lon_count, heads)
    windows = cols // WW
    struct = jax.ShapeDtypeStruct
    half, side = WZ * HALF_ROWS * cols, WZ * HALF_ROWS * SIDE
    gain = norm_gain.reshape(1, channels)
    side_table = side_order(cols)

    bias = bias.reshape(level_windows, heads, WT, WT)
    both = jnp.concatenate([tokens, cotangent], axis=-1)
    narrow = round_up(WZ * HALF_ROWS * (cols - HALF_COLS), 16)
    inner, below, right, corner, tail = call(
        send_kernel,
        [struct((level_windows, size, 2 * channels), BF16) for size in (half, narrow, side, side, side)],
        (both,),
    )
    below = shift(below, -1, 0)
    right = shift(right, 0, -1)
    corner = shift(corner, -1, -1)
    (bias_t,) = call(
        functools.partial(prep_kernel, chunks, lat_count),
        [struct((level_windows, lon_count, WT, chunks.width), F32)],
        (bias,),
    )
    packed = level_windows * chunks.used * WT // LANES
    per_window = []
    total = []
    for c in range(windows):
        last = c == windows - 1
        pieces = (tail, below, right, corner) if last else (inner, below)
        sums = [struct((level_windows, lon_count, WT, chunks.width), F32)]
        order = jnp.asarray(window_order(cols, c, False), BF16)
        results = call(
            functools.partial(scores_kernel, chunks, len(pieces), c == 0, last),
            [
                struct((level_windows * WT, channels), F32),
                struct((level_windows * WT, LANES), F32),
                struct((level_windows * WT, channels), BF16),
                struct((level_windows * WT, channels), F32),
                struct((level_windows * WT, channels), F32),
                struct((level_windows, WT, lon_count * chunks.width), BF16),
                struct((level_windows, WT, lon_count * chunks.width), BF16),
            ]
            + sums,
            (*pieces, gain, inproj_weight, outproj_weight, bias_t, order, *total),
            flops=10**9,
        )
        per_window.append(results[:7])
        total = results[7:]
    wide = struct((level_windows, half, channels), BF16)
    grads = []
    for c in reversed(range(windows)):
        order = jnp.asarray(window_order(cols, c, True).T, BF16)
        ins = (*per_window[c], gain, inproj_weight, order)
        if c == windows - 1:
            results = call(
                functools.partial(first_kernel, chunks),
                [wide, wide, struct((level_windows, side_table.shape[0], channels), BF16)]
                + [struct((packed, LANES), BF16)] * lon_count,
                (*ins, *total),
            )
            left = shift(results[2], 0, 1)
            arrived = [results[3]]
            for d in range(1, lon_count):
                pairs = [(i, partner(i, d, lon_count)) for i in range(lon_count)]
                arrived.append(lax.ppermute(results[3 + d], "lon", pairs))
        else:
            results = call(functools.partial(tokens_kernel, chunks, False), [wide] * 2, (*ins, *grads))
        grads = results[:2]
    g_inner, g_below = call(
        merge_kernel,
        [wide, struct((half, level_windows * channels), BF16)],
        (*grads, left, jnp.asarray(side_table.T, BF16)),
    )
    above = shift(g_below, 1, 0)
    anywhere = [pl.BlockSpec(memory_space=pl.ANY)]
    rows_scratch = [pltpu.VMEM((levels, HALF_ROWS, cols, channels), BF16), pltpu.SemaphoreType.DMA(())]
    token = struct((8, LANES), F32)
    grad_input, done = call(
        upper_kernel, [struct(tokens.shape, BF16), token], (g_inner,), scratch=rows_scratch, specs=anywhere + vmem(1)
    )
    bias_grad, after = call(
        functools.partial(bias_kernel, chunks),
        [struct((level_windows * heads * chunks.size, 1, WT), F32), token],
        arrived + [done],
    )
    (grad_input,) = call(
        lower_kernel,
        [struct(tokens.shape, BF16)],
        (above, after, grad_input),
        scratch=rows_scratch,
        ins=vmem(2) + anywhere,
        specs=anywhere,
        aliases={2: 0},
    )
    bias_grad = bias_grad.reshape(level_windows, heads, chunks.size, 1, WT)
    return grad_input, jnp.transpose(bias_grad, (0, 3, 1, 2, 4))


def solution(mesh):
    placed = (
        P(None, "lat", "lon", None),
        P(None, "lat", "lon", None),
        P(),
        P(),
        P(),
        P(None, "lat", None, None, None),
    )
    return jax.shard_map(
        local,
        mesh=mesh,
        in_specs=placed,
        out_specs=(P(None, "lat", "lon", None), P(None, "lat", None, "lon", None)),
        check_vma=False,
    )
```

```python
import functools

import jax
import jax.numpy as jnp
import numpy as np
from jax import lax
from jax.experimental import pallas as pl
from jax.experimental.pallas import tpu as pltpu
from jax.sharding import PartitionSpec as P

WZ = 2
WH = 6
WW = 12
WT = WZ * WH * WW
HALF_ROWS = WH // 2
HALF_COLS = WW // 2
SIDE = 8
LEVEL = WH * WW
LANES = 128
LOG2E = 1.4426950408889634
epsilon = 1e-05
F32 = jnp.float32
BF16 = jnp.bfloat16
NT = (((1,), (1,)), ((), ()))


def dot(a, b):
    return jnp.dot(a, b, preferred_element_type=F32)


def dot_nt(a, b):
    return lax.dot_general(a, b, NT, preferred_element_type=F32)


def round_up(value, to):
    return (value + to - 1) // to * to


class Chunks:
    def __init__(self, parts, heads):
        self.parts, self.heads = parts, heads
        self.size = WT // parts
        self.main = self.size // 16 * 16
        self.rest = self.size - self.main
        self.rest_rows = round_up(heads * self.rest, 16)
        self.rows = self.main + self.rest_rows
        self.used = heads * self.main + self.rest_rows
        self.width = round_up(self.used, LANES)

    def columns(self, j):
        lane = lax.broadcasted_iota(jnp.int32, (1, self.width), 1)
        low = self.heads * self.main
        main, left = lane, self.main + lane - low
        for h in range(1, self.heads):
            main -= jnp.where(lane >= h * self.main, self.main, 0)
            left -= jnp.where(lane >= low + h * self.rest, self.rest, 0)
        return j * self.size + jnp.where(lane < low, main, left)


def side_order(cols):
    part = HALF_ROWS * cols
    table = np.zeros((round_up(WZ * WH * HALF_COLS, 16), 2 * WZ * part), np.float32)
    for z in range(WZ):
        for r in range(WH):
            low, row = divmod(r, HALF_ROWS)
            for w in range(HALF_COLS):
                table[(z * WH + r) * HALF_COLS + w, (low * WZ + z) * part + row * cols + w] = 1.0
    return table


def window_order(cols, c, out):
    last = c == cols // WW - 1
    part, side = HALF_ROWS * cols, HALF_ROWS * SIDE
    kept = cols if out else cols - HALF_COLS
    tail = last and not out
    inner = WZ * (side if tail else part)
    near = inner + round_up(WZ * HALF_ROWS * kept, 16)
    extra = round_up(WZ * WH * HALF_COLS, 16) if out else 2 * WZ * side
    table = np.zeros((WT, near + last * extra), np.float32)
    for z in range(WZ):
        for r in range(WH):
            for w in range(WW):
                col = c * WW + w + HALF_COLS
                low, row = divmod(r, HALF_ROWS)
                if col >= cols and out:
                    at = near + (z * WH + r) * HALF_COLS + col - cols
                elif col >= cols:
                    at = near + (low * WZ + z) * side + row * SIDE + col - cols
                elif low:
                    at = inner + (z * HALF_ROWS + row) * kept + col - (cols - kept)
                elif tail:
                    at = z * side + row * SIDE + col - (cols - SIDE)
                else:
                    at = z * part + row * cols + col
                table[(z * WH + r) * WW + w, at] = 1.0
    return table


def level_rows(field, a, base):
    levels = field.shape[0]
    at = [(a * WZ + WZ // 2 + z) % levels for z in range(WZ)]
    return [field[level, base + row].astype(F32) for level in at for row in range(HALF_ROWS)]


def send_kernel(both, inner, below, right, corner, tail):
    cols = both.shape[2]
    kept = cols - HALF_COLS
    shape = (below.shape[1], WZ * HALF_ROWS * cols)
    row = lax.broadcasted_iota(jnp.int32, shape, 0)
    target = row + HALF_COLS
    for i in range(1, WZ * HALF_ROWS):
        target += jnp.where(row >= i * kept, HALF_COLS, 0)
    kept_rows = (lax.broadcasted_iota(jnp.int32, shape, 1) == target) & (row < WZ * HALF_ROWS * kept)
    narrow = kept_rows.astype(F32).astype(BF16)
    for a in range(inner.shape[0]):
        low, high = level_rows(both, a, 0), level_rows(both, a, HALF_ROWS)
        below[a] = dot(narrow, jnp.concatenate(low, axis=0).astype(BF16)).astype(BF16)
        inner[a] = jnp.concatenate(high, axis=0).astype(BF16)
        right[a] = jnp.concatenate([row[:SIDE] for row in high], axis=0).astype(BF16)
        tail[a] = jnp.concatenate([row[cols - SIDE :] for row in high], axis=0).astype(BF16)
        corner[a] = jnp.concatenate([row[:SIDE] for row in low], axis=0).astype(BF16)


def prep_kernel(chunks, lat_count, bias, bias_t):
    level_windows = bias.shape[0]
    last_lat = lax.axis_index("lat") == lat_count - 1
    parts, size, main = chunks.parts, chunks.size, chunks.main

    def labels(index, window):
        level_label = (index >= LEVEL) & (window == level_windows - 1)
        in_level = jnp.where(index >= LEVEL, index - LEVEL, index)
        row_label = (in_level >= LEVEL // 2) & last_lat
        return level_label.astype(jnp.int32) * 2 + row_label.astype(jnp.int32)

    key_index = lax.broadcasted_iota(jnp.int32, (WT, chunks.width), 0)
    for window in range(level_windows):
        key_labels = labels(key_index, window)
        for j in range(parts):
            heads = range(chunks.heads)
            low = j * size
            rows = []
            if main:
                rows += [bias[window, h, low : low + main, :] for h in heads]
            if chunks.rest:
                rows += [bias[window, h, low + main : low + size, :] for h in heads]
            spare = chunks.width - chunks.heads * size
            if spare:
                rows.append(jnp.zeros((spare, WT), F32))
            turned = jnp.transpose(jnp.concatenate(rows, axis=0)) * LOG2E
            allowed = key_labels == labels(chunks.columns(j), window)
            bias_t[window, j] = jnp.where(allowed, turned, -1e30)


def head_masks(chunks, channels):
    head_dim = channels // chunks.heads
    lane_head = lax.broadcasted_iota(jnp.int32, (1, channels), 1) // head_dim
    lanes = [lane_head == h for h in range(chunks.heads)]
    rest = None
    if chunks.rest:
        row = lax.broadcasted_iota(jnp.int32, (chunks.rest_rows, channels), 0)
        lane = lax.broadcasted_iota(jnp.int32, (chunks.rest_rows, channels), 1) // head_dim
        rest = jnp.zeros((chunks.rest_rows, channels), F32)
        for h in range(chunks.heads):
            inside = (row >= h * chunks.rest) & (row < (h + 1) * chunks.rest) & (lane == h)
            rest = jnp.where(inside, 1.0, rest)
    return lanes, rest


def stack_heads(chunks, value, j, lane_masks, rest_mask):
    low = j * chunks.size
    pieces = []
    if chunks.main:
        main = value[low : low + chunks.main].astype(BF16)
        pieces += [main * mask for mask in lane_masks]
    if chunks.rest:
        rows = [value[low + chunks.main : low + chunks.size]] * chunks.heads
        spare = chunks.rest_rows - chunks.heads * chunks.rest
        if spare:
            rows.append(jnp.zeros((spare, value.shape[1]), F32))
        pieces.append(jnp.concatenate(rows, axis=0).astype(BF16) * rest_mask)
    if chunks.width > chunks.used:
        pieces.append(jnp.zeros((chunks.width - chunks.used, value.shape[1]), BF16))
    return jnp.concatenate(pieces, axis=0)


def split(inproj):
    channels = inproj.shape[0]
    return [inproj[:, part * channels : (part + 1) * channels] for part in range(3)]


def pack(columns):
    used = columns[0].shape[1]
    whole = used // LANES * LANES
    tiles = [part[:, i : i + LANES] for part in columns for i in range(0, whole, LANES)]
    left = jnp.concatenate([part[:, whole:] for part in columns], axis=1)
    while left.shape[1] >= LANES:
        tiles.append(left[:, :LANES])
        left = left[:, LANES:]
    if left.shape[1]:
        tiles.append(jnp.concatenate([left[: WT // 2, : LANES // 2], left[WT // 2 :, : LANES // 2]], axis=1))
    return jnp.concatenate(tiles, axis=0)


def unpack(rows, many, used):
    whole = used // LANES
    tiles = [rows[i * WT : (i + 1) * WT] for i in range(rows.shape[0] // WT)]
    left = tiles[many * whole :]
    if rows.shape[0] % WT:
        last = rows[len(tiles) * WT :]
        left.append(jnp.concatenate([last[:, : LANES // 2], last[:, LANES // 2 :]], axis=0))
    left = jnp.concatenate(left, axis=1) if left else None
    rest = used - whole * LANES
    columns = []
    for a in range(many):
        part = tiles[a * whole : (a + 1) * whole]
        if rest:
            part.append(left[:, a * rest : (a + 1) * rest])
        columns.append(jnp.concatenate(part, axis=1))
    return columns


def partner(me, d, parts):
    return me ^ d if parts & (parts - 1) == 0 else (me + d) % parts


def scores_kernel(chunks, near, first, last, *refs):
    pieces, refs = refs[:near], refs[near:]
    gain_ref, inproj, outproj, bias_t, perm, *refs = refs
    weights = split(inproj)
    before = None
    if not first:
        before, *refs = refs
    standard_out, scale_out, keys_out, query_out, up_out, p_out, ds_out, total_out = refs
    parts, width = chunks.parts, chunks.width
    channels = outproj.shape[0]
    scaling = (channels // chunks.heads) ** (-0.5)
    lanes, rest_mask = head_masks(chunks, channels)
    lanes = [mask.astype(F32).astype(BF16) for mask in lanes]
    rest_mask = rest_mask.astype(BF16) if chunks.rest else None
    me = lax.axis_index("lon")
    level_windows = pieces[0].shape[0]
    tile = channels // LANES * LANES
    from_tile = jnp.concatenate([jnp.zeros((channels, channels - tile), BF16), outproj[...]], axis=1)
    ts, us = [], []
    for a in range(level_windows):
        moved = dot(perm[...], jnp.concatenate([piece[a] for piece in pieces], axis=0))
        ts.append(moved[:, :channels])
        us.append(dot_nt(moved[:, tile:].astype(BF16), from_tile))
    t = jnp.concatenate(ts, axis=0)
    centred = t - jnp.mean(t, axis=-1, keepdims=True)
    inverse_rms = lax.rsqrt(jnp.mean(centred * centred, axis=-1, keepdims=True) + epsilon)
    standard = centred * inverse_rms
    standard_out[...] = standard
    scale_out[...] = jnp.broadcast_to(inverse_rms, scale_out.shape)
    normed = (standard * gain_ref[...]).astype(BF16)
    q = dot(normed, weights[0])
    query_out[...] = q
    k = dot(normed, weights[1]).astype(BF16)
    v = dot(normed, weights[2]).astype(BF16)
    keys_out[...] = k
    for a in range(level_windows):
        cut = slice(a * WT, (a + 1) * WT)
        query, up = q[cut], us[a]
        up_out[cut] = up
        for d in range(parts):
            at = slice(d * width, (d + 1) * width)
            s = dot_nt(k[cut], stack_heads(chunks, query, d, lanes, rest_mask))
            dp = dot_nt(v[cut], stack_heads(chunks, up, d, lanes, rest_mask))
            e = jnp.exp2(s * (scaling * LOG2E) + bias_t[a, d])
            p = e * (1.0 / jnp.sum(e, axis=0, keepdims=True))
            ds = p * (dp - jnp.sum(p * dp, axis=0, keepdims=True))
            p_out[a, :, at] = p.astype(BF16)
            ds_out[a, :, at] = ds.astype(BF16)
            if not first:
                ds += before[a, d]
            if last:
                total_out[a, d] = ds
            else:
                total_out[a, d] = ds


def tokens_kernel(chunks, first, *refs):
    standard_in, scale_in, keys, queries_in, ups, p_in, ds_in, gain_ref, inproj, perm_t, *refs = refs
    weights = split(inproj)
    before = None
    if not first:
        before, refs = refs[:2], refs[2:]
    outs = refs
    parts, width = chunks.parts, chunks.width
    channels = keys.shape[-1]
    head_dim = channels // chunks.heads
    scaling = head_dim ** (-0.5)
    lanes, rest_mask = head_masks(chunks, channels)
    low_lanes = [mask.astype(F32).astype(BF16) for mask in lanes]
    low_rest = rest_mask.astype(BF16) if chunks.rest else None
    level_windows = p_in.shape[0]
    dqs, dks, dvs = [], [], []
    for a in range(level_windows):
        cut = slice(a * WT, (a + 1) * WT)
        query, up = queries_in[cut], ups[cut]
        qs = jnp.concatenate(
            [stack_heads(chunks, query, d, low_lanes, low_rest) for d in range(parts)], axis=0
        )
        us = jnp.concatenate(
            [stack_heads(chunks, up, d, low_lanes, low_rest) for d in range(parts)], axis=0
        )
        ds = ds_in[a]
        dks.append((dot(ds, qs) * scaling).astype(BF16))
        dvs.append(dot(p_in[a], us).astype(BF16))
        turned = jnp.transpose(ds)
        key = keys[a * WT : (a + 1) * WT]
        main = []
        for lane in range(0, channels, LANES):
            low = lane // head_dim
            many = min(LANES // head_dim, chunks.heads - low)
            if not chunks.main:
                break
            some = [turned[d * width + low * chunks.main :][: many * chunks.main] for d in range(parts)]
            flat = dot(jnp.concatenate(some, axis=0), key[:, lane : lane + LANES])
            tiles = []
            for d in range(parts):
                picked = flat[d * many * chunks.main :][: chunks.main]
                for h in range(1, many):
                    mask = lanes[low + h][:, lane : lane + LANES]
                    picked = jnp.where(mask, flat[(d * many + h) * chunks.main :][: chunks.main], picked)
                tiles.append(picked)
            main.append(tiles)
        if chunks.rest:
            low = chunks.heads * chunks.main
            some = [turned[d * width + low :][: chunks.rest_rows] for d in range(parts)]
            left = dot(jnp.concatenate(some, axis=0), key)
        rows = []
        for d in range(parts):
            if chunks.main:
                rows.append(jnp.concatenate([tiles[d] for tiles in main], axis=1))
            if chunks.rest:
                some = left[d * chunks.rest_rows : (d + 1) * chunks.rest_rows] * rest_mask
                total = some[: chunks.rest]
                for h in range(1, chunks.heads):
                    total += some[h * chunks.rest : (h + 1) * chunks.rest]
                rows.append(total)
        dqs.append((jnp.concatenate(rows, axis=0) * scaling).astype(BF16))
    dq, dk, dv = (jnp.concatenate(parts_of, axis=0) for parts_of in (dqs, dks, dvs))
    scaled = (dot_nt(dq, weights[0]) + dot_nt(dk, weights[1]) + dot_nt(dv, weights[2])) * gain_ref[...]
    standard = standard_in[...]
    inverse_rms = scale_in[:, :1]
    grad = inverse_rms * (
        scaled
        - jnp.mean(scaled, axis=-1, keepdims=True)
        - standard * jnp.mean(scaled * standard, axis=-1, keepdims=True)
    )
    grad = grad.astype(BF16)
    for a in range(level_windows):
        spread = dot(perm_t[...], grad[a * WT : (a + 1) * WT])
        base = 0
        for i, out in enumerate(outs):
            rows = out.shape[1]
            part = spread[base : base + rows]
            if not first and i < 2:
                part += before[i][a].astype(F32)
            out[a] = part.astype(BF16)
            base += rows


def first_kernel(chunks, *refs):
    *ins, total, inner, below, side = refs[:14]
    messages = refs[14:]
    me = lax.axis_index("lon")
    for d, message in enumerate(messages):
        j = partner(me, d, chunks.parts)
        columns = [total[a, j][:, : chunks.used] for a in range(total.shape[0])]
        message[...] = pack(columns).astype(BF16)
    tokens_kernel(chunks, True, *ins, inner, below, side)


def merge_kernel(inner_in, below_in, side, order_t, inner, below):
    half = inner.shape[1]
    lows = []
    for a in range(inner.shape[0]):
        spread = dot(order_t[...], side[a])
        inner[a] = (inner_in[a].astype(F32) + spread[:half]).astype(BF16)
        lows.append(below_in[a].astype(F32) + spread[half:])
    packed = [low[:, :LANES] for low in lows] + [low[:, LANES:] for low in lows]
    below[...] = jnp.concatenate(packed, axis=1).astype(BF16)


def join_kernel(inner, below, after, grad_input):
    levels, _, cols, channels = grad_input.shape
    level_windows = levels // WZ
    whole = below[...].astype(F32)
    for a in range(level_windows):
        rest_at = level_windows * LANES + a * (channels - LANES)
        low = jnp.concatenate(
            [whole[:, a * LANES : (a + 1) * LANES], whole[:, rest_at : rest_at + channels - LANES]], axis=1
        )
        high = inner[a].astype(F32)
        for z in range(WZ):
            level = (a * WZ + WZ // 2 + z) % levels
            for row in range(HALF_ROWS):
                at = slice((z * HALF_ROWS + row) * cols, (z * HALF_ROWS + row + 1) * cols)
                grad_input[level, row] = low[at].astype(BF16)
                grad_input[level, HALF_ROWS + row] = high[at].astype(BF16)


def bias_kernel(chunks, *refs):
    *arrived, bias_grad, after = refs
    after[...] = jnp.zeros(after.shape, F32)
    main, rest, heads = chunks.main, chunks.rest, chunks.heads
    total = arrived[0][...].astype(F32)
    for other in arrived[1:]:
        total += other[...].astype(F32)
    many = bias_grad.shape[0] // (heads * chunks.size)
    for a, columns in enumerate(unpack(total, many, chunks.used)):
        turned = jnp.transpose(columns)
        for h in range(heads):
            at = (a * heads + h) * chunks.size
            if main:
                bias_grad[at : at + main, 0, :] = turned[h * main : (h + 1) * main]
            if rest:
                low = heads * main + h * rest
                bias_grad[at + main : at + chunks.size, 0, :] = turned[low : low + rest]


def vmem(count):
    return [pl.BlockSpec(memory_space=pltpu.VMEM)] * count


def call(kernel, outs, args, flops=0, scratch=()):
    return pl.pallas_call(
        kernel,
        out_shape=outs,
        in_specs=vmem(len(args)),
        out_specs=vmem(len(outs)),
        scratch_shapes=list(scratch),
        compiler_params=pltpu.CompilerParams(vmem_limit_bytes=40 * 2**20),
        cost_estimate=pl.CostEstimate(flops=flops, bytes_accessed=0, transcendentals=0),
    )(*args)


def shift(value, rows, cols):
    lat_count, lon_count = lax.axis_size("lat"), lax.axis_size("lon")
    pairs = []
    for i in range(lat_count):
        for j in range(lon_count):
            to = (i + rows) % lat_count * lon_count + (j + cols) % lon_count
            pairs.append((i * lon_count + j, to))
    return lax.ppermute(value, ("lat", "lon"), pairs)


def local(tokens, cotangent, norm_gain, inproj_weight, outproj_weight, bias):
    levels, rows, cols, channels = tokens.shape
    level_windows, _, heads = bias.shape[:3]
    lat_count, lon_count = lax.axis_size("lat"), lax.axis_size("lon")
    chunks = Chunks(lon_count, heads)
    windows = cols // WW
    struct = jax.ShapeDtypeStruct
    half, side = WZ * HALF_ROWS * cols, WZ * HALF_ROWS * SIDE
    gain = norm_gain.reshape(1, channels)
    side_table = side_order(cols)

    bias = bias.reshape(level_windows, heads, WT, WT)
    both = jnp.concatenate([tokens, cotangent], axis=-1)
    narrow = round_up(WZ * HALF_ROWS * (cols - HALF_COLS), 16)
    inner, below, right, corner, tail = call(
        send_kernel,
        [struct((level_windows, size, 2 * channels), BF16) for size in (half, narrow, side, side, side)],
        (both,),
    )
    below = shift(below, -1, 0)
    right = shift(right, 0, -1)
    corner = shift(corner, -1, -1)
    (bias_t,) = call(
        functools.partial(prep_kernel, chunks, lat_count),
        [struct((level_windows, lon_count, WT, chunks.width), F32)],
        (bias,),
    )
    packed = level_windows * chunks.used * WT // LANES
    per_window = []
    total = []
    for c in range(windows):
        last = c == windows - 1
        pieces = (tail, below, right, corner) if last else (inner, below)
        sums = [struct((level_windows, lon_count, WT, chunks.width), F32)]
        order = jnp.asarray(window_order(cols, c, False), BF16)
        results = call(
            functools.partial(scores_kernel, chunks, len(pieces), c == 0, last),
            [
                struct((level_windows * WT, channels), F32),
                struct((level_windows * WT, LANES), F32),
                struct((level_windows * WT, channels), BF16),
                struct((level_windows * WT, channels), F32),
                struct((level_windows * WT, channels), F32),
                struct((level_windows, WT, lon_count * chunks.width), BF16),
                struct((level_windows, WT, lon_count * chunks.width), BF16),
            ]
            + sums,
            (*pieces, gain, inproj_weight, outproj_weight, bias_t, order, *total),
            flops=10**9,
        )
        per_window.append(results[:7])
        total = results[7:]
    wide = struct((level_windows, half, channels), BF16)
    grads = []
    for c in reversed(range(windows)):
        order = jnp.asarray(window_order(cols, c, True).T, BF16)
        ins = (*per_window[c], gain, inproj_weight, order)
        if c == windows - 1:
            results = call(
                functools.partial(first_kernel, chunks),
                [wide, wide, struct((level_windows, side_table.shape[0], channels), BF16)]
                + [struct((packed, LANES), BF16)] * lon_count,
                (*ins, *total),
            )
            left = shift(results[2], 0, 1)
            arrived = [results[3]]
            for d in sorted(range(1, lon_count), key=lambda d: -d.bit_count()):
                pairs = [(i, partner(i, d, lon_count)) for i in range(lon_count)]
                arrived.append(lax.ppermute(results[3 + d], "lon", pairs))
        else:
            results = call(functools.partial(tokens_kernel, chunks, False), [wide] * 2, (*ins, *grads))
        grads = results[:2]
    g_inner, g_below = call(
        merge_kernel,
        [wide, struct((half, level_windows * channels), BF16)],
        (*grads, left, jnp.asarray(side_table.T, BF16)),
    )
    above = shift(g_below, 1, 0)
    bias_grad, after = call(
        functools.partial(bias_kernel, chunks),
        [struct((level_windows * heads * chunks.size, 1, WT), F32), struct((8, LANES), F32)],
        arrived,
    )
    (grad_input,) = call(join_kernel, [struct(tokens.shape, BF16)], (g_inner, above, after))
    bias_grad = bias_grad.reshape(level_windows, heads, chunks.size, 1, WT)
    return grad_input, jnp.transpose(bias_grad, (0, 3, 1, 2, 4))


def solution(mesh):
    placed = (
        P(None, "lat", "lon", None),
        P(None, "lat", "lon", None),
        P(),
        P(),
        P(),
        P(None, "lat", None, None, None),
    )
    return jax.shard_map(
        local,
        mesh=mesh,
        in_specs=placed,
        out_specs=(P(None, "lat", "lon", None), P(None, "lat", None, "lon", None)),
        check_vma=False,
    )
```

```python
import functools

import jax
import jax.numpy as jnp
import numpy as np
from jax import lax
from jax.experimental import pallas as pl
from jax.experimental.pallas import tpu as pltpu
from jax.sharding import PartitionSpec as P

WZ = 2
WH = 6
WW = 12
WT = WZ * WH * WW
HALF_ROWS = WH // 2
HALF_COLS = WW // 2
SIDE = 8
LEVEL = WH * WW
LANES = 128
LOG2E = 1.4426950408889634
epsilon = 1e-05
F32 = jnp.float32
BF16 = jnp.bfloat16
NT = (((1,), (1,)), ((), ()))


def dot(a, b):
    return jnp.dot(a, b, preferred_element_type=F32)


def dot_nt(a, b):
    return lax.dot_general(a, b, NT, preferred_element_type=F32)


def round_up(value, to):
    return (value + to - 1) // to * to


class Chunks:
    def __init__(self, parts, heads):
        self.parts, self.heads = parts, heads
        self.size = WT // parts
        self.main = self.size // 16 * 16
        self.rest = self.size - self.main
        self.rest_rows = round_up(heads * self.rest, 16)
        self.rows = self.main + self.rest_rows
        self.used = heads * self.main + self.rest_rows
        self.width = round_up(self.used, LANES)

    def columns(self, j):
        lane = lax.broadcasted_iota(jnp.int32, (1, self.width), 1)
        low = self.heads * self.main
        main, left = lane, self.main + lane - low
        for h in range(1, self.heads):
            main -= jnp.where(lane >= h * self.main, self.main, 0)
            left -= jnp.where(lane >= low + h * self.rest, self.rest, 0)
        return j * self.size + jnp.where(lane < low, main, left)


def side_order(cols):
    part = HALF_ROWS * cols
    table = np.zeros((round_up(WZ * WH * HALF_COLS, 16), 2 * WZ * part), np.float32)
    for z in range(WZ):
        for r in range(WH):
            low, row = divmod(r, HALF_ROWS)
            for w in range(HALF_COLS):
                table[(z * WH + r) * HALF_COLS + w, (low * WZ + z) * part + row * cols + w] = 1.0
    return table


def window_order(cols, c, out):
    last = c == cols // WW - 1
    part, side = HALF_ROWS * cols, HALF_ROWS * SIDE
    kept = cols if out else cols - HALF_COLS
    tail = last and not out
    inner = WZ * (side if tail else part)
    near = inner + round_up(WZ * HALF_ROWS * kept, 16)
    extra = round_up(WZ * WH * HALF_COLS, 16) if out else 2 * WZ * side
    table = np.zeros((WT, near + last * extra), np.float32)
    for z in range(WZ):
        for r in range(WH):
            for w in range(WW):
                col = c * WW + w + HALF_COLS
                low, row = divmod(r, HALF_ROWS)
                if col >= cols and out:
                    at = near + (z * WH + r) * HALF_COLS + col - cols
                elif col >= cols:
                    at = near + (low * WZ + z) * side + row * SIDE + col - cols
                elif low:
                    at = inner + (z * HALF_ROWS + row) * kept + col - (cols - kept)
                elif tail:
                    at = z * side + row * SIDE + col - (cols - SIDE)
                else:
                    at = z * part + row * cols + col
                table[(z * WH + r) * WW + w, at] = 1.0
    return table


def level_rows(field, a, base):
    levels = field.shape[0]
    at = [(a * WZ + WZ // 2 + z) % levels for z in range(WZ)]
    return [field[level, base + row].astype(F32) for level in at for row in range(HALF_ROWS)]


def send_kernel(both, inner, below, right, corner, tail):
    cols = both.shape[2]
    kept = cols - HALF_COLS
    shape = (below.shape[1], WZ * HALF_ROWS * cols)
    row = lax.broadcasted_iota(jnp.int32, shape, 0)
    target = row + HALF_COLS
    for i in range(1, WZ * HALF_ROWS):
        target += jnp.where(row >= i * kept, HALF_COLS, 0)
    kept_rows = (lax.broadcasted_iota(jnp.int32, shape, 1) == target) & (row < WZ * HALF_ROWS * kept)
    narrow = kept_rows.astype(F32).astype(BF16)
    for a in range(inner.shape[0]):
        low, high = level_rows(both, a, 0), level_rows(both, a, HALF_ROWS)
        below[a] = dot(narrow, jnp.concatenate(low, axis=0).astype(BF16)).astype(BF16)
        inner[a] = jnp.concatenate(high, axis=0).astype(BF16)
        right[a] = jnp.concatenate([row[:SIDE] for row in high], axis=0).astype(BF16)
        tail[a] = jnp.concatenate([row[cols - SIDE :] for row in high], axis=0).astype(BF16)
        corner[a] = jnp.concatenate([row[:SIDE] for row in low], axis=0).astype(BF16)


def prep_kernel(chunks, lat_count, bias, bias_t):
    level_windows = bias.shape[0]
    last_lat = lax.axis_index("lat") == lat_count - 1
    parts, size, main = chunks.parts, chunks.size, chunks.main

    def labels(index, window):
        level_label = (index >= LEVEL) & (window == level_windows - 1)
        in_level = jnp.where(index >= LEVEL, index - LEVEL, index)
        row_label = (in_level >= LEVEL // 2) & last_lat
        return level_label.astype(jnp.int32) * 2 + row_label.astype(jnp.int32)

    key_index = lax.broadcasted_iota(jnp.int32, (WT, chunks.width), 0)
    for window in range(level_windows):
        key_labels = labels(key_index, window)
        for j in range(parts):
            heads = range(chunks.heads)
            low = j * size
            rows = []
            if main:
                rows += [bias[window, h, low : low + main, :] for h in heads]
            if chunks.rest:
                rows += [bias[window, h, low + main : low + size, :] for h in heads]
            spare = chunks.width - chunks.heads * size
            if spare:
                rows.append(jnp.zeros((spare, WT), F32))
            turned = jnp.transpose(jnp.concatenate(rows, axis=0)) * LOG2E
            allowed = key_labels == labels(chunks.columns(j), window)
            bias_t[window, j] = jnp.where(allowed, turned, -1e30)


def head_masks(chunks, channels):
    head_dim = channels // chunks.heads
    lane_head = lax.broadcasted_iota(jnp.int32, (1, channels), 1) // head_dim
    lanes = [lane_head == h for h in range(chunks.heads)]
    rest = None
    if chunks.rest:
        row = lax.broadcasted_iota(jnp.int32, (chunks.rest_rows, channels), 0)
        lane = lax.broadcasted_iota(jnp.int32, (chunks.rest_rows, channels), 1) // head_dim
        rest = jnp.zeros((chunks.rest_rows, channels), F32)
        for h in range(chunks.heads):
            inside = (row >= h * chunks.rest) & (row < (h + 1) * chunks.rest) & (lane == h)
            rest = jnp.where(inside, 1.0, rest)
    return lanes, rest


def stack_heads(chunks, value, j, lane_masks, rest_mask):
    low = j * chunks.size
    pieces = []
    if chunks.main:
        main = value[low : low + chunks.main].astype(BF16)
        pieces += [main * mask for mask in lane_masks]
    if chunks.rest:
        rows = [value[low + chunks.main : low + chunks.size]] * chunks.heads
        spare = chunks.rest_rows - chunks.heads * chunks.rest
        if spare:
            rows.append(jnp.zeros((spare, value.shape[1]), F32))
        pieces.append(jnp.concatenate(rows, axis=0).astype(BF16) * rest_mask)
    if chunks.width > chunks.used:
        pieces.append(jnp.zeros((chunks.width - chunks.used, value.shape[1]), BF16))
    return jnp.concatenate(pieces, axis=0)


def split(inproj):
    channels = inproj.shape[0]
    return [inproj[:, part * channels : (part + 1) * channels] for part in range(3)]


def pack(columns):
    used = columns[0].shape[1]
    whole = used // LANES * LANES
    tiles = [part[:, i : i + LANES] for part in columns for i in range(0, whole, LANES)]
    left = jnp.concatenate([part[:, whole:] for part in columns], axis=1)
    while left.shape[1] >= LANES:
        tiles.append(left[:, :LANES])
        left = left[:, LANES:]
    if left.shape[1]:
        tiles.append(jnp.concatenate([left[: WT // 2, : LANES // 2], left[WT // 2 :, : LANES // 2]], axis=1))
    return jnp.concatenate(tiles, axis=0)


def unpack(rows, many, used):
    whole = used // LANES
    tiles = [rows[i * WT : (i + 1) * WT] for i in range(rows.shape[0] // WT)]
    left = tiles[many * whole :]
    if rows.shape[0] % WT:
        last = rows[len(tiles) * WT :]
        left.append(jnp.concatenate([last[:, : LANES // 2], last[:, LANES // 2 :]], axis=0))
    left = jnp.concatenate(left, axis=1) if left else None
    rest = used - whole * LANES
    columns = []
    for a in range(many):
        part = tiles[a * whole : (a + 1) * whole]
        if rest:
            part.append(left[:, a * rest : (a + 1) * rest])
        columns.append(jnp.concatenate(part, axis=1))
    return columns


def partner(me, d, parts):
    return me ^ d if parts & (parts - 1) == 0 else (me + d) % parts


def scores_kernel(chunks, near, first, last, *refs):
    pieces, refs = refs[:near], refs[near:]
    gain_ref, inproj, outproj, bias_t, perm, *refs = refs
    weights = split(inproj)
    before = None
    if not first:
        before, *refs = refs
    standard_out, scale_out, keys_out, query_out, up_out, p_out, ds_out, total_out = refs
    parts, width = chunks.parts, chunks.width
    channels = outproj.shape[0]
    scaling = (channels // chunks.heads) ** (-0.5)
    lanes, rest_mask = head_masks(chunks, channels)
    lanes = [mask.astype(F32).astype(BF16) for mask in lanes]
    rest_mask = rest_mask.astype(BF16) if chunks.rest else None
    me = lax.axis_index("lon")
    level_windows = pieces[0].shape[0]
    tile = channels // LANES * LANES
    from_tile = jnp.concatenate([jnp.zeros((channels, channels - tile), BF16), outproj[...]], axis=1)
    ts, us = [], []
    for a in range(level_windows):
        moved = dot(perm[...], jnp.concatenate([piece[a] for piece in pieces], axis=0))
        ts.append(moved[:, :channels])
        us.append(dot_nt(moved[:, tile:].astype(BF16), from_tile))
    t = jnp.concatenate(ts, axis=0)
    centred = t - jnp.mean(t, axis=-1, keepdims=True)
    inverse_rms = lax.rsqrt(jnp.mean(centred * centred, axis=-1, keepdims=True) + epsilon)
    standard = centred * inverse_rms
    standard_out[...] = standard
    scale_out[...] = jnp.broadcast_to(inverse_rms, scale_out.shape)
    normed = (standard * gain_ref[...]).astype(BF16)
    q = dot(normed, weights[0])
    query_out[...] = q
    k = dot(normed, weights[1]).astype(BF16)
    v = dot(normed, weights[2]).astype(BF16)
    keys_out[...] = k
    for a in range(level_windows):
        cut = slice(a * WT, (a + 1) * WT)
        query, up = q[cut], us[a]
        up_out[cut] = up
        for d in range(parts):
            at = slice(d * width, (d + 1) * width)
            s = dot_nt(k[cut], stack_heads(chunks, query, d, lanes, rest_mask))
            dp = dot_nt(v[cut], stack_heads(chunks, up, d, lanes, rest_mask))
            e = jnp.exp2(s * (scaling * LOG2E) + bias_t[a, d])
            p = e * (1.0 / jnp.sum(e, axis=0, keepdims=True))
            ds = p * (dp - jnp.sum(p * dp, axis=0, keepdims=True))
            p_out[a, :, at] = p.astype(BF16)
            ds_out[a, :, at] = ds.astype(BF16)
            if not first:
                ds += before[a, d]
            if last:
                total_out[a, d] = ds
            else:
                total_out[a, d] = ds


def tokens_kernel(chunks, first, *refs):
    standard_in, scale_in, keys, queries_in, ups, p_in, ds_in, gain_ref, inproj, perm_t, *refs = refs
    weights = split(inproj)
    before = None
    if not first:
        before, refs = refs[:2], refs[2:]
    outs = refs
    parts, width = chunks.parts, chunks.width
    channels = keys.shape[-1]
    head_dim = channels // chunks.heads
    scaling = head_dim ** (-0.5)
    lanes, rest_mask = head_masks(chunks, channels)
    low_lanes = [mask.astype(F32).astype(BF16) for mask in lanes]
    low_rest = rest_mask.astype(BF16) if chunks.rest else None
    level_windows = p_in.shape[0]
    dqs, dks, dvs = [], [], []
    for a in range(level_windows):
        cut = slice(a * WT, (a + 1) * WT)
        query, up = queries_in[cut], ups[cut]
        qs = jnp.concatenate(
            [stack_heads(chunks, query, d, low_lanes, low_rest) for d in range(parts)], axis=0
        )
        us = jnp.concatenate(
            [stack_heads(chunks, up, d, low_lanes, low_rest) for d in range(parts)], axis=0
        )
        ds = ds_in[a]
        dks.append((dot(ds, qs) * scaling).astype(BF16))
        dvs.append(dot(p_in[a], us).astype(BF16))
        turned = jnp.transpose(ds)
        key = keys[a * WT : (a + 1) * WT]
        main = []
        for lane in range(0, channels, LANES):
            low = lane // head_dim
            many = min(LANES // head_dim, chunks.heads - low)
            if not chunks.main:
                break
            some = [turned[d * width + low * chunks.main :][: many * chunks.main] for d in range(parts)]
            flat = dot(jnp.concatenate(some, axis=0), key[:, lane : lane + LANES])
            tiles = []
            for d in range(parts):
                picked = flat[d * many * chunks.main :][: chunks.main]
                for h in range(1, many):
                    mask = lanes[low + h][:, lane : lane + LANES]
                    picked = jnp.where(mask, flat[(d * many + h) * chunks.main :][: chunks.main], picked)
                tiles.append(picked)
            main.append(tiles)
        if chunks.rest:
            low = chunks.heads * chunks.main
            some = [turned[d * width + low :][: chunks.rest_rows] for d in range(parts)]
            left = dot(jnp.concatenate(some, axis=0), key)
        rows = []
        for d in range(parts):
            if chunks.main:
                rows.append(jnp.concatenate([tiles[d] for tiles in main], axis=1))
            if chunks.rest:
                some = left[d * chunks.rest_rows : (d + 1) * chunks.rest_rows] * rest_mask
                total = some[: chunks.rest]
                for h in range(1, chunks.heads):
                    total += some[h * chunks.rest : (h + 1) * chunks.rest]
                rows.append(total)
        dqs.append((jnp.concatenate(rows, axis=0) * scaling).astype(BF16))
    dq, dk, dv = (jnp.concatenate(parts_of, axis=0) for parts_of in (dqs, dks, dvs))
    scaled = (dot_nt(dq, weights[0]) + dot_nt(dk, weights[1]) + dot_nt(dv, weights[2])) * gain_ref[...]
    standard = standard_in[...]
    inverse_rms = scale_in[:, :1]
    grad = inverse_rms * (
        scaled
        - jnp.mean(scaled, axis=-1, keepdims=True)
        - standard * jnp.mean(scaled * standard, axis=-1, keepdims=True)
    )
    grad = grad.astype(BF16)
    for a in range(level_windows):
        spread = dot(perm_t[...], grad[a * WT : (a + 1) * WT])
        base = 0
        for i, out in enumerate(outs):
            rows = out.shape[1]
            part = spread[base : base + rows]
            if not first and i < 2:
                part += before[i][a].astype(F32)
            out[a] = part.astype(BF16)
            base += rows


def first_kernel(chunks, *refs):
    *ins, total, inner, below, side = refs[:14]
    messages = refs[14:]
    me = lax.axis_index("lon")
    for d, message in enumerate(messages):
        j = partner(me, d, chunks.parts)
        columns = [total[a, j][:, : chunks.used] for a in range(total.shape[0])]
        message[...] = pack(columns).astype(BF16)
    tokens_kernel(chunks, True, *ins, inner, below, side)


def last_kernel(chunks, near, *refs):
    many = near + 6
    ins, order, refs = refs[:many], refs[many], refs[many + 1 :]
    outs, kept = refs[: 3 + chunks.parts], refs[3 + chunks.parts :]
    scores_kernel(chunks, near, False, True, *ins, *kept)
    first_kernel(chunks, *kept[:7], ins[near], ins[near + 1], order, kept[7], *outs)


def merge_kernel(inner_in, below_in, side, order_t, inner, below):
    half = inner.shape[1]
    lows = []
    for a in range(inner.shape[0]):
        spread = dot(order_t[...], side[a])
        inner[a] = (inner_in[a].astype(F32) + spread[:half]).astype(BF16)
        lows.append(below_in[a].astype(F32) + spread[half:])
    packed = [low[:, :LANES] for low in lows] + [low[:, LANES:] for low in lows]
    below[...] = jnp.concatenate(packed, axis=1).astype(BF16)


def join_kernel(inner, below, after, grad_input):
    levels, _, cols, channels = grad_input.shape
    level_windows = levels // WZ
    whole = below[...].astype(F32)
    for a in range(level_windows):
        rest_at = level_windows * LANES + a * (channels - LANES)
        low = jnp.concatenate(
            [whole[:, a * LANES : (a + 1) * LANES], whole[:, rest_at : rest_at + channels - LANES]], axis=1
        )
        high = inner[a].astype(F32)
        for z in range(WZ):
            level = (a * WZ + WZ // 2 + z) % levels
            for row in range(HALF_ROWS):
                at = slice((z * HALF_ROWS + row) * cols, (z * HALF_ROWS + row + 1) * cols)
                grad_input[level, row] = low[at].astype(BF16)
                grad_input[level, HALF_ROWS + row] = high[at].astype(BF16)


def bias_kernel(chunks, *refs):
    *arrived, bias_grad, after = refs
    after[...] = jnp.zeros(after.shape, F32)
    main, rest, heads = chunks.main, chunks.rest, chunks.heads
    total = arrived[0][...].astype(F32)
    for other in arrived[1:]:
        total += other[...].astype(F32)
    many = bias_grad.shape[0] // (heads * chunks.size)
    for a, columns in enumerate(unpack(total, many, chunks.used)):
        turned = jnp.transpose(columns)
        for h in range(heads):
            at = (a * heads + h) * chunks.size
            if main:
                bias_grad[at : at + main, 0, :] = turned[h * main : (h + 1) * main]
            if rest:
                low = heads * main + h * rest
                bias_grad[at + main : at + chunks.size, 0, :] = turned[low : low + rest]


def vmem(count):
    return [pl.BlockSpec(memory_space=pltpu.VMEM)] * count


def call(kernel, outs, args, flops=0, scratch=()):
    return pl.pallas_call(
        kernel,
        out_shape=outs,
        in_specs=vmem(len(args)),
        out_specs=vmem(len(outs)),
        scratch_shapes=list(scratch),
        compiler_params=pltpu.CompilerParams(vmem_limit_bytes=40 * 2**20),
        cost_estimate=pl.CostEstimate(flops=flops, bytes_accessed=0, transcendentals=0),
    )(*args)


def shift(value, rows, cols):
    lat_count, lon_count = lax.axis_size("lat"), lax.axis_size("lon")
    pairs = []
    for i in range(lat_count):
        for j in range(lon_count):
            to = (i + rows) % lat_count * lon_count + (j + cols) % lon_count
            pairs.append((i * lon_count + j, to))
    return lax.ppermute(value, ("lat", "lon"), pairs)


def local(tokens, cotangent, norm_gain, inproj_weight, outproj_weight, bias):
    levels, rows, cols, channels = tokens.shape
    level_windows, _, heads = bias.shape[:3]
    lat_count, lon_count = lax.axis_size("lat"), lax.axis_size("lon")
    chunks = Chunks(lon_count, heads)
    windows = cols // WW
    struct = jax.ShapeDtypeStruct
    half, side = WZ * HALF_ROWS * cols, WZ * HALF_ROWS * SIDE
    gain = norm_gain.reshape(1, channels)
    side_table = side_order(cols)

    bias = bias.reshape(level_windows, heads, WT, WT)
    both = jnp.concatenate([tokens, cotangent], axis=-1)
    narrow = round_up(WZ * HALF_ROWS * (cols - HALF_COLS), 16)
    inner, below, right, corner, tail = call(
        send_kernel,
        [struct((level_windows, size, 2 * channels), BF16) for size in (half, narrow, side, side, side)],
        (both,),
    )
    below = shift(below, -1, 0)
    right = shift(right, 0, -1)
    corner = shift(corner, -1, -1)
    (bias_t,) = call(
        functools.partial(prep_kernel, chunks, lat_count),
        [struct((level_windows, lon_count, WT, chunks.width), F32)],
        (bias,),
    )
    packed = level_windows * chunks.used * WT // LANES
    per_window = []
    total = []
    for c in range(windows):
        last = c == windows - 1
        pieces = (tail, below, right, corner) if last else (inner, below)
        sums = [struct((level_windows, lon_count, WT, chunks.width), F32)]
        order = jnp.asarray(window_order(cols, c, False), BF16)
        kept = (
            [
                struct((level_windows * WT, channels), F32),
                struct((level_windows * WT, LANES), F32),
                struct((level_windows * WT, channels), BF16),
                struct((level_windows * WT, channels), F32),
                struct((level_windows * WT, channels), F32),
                struct((level_windows, WT, lon_count * chunks.width), BF16),
                struct((level_windows, WT, lon_count * chunks.width), BF16),
            ]
            + sums
        )
        ins = (*pieces, gain, inproj_weight, outproj_weight, bias_t, order, *total)
        if last:
            break
        results = call(
            functools.partial(scores_kernel, chunks, len(pieces), c == 0, last), kept, ins, flops=10**9
        )
        per_window.append(results[:7])
        total = results[7:]
    wide = struct((level_windows, half, channels), BF16)
    grads = []
    for c in reversed(range(windows)):
        order = jnp.asarray(window_order(cols, c, True).T, BF16)
        if c == windows - 1:
            results = call(
                functools.partial(last_kernel, chunks, len(pieces)),
                [wide, wide, struct((level_windows, side_table.shape[0], channels), BF16)]
                + [struct((packed, LANES), BF16)] * lon_count,
                (*ins, order),
                scratch=[pltpu.VMEM(part.shape, part.dtype) for part in kept],
            )
            left = shift(results[2], 0, 1)
            arrived = [results[3]]
            for d in range(1, lon_count):
                pairs = [(i, partner(i, d, lon_count)) for i in range(lon_count)]
                arrived.append(lax.ppermute(results[3 + d], "lon", pairs))
        else:
            ins = (*per_window[c], gain, inproj_weight, order)
            results = call(functools.partial(tokens_kernel, chunks, False), [wide] * 2, (*ins, *grads))
        grads = results[:2]
    g_inner, g_below = call(
        merge_kernel,
        [wide, struct((half, level_windows * channels), BF16)],
        (*grads, left, jnp.asarray(side_table.T, BF16)),
    )
    above = shift(g_below, 1, 0)
    bias_grad, after = call(
        functools.partial(bias_kernel, chunks),
        [struct((level_windows * heads * chunks.size, 1, WT), F32), struct((8, LANES), F32)],
        arrived,
    )
    (grad_input,) = call(join_kernel, [struct(tokens.shape, BF16)], (g_inner, above, after))
    bias_grad = bias_grad.reshape(level_windows, heads, chunks.size, 1, WT)
    return grad_input, jnp.transpose(bias_grad, (0, 3, 1, 2, 4))


def solution(mesh):
    placed = (
        P(None, "lat", "lon", None),
        P(None, "lat", "lon", None),
        P(),
        P(),
        P(),
        P(None, "lat", None, None, None),
    )
    return jax.shard_map(
        local,
        mesh=mesh,
        in_specs=placed,
        out_specs=(P(None, "lat", "lon", None), P(None, "lat", None, "lon", None)),
        check_vma=False,
    )
```

```python
import functools

import jax
import jax.numpy as jnp
import numpy as np
from jax import lax
from jax.experimental import pallas as pl
from jax.experimental.pallas import tpu as pltpu
from jax.sharding import PartitionSpec as P

WZ = 2
WH = 6
WW = 12
WT = WZ * WH * WW
HALF_ROWS = WH // 2
HALF_COLS = WW // 2
SIDE = 8
LEVEL = WH * WW
LANES = 128
LOG2E = 1.4426950408889634
epsilon = 1e-05
F32 = jnp.float32
BF16 = jnp.bfloat16
NT = (((1,), (1,)), ((), ()))


def dot(a, b):
    return jnp.dot(a, b, preferred_element_type=F32)


def dot_nt(a, b):
    return lax.dot_general(a, b, NT, preferred_element_type=F32)


def round_up(value, to):
    return (value + to - 1) // to * to


class Chunks:
    def __init__(self, parts, heads):
        self.parts, self.heads = parts, heads
        self.size = WT // parts
        self.main = self.size // 16 * 16
        self.rest = self.size - self.main
        self.rest_rows = round_up(heads * self.rest, 16)
        self.rows = self.main + self.rest_rows
        self.used = heads * self.main + self.rest_rows
        self.width = round_up(self.used, LANES)

    def columns(self, j):
        lane = lax.broadcasted_iota(jnp.int32, (1, self.width), 1)
        low = self.heads * self.main
        main, left = lane, self.main + lane - low
        for h in range(1, self.heads):
            main -= jnp.where(lane >= h * self.main, self.main, 0)
            left -= jnp.where(lane >= low + h * self.rest, self.rest, 0)
        return j * self.size + jnp.where(lane < low, main, left)


def side_order(cols):
    part = HALF_ROWS * cols
    table = np.zeros((round_up(WZ * WH * HALF_COLS, 16), 2 * WZ * part), np.float32)
    for z in range(WZ):
        for r in range(WH):
            low, row = divmod(r, HALF_ROWS)
            for w in range(HALF_COLS):
                table[(z * WH + r) * HALF_COLS + w, (low * WZ + z) * part + row * cols + w] = 1.0
    return table


def window_order(cols, c, out):
    last = c == cols // WW - 1
    part, side = HALF_ROWS * cols, HALF_ROWS * SIDE
    kept = cols if out else cols - HALF_COLS
    tail = last and not out
    inner = WZ * (side if tail else part)
    near = inner + round_up(WZ * HALF_ROWS * kept, 16)
    extra = round_up(WZ * WH * HALF_COLS, 16) if out else 2 * WZ * side
    table = np.zeros((WT, near + last * extra), np.float32)
    for z in range(WZ):
        for r in range(WH):
            for w in range(WW):
                col = c * WW + w + HALF_COLS
                low, row = divmod(r, HALF_ROWS)
                if col >= cols and out:
                    at = near + (z * WH + r) * HALF_COLS + col - cols
                elif col >= cols:
                    at = near + (low * WZ + z) * side + row * SIDE + col - cols
                elif low:
                    at = inner + (z * HALF_ROWS + row) * kept + col - (cols - kept)
                elif tail:
                    at = z * side + row * SIDE + col - (cols - SIDE)
                else:
                    at = z * part + row * cols + col
                table[(z * WH + r) * WW + w, at] = 1.0
    return table


def level_rows(field, a, base):
    levels = field.shape[0]
    at = [(a * WZ + WZ // 2 + z) % levels for z in range(WZ)]
    return [field[level, base + row].astype(F32) for level in at for row in range(HALF_ROWS)]


def send_kernel(both, inner, below, right, corner, tail):
    cols = both.shape[2]
    kept = cols - HALF_COLS
    shape = (below.shape[1], WZ * HALF_ROWS * cols)
    row = lax.broadcasted_iota(jnp.int32, (shape[0], 1), 0)
    target = row + HALF_COLS
    for i in range(1, WZ * HALF_ROWS):
        target += jnp.where(row >= i * kept, HALF_COLS, 0)
    kept_rows = (lax.broadcasted_iota(jnp.int32, shape, 1) == target) & (row < WZ * HALF_ROWS * kept)
    narrow = kept_rows.astype(F32).astype(BF16)
    for a in range(inner.shape[0]):
        low, high = level_rows(both, a, 0), level_rows(both, a, HALF_ROWS)
        below[a] = dot(narrow, jnp.concatenate(low, axis=0).astype(BF16)).astype(BF16)
        inner[a] = jnp.concatenate(high, axis=0).astype(BF16)
        right[a] = jnp.concatenate([row[:SIDE] for row in high], axis=0).astype(BF16)
        tail[a] = jnp.concatenate([row[cols - SIDE :] for row in high], axis=0).astype(BF16)
        corner[a] = jnp.concatenate([row[:SIDE] for row in low], axis=0).astype(BF16)


def prep_kernel(chunks, lat_count, bias, bias_t):
    level_windows = bias.shape[0]
    last_lat = lax.axis_index("lat") == lat_count - 1
    parts, size, main = chunks.parts, chunks.size, chunks.main

    def labels(index, window):
        level_label = (index >= LEVEL) & (window == level_windows - 1)
        in_level = jnp.where(index >= LEVEL, index - LEVEL, index)
        row_label = (in_level >= LEVEL // 2) & last_lat
        return level_label.astype(jnp.int32) * 2 + row_label.astype(jnp.int32)

    key_index = lax.broadcasted_iota(jnp.int32, (WT, chunks.width), 0)
    for window in range(level_windows):
        key_labels = labels(key_index, window)
        for j in range(parts):
            heads = range(chunks.heads)
            low = j * size
            rows = []
            if main:
                rows += [bias[window, h, low : low + main, :] for h in heads]
            if chunks.rest:
                rows += [bias[window, h, low + main : low + size, :] for h in heads]
            spare = chunks.width - chunks.heads * size
            if spare:
                rows.append(jnp.zeros((spare, WT), F32))
            turned = jnp.transpose(jnp.concatenate(rows, axis=0)) * LOG2E
            allowed = key_labels == labels(chunks.columns(j), window)
            bias_t[window, j] = jnp.where(allowed, turned, -1e30)


def head_masks(chunks, channels):
    head_dim = channels // chunks.heads
    lane_head = lax.broadcasted_iota(jnp.int32, (1, channels), 1) // head_dim
    lanes = [lane_head == h for h in range(chunks.heads)]
    rest = None
    if chunks.rest:
        row = lax.broadcasted_iota(jnp.int32, (chunks.rest_rows, channels), 0)
        lane = lax.broadcasted_iota(jnp.int32, (chunks.rest_rows, channels), 1) // head_dim
        rest = jnp.zeros((chunks.rest_rows, channels), F32)
        for h in range(chunks.heads):
            inside = (row >= h * chunks.rest) & (row < (h + 1) * chunks.rest) & (lane == h)
            rest = jnp.where(inside, 1.0, rest)
    return lanes, rest


def stack_heads(chunks, value, j, lane_masks, rest_mask):
    low = j * chunks.size
    pieces = []
    if chunks.main:
        main = value[low : low + chunks.main].astype(BF16)
        pieces += [main * mask for mask in lane_masks]
    if chunks.rest:
        rows = [value[low + chunks.main : low + chunks.size]] * chunks.heads
        spare = chunks.rest_rows - chunks.heads * chunks.rest
        if spare:
            rows.append(jnp.zeros((spare, value.shape[1]), F32))
        pieces.append(jnp.concatenate(rows, axis=0).astype(BF16) * rest_mask)
    if chunks.width > chunks.used:
        pieces.append(jnp.zeros((chunks.width - chunks.used, value.shape[1]), BF16))
    return jnp.concatenate(pieces, axis=0)


def split(inproj):
    channels = inproj.shape[0]
    return [inproj[:, part * channels : (part + 1) * channels] for part in range(3)]


def pack(columns):
    used = columns[0].shape[1]
    whole = used // LANES * LANES
    tiles = [part[:, i : i + LANES] for part in columns for i in range(0, whole, LANES)]
    left = jnp.concatenate([part[:, whole:] for part in columns], axis=1)
    while left.shape[1] >= LANES:
        tiles.append(left[:, :LANES])
        left = left[:, LANES:]
    if left.shape[1]:
        tiles.append(jnp.concatenate([left[: WT // 2, : LANES // 2], left[WT // 2 :, : LANES // 2]], axis=1))
    return jnp.concatenate(tiles, axis=0)


def unpack(rows, many, used):
    whole = used // LANES
    tiles = [rows[i * WT : (i + 1) * WT] for i in range(rows.shape[0] // WT)]
    left = tiles[many * whole :]
    if rows.shape[0] % WT:
        last = rows[len(tiles) * WT :]
        left.append(jnp.concatenate([last[:, : LANES // 2], last[:, LANES // 2 :]], axis=0))
    left = jnp.concatenate(left, axis=1) if left else None
    rest = used - whole * LANES
    columns = []
    for a in range(many):
        part = tiles[a * whole : (a + 1) * whole]
        if rest:
            part.append(left[:, a * rest : (a + 1) * rest])
        columns.append(jnp.concatenate(part, axis=1))
    return columns


def partner(me, d, parts):
    return me ^ d if parts & (parts - 1) == 0 else (me + d) % parts


def scores_kernel(chunks, near, first, last, *refs):
    pieces, refs = refs[:near], refs[near:]
    gain_ref, inproj, outproj, bias_t, perm, *refs = refs
    weights = split(inproj)
    before = None
    if not first:
        before, *refs = refs
    standard_out, scale_out, keys_out, query_out, up_out, p_out, ds_out, total_out = refs
    parts, width = chunks.parts, chunks.width
    channels = outproj.shape[0]
    scaling = (channels // chunks.heads) ** (-0.5)
    lanes, rest_mask = head_masks(chunks, channels)
    lanes = [mask.astype(F32).astype(BF16) for mask in lanes]
    rest_mask = rest_mask.astype(BF16) if chunks.rest else None
    me = lax.axis_index("lon")
    level_windows = pieces[0].shape[0]
    tile = channels // LANES * LANES
    from_tile = jnp.concatenate([jnp.zeros((channels, channels - tile), BF16), outproj[...]], axis=1)
    ts, us = [], []
    for a in range(level_windows):
        moved = dot(perm[...], jnp.concatenate([piece[a] for piece in pieces], axis=0))
        ts.append(moved[:, :channels])
        us.append(dot_nt(moved[:, tile:].astype(BF16), from_tile))
    t = jnp.concatenate(ts, axis=0)
    centred = t - jnp.mean(t, axis=-1, keepdims=True)
    inverse_rms = lax.rsqrt(jnp.mean(centred * centred, axis=-1, keepdims=True) + epsilon)
    standard = centred * inverse_rms
    standard_out[...] = standard
    scale_out[...] = jnp.broadcast_to(inverse_rms, scale_out.shape)
    normed = (standard * gain_ref[...]).astype(BF16)
    q = dot(normed, weights[0])
    query_out[...] = q
    k = dot(normed, weights[1]).astype(BF16)
    v = dot(normed, weights[2]).astype(BF16)
    keys_out[...] = k
    for a in range(level_windows):
        cut = slice(a * WT, (a + 1) * WT)
        query, up = q[cut], us[a]
        up_out[cut] = up
        for d in range(parts):
            at = slice(d * width, (d + 1) * width)
            s = dot_nt(k[cut], stack_heads(chunks, query, d, lanes, rest_mask))
            dp = dot_nt(v[cut], stack_heads(chunks, up, d, lanes, rest_mask))
            e = jnp.exp2(s * (scaling * LOG2E) + bias_t[a, d])
            p = e * (1.0 / jnp.sum(e, axis=0, keepdims=True))
            ds = p * (dp - jnp.sum(p * dp, axis=0, keepdims=True))
            p_out[a, :, at] = p.astype(BF16)
            ds_out[a, :, at] = ds.astype(BF16)
            if not first:
                ds += before[a, d]
            if last:
                total_out[a, d] = ds
            else:
                total_out[a, d] = ds


def tokens_kernel(chunks, first, *refs):
    standard_in, scale_in, keys, queries_in, ups, p_in, ds_in, gain_ref, inproj, perm_t, *refs = refs
    weights = split(inproj)
    before = None
    if not first:
        before, refs = refs[:2], refs[2:]
    outs = refs
    parts, width = chunks.parts, chunks.width
    channels = keys.shape[-1]
    head_dim = channels // chunks.heads
    scaling = head_dim ** (-0.5)
    lanes, rest_mask = head_masks(chunks, channels)
    low_lanes = [mask.astype(F32).astype(BF16) for mask in lanes]
    low_rest = rest_mask.astype(BF16) if chunks.rest else None
    level_windows = p_in.shape[0]
    dqs, dks, dvs = [], [], []
    for a in range(level_windows):
        cut = slice(a * WT, (a + 1) * WT)
        query, up = queries_in[cut], ups[cut]
        qs = jnp.concatenate(
            [stack_heads(chunks, query, d, low_lanes, low_rest) for d in range(parts)], axis=0
        )
        us = jnp.concatenate(
            [stack_heads(chunks, up, d, low_lanes, low_rest) for d in range(parts)], axis=0
        )
        ds = ds_in[a]
        dks.append((dot(ds, qs) * scaling).astype(BF16))
        dvs.append(dot(p_in[a], us).astype(BF16))
        turned = jnp.transpose(ds)
        key = keys[a * WT : (a + 1) * WT]
        main = []
        for lane in range(0, channels, LANES):
            low = lane // head_dim
            many = min(LANES // head_dim, chunks.heads - low)
            if not chunks.main:
                break
            some = [turned[d * width + low * chunks.main :][: many * chunks.main] for d in range(parts)]
            flat = dot(jnp.concatenate(some, axis=0), key[:, lane : lane + LANES])
            tiles = []
            for d in range(parts):
                picked = flat[d * many * chunks.main :][: chunks.main]
                for h in range(1, many):
                    mask = lanes[low + h][:, lane : lane + LANES]
                    picked = jnp.where(mask, flat[(d * many + h) * chunks.main :][: chunks.main], picked)
                tiles.append(picked)
            main.append(tiles)
        if chunks.rest:
            low = chunks.heads * chunks.main
            some = [turned[d * width + low :][: chunks.rest_rows] for d in range(parts)]
            left = dot(jnp.concatenate(some, axis=0), key)
        rows = []
        for d in range(parts):
            if chunks.main:
                rows.append(jnp.concatenate([tiles[d] for tiles in main], axis=1))
            if chunks.rest:
                some = left[d * chunks.rest_rows : (d + 1) * chunks.rest_rows] * rest_mask
                total = some[: chunks.rest]
                for h in range(1, chunks.heads):
                    total += some[h * chunks.rest : (h + 1) * chunks.rest]
                rows.append(total)
        dqs.append((jnp.concatenate(rows, axis=0) * scaling).astype(BF16))
    dq, dk, dv = (jnp.concatenate(parts_of, axis=0) for parts_of in (dqs, dks, dvs))
    scaled = (dot_nt(dq, weights[0]) + dot_nt(dk, weights[1]) + dot_nt(dv, weights[2])) * gain_ref[...]
    standard = standard_in[...]
    inverse_rms = scale_in[:, :1]
    grad = inverse_rms * (
        scaled
        - jnp.mean(scaled, axis=-1, keepdims=True)
        - standard * jnp.mean(scaled * standard, axis=-1, keepdims=True)
    )
    grad = grad.astype(BF16)
    for a in range(level_windows):
        spread = dot(perm_t[...], grad[a * WT : (a + 1) * WT])
        base = 0
        for i, out in enumerate(outs):
            rows = out.shape[1]
            part = spread[base : base + rows]
            if not first and i < 2:
                part += before[i][a].astype(F32)
            out[a] = part.astype(BF16)
            base += rows


def first_kernel(chunks, *refs):
    *ins, total, inner, below, side = refs[:14]
    messages = refs[14:]
    me = lax.axis_index("lon")
    for d, message in enumerate(messages):
        j = partner(me, d, chunks.parts)
        columns = [total[a, j][:, : chunks.used] for a in range(total.shape[0])]
        message[...] = pack(columns).astype(BF16)
    tokens_kernel(chunks, True, *ins, inner, below, side)


def last_kernel(chunks, near, *refs):
    many = near + 6
    ins, order, refs = refs[:many], refs[many], refs[many + 1 :]
    outs, kept = refs[: 3 + chunks.parts], refs[3 + chunks.parts :]
    scores_kernel(chunks, near, False, True, *ins, *kept)
    first_kernel(chunks, *kept[:7], ins[near], ins[near + 1], order, kept[7], *outs)


def merge_kernel(inner_in, below_in, side, order_t, inner, below):
    half = inner.shape[1]
    lows = []
    for a in range(inner.shape[0]):
        spread = dot(order_t[...], side[a])
        inner[a] = (inner_in[a].astype(F32) + spread[:half]).astype(BF16)
        lows.append(below_in[a].astype(F32) + spread[half:])
    packed = [low[:, :LANES] for low in lows] + [low[:, LANES:] for low in lows]
    below[...] = jnp.concatenate(packed, axis=1).astype(BF16)


def join_kernel(inner, below, after, grad_input):
    levels, _, cols, channels = grad_input.shape
    level_windows = levels // WZ
    whole = below[...].astype(F32)
    for a in range(level_windows):
        rest_at = level_windows * LANES + a * (channels - LANES)
        low = jnp.concatenate(
            [whole[:, a * LANES : (a + 1) * LANES], whole[:, rest_at : rest_at + channels - LANES]], axis=1
        )
        high = inner[a].astype(F32)
        for z in range(WZ):
            level = (a * WZ + WZ // 2 + z) % levels
            for row in range(HALF_ROWS):
                at = slice((z * HALF_ROWS + row) * cols, (z * HALF_ROWS + row + 1) * cols)
                grad_input[level, row] = low[at].astype(BF16)
                grad_input[level, HALF_ROWS + row] = high[at].astype(BF16)


def bias_kernel(chunks, *refs):
    *arrived, bias_grad, after = refs
    after[...] = jnp.zeros(after.shape, F32)
    main, rest, heads = chunks.main, chunks.rest, chunks.heads
    total = arrived[0][...].astype(F32)
    for other in arrived[1:]:
        total += other[...].astype(F32)
    many = bias_grad.shape[0] // (heads * chunks.size)
    for a, columns in enumerate(unpack(total, many, chunks.used)):
        turned = jnp.transpose(columns)
        for h in range(heads):
            at = (a * heads + h) * chunks.size
            if main:
                bias_grad[at : at + main, 0, :] = turned[h * main : (h + 1) * main]
            if rest:
                low = heads * main + h * rest
                bias_grad[at + main : at + chunks.size, 0, :] = turned[low : low + rest]


def vmem(count):
    return [pl.BlockSpec(memory_space=pltpu.VMEM)] * count


def call(kernel, outs, args, flops=0, scratch=()):
    return pl.pallas_call(
        kernel,
        out_shape=outs,
        in_specs=vmem(len(args)),
        out_specs=vmem(len(outs)),
        scratch_shapes=list(scratch),
        compiler_params=pltpu.CompilerParams(vmem_limit_bytes=40 * 2**20),
        cost_estimate=pl.CostEstimate(flops=flops, bytes_accessed=0, transcendentals=0),
    )(*args)


def shift(value, rows, cols):
    lat_count, lon_count = lax.axis_size("lat"), lax.axis_size("lon")
    pairs = []
    for i in range(lat_count):
        for j in range(lon_count):
            to = (i + rows) % lat_count * lon_count + (j + cols) % lon_count
            pairs.append((i * lon_count + j, to))
    return lax.ppermute(value, ("lat", "lon"), pairs)


def local(tokens, cotangent, norm_gain, inproj_weight, outproj_weight, bias):
    levels, rows, cols, channels = tokens.shape
    level_windows, _, heads = bias.shape[:3]
    lat_count, lon_count = lax.axis_size("lat"), lax.axis_size("lon")
    chunks = Chunks(lon_count, heads)
    windows = cols // WW
    struct = jax.ShapeDtypeStruct
    half, side = WZ * HALF_ROWS * cols, WZ * HALF_ROWS * SIDE
    gain = norm_gain.reshape(1, channels)
    side_table = side_order(cols)

    bias = bias.reshape(level_windows, heads, WT, WT)
    both = jnp.concatenate([tokens, cotangent], axis=-1)
    narrow = round_up(WZ * HALF_ROWS * (cols - HALF_COLS), 16)
    inner, below, right, corner, tail = call(
        send_kernel,
        [struct((level_windows, size, 2 * channels), BF16) for size in (half, narrow, side, side, side)],
        (both,),
    )
    below = shift(below, -1, 0)
    right = shift(right, 0, -1)
    corner = shift(corner, -1, -1)
    (bias_t,) = call(
        functools.partial(prep_kernel, chunks, lat_count),
        [struct((level_windows, lon_count, WT, chunks.width), F32)],
        (bias,),
    )
    packed = level_windows * chunks.used * WT // LANES
    per_window = []
    total = []
    for c in range(windows):
        last = c == windows - 1
        pieces = (tail, below, right, corner) if last else (inner, below)
        sums = [struct((level_windows, lon_count, WT, chunks.width), F32)]
        order = jnp.asarray(window_order(cols, c, False), BF16)
        kept = (
            [
                struct((level_windows * WT, channels), F32),
                struct((level_windows * WT, LANES), F32),
                struct((level_windows * WT, channels), BF16),
                struct((level_windows * WT, channels), F32),
                struct((level_windows * WT, channels), F32),
                struct((level_windows, WT, lon_count * chunks.width), BF16),
                struct((level_windows, WT, lon_count * chunks.width), BF16),
            ]
            + sums
        )
        ins = (*pieces, gain, inproj_weight, outproj_weight, bias_t, order, *total)
        if last:
            break
        results = call(
            functools.partial(scores_kernel, chunks, len(pieces), c == 0, last), kept, ins, flops=10**9
        )
        per_window.append(results[:7])
        total = results[7:]
    wide = struct((level_windows, half, channels), BF16)
    grads = []
    for c in reversed(range(windows)):
        order = jnp.asarray(window_order(cols, c, True).T, BF16)
        if c == windows - 1:
            results = call(
                functools.partial(last_kernel, chunks, len(pieces)),
                [wide, wide, struct((level_windows, side_table.shape[0], channels), BF16)]
                + [struct((packed, LANES), BF16)] * lon_count,
                (*ins, order),
                scratch=[pltpu.VMEM(part.shape, part.dtype) for part in kept],
            )
            left = shift(results[2], 0, 1)
            arrived = [results[3]]
            for d in range(1, lon_count):
                pairs = [(i, partner(i, d, lon_count)) for i in range(lon_count)]
                arrived.append(lax.ppermute(results[3 + d], "lon", pairs))
        else:
            ins = (*per_window[c], gain, inproj_weight, order)
            results = call(functools.partial(tokens_kernel, chunks, False), [wide] * 2, (*ins, *grads))
        grads = results[:2]
    g_inner, g_below = call(
        merge_kernel,
        [wide, struct((half, level_windows * channels), BF16)],
        (*grads, left, jnp.asarray(side_table.T, BF16)),
    )
    above = shift(g_below, 1, 0)
    bias_grad, after = call(
        functools.partial(bias_kernel, chunks),
        [struct((level_windows * heads * chunks.size, 1, WT), F32), struct((8, LANES), F32)],
        arrived,
    )
    (grad_input,) = call(join_kernel, [struct(tokens.shape, BF16)], (g_inner, above, after))
    bias_grad = bias_grad.reshape(level_windows, heads, chunks.size, 1, WT)
    return grad_input, jnp.transpose(bias_grad, (0, 3, 1, 2, 4))


def solution(mesh):
    placed = (
        P(None, "lat", "lon", None),
        P(None, "lat", "lon", None),
        P(),
        P(),
        P(),
        P(None, "lat", None, None, None),
    )
    return jax.shard_map(
        local,
        mesh=mesh,
        in_specs=placed,
        out_specs=(P(None, "lat", "lon", None), P(None, "lat", None, "lon", None)),
        check_vma=False,
    )
```
